32 devices in a mesh: rows: 8 (over y, x, core), rep: 4 (over z).
Axes of the slice: x: 2, y: 2, z: 4, core: 2. Of those that a mesh axis runs over, the one named last changes fastest.
Arguments:
- node_feats: bfloat16 [8192, 256], P('rows'), may hold values from -6 to 6
- weight: bfloat16 [256, 256], replicated, may hold values from -0.375 to 0.375
- cotangent: bfloat16 [8192, 256], P('rows'), may hold values from -6 to 6
- tile_values: bfloat16 [8, 5, 32, 128, 128], P('rows', None, 'rep'), may hold values from -1 to 1, as said below
- tile_coords: int32 [2, 8, 5, 32], P(None, 'rows', None, 'rep'), may hold values from 0 to 7, as said below
- tile_counts: int32 [8, 5], P('rows'), may hold values from 0 to 32, as said below
Outputs:
- activated: bfloat16 [8192, 256], P('rows')
- input_grad: bfloat16 [8192, 256], P('rows')
- weight_grad: float32 [256, 256], replicated
The draws below stay inside these ranges and needn't reach their ends.
Inputs may be any that keep to these rules, and one draw needn't show every extreme that they name: tile_counts[r, d] = tile_counts[(r + d - 2) mod 8, 4 - d]; tile_counts[r, 2] = 32. tile_coords[0, r, d, k] = tile_coords[1, s, 4 - d, k] and tile_coords[1, r, d, k] = tile_coords[0, s, 4 - d, k] with s = (r + d - 2) mod 8, for d other than 2; for d = 2, slots 2m and 2m + 1 hold swapped coordinates. tile_values[r, d, k] is the transpose of tile_values[s, 4 - d, k] with s as above for d other than 2; for d = 2, slot 2m + 1 is the transpose of slot 2m.
All inputs are finite; a program needn't handle non-finite values.
Results may differ from the reference program's by a relative error of at most 0.006.
Values may be sent and summed in bfloat16 or wider, within the bound.
No kernel may reach another device: no remote copies, remote signals or barrier semaphores. Data moves between devices by JAX's collectives and lax.ppermute only.
A program may use at most 64 MiB of HBM per device.

```python
import jax
import jax.numpy as jnp
from jax import lax

F = 256
TILE = 128
BLK = 8
HOPS = 2
SLOT_DEV = 8
REACH = 5
SLOTS = 32
GROUPS = 8
NODES = 8192


def partner_index():
    index = jnp.arange(GROUPS, dtype=jnp.int32)
    offsets = jnp.arange(REACH, dtype=jnp.int32)
    joined = (index[:, None] + offsets[None, :] - HOPS) % GROUPS
    mirror = jnp.broadcast_to(2 * HOPS - offsets[None, :], (GROUPS, REACH))
    return (joined, mirror, offsets)


def pair_layout(key):
    combos = BLK * BLK
    joined, mirror, offsets = partner_index()
    hub = jax.random.randint(jax.random.fold_in(key, 11), (GROUPS,), 0, 3).astype(jnp.int32)
    pick = jax.random.randint(jax.random.fold_in(key, 12), (GROUPS, REACH), 0, SLOTS + 1).astype(jnp.int32)
    base = jnp.clip(pick + hub[:, None] * SLOT_DEV, 0, SLOTS)
    low = offsets[None, :] < HOPS
    centre = offsets[None, :] == HOPS
    counts = jnp.where(low, base, jnp.where(centre, SLOTS, base[joined, mirror])).astype(jnp.int32)
    scores = jax.random.randint(jax.random.fold_in(key, 13), (GROUPS, REACH, combos), 0, 1 << 20).astype(jnp.int32)
    scores = scores * combos + jnp.arange(combos, dtype=jnp.int32)
    order = jnp.argsort(scores, axis=-1)[:, :, :SLOTS].astype(jnp.int32)
    first = order // BLK
    second = order % BLK
    slot = jnp.arange(SLOTS, dtype=jnp.int32)
    odd = (slot % 2 == 1)[None, None, :]
    half_first = first[:, :, slot // 2]
    half_second = second[:, :, slot // 2]
    diag_row = jnp.where(odd, half_second, half_first)
    diag_col = jnp.where(odd, half_first, half_second)
    row_coord = jnp.where(low[:, :, None], first, jnp.where(centre[:, :, None], diag_row, second[joined, mirror]))
    col_coord = jnp.where(low[:, :, None], second, jnp.where(centre[:, :, None], diag_col, first[joined, mirror]))
    return (counts, jnp.stack([row_coord, col_coord]).astype(jnp.int32))


def draw_tile_counts(key, part):
    counts, coords = pair_layout(key)
    return counts


def draw_tile_coords(key, part):
    counts, coords = pair_layout(key)
    return coords


def draw_tile_values(key, part):
    shape = (GROUPS, REACH, SLOTS, TILE, TILE)
    raw = jnp.clip(jax.random.normal(jax.random.fold_in(key, 21), shape, jnp.float32), -6.0, 6.0)
    joined, mirror, offsets = partner_index()
    low = (offsets < HOPS)[None, :, None, None, None]
    centre = (offsets == HOPS)[None, :, None, None, None]
    mirrored = jnp.swapaxes(raw[joined, mirror], 3, 4)
    slot = jnp.arange(SLOTS, dtype=jnp.int32)
    odd = (slot % 2 == 1)[None, None, :, None, None]
    paired = raw[:, :, slot - slot % 2]
    diag = jnp.where(odd, jnp.swapaxes(paired, 3, 4), paired)
    sym = jnp.where(low, raw, jnp.where(centre, diag, mirrored))
    return (sym * (REACH * SLOTS * TILE // BLK) ** (-0.5)).astype(jnp.bfloat16)


def steps_of(stream_key, shape, split, smallest, largest):
    def one(dim, parts):
        draws = jax.random.uniform(jax.random.fold_in(jax.random.fold_in(stream_key, 6), dim), (parts,), jnp.float32, smallest / len(split), largest / len(split))
        return jnp.repeat(jnp.exp(draws), shape[dim] // parts).reshape((-1,) + (1,) * (len(shape) - dim - 1))

    level = one(*split[0])
    for cut in split[1:]:
        level = level * one(*cut)
    return level


def normal_values(stream_key, dims, scale, most, cuts=(), kind=jnp.bfloat16):
    drawn = jax.random.normal(stream_key, dims, jnp.float32) * scale
    if len(cuts) > 0:
        drawn = steps_of(stream_key, dims, cuts, -0.22, 0.18) * drawn
    return jnp.clip(drawn, min=-most, max=most).astype(kind)


def setup_inputs(seed: int = 0) -> dict:
    streams_of = jax.random.split(jax.random.key(seed), 7)
    return {
        "node_feats": normal_values(streams_of[0], (NODES, F), 1.0, 6.0, ((0, 8),)),
        "weight": normal_values(streams_of[1], (F, F), F ** -0.5, 0.375),
        "cotangent": normal_values(streams_of[2], (NODES, F), 1.0, 6.0, ((0, 8),)),
        "tile_values": draw_tile_values(jax.random.fold_in(streams_of[6], 71), 0),
        "tile_coords": draw_tile_coords(jax.random.fold_in(streams_of[6], 71), 0),
        "tile_counts": draw_tile_counts(jax.random.fold_in(streams_of[6], 71), 0),
    }


def silu_slope(value):
    sig = jax.nn.sigmoid(value)
    return sig * (1.0 + value * (1.0 - sig))


def propagate(tile_values, tile_coords, tile_counts, source):
    panels = source.reshape(GROUPS, BLK, TILE, F)
    group_ids = jnp.arange(GROUPS, dtype=jnp.int32)
    offsets = jnp.arange(REACH, dtype=jnp.int32)
    slot_ids = jnp.arange(SLOTS, dtype=jnp.int32)
    block_ids = jnp.arange(BLK, dtype=jnp.int32)

    def one_group(items):
        group, values_row, rows_row, cols_row, count_row = items
        joined = (group + offsets - HOPS) % GROUPS
        picked = panels[joined[:, None], cols_row.astype(jnp.int32)]
        product = jnp.einsum("dkuv,dkvf->dkuf", values_row.astype(jnp.float32), picked.astype(jnp.float32), precision=lax.Precision.HIGHEST)
        live = slot_ids[None, :] < count_row[:, None]
        place = ((rows_row[:, :, None] == block_ids[None, None, :]) & live[:, :, None]).astype(jnp.float32)
        return jnp.einsum("dkb,dkuf->buf", place, product, precision=lax.Precision.HIGHEST)

    summed = lax.map(one_group, (group_ids, tile_values, tile_coords[0], tile_coords[1], tile_counts))
    return summed.reshape(NODES, F)


def reference(node_feats, weight, cotangent, tile_values, tile_coords, tile_counts):
    transformed = jnp.dot(node_feats, weight, preferred_element_type=jnp.float32).astype(jnp.bfloat16)
    aggregated = propagate(tile_values, tile_coords, tile_counts, transformed)
    activated = jax.nn.silu(aggregated).astype(jnp.bfloat16)
    adjoint = (cotangent.astype(jnp.float32) * silu_slope(aggregated)).astype(jnp.bfloat16)
    back_sum = propagate(tile_values, tile_coords, tile_counts, adjoint).astype(jnp.bfloat16)
    weight_grad = jnp.dot(node_feats.T, back_sum, preferred_element_type=jnp.float32) * (NODES ** -0.5)
    input_grad = jnp.dot(back_sum, weight.T, preferred_element_type=jnp.float32).astype(jnp.bfloat16)
    return activated, input_grad, weight_grad
```

```python
import functools

import jax
import jax.numpy as jnp
from jax import lax
from jax.experimental import pallas as pl
from jax.experimental.pallas import tpu as pltpu
from jax.sharding import PartitionSpec as P

AXES = ("rows", "rep")


def route(shape, move):
    chips, reps = shape
    pairs = []
    for c in range(chips):
        for j in range(2):
            for z in range(reps):
                to = move(c, j, z)
                if to is not None:
                    target = ((to[0] % chips) * 2 + to[1]) * reps + to[2]
                    pairs.append(((c * 2 + j) * reps + z, target))
    return pairs


def tile_kernel(blocks, dsel_ref, meta_a_ref, meta_b_ref, own_ref, first_ref, second_ref, *refs):
    panels = refs[:5]
    out_ref = refs[5]
    acc_ref = refs[6]
    tile = own_ref.shape[-1]
    slots = own_ref.shape[1]
    mine = dsel_ref[5] == 1
    acc_ref[...] = jnp.zeros_like(acc_ref)
    for i in range(5):
        d = dsel_ref[i]
        for k in range(slots):
            for use_first in (False, True):
                if use_first:
                    values = first_ref[d, k]
                    meta = meta_b_ref
                else:
                    values = jnp.where(mine, own_ref[d, k], second_ref[d, k])
                    meta = meta_a_ref
                row = pl.multiple_of(meta[0, d * slots + k] * tile, tile)
                col = pl.multiple_of(meta[1, d * slots + k] * tile, tile)
                prod = jnp.dot(
                    values, panels[i][pl.ds(col, tile), :], preferred_element_type=jnp.float32
                )
                acc_ref[pl.ds(row, tile), :] += prod
    out_ref[...] = acc_ref[: blocks * tile, :].astype(out_ref.dtype)


def tile_product(dsel, meta_a, meta_b, own, first, second, panels):
    rows, width = panels[0].shape
    tile = own.shape[-1]
    blocks = rows // tile
    smem = pl.BlockSpec(memory_space=pltpu.SMEM)
    vmem = pl.BlockSpec(memory_space=pltpu.VMEM)
    count = own.shape[0] * own.shape[1] * 2
    return pl.pallas_call(
        functools.partial(tile_kernel, blocks),
        out_shape=jax.ShapeDtypeStruct((rows, width), jnp.bfloat16),
        in_specs=[smem] * 3 + [vmem] * 8,
        out_specs=vmem,
        scratch_shapes=[pltpu.VMEM(((blocks + 1) * tile, width), jnp.float32)],
        compiler_params=pltpu.CompilerParams(vmem_limit_bytes=32 * 1024 * 1024),
        cost_estimate=pl.CostEstimate(
            flops=2 * count * tile * tile * width,
            bytes_accessed=count * tile * tile * 3 + 6 * rows * width * 2,
            transcendentals=0,
        ),
        name="tile_product",
    )(dsel, meta_a, meta_b, own, first, second, *panels)


def middle_kernel(near_ref, far_ref, w_near_ref, w_far_ref, cot_ref, act_ref, adj_ref):
    agg = jnp.dot(near_ref[...], w_near_ref[...], preferred_element_type=jnp.float32)
    agg += jnp.dot(far_ref[...], w_far_ref[...], preferred_element_type=jnp.float32)
    sig = jax.nn.sigmoid(agg)
    act_ref[...] = (agg * sig).astype(act_ref.dtype)
    slope = sig * (1.0 + agg * (1.0 - sig))
    adj_ref[...] = (cot_ref[...].astype(jnp.float32) * slope).astype(adj_ref.dtype)


def middle(near, far, w_near, w_far, cot):
    vmem = pl.BlockSpec(memory_space=pltpu.VMEM)
    rows, width = near.shape
    out = jax.ShapeDtypeStruct((rows, width), jnp.bfloat16)
    return pl.pallas_call(
        middle_kernel,
        out_shape=(out, out),
        in_specs=[vmem] * 5,
        out_specs=(vmem, vmem),
        compiler_params=pltpu.CompilerParams(vmem_limit_bytes=32 * 1024 * 1024),
        cost_estimate=pl.CostEstimate(
            flops=4 * rows * width * width,
            bytes_accessed=10 * rows * width,
            transcendentals=rows * width,
        ),
        name="middle",
    )(near, far, w_near, w_far, cot)


def final_kernel(flag_ref, self_ref, one_ref, two_ref, w_near_ref, w_far_ref, out_ref):
    mine = flag_ref[0] == 1
    near = jnp.where(mine, self_ref[...], one_ref[...])
    far = jnp.where(mine, one_ref[...], two_ref[...])
    dims = (((1,), (1,)), ((), ()))
    total = lax.dot_general(near, w_near_ref[...], dims, preferred_element_type=jnp.float32)
    total += lax.dot_general(far, w_far_ref[...], dims, preferred_element_type=jnp.float32)
    out_ref[...] = total.astype(out_ref.dtype)


def final(flag, own, one, two, w_near, w_far):
    smem = pl.BlockSpec(memory_space=pltpu.SMEM)
    vmem = pl.BlockSpec(memory_space=pltpu.VMEM)
    rows = own.shape[0]
    wide = w_near.shape[0]
    return pl.pallas_call(
        final_kernel,
        out_shape=jax.ShapeDtypeStruct((rows, wide), jnp.bfloat16),
        in_specs=[smem] + [vmem] * 5,
        out_specs=vmem,
        compiler_params=pltpu.CompilerParams(vmem_limit_bytes=32 * 1024 * 1024),
        cost_estimate=pl.CostEstimate(
            flops=2 * rows * wide * wide, bytes_accessed=8 * rows * wide, transcendentals=0
        ),
        name="final",
    )(flag, own, one, two, w_near, w_far)


def per_device(node_feats, weight, cotangent, tile_values, tile_coords, tile_counts):
    groups = lax.axis_size("rows")
    reps = lax.axis_size("rep")
    shape = (groups // 2, reps)
    r = lax.axis_index("rows")
    z = lax.axis_index("rep")
    j = r % 2
    p = z % 2
    a = z // 2
    home = j == p
    scale = (node_feats.shape[0] * groups) ** (-0.5)
    half = node_feats.shape[1] // 2

    def send(value, move):
        return lax.ppermute(value, AXES, route(shape, move))

    def split(value):
        low, high = value[:, :half], value[:, half:]
        return jnp.where(j == 0, low, high), jnp.where(j == 0, high, low)

    def sibling(c, j, z):
        return (c, 1 - j, z)

    def across(c, j, z):
        return (c, j, (z + reps // 2) % reps)

    own = tile_values[0]
    slots = own.shape[1]
    slot_ids = z * slots + jnp.arange(slots, dtype=jnp.int32)
    blocks = node_feats.shape[0] // own.shape[-1]
    live = slot_ids[None, :] < tile_counts[0][:, None]
    meta = jnp.stack([jnp.where(live, tile_coords[0, 0], blocks), tile_coords[1, 0]])
    meta = meta.reshape(2, -1)

    def to_home(c, j, z):
        return (c, 1 - j, z) if j == z % 2 else (c, j, z ^ 1)

    def forward_x(c, j, z):
        return (c + 1, j, z) if j == z % 2 or z % 2 == 0 else (c - 1, j, z)

    def forward_x_cross(c, j, z):
        to = forward_x(c, j, z)
        return (to[0], 1 - j, to[2])

    mine, yours = split(node_feats)
    swapped = send(yours, sibling)
    one = send(mine, forward_x)
    two = send(yours, forward_x_cross)
    first = send(own, to_home)
    meta_b = send(meta, to_home)
    meta_far = send(meta, lambda c, j, z: None if j == z % 2 else (c, 1 - j, z ^ 1))
    group_half = jnp.where(home, mine, swapped)
    right = send(group_half, lambda c, j, z: (c - 1, j, z))
    second = send(first, lambda c, j, z: (c, 1 - j, z) if j == z % 2 else None)
    meta_a = jnp.where(home, meta, meta_far)
    cot_mine, cot_yours = split(cotangent)
    cot = jnp.where(home, cot_mine, send(cot_yours, sibling))

    d_other = jnp.where(p == 0, 3, 1)
    d_third = jnp.where(p == 0, 1, 3)
    flag = home.astype(jnp.int32)
    dsel = jnp.stack(
        [
            jnp.where(home, 2, d_other),
            jnp.where(home, d_other, 2),
            jnp.where(home, 0, d_third),
            jnp.where(home, d_third, 0),
            jnp.asarray(4),
            flag,
        ]
    ).astype(jnp.int32)
    part = tile_product(
        dsel, meta_a, meta_b, own, first, second, [mine, swapped, one, two, right]
    )

    def join(value):
        other = send(value, across)
        return (value.astype(jnp.float32) + other.astype(jnp.float32)).astype(jnp.bfloat16)

    near = join(part)
    far = send(near, sibling)
    w_cols, _ = split(weight)
    w_near = jnp.where(j == 0, w_cols[:half], w_cols[half:])
    w_far = jnp.where(j == 0, w_cols[half:], w_cols[:half])
    act, adj = middle(near, far, w_near, w_far, cot)

    dsel_back = jnp.stack([jnp.asarray(2), d_other, jnp.asarray(0), jnp.asarray(4), d_third, flag])
    dsel_back = dsel_back.astype(jnp.int32)
    left = send(adj, lambda c, j, z: (c + 1, j, z))
    right = send(adj, lambda c, j, z: (c - 1, j, z))
    third = send(adj, lambda c, j, z: (c + 1 if z % 2 else c - 1, j, z ^ 1))
    other = send(adj, lambda c, j, z: (c, j, z ^ 1))
    back_part = tile_product(
        dsel_back, meta_a, meta_b, own, first, second, [adj, other, left, right, third]
    )

    def deliver(value):
        one = send(value, lambda c, j, z: (c, j, z ^ 1) if j == z % 2 else (c, 1 - j, z))
        two = send(value, lambda c, j, z: None if j == z % 2 else (c, 1 - j, z ^ 1))
        return one, two

    act_one, act_two = deliver(act)
    act_near = jnp.where(home, act, act_one)
    act_far = jnp.where(home, act_one, act_two)
    activated = jnp.concatenate(
        [jnp.where(j == 0, act_near, act_far), jnp.where(j == 0, act_far, act_near)], axis=1
    )

    contract = (((0,), (0,)), ((), ()))
    grad = lax.dot_general(
        jnp.where(a == j, near, far), adj, contract, preferred_element_type=jnp.float32
    )
    grad = grad + send(grad, lambda c, j, z: (c, j, z ^ 1))
    step = 1
    while step < shape[0]:
        grad = grad + send(grad, lambda c, j, z, s=step: (c ^ s, j, z))
        step *= 2
    grad = grad * scale
    grad_across = send(grad, across)
    tall = jnp.concatenate(
        [jnp.where(a == 0, grad, grad_across), jnp.where(a == 0, grad_across, grad)], axis=0
    )
    tall_far = send(tall, sibling)
    weight_grad = jnp.concatenate(
        [jnp.where(j == 0, tall, tall_far), jnp.where(j == 0, tall_far, tall)], axis=1
    )

    back = join(back_part)
    back_one, back_two = deliver(back)
    w_cols, w_rest = split(weight)
    input_grad = final(flag[None], back, back_one, back_two, w_cols, w_rest)
    return (activated, input_grad, weight_grad)


def solution(mesh):
    return jax.shard_map(
        per_device,
        mesh=mesh,
        in_specs=(
            P("rows", None),
            P(),
            P("rows", None),
            P("rows", None, "rep", None, None),
            P(None, "rows", None, "rep"),
            P("rows", None),
        ),
        out_specs=(P("rows", None), P("rows", None), P()),
        check_vma=False,
    )
```

```python
import functools

import jax
import jax.numpy as jnp
from jax import lax
from jax.experimental import pallas as pl
from jax.experimental.pallas import tpu as pltpu
from jax.sharding import PartitionSpec as P

AXES = ("rows", "rep")


def route(shape, move):
    chips, reps = shape
    pairs = []
    for c in range(chips):
        for j in range(2):
            for z in range(reps):
                to = move(c, j, z)
                if to is not None:
                    target = ((to[0] % chips) * 2 + to[1]) * reps + to[2]
                    pairs.append(((c * 2 + j) * reps + z, target))
    return pairs


def place():
    r = lax.axis_index("rows")
    z = lax.axis_index("rep")
    return r % 2, z, z % 2


def halves_kernel(x_ref, cot_ref, *refs):
    outs, sems = refs[:4], refs[4]
    j, _, _ = place()
    half = outs[0].shape[1]
    near = pl.ds(pl.multiple_of(j * half, half), half)
    far = pl.ds(pl.multiple_of((1 - j) * half, half), half)
    parts = ((x_ref, near), (x_ref, far), (cot_ref, near), (cot_ref, far))
    copies = []
    for i, (source, cols) in enumerate(parts):
        copy = pltpu.make_async_copy(source.at[:, cols], outs[i], sems.at[i])
        copy.start()
        copies.append(copy)
    for copy in copies:
        copy.wait()


def halves(feats, cot):
    rows, width = feats.shape
    part = jax.ShapeDtypeStruct((rows, width // 2), feats.dtype)
    vmem = pl.BlockSpec(memory_space=pltpu.VMEM)
    return pl.pallas_call(
        halves_kernel,
        out_shape=(part,) * 4,
        in_specs=[pl.BlockSpec(memory_space=pl.ANY)] * 2,
        out_specs=(vmem,) * 4,
        scratch_shapes=[pltpu.SemaphoreType.DMA((4,))],
        compiler_params=pltpu.CompilerParams(vmem_limit_bytes=16 * 1024 * 1024),
        name="halves",
    )(feats, cot)


def slots_kernel(dead, coords_ref, counts_ref, out_ref):
    _, z, _ = place()
    _, reach, slots = coords_ref.shape
    for d in range(reach):
        for k in range(slots):
            live = z * slots + k < counts_ref[d]
            out_ref[0, d * slots + k] = jnp.where(live, coords_ref[0, d, k], dead)
            out_ref[1, d * slots + k] = coords_ref[1, d, k]


def slot_blocks(coords, counts, dead):
    smem = pl.BlockSpec(memory_space=pltpu.SMEM)
    return pl.pallas_call(
        functools.partial(slots_kernel, dead),
        out_shape=jax.ShapeDtypeStruct((2, coords.shape[1] * coords.shape[2]), jnp.int32),
        in_specs=[smem, smem],
        out_specs=smem,
        name="slot_blocks",
    )(coords, counts)


def tile_kernel(blocks, dsel_ref, meta_a_ref, meta_b_ref, own_ref, first_ref, second_ref, *refs):
    panels, out_ref, acc_ref = refs[:-2], refs[-2], refs[-1]
    tile = own_ref.shape[-1]
    slots = own_ref.shape[1]
    j, _, p = place()
    home = j == p
    acc_ref[...] = jnp.zeros_like(acc_ref)
    for i in range(5):
        d = dsel_ref[i]
        for k in range(slots):
            for use_first in (False, True):
                if use_first:
                    values = first_ref[d, k]
                    meta = meta_b_ref
                else:
                    values = jnp.where(home, own_ref[d, k], second_ref[d, k])
                    meta = meta_a_ref
                row = pl.multiple_of(meta[0, d * slots + k] * tile, tile)
                col = pl.multiple_of(meta[1, d * slots + k] * tile, tile)
                source = panels[i][pl.ds(col, tile), :]
                if i == 4 and len(panels) == 6:
                    source = jnp.where(home, source, panels[5][pl.ds(col, tile), :])
                prod = jnp.dot(values, source, preferred_element_type=jnp.float32)
                acc_ref[pl.ds(row, tile), :] += prod
    out_ref[...] = acc_ref[: blocks * tile, :].astype(out_ref.dtype)


def tile_product(dsel, meta_a, meta_b, own, first, second, panels):
    rows, width = panels[0].shape
    tile = own.shape[-1]
    blocks = rows // tile
    smem = pl.BlockSpec(memory_space=pltpu.SMEM)
    vmem = pl.BlockSpec(memory_space=pltpu.VMEM)
    count = own.shape[0] * own.shape[1] * 2
    return pl.pallas_call(
        functools.partial(tile_kernel, blocks),
        out_shape=jax.ShapeDtypeStruct((rows, width), jnp.bfloat16),
        in_specs=[smem] * 3 + [vmem] * (3 + len(panels)),
        out_specs=vmem,
        scratch_shapes=[pltpu.VMEM(((blocks + 1) * tile, width), jnp.float32)],
        compiler_params=pltpu.CompilerParams(vmem_limit_bytes=32 * 1024 * 1024),
        cost_estimate=pl.CostEstimate(
            flops=2 * count * tile * tile * width,
            bytes_accessed=count * tile * tile * 3 + 6 * rows * width * 2,
            transcendentals=0,
        ),
        name="tile_product",
    )(dsel, meta_a, meta_b, own, first, second, *panels)


def middle_kernel(near_ref, far_ref, w_ref, cot_ref, cot_swap_ref, act_ref, adj_ref):
    j, _, p = place()
    half = near_ref.shape[1]
    near = pl.multiple_of(j * half, half)
    far = pl.multiple_of((1 - j) * half, half)
    cols = pl.ds(near, half)
    agg = jnp.dot(
        near_ref[...], w_ref[pl.ds(near, half), cols], preferred_element_type=jnp.float32
    )
    agg += jnp.dot(far_ref[...], w_ref[pl.ds(far, half), cols], preferred_element_type=jnp.float32)
    sig = jax.nn.sigmoid(agg)
    act_ref[...] = (agg * sig).astype(act_ref.dtype)
    slope = sig * (1.0 + agg * (1.0 - sig))
    cot = jnp.where(j == p, cot_ref[...], cot_swap_ref[...])
    adj_ref[...] = (cot.astype(jnp.float32) * slope).astype(adj_ref.dtype)


def middle(near, far, weight, cot, cot_swap):
    vmem = pl.BlockSpec(memory_space=pltpu.VMEM)
    rows, width = near.shape
    out = jax.ShapeDtypeStruct((rows, width), jnp.bfloat16)
    return pl.pallas_call(
        middle_kernel,
        out_shape=(out, out),
        in_specs=[vmem] * 5,
        out_specs=(vmem, vmem),
        compiler_params=pltpu.CompilerParams(vmem_limit_bytes=32 * 1024 * 1024),
        cost_estimate=pl.CostEstimate(
            flops=4 * rows * width * width,
            bytes_accessed=10 * rows * width,
            transcendentals=rows * width,
        ),
        name="middle",
    )(near, far, weight, cot, cot_swap)


def grad_kernel(scale, near_ref, far_ref, adj_ref, after_ref, out_ref):
    j, z, _ = place()
    lhs = jnp.where(z // 2 == j, near_ref[...], far_ref[...])
    dims = (((0,), (0,)), ((), ()))
    out_ref[...] = scale * lax.dot_general(
        lhs, adj_ref[...], dims, preferred_element_type=jnp.float32
    )


def grad_block(scale, near, far, adj, after):
    vmem = pl.BlockSpec(memory_space=pltpu.VMEM)
    rows, width = near.shape
    return pl.pallas_call(
        functools.partial(grad_kernel, scale),
        out_shape=jax.ShapeDtypeStruct((width, width), jnp.float32),
        in_specs=[vmem] * 3 + [pl.BlockSpec(memory_space=pl.ANY)],
        out_specs=vmem,
        compiler_params=pltpu.CompilerParams(vmem_limit_bytes=16 * 1024 * 1024),
        cost_estimate=pl.CostEstimate(
            flops=2 * rows * width * width, bytes_accessed=8 * rows * width, transcendentals=0
        ),
        name="grad_block",
    )(near, far, adj, after)


def final_kernel(self_ref, one_ref, two_ref, w_ref, out_ref):
    j, _, p = place()
    half = self_ref.shape[1]
    near = jnp.where(j == p, self_ref[...], one_ref[...])
    far = jnp.where(j == p, one_ref[...], two_ref[...])
    w_near = w_ref[:, pl.ds(pl.multiple_of(j * half, half), half)]
    w_far = w_ref[:, pl.ds(pl.multiple_of((1 - j) * half, half), half)]
    dims = (((1,), (1,)), ((), ()))
    total = lax.dot_general(near, w_near, dims, preferred_element_type=jnp.float32)
    total += lax.dot_general(far, w_far, dims, preferred_element_type=jnp.float32)
    out_ref[...] = total.astype(out_ref.dtype)


def final(own, one, two, weight):
    vmem = pl.BlockSpec(memory_space=pltpu.VMEM)
    rows = own.shape[0]
    wide = weight.shape[0]
    return pl.pallas_call(
        final_kernel,
        out_shape=jax.ShapeDtypeStruct((rows, wide), jnp.bfloat16),
        in_specs=[vmem] * 4,
        out_specs=vmem,
        compiler_params=pltpu.CompilerParams(vmem_limit_bytes=32 * 1024 * 1024),
        cost_estimate=pl.CostEstimate(
            flops=2 * rows * wide * wide, bytes_accessed=8 * rows * wide, transcendentals=0
        ),
        name="final",
    )(own, one, two, weight)


def per_device(node_feats, weight, cotangent, tile_values, tile_coords, tile_counts):
    groups = lax.axis_size("rows")
    reps = lax.axis_size("rep")
    shape = (groups // 2, reps)
    j, z, p = place()
    a = z // 2
    home = j == p
    scale = (node_feats.shape[0] * groups) ** (-0.5)

    def send(value, move):
        return lax.ppermute(value, AXES, route(shape, move))

    def sibling(c, j, z):
        return (c, 1 - j, z)

    def across(c, j, z):
        return (c, j, (z + reps // 2) % reps)

    def sibling_across(c, j, z):
        return (c, 1 - j, (z + reps // 2) % reps)

    own = tile_values[0]
    blocks = node_feats.shape[0] // own.shape[-1]

    def to_home(c, j, z):
        return (c, 1 - j, z) if j == z % 2 else (c, j, z ^ 1)

    def forward_x(c, j, z):
        return (c + 1, j, z) if j == z % 2 or z % 2 == 0 else (c - 1, j, z)

    def forward_x_cross(c, j, z):
        to = forward_x(c, j, z)
        return (to[0], 1 - j, to[2])

    first = send(own, to_home)
    mine, yours, cot, cot_yours = halves(node_feats, cotangent)
    one = send(mine, forward_x)
    two = send(yours, forward_x_cross)
    right = send(mine, lambda c, j, z: (c - 1, j, z) if j == z % 2 else None)
    right_cross = send(yours, lambda c, j, z: (c - 1, 1 - j, z) if j == z % 2 else None)
    swapped = send(yours, sibling)
    coords, counts, swapped = lax.optimization_barrier((tile_coords, tile_counts, swapped))
    meta = slot_blocks(coords[:, 0], counts[0], blocks)
    meta_b = send(meta, to_home)
    meta_far = send(meta, lambda c, j, z: None if j == z % 2 else (c, 1 - j, z ^ 1))
    cot_swap = send(cot_yours, sibling)
    first, one, two, right, right_cross, swapped, meta_b, meta_far = lax.optimization_barrier(
        (first, one, two, right, right_cross, swapped, meta_b, meta_far)
    )
    second = send(first, lambda c, j, z: (c, 1 - j, z) if j == z % 2 else None)
    meta_a = jnp.where(home, meta, meta_far)

    d_other = jnp.where(p == 0, 3, 1)
    d_third = jnp.where(p == 0, 1, 3)
    dsel = jnp.stack(
        [
            jnp.where(home, 2, d_other),
            jnp.where(home, d_other, 2),
            jnp.where(home, 0, d_third),
            jnp.where(home, d_third, 0),
            jnp.asarray(4),
        ]
    ).astype(jnp.int32)
    part = tile_product(
        dsel, meta_a, meta_b, own, first, second, [mine, swapped, one, two, right, right_cross]
    )

    def join(value):
        other = send(value, across)
        return (value.astype(jnp.float32) + other.astype(jnp.float32)).astype(jnp.bfloat16)

    near = join(part)
    far = send(near, sibling)
    act, adj = middle(near, far, weight, cot, cot_swap)

    dsel_back = jnp.stack([jnp.asarray(2), d_other, jnp.asarray(0), jnp.asarray(4), d_third])
    dsel_back = dsel_back.astype(jnp.int32)
    left = send(adj, lambda c, j, z: (c + 1, j, z))
    right = send(adj, lambda c, j, z: (c - 1, j, z))
    third = send(adj, lambda c, j, z: (c + 1 if z % 2 else c - 1, j, z ^ 1))
    other = send(adj, lambda c, j, z: (c, j, z ^ 1))
    back_part = tile_product(
        dsel_back, meta_a, meta_b, own, first, second, [adj, other, left, right, third]
    )

    def deliver(value):
        one = send(value, lambda c, j, z: (c, j, z ^ 1) if j == z % 2 else (c, 1 - j, z))
        two = send(value, lambda c, j, z: None if j == z % 2 else (c, 1 - j, z ^ 1))
        return one, two

    act_one, act_two = deliver(act)
    act_near = jnp.where(home, act, act_one)
    act_far = jnp.where(home, act_one, act_two)
    activated = jnp.concatenate(
        [jnp.where(j == 0, act_near, act_far), jnp.where(j == 0, act_far, act_near)], axis=1
    )

    back = join(back_part)
    back_one, back_two = deliver(back)
    input_grad = final(back, back_one, back_two, weight)

    grad = grad_block(scale, near, far, adj, other)
    step = 1
    while step < shape[0]:
        flips = [step] if step * 2 >= shape[0] else [step, 2 * step, 3 * step]
        got = [send(grad, lambda c, j, z, s=s: (c ^ s, j, z)) for s in flips]
        grad = grad + got[0]
        if len(got) == 3:
            grad = grad + (got[1] + got[2])
        step *= 2 if len(flips) == 1 else 4
    grad = grad + send(grad, lambda c, j, z: (c, j, z ^ 1))
    grad_across = send(grad, across)
    grad_sib = send(grad, sibling)
    grad_sib_across = send(grad, sibling_across)
    tall = jnp.concatenate(
        [jnp.where(a == 0, grad, grad_across), jnp.where(a == 0, grad_across, grad)], axis=0
    )
    tall_far = jnp.concatenate(
        [
            jnp.where(a == 0, grad_sib, grad_sib_across),
            jnp.where(a == 0, grad_sib_across, grad_sib),
        ],
        axis=0,
    )
    weight_grad = jnp.concatenate(
        [jnp.where(j == 0, tall, tall_far), jnp.where(j == 0, tall_far, tall)], axis=1
    )
    return (activated, input_grad, weight_grad)


def solution(mesh):
    return jax.shard_map(
        per_device,
        mesh=mesh,
        in_specs=(
            P("rows", None),
            P(),
            P("rows", None),
            P("rows", None, "rep", None, None),
            P(None, "rows", None, "rep"),
            P("rows", None),
        ),
        out_specs=(P("rows", None), P("rows", None), P()),
        check_vma=False,
    )
```

```python
import functools

import jax
import jax.numpy as jnp
from jax import lax
from jax.experimental import pallas as pl
from jax.experimental.pallas import tpu as pltpu
from jax.sharding import PartitionSpec as P

AXES = ("rows", "rep")


def route(shape, move):
    chips, reps = shape
    pairs = []
    for c in range(chips):
        for j in range(2):
            for z in range(reps):
                to = move(c, j, z)
                if to is not None:
                    target = ((to[0] % chips) * 2 + to[1]) * reps + to[2]
                    pairs.append(((c * 2 + j) * reps + z, target))
    return pairs


def place():
    r = lax.axis_index("rows")
    z = lax.axis_index("rep")
    return r % 2, z, z % 2


def halves_kernel(x_ref, near_ref, far_ref, sems):
    j, _, _ = place()
    half = near_ref.shape[1]
    copies = []
    for i, out in enumerate((near_ref, far_ref)):
        start = pl.multiple_of((j if i == 0 else 1 - j) * half, half)
        copy = pltpu.make_async_copy(x_ref.at[:, pl.ds(start, half)], out, sems.at[i])
        copy.start()
        copies.append(copy)
    for copy in copies:
        copy.wait()


def halves(value):
    rows, width = value.shape
    part = jax.ShapeDtypeStruct((rows, width // 2), value.dtype)
    hbm = pl.BlockSpec(memory_space=pltpu.HBM)
    return pl.pallas_call(
        halves_kernel,
        out_shape=(part, part),
        in_specs=[hbm],
        out_specs=(hbm, hbm),
        scratch_shapes=[pltpu.SemaphoreType.DMA((2,))],
        compiler_params=pltpu.CompilerParams(vmem_limit_bytes=1024 * 1024),
        name="halves",
    )(value)


def pick_kernel(home_ref, away_ref, out_ref, sem):
    j, _, p = place()

    @pl.when(j == p)
    def _():
        copy = pltpu.make_async_copy(home_ref, out_ref, sem)
        copy.start()
        copy.wait()

    @pl.when(j != p)
    def _():
        copy = pltpu.make_async_copy(away_ref, out_ref, sem)
        copy.start()
        copy.wait()


def pick(home, away):
    hbm = pl.BlockSpec(memory_space=pltpu.HBM)
    return pl.pallas_call(
        pick_kernel,
        out_shape=jax.ShapeDtypeStruct(home.shape, home.dtype),
        in_specs=[hbm, hbm],
        out_specs=hbm,
        scratch_shapes=[pltpu.SemaphoreType.DMA],
        compiler_params=pltpu.CompilerParams(vmem_limit_bytes=1024 * 1024),
        name="pick",
    )(home, away)


def slots_kernel(dead, coords_ref, counts_ref, out_ref):
    _, z, _ = place()
    _, reach, slots = coords_ref.shape
    for d in range(reach):
        for k in range(slots):
            live = z * slots + k < counts_ref[d]
            out_ref[0, d * slots + k] = jnp.where(live, coords_ref[0, d, k], dead)
            out_ref[1, d * slots + k] = coords_ref[1, d, k]


def slot_blocks(coords, counts, dead):
    smem = pl.BlockSpec(memory_space=pltpu.SMEM)
    return pl.pallas_call(
        functools.partial(slots_kernel, dead),
        out_shape=jax.ShapeDtypeStruct((2, coords.shape[1] * coords.shape[2]), jnp.int32),
        in_specs=[smem, smem],
        out_specs=smem,
        compiler_params=pltpu.CompilerParams(vmem_limit_bytes=1024 * 1024),
        name="slot_blocks",
    )(coords, counts)


def offset_of(kind):
    j, _, p = place()
    home = j == p
    near, far = jnp.where(p == 0, 3, 1), jnp.where(p == 0, 1, 3)
    return {
        "self": 2,
        "left": 0,
        "right": 4,
        "near": near,
        "far": far,
        "mine": jnp.where(home, 2, near),
        "swapped": jnp.where(home, near, 2),
        "one": jnp.where(home, 0, far),
        "two": jnp.where(home, far, 0),
    }[kind]


def tile_kernel(kinds, sets, summed, *refs):
    refs = list(refs)
    metas = [refs.pop(0) for _ in range(sum(len(s) for s in sets))]
    tiles = [refs.pop(0) for _ in range(sum(len(s) for s in sets))]
    panels = [refs.pop(0) for _ in kinds]
    before = refs.pop(0) if summed else None
    out_ref, acc_ref, tile_buf, panel_buf, tile_sems, panel_sems = refs
    slots, tile = tile_buf.shape[2], tile_buf.shape[-1]
    rows = out_ref.shape[0]
    j, _, p = place()
    home = j == p
    offsets = [offset_of(kind) for kind in kinds]

    def tile_copy(ref, i, s):
        return pltpu.make_async_copy(ref.at[offsets[i]], tile_buf.at[i, s], tile_sems.at[i, s])

    def panel_copy(i):
        return pltpu.make_async_copy(panels[i], panel_buf.at[i], panel_sems.at[i])

    for i in range(len(kinds)):
        panel_copy(i).start()
        at = 0
        for s, members in enumerate(sets):
            if len(members) == 1:
                tile_copy(tiles[at], i, s).start()
            else:

                @pl.when(home)
                def _(ref=tiles[at], i=i, s=s):
                    tile_copy(ref, i, s).start()

                @pl.when(jnp.logical_not(home))
                def _(ref=tiles[at + 1], i=i, s=s):
                    tile_copy(ref, i, s).start()

            at += len(members)
    if summed:
        acc_ref[:rows, :] = before[...]
    else:
        acc_ref[...] = jnp.zeros_like(acc_ref)
    for i in range(len(kinds)):
        d = offsets[i]
        panel_copy(i).wait()
        at = 0
        for s, members in enumerate(sets):
            tile_copy(tiles[at], i, s).wait()
            for k in range(slots):
                row = metas[at][0, d * slots + k]
                col = metas[at][1, d * slots + k]
                if len(members) == 2:
                    row = jnp.where(home, row, metas[at + 1][0, d * slots + k])
                    col = jnp.where(home, col, metas[at + 1][1, d * slots + k])
                row = pl.multiple_of(row * tile, tile)
                col = pl.multiple_of(col * tile, tile)
                prod = jnp.dot(
                    tile_buf[i, s, k],
                    panel_buf[i, pl.ds(col, tile), :],
                    preferred_element_type=jnp.float32,
                )
                acc_ref[pl.ds(row, tile), :] += prod
            at += len(members)
    out_ref[...] = acc_ref[:rows, :].astype(out_ref.dtype)


def tile_product(named, sets, dtype, before=None):
    kinds = [kind for kind, _ in named]
    panels = [panel for _, panel in named]
    metas = [meta for members in sets for meta, _ in members]
    tiles = [values for members in sets for _, values in members]
    rows, width = panels[0].shape
    _, slots, tile, _ = tiles[0].shape
    smem = pl.BlockSpec(memory_space=pltpu.SMEM)
    vmem = pl.BlockSpec(memory_space=pltpu.VMEM)
    hbm = pl.BlockSpec(memory_space=pltpu.HBM)
    anywhere = pl.BlockSpec(memory_space=pl.ANY)
    count = len(kinds) * len(sets) * slots
    summed = before is not None
    return pl.pallas_call(
        functools.partial(tile_kernel, kinds, [[0] * len(m) for m in sets], summed),
        out_shape=jax.ShapeDtypeStruct((rows, width), dtype),
        in_specs=[smem] * len(metas)
        + [hbm] * len(tiles)
        + [anywhere] * len(panels)
        + [vmem] * summed,
        out_specs=vmem,
        scratch_shapes=[
            pltpu.VMEM((rows + tile, width), jnp.float32),
            pltpu.VMEM((len(kinds), len(sets), slots, tile, tile), tiles[0].dtype),
            pltpu.VMEM((len(kinds), rows, width), panels[0].dtype),
            pltpu.SemaphoreType.DMA((len(kinds), len(sets))),
            pltpu.SemaphoreType.DMA((len(kinds),)),
        ],
        compiler_params=pltpu.CompilerParams(vmem_limit_bytes=8 * 1024 * 1024),
        cost_estimate=pl.CostEstimate(
            flops=2 * count * tile * tile * width,
            bytes_accessed=count * tile * tile * 2 + len(kinds) * rows * width * 2,
            transcendentals=0,
        ),
        name="tile_product",
    )(*metas, *tiles, *panels, *([before] if summed else []))


def middle_kernel(near_ref, far_ref, w_ref, cot_ref, cot_swap_ref, act_ref, adj_ref):
    j, _, p = place()
    half = near_ref.shape[1]
    near = pl.multiple_of(j * half, half)
    far = pl.multiple_of((1 - j) * half, half)
    cols = pl.ds(near, half)
    agg = jnp.dot(
        near_ref[...], w_ref[pl.ds(near, half), cols], preferred_element_type=jnp.float32
    )
    agg += jnp.dot(far_ref[...], w_ref[pl.ds(far, half), cols], preferred_element_type=jnp.float32)
    sig = jax.nn.sigmoid(agg)
    act_ref[...] = (agg * sig).astype(act_ref.dtype)
    slope = sig * (1.0 + agg * (1.0 - sig))
    cot = jnp.where(j == p, cot_ref[...], cot_swap_ref[...])
    adj_ref[...] = (cot.astype(jnp.float32) * slope).astype(adj_ref.dtype)


def middle(near, far, weight, cot, cot_swap):
    vmem = pl.BlockSpec(memory_space=pltpu.VMEM)
    rows, width = near.shape
    out = jax.ShapeDtypeStruct((rows, width), jnp.bfloat16)
    return pl.pallas_call(
        middle_kernel,
        out_shape=(out, out),
        in_specs=[vmem] * 5,
        out_specs=(vmem, vmem),
        compiler_params=pltpu.CompilerParams(vmem_limit_bytes=8 * 1024 * 1024),
        cost_estimate=pl.CostEstimate(
            flops=4 * rows * width * width,
            bytes_accessed=10 * rows * width,
            transcendentals=rows * width,
        ),
        name="middle",
    )(near, far, weight, cot, cot_swap)


def grad_kernel(scale, near_ref, far_ref, adj_ref, after_ref, out_ref):
    j, _, _ = place()
    half = near_ref.shape[1]
    dims = (((0,), (0,)), ((), ()))
    for i, ref in enumerate((near_ref, far_ref)):
        start = pl.multiple_of((j if i == 0 else 1 - j) * half, half)
        out_ref[pl.ds(start, half), :] = scale * lax.dot_general(
            ref[...], adj_ref[...], dims, preferred_element_type=jnp.float32
        )


def grad_block(scale, near, far, adj, after):
    vmem = pl.BlockSpec(memory_space=pltpu.VMEM)
    rows, width = near.shape
    return pl.pallas_call(
        functools.partial(grad_kernel, scale),
        out_shape=jax.ShapeDtypeStruct((2 * width, width), jnp.float32),
        in_specs=[vmem] * 3 + [pl.BlockSpec(memory_space=pl.ANY)],
        out_specs=vmem,
        compiler_params=pltpu.CompilerParams(vmem_limit_bytes=8 * 1024 * 1024),
        cost_estimate=pl.CostEstimate(
            flops=4 * rows * width * width, bytes_accessed=8 * rows * width, transcendentals=0
        ),
        name="grad_block",
    )(near, far, adj, after)


def add_kernel(first_ref, second_ref, after_ref, out_ref):
    out_ref[...] = first_ref[...] + second_ref[...]


def add_after(first, second, after):
    vmem = pl.BlockSpec(memory_space=pltpu.VMEM)
    return pl.pallas_call(
        add_kernel,
        out_shape=jax.ShapeDtypeStruct(first.shape, first.dtype),
        in_specs=[vmem, vmem, pl.BlockSpec(memory_space=pl.ANY)],
        out_specs=vmem,
        compiler_params=pltpu.CompilerParams(vmem_limit_bytes=1024 * 1024),
        name="add_after",
    )(first, second, after)


def final_kernel(self_ref, one_ref, two_ref, w_ref, out_ref):
    j, _, p = place()
    half = self_ref.shape[1]
    near = jnp.where(j == p, self_ref[...], one_ref[...])
    far = jnp.where(j == p, one_ref[...], two_ref[...])
    w_near = w_ref[:, pl.ds(pl.multiple_of(j * half, half), half)]
    w_far = w_ref[:, pl.ds(pl.multiple_of((1 - j) * half, half), half)]
    dims = (((1,), (1,)), ((), ()))
    total = lax.dot_general(near, w_near, dims, preferred_element_type=jnp.float32)
    total += lax.dot_general(far, w_far, dims, preferred_element_type=jnp.float32)
    out_ref[...] = total.astype(out_ref.dtype)


def final(own, one, two, weight):
    vmem = pl.BlockSpec(memory_space=pltpu.VMEM)
    rows = own.shape[0]
    wide = weight.shape[0]
    return pl.pallas_call(
        final_kernel,
        out_shape=jax.ShapeDtypeStruct((rows, wide), jnp.bfloat16),
        in_specs=[vmem] * 4,
        out_specs=vmem,
        compiler_params=pltpu.CompilerParams(vmem_limit_bytes=8 * 1024 * 1024),
        cost_estimate=pl.CostEstimate(
            flops=2 * rows * wide * wide, bytes_accessed=8 * rows * wide, transcendentals=0
        ),
        name="final",
    )(own, one, two, weight)


def per_device(node_feats, weight, cotangent, tile_values, tile_coords, tile_counts):
    groups = lax.axis_size("rows")
    reps = lax.axis_size("rep")
    shape = (groups // 2, reps)
    j, z, p = place()
    home = j == p
    scale = (node_feats.shape[0] * groups) ** (-0.5)

    def send(value, move):
        return lax.ppermute(value, AXES, route(shape, move))

    def sibling(c, j, z):
        return (c, 1 - j, z)

    def across(c, j, z):
        return (c, j, (z + reps // 2) % reps)

    own = tile_values[0]
    blocks = node_feats.shape[0] // own.shape[-1]

    def to_home(c, j, z):
        return (c, 1 - j, z) if j == z % 2 else (c, j, z ^ 1)

    def forward_x(c, j, z):
        return (c + 1, j, z) if j == z % 2 or z % 2 == 0 else (c - 1, j, z)

    def forward_x_cross(c, j, z):
        to = forward_x(c, j, z)
        return (to[0], 1 - j, to[2])

    first = send(own, to_home)
    mine, yours = halves(node_feats)
    one = send(mine, forward_x)
    two = send(yours, forward_x_cross)
    swapped = send(yours, sibling)
    right = send(pick(mine, swapped), lambda c, j, z: (c - 1, j, z))
    coords, counts, swapped = lax.optimization_barrier((tile_coords, tile_counts, swapped))
    meta = slot_blocks(coords[:, 0], counts[0], blocks)
    meta_b = send(meta, to_home)
    meta_far = send(meta, lambda c, j, z: None if j == z % 2 else (c, 1 - j, z ^ 1))
    first, one, two, right, meta_b, meta_far = lax.optimization_barrier(
        (first, one, two, right, meta_b, meta_far)
    )
    second = send(first, lambda c, j, z: (c, 1 - j, z) if j == z % 2 else None)

    set_first = [(meta_b, first)]
    set_rest = [(meta, own), (meta_far, second)]
    panels = [("mine", mine), ("swapped", swapped), ("one", one), ("two", two), ("right", right)]
    part = tile_product(panels, [set_first], jnp.float32)
    part = tile_product(panels, [set_rest], jnp.bfloat16, part)

    def join(value):
        other = send(value, across)
        return (value.astype(jnp.float32) + other.astype(jnp.float32)).astype(jnp.bfloat16)

    near = join(part)
    far = send(near, sibling)
    cot, cot_yours = halves(cotangent)
    act, adj = middle(near, far, weight, cot, send(cot_yours, sibling))

    left = send(adj, lambda c, j, z: (c + 1, j, z))
    right = send(adj, lambda c, j, z: (c - 1, j, z))
    third = send(adj, lambda c, j, z: (c + 1 if z % 2 else c - 1, j, z ^ 1))
    other = send(adj, lambda c, j, z: (c, j, z ^ 1))
    back_part = tile_product([("self", adj), ("near", other)], [set_first, set_rest], jnp.float32)
    far_panels = [("left", left), ("right", right), ("far", third)]
    back_part = tile_product(far_panels, [set_first, set_rest], jnp.bfloat16, back_part)

    def deliver(value):
        one = send(value, lambda c, j, z: (c, j, z ^ 1) if j == z % 2 else (c, 1 - j, z))
        two = send(value, lambda c, j, z: None if j == z % 2 else (c, 1 - j, z ^ 1))
        return one, two

    act_one, act_two = deliver(act)
    act_near = jnp.where(home, act, act_one)
    act_far = jnp.where(home, act_one, act_two)
    activated = jnp.concatenate(
        [jnp.where(j == 0, act_near, act_far), jnp.where(j == 0, act_far, act_near)], axis=1
    )

    back = join(back_part)
    back_one, back_two = deliver(back)
    input_grad = final(back, back_one, back_two, weight)

    grad = grad_block(scale, near, far, adj, other)
    grad = add_after(grad, send(grad, lambda c, j, z: (c, j, z ^ 1)), back_part)
    step = 1
    while step < shape[0]:
        flips = [step] if step * 2 >= shape[0] else [step, 2 * step, 3 * step]
        got = [send(grad, lambda c, j, z, s=s: (c ^ s, j, z)) for s in flips]
        grad = grad + got[0]
        if len(got) == 3:
            grad = grad + (got[1] + got[2])
        step *= 2 if len(flips) == 1 else 4
    rest = send(grad, sibling)
    weight_grad = jnp.concatenate(
        [jnp.where(j == 0, grad, rest), jnp.where(j == 0, rest, grad)], axis=1
    )
    return (activated, input_grad, weight_grad)


def solution(mesh):
    return jax.shard_map(
        per_device,
        mesh=mesh,
        in_specs=(
            P("rows", None),
            P(),
            P("rows", None),
            P("rows", None, "rep", None, None),
            P(None, "rows", None, "rep"),
            P("rows", None),
        ),
        out_specs=(P("rows", None), P("rows", None), P()),
        check_vma=False,
    )
```

```python
import functools

import jax
import jax.numpy as jnp
from jax import lax
from jax.experimental import pallas as pl
from jax.experimental.pallas import tpu as pltpu
from jax.sharding import PartitionSpec as P

AXES = ("rows", "rep")


def cut(rows):
    first = rows * 5 // 16 // 16 * 16
    return first, rows - first


def route(shape, move):
    chips, reps = shape
    pairs = []
    for c in range(chips):
        for j in range(2):
            for z in range(reps):
                to = move(c, j, z)
                if to is not None:
                    target = ((to[0] % chips) * 2 + to[1]) * reps + to[2]
                    pairs.append(((c * 2 + j) * reps + z, target))
    return pairs


def place():
    r = lax.axis_index("rows")
    z = lax.axis_index("rep")
    return r % 2, z, z % 2


def halves_kernel(x_ref, near_ref, far_ref, sems):
    j, _, _ = place()
    half = near_ref.shape[1]
    copies = []
    for i, out in enumerate((near_ref, far_ref)):
        start = pl.multiple_of((j if i == 0 else 1 - j) * half, half)
        copy = pltpu.make_async_copy(x_ref.at[:, pl.ds(start, half)], out, sems.at[i])
        copy.start()
        copies.append(copy)
    for copy in copies:
        copy.wait()


def halves(value):
    rows, width = value.shape
    part = jax.ShapeDtypeStruct((rows, width // 2), value.dtype)
    hbm = pl.BlockSpec(memory_space=pltpu.HBM)
    return pl.pallas_call(
        halves_kernel,
        out_shape=(part, part),
        in_specs=[hbm],
        out_specs=(hbm, hbm),
        scratch_shapes=[pltpu.SemaphoreType.DMA((2,))],
        compiler_params=pltpu.CompilerParams(vmem_limit_bytes=1024 * 1024),
        name="halves",
    )(value)


def pick_kernel(mine_ref, swapped_ref, *refs):
    outs, sems = refs[:3], refs[3]
    rows, rest = outs[0].shape[0], outs[1].shape[0]
    j, _, p = place()

    def copies(own, other):
        return [
            pltpu.make_async_copy(own.at[pl.ds(0, rows), :], outs[0], sems.at[0]),
            pltpu.make_async_copy(own.at[pl.ds(rows, rest), :], outs[1], sems.at[1]),
            pltpu.make_async_copy(other, outs[2], sems.at[2]),
        ]

    @pl.when(j == p)
    def _():
        for copy in copies(mine_ref, swapped_ref):
            copy.start()
        for copy in copies(mine_ref, swapped_ref):
            copy.wait()

    @pl.when(j != p)
    def _():
        for copy in copies(swapped_ref, mine_ref):
            copy.start()
        for copy in copies(swapped_ref, mine_ref):
            copy.wait()


def pick(mine, swapped):
    hbm = pl.BlockSpec(memory_space=pltpu.HBM)
    rows, width = mine.shape
    shapes = [jax.ShapeDtypeStruct((n, width), mine.dtype) for n in (*cut(rows), rows)]
    return pl.pallas_call(
        pick_kernel,
        out_shape=tuple(shapes),
        in_specs=[hbm, hbm],
        out_specs=(hbm, hbm, hbm),
        scratch_shapes=[pltpu.SemaphoreType.DMA((3,))],
        compiler_params=pltpu.CompilerParams(vmem_limit_bytes=1024 * 1024),
        name="pick",
    )(mine, swapped)


def slots_kernel(dead, coords_ref, counts_ref, out_ref):
    _, z, _ = place()
    _, reach, slots = coords_ref.shape
    for d in range(reach):
        for k in range(slots):
            live = z * slots + k < counts_ref[d]
            out_ref[0, d * slots + k] = jnp.where(live, coords_ref[0, d, k], dead)
            out_ref[1, d * slots + k] = coords_ref[1, d, k]


def slot_blocks(coords, counts, dead):
    smem = pl.BlockSpec(memory_space=pltpu.SMEM)
    return pl.pallas_call(
        functools.partial(slots_kernel, dead),
        out_shape=jax.ShapeDtypeStruct((2, coords.shape[1] * coords.shape[2]), jnp.int32),
        in_specs=[smem, smem],
        out_specs=smem,
        compiler_params=pltpu.CompilerParams(vmem_limit_bytes=1024 * 1024),
        name="slot_blocks",
    )(coords, counts)


def offset_of(kind):
    _, _, p = place()
    even = (lax.axis_index("rows") // 2) % 2 == 0
    return {
        "self": 2,
        "near": jnp.where(p == 0, 3, 1),
        "far": jnp.where(p == 0, 1, 3),
        "direct": jnp.where(even, 4, 0),
        "second": jnp.where(even, 0, 4),
    }[kind]


def tile_kernel(kinds, pieces, sets, outs, summed, waits, *refs):
    refs = list(refs)
    metas = [refs.pop(0) for _ in range(sum(sets))]
    tiles = [refs.pop(0) for _ in range(sum(sets))]
    panels = [[refs.pop(0) for _ in range(count)] for count in pieces]
    before = refs.pop(0) if summed else None
    refs = refs[waits:]
    out_refs = [refs.pop(0) for _ in range(outs)]
    acc_ref, tile_buf, panel_buf, tile_sems, panel_sems = refs
    slots, tile = tile_buf.shape[2], tile_buf.shape[-1]
    rows = panel_buf.shape[1]
    j, _, p = place()
    home = j == p
    offsets = [offset_of(kind) for kind in kinds]

    def tile_copy(ref, i, s):
        return pltpu.make_async_copy(ref.at[offsets[i]], tile_buf.at[i, s], tile_sems.at[i, s])

    def panel_copies(i):
        starts = (0, panels[i][0].shape[0])
        return [
            pltpu.make_async_copy(
                ref, panel_buf.at[i, pl.ds(starts[n], ref.shape[0]), :], panel_sems.at[i, n]
            )
            for n, ref in enumerate(panels[i])
        ]

    for i in range(len(kinds)):
        for copy in panel_copies(i):
            copy.start()
        at = 0
        for s, members in enumerate(sets):
            if members == 1:
                tile_copy(tiles[at], i, s).start()
            else:

                @pl.when(home)
                def _(ref=tiles[at], i=i, s=s):
                    tile_copy(ref, i, s).start()

                @pl.when(jnp.logical_not(home))
                def _(ref=tiles[at + 1], i=i, s=s):
                    tile_copy(ref, i, s).start()

            at += members
    if summed:
        acc_ref[:rows, :] = before[...]
    else:
        acc_ref[...] = jnp.zeros_like(acc_ref)
    for i in range(len(kinds)):
        d = offsets[i]
        for copy in panel_copies(i):
            copy.wait()
        at = 0
        for s, members in enumerate(sets):
            tile_copy(tiles[at], i, s).wait()
            for k in range(slots):
                row = metas[at][0, d * slots + k]
                col = metas[at][1, d * slots + k]
                if members == 2:
                    row = jnp.where(home, row, metas[at + 1][0, d * slots + k])
                    col = jnp.where(home, col, metas[at + 1][1, d * slots + k])
                row = pl.multiple_of(row * tile, tile)
                col = pl.multiple_of(col * tile, tile)
                prod = jnp.dot(
                    tile_buf[i, s, k],
                    panel_buf[i, pl.ds(col, tile), :],
                    preferred_element_type=jnp.float32,
                )
                acc_ref[pl.ds(row, tile), :] += prod
            at += members
    start = 0
    for out_ref in out_refs:
        size = out_ref.shape[0]
        out_ref[...] = acc_ref[start : start + size, :].astype(out_ref.dtype)
        start += size


def tile_product(named, sets, dtype, outs=1, before=None, after=()):
    kinds = [kind for kind, _ in named]
    pieces = [len(panel) for _, panel in named]
    panels = [piece for _, panel in named for piece in panel]
    metas = [meta for members in sets for meta, _ in members]
    tiles = [values for members in sets for _, values in members]
    width = panels[0].shape[1]
    rows = sum(piece.shape[0] for piece in named[0][1])
    _, slots, tile, _ = tiles[0].shape
    smem = pl.BlockSpec(memory_space=pltpu.SMEM)
    vmem = pl.BlockSpec(memory_space=pltpu.VMEM)
    hbm = pl.BlockSpec(memory_space=pltpu.HBM)
    anywhere = pl.BlockSpec(memory_space=pl.ANY)
    count = len(kinds) * len(sets) * slots
    summed = before is not None
    return pl.pallas_call(
        functools.partial(tile_kernel, kinds, pieces, [len(m) for m in sets], outs, summed, len(after)),
        out_shape=tuple(
            jax.ShapeDtypeStruct((n, width), dtype) for n in (cut(rows) if outs == 2 else [rows])
        ),
        in_specs=[smem] * len(metas)
        + [hbm] * len(tiles)
        + [anywhere] * len(panels)
        + [vmem] * summed
        + [anywhere] * len(after),
        out_specs=(vmem,) * outs,
        scratch_shapes=[
            pltpu.VMEM((rows + tile, width), jnp.float32),
            pltpu.VMEM((len(kinds), len(sets), slots, tile, tile), tiles[0].dtype),
            pltpu.VMEM((len(kinds), rows, width), panels[0].dtype),
            pltpu.SemaphoreType.DMA((len(kinds), len(sets))),
            pltpu.SemaphoreType.DMA((len(kinds), 2)),
        ],
        compiler_params=pltpu.CompilerParams(vmem_limit_bytes=8 * 1024 * 1024),
        cost_estimate=pl.CostEstimate(
            flops=2 * count * tile * tile * width,
            bytes_accessed=count * tile * tile * 2 + len(kinds) * rows * width * 2,
            transcendentals=0,
        ),
        name="tile_product",
    )(*metas, *tiles, *panels, *([before] if summed else []), *after)


def middle_kernel(chunk, near_ref, far_ref, w_ref, cot_ref, swap_ref, *refs):
    j, _, p = place()
    rows, half = near_ref.shape
    near = pl.multiple_of(j * half, half)
    far = pl.multiple_of((1 - j) * half, half)
    cols = pl.ds(near, half)
    agg = jnp.dot(
        near_ref[...], w_ref[pl.ds(near, half), cols], preferred_element_type=jnp.float32
    )
    agg += jnp.dot(far_ref[...], w_ref[pl.ds(far, half), cols], preferred_element_type=jnp.float32)
    sig = jax.nn.sigmoid(agg)
    slope = sig * (1.0 + agg * (1.0 - sig))
    start = cot_ref.shape[0] - rows if chunk else 0
    mine = pl.ds(start, rows)
    cot = jnp.where(j == p, cot_ref[mine, :], swap_ref[mine, :]).astype(jnp.float32)
    act = (agg * sig).astype(jnp.bfloat16)
    adj = (cot * slope).astype(jnp.bfloat16)
    if chunk == 0:
        act_ref, adj_ref = refs
        act_ref[...] = act
        adj_ref[...] = adj
    else:
        act_first_ref, adj_first_ref, _, act_ref, adj_ref, whole_ref = refs
        act_ref[:start, :] = act_first_ref[...]
        act_ref[start:, :] = act
        adj_ref[...] = adj
        whole_ref[:start, :] = adj_first_ref[...]
        whole_ref[start:, :] = adj


def middle(near, far, weight, cot, cot_swap, first=None):
    vmem = pl.BlockSpec(memory_space=pltpu.VMEM)
    rows, width = near.shape
    part = jax.ShapeDtypeStruct((rows, width), jnp.bfloat16)
    whole = jax.ShapeDtypeStruct(cot.shape, jnp.bfloat16)
    return pl.pallas_call(
        functools.partial(middle_kernel, 0 if first is None else 1),
        out_shape=(part, part) if first is None else (whole, part, whole),
        in_specs=[vmem] * 5 + ([vmem, vmem, pl.BlockSpec(memory_space=pl.ANY)] if first else []),
        out_specs=(vmem,) * (2 if first is None else 3),
        compiler_params=pltpu.CompilerParams(vmem_limit_bytes=8 * 1024 * 1024),
        cost_estimate=pl.CostEstimate(flops=1, bytes_accessed=1, transcendentals=0),
        name="middle",
    )(near, far, weight, cot, cot_swap, *(first or ()))


def grad_kernel(scale, near_a, near_b, far_a, far_b, adj_ref, after_ref, out_ref):
    j, _, _ = place()
    cut_at, half = near_a.shape
    dims = (((0,), (0,)), ((), ()))
    for i, refs in enumerate(((near_a, near_b), (far_a, far_b))):
        start = pl.multiple_of((j if i == 0 else 1 - j) * half, half)
        total = jnp.zeros((half, half), jnp.float32)
        for n, ref in enumerate(refs):
            adj = adj_ref[cut_at:, :] if n else adj_ref[:cut_at, :]
            total += lax.dot_general(ref[...], adj, dims, preferred_element_type=jnp.float32)
        out_ref[pl.ds(start, half), :] = scale * total


def grad_block(scale, nears, fars, adj, after):
    vmem = pl.BlockSpec(memory_space=pltpu.VMEM)
    rows, width = adj.shape
    return pl.pallas_call(
        functools.partial(grad_kernel, scale),
        out_shape=jax.ShapeDtypeStruct((2 * width, width), jnp.float32),
        in_specs=[vmem] * 5 + [pl.BlockSpec(memory_space=pl.ANY)],
        out_specs=vmem,
        compiler_params=pltpu.CompilerParams(vmem_limit_bytes=8 * 1024 * 1024),
        cost_estimate=pl.CostEstimate(
            flops=4 * rows * width * width, bytes_accessed=8 * rows * width, transcendentals=0
        ),
        name="grad_block",
    )(*nears, *fars, adj, after)


def add_kernel(count, *refs):
    total = refs[0][...].astype(jnp.float32) + refs[1][...].astype(jnp.float32)
    if count == 4:
        total = total + (refs[2][...] + refs[3][...])
    refs[-1][...] = total.astype(refs[-1].dtype)


def add_after(values, *after):
    vmem = pl.BlockSpec(memory_space=pltpu.VMEM)
    return pl.pallas_call(
        functools.partial(add_kernel, len(values)),
        out_shape=jax.ShapeDtypeStruct(values[0].shape, values[0].dtype),
        in_specs=[vmem] * len(values) + [pl.BlockSpec(memory_space=pl.ANY)] * len(after),
        out_specs=vmem,
        compiler_params=pltpu.CompilerParams(vmem_limit_bytes=4 * 1024 * 1024),
        name="add_after",
    )(*values, *after)


def final_kernel(own_ref, one_ref, two_ref, w_ref, grad_ref, rest_ref, out_ref, grad_out_ref):
    j, _, p = place()
    half = own_ref.shape[1]
    near_cols = pl.ds(pl.multiple_of(j * half, half), half)
    far_cols = pl.ds(pl.multiple_of((1 - j) * half, half), half)
    grad_out_ref[:, near_cols] = grad_ref[...]
    grad_out_ref[:, far_cols] = rest_ref[...]
    near = jnp.where(j == p, own_ref[...], one_ref[...])
    far = jnp.where(j == p, one_ref[...], two_ref[...])
    dims = (((1,), (1,)), ((), ()))
    total = lax.dot_general(near, w_ref[:, near_cols], dims, preferred_element_type=jnp.float32)
    total += lax.dot_general(far, w_ref[:, far_cols], dims, preferred_element_type=jnp.float32)
    out_ref[...] = total.astype(out_ref.dtype)


def final(own, one, two, weight, grad, rest):
    vmem = pl.BlockSpec(memory_space=pltpu.VMEM)
    rows = own.shape[0]
    wide = weight.shape[0]
    return pl.pallas_call(
        final_kernel,
        out_shape=(
            jax.ShapeDtypeStruct((rows, wide), jnp.bfloat16),
            jax.ShapeDtypeStruct(weight.shape, jnp.float32),
        ),
        in_specs=[vmem] * 6,
        out_specs=(vmem, vmem),
        compiler_params=pltpu.CompilerParams(vmem_limit_bytes=8 * 1024 * 1024),
        cost_estimate=pl.CostEstimate(
            flops=2 * rows * wide * wide, bytes_accessed=8 * rows * wide, transcendentals=0
        ),
        name="final",
    )(own, one, two, weight, grad, rest)


def per_device(node_feats, weight, cotangent, tile_values, tile_coords, tile_counts):
    groups = lax.axis_size("rows")
    reps = lax.axis_size("rep")
    shape = (groups // 2, reps)
    j, z, p = place()
    home = j == p
    scale = (node_feats.shape[0] * groups) ** (-0.5)

    def send(value, move):
        return lax.ppermute(value, AXES, route(shape, move))

    def sibling(c, j, z):
        return (c, 1 - j, z)

    def across(c, j, z):
        return (c, j, (z + reps // 2) % reps)

    own = tile_values[0]
    blocks = node_feats.shape[0] // own.shape[-1]

    def to_home(c, j, z):
        return (c, 1 - j, z) if j == z % 2 else (c, j, z ^ 1)

    def to_direct(c, j, z):
        return (c ^ 1, j, z)

    def to_second(c, j, z):
        return (c ^ 2, j, z) if shape[0] == 4 else (c + 1 if c % 2 else c - 1, j, z)

    def hand_on(value, direct):
        return send(direct if shape[0] == 4 else value, to_second)

    first = send(own, to_home)
    mine, yours = halves(node_feats)
    swapped = send(yours, sibling)
    feats_a, feats_b, feats_other = pick(mine, swapped)
    feats = [feats_a, feats_b]
    direct = [send(value, to_direct) for value in feats]
    far = send(feats_other, lambda c, j, z: (c - 1 if z % 2 else c + 1, j, z))
    second = [hand_on(value, got) for value, got in zip(feats, direct)]
    coords, counts, feats_other = lax.optimization_barrier((tile_coords, tile_counts, feats_other))
    meta = slot_blocks(coords[:, 0], counts[0], blocks)
    meta_b = send(meta, to_home)
    meta_far = send(meta, lambda c, j, z: None if j == z % 2 else (c, 1 - j, z ^ 1))
    first, second, far, meta_b, meta_far = lax.optimization_barrier(
        (first, second, far, meta_b, meta_far)
    )
    other_first = send(first, lambda c, j, z: (c, 1 - j, z) if j == z % 2 else None)

    set_first = [(meta_b, first)]
    set_rest = [(meta, own), (meta_far, other_first)]
    panels = [
        ("self", feats),
        ("near", [feats_other]),
        ("direct", direct),
        ("second", second),
        ("far", [far]),
    ]
    (part,) = tile_product(panels, [set_first], jnp.float32)
    parts = tile_product(panels, [set_rest], jnp.bfloat16, 2, part)

    def join(value, other):
        return (value.astype(jnp.float32) + other.astype(jnp.float32)).astype(jnp.bfloat16)

    cot, cot_yours = halves(cotangent)
    cot_swap = send(cot_yours, sibling)

    def to_far(c, j, z):
        return (c + 1 if z % 2 else c - 1, j, z ^ 1)

    across_a, across_b = [send(value, across) for value in parts]
    near_a = join(parts[0], across_a)
    far_a = send(near_a, sibling)
    act_a, adj_a = middle(near_a, far_a, weight, cot, cot_swap)
    direct = [send(adj_a, to_direct)]
    far = [send(adj_a, to_far)]
    second = [hand_on(adj_a, direct[0])]
    near_b = add_after([parts[1], across_b], direct[0], far[0])
    far_b = send(near_b, sibling)
    act, adj_b, adj = middle(near_b, far_b, weight, cot, cot_swap, (act_a, adj_a, second[0]))
    direct.append(send(adj_b, to_direct))
    far.append(send(adj_b, to_far))
    second.append(hand_on(adj_b, direct[1]))
    other = send(adj, lambda c, j, z: (c, j, z ^ 1))
    panels = [("self", [adj]), ("near", [other])]
    (back_part,) = tile_product(panels, [set_first, set_rest], jnp.float32)
    panels = [("direct", direct), ("far", far), ("second", second)]
    grad = grad_block(scale, [near_a, near_b], [far_a, far_b], adj, other)
    grad_got = send(grad, lambda c, j, z: (c, j, z ^ 1))
    (back_part,) = tile_product(
        panels, [set_first, set_rest], jnp.bfloat16, 1, back_part, [grad_got]
    )

    def deliver(value):
        one = send(value, lambda c, j, z: (c, j, z ^ 1) if j == z % 2 else (c, 1 - j, z))
        two = send(value, lambda c, j, z: None if j == z % 2 else (c, 1 - j, z ^ 1))
        return one, two

    act_one, act_two = deliver(act)
    act_near = jnp.where(home, act, act_one)
    act_far = jnp.where(home, act_one, act_two)
    activated = jnp.concatenate(
        [jnp.where(j == 0, act_near, act_far), jnp.where(j == 0, act_far, act_near)], axis=1
    )

    back = join(back_part, send(back_part, across))
    back_one, back_two = deliver(back)

    grad = add_after([grad, grad_got], back_part)
    step = 1
    while step < shape[0]:
        flips = [step] if step * 2 >= shape[0] else [step, 2 * step, 3 * step]
        got = [send(grad, lambda c, j, z, s=s: (c ^ s, j, z)) for s in flips]
        grad = add_after([grad, *got], back)
        step *= 2 if len(flips) == 1 else 4
    grad_rest = send(grad, sibling)
    input_grad, weight_grad = final(back, back_one, back_two, weight, grad, grad_rest)
    return (activated, input_grad, weight_grad)


def solution(mesh):
    return jax.shard_map(
        per_device,
        mesh=mesh,
        in_specs=(
            P("rows", None),
            P(),
            P("rows", None),
            P("rows", None, "rep", None, None),
            P(None, "rows", None, "rep"),
            P("rows", None),
        ),
        out_specs=(P("rows", None), P("rows", None), P()),
        check_vma=False,
    )
```

```python
import functools

import jax
import jax.numpy as jnp
from jax import lax
from jax.experimental import pallas as pl
from jax.experimental.pallas import tpu as pltpu
from jax.sharding import PartitionSpec as P

AXES = ("rows", "rep")
TOGETHER = 4


def route(shape, move):
    chips, reps = shape
    pairs = []
    for c in range(chips):
        for j in range(2):
            for z in range(reps):
                to = move(c, j, z)
                if to is not None:
                    target = ((to[0] % chips) * 2 + to[1]) * reps + to[2]
                    pairs.append(((c * 2 + j) * reps + z, target))
    return pairs


def place():
    r = lax.axis_index("rows")
    z = lax.axis_index("rep")
    return r % 2, z, z % 2


def halves_kernel(x_ref, near_ref, far_ref, sems):
    j, _, _ = place()
    half = near_ref.shape[1]
    copies = []
    for i, out in enumerate((near_ref, far_ref)):
        start = pl.multiple_of((j if i == 0 else 1 - j) * half, half)
        copy = pltpu.make_async_copy(x_ref.at[:, pl.ds(start, half)], out, sems.at[i])
        copy.start()
        copies.append(copy)
    for copy in copies:
        copy.wait()


def halves(value):
    rows, width = value.shape
    part = jax.ShapeDtypeStruct((rows, width // 2), value.dtype)
    hbm = pl.BlockSpec(memory_space=pltpu.HBM)
    return pl.pallas_call(
        halves_kernel,
        out_shape=(part, part),
        in_specs=[hbm],
        out_specs=(hbm, hbm),
        scratch_shapes=[pltpu.SemaphoreType.DMA((2,))],
        compiler_params=pltpu.CompilerParams(vmem_limit_bytes=1024 * 1024),
        name="halves",
    )(value)


def pick_kernel(mine_ref, swapped_ref, group_ref, other_ref, sems):
    j, _, p = place()

    def copies(own, other):
        return [
            pltpu.make_async_copy(own, group_ref, sems.at[0]),
            pltpu.make_async_copy(other, other_ref, sems.at[1]),
        ]

    @pl.when(j == p)
    def _():
        for copy in copies(mine_ref, swapped_ref):
            copy.start()
        for copy in copies(mine_ref, swapped_ref):
            copy.wait()

    @pl.when(j != p)
    def _():
        for copy in copies(swapped_ref, mine_ref):
            copy.start()
        for copy in copies(swapped_ref, mine_ref):
            copy.wait()


def pick(mine, swapped):
    hbm = pl.BlockSpec(memory_space=pltpu.HBM)
    shape = jax.ShapeDtypeStruct(mine.shape, mine.dtype)
    return pl.pallas_call(
        pick_kernel,
        out_shape=(shape, shape),
        in_specs=[hbm, hbm],
        out_specs=(hbm, hbm),
        scratch_shapes=[pltpu.SemaphoreType.DMA((2,))],
        compiler_params=pltpu.CompilerParams(vmem_limit_bytes=1024 * 1024),
        name="pick",
    )(mine, swapped)


def slots_kernel(dead, coords_ref, counts_ref, out_ref):
    _, z, _ = place()
    _, reach, slots = coords_ref.shape
    for d in range(reach):
        for k in range(slots):
            live = z * slots + k < counts_ref[d]
            out_ref[0, d * slots + k] = jnp.where(live, coords_ref[0, d, k], dead)
            out_ref[1, d * slots + k] = coords_ref[1, d, k]


def slot_blocks(coords, counts, dead):
    smem = pl.BlockSpec(memory_space=pltpu.SMEM)
    return pl.pallas_call(
        functools.partial(slots_kernel, dead),
        out_shape=jax.ShapeDtypeStruct((2, coords.shape[1] * coords.shape[2]), jnp.int32),
        in_specs=[smem, smem],
        out_specs=smem,
        compiler_params=pltpu.CompilerParams(vmem_limit_bytes=1024 * 1024),
        name="slot_blocks",
    )(coords, counts)


def offset_of(kind):
    _, _, p = place()
    even = (lax.axis_index("rows") // 2) % 2 == 0
    return {
        "self": 2,
        "near": jnp.where(p == 0, 3, 1),
        "far": jnp.where(p == 0, 1, 3),
        "direct": jnp.where(even, 4, 0),
        "second": jnp.where(even, 0, 4),
    }[kind]


def tile_kernel(kinds, sets, summed, waits, *refs):
    refs = list(refs)
    metas = [refs.pop(0) for _ in range(sum(sets))]
    tiles = [refs.pop(0) for _ in range(sum(sets))]
    panels = [refs.pop(0) for _ in kinds]
    before = refs.pop(0) if summed else None
    out_ref, acc_ref, tile_buf, panel_buf, tile_sems, panel_sems = refs[waits:]
    slots, tile = tile_buf.shape[2], tile_buf.shape[-1]
    rows = out_ref.shape[0]
    j, _, p = place()
    home = j == p
    offsets = [offset_of(kind) for kind in kinds]

    def tile_copy(ref, i, s):
        return pltpu.make_async_copy(ref.at[offsets[i]], tile_buf.at[i, s], tile_sems.at[i, s])

    def panel_copy(i):
        return pltpu.make_async_copy(panels[i], panel_buf.at[i], panel_sems.at[i])

    for i in range(len(kinds)):
        panel_copy(i).start()
        at = 0
        for s, members in enumerate(sets):
            if members == 1:
                tile_copy(tiles[at], i, s).start()
            else:

                @pl.when(home)
                def _(ref=tiles[at], i=i, s=s):
                    tile_copy(ref, i, s).start()

                @pl.when(jnp.logical_not(home))
                def _(ref=tiles[at + 1], i=i, s=s):
                    tile_copy(ref, i, s).start()

            at += members
    if summed:
        acc_ref[:rows, :] = before[...]
    else:
        acc_ref[...] = jnp.zeros_like(acc_ref)
    for i in range(len(kinds)):
        d = offsets[i]
        panel_copy(i).wait()
        at = 0
        for s, members in enumerate(sets):
            tile_copy(tiles[at], i, s).wait()
            for first in range(0, slots, TOGETHER):
                prods = []
                for k in range(first, min(first + TOGETHER, slots)):
                    row = metas[at][0, d * slots + k]
                    col = metas[at][1, d * slots + k]
                    if members == 2:
                        row = jnp.where(home, row, metas[at + 1][0, d * slots + k])
                        col = jnp.where(home, col, metas[at + 1][1, d * slots + k])
                    col = pl.multiple_of(col * tile, tile)
                    prod = jnp.dot(
                        tile_buf[i, s, k],
                        panel_buf[i, pl.ds(col, tile), :],
                        preferred_element_type=jnp.float32,
                    )
                    prods.append((pl.multiple_of(row * tile, tile), prod))
                for row, prod in prods:
                    acc_ref[pl.ds(row, tile), :] += prod
            at += members
    out_ref[...] = acc_ref[:rows, :].astype(out_ref.dtype)


def tile_product(named, sets, dtype, before=None, after=()):
    kinds = [kind for kind, _ in named]
    panels = [panel for _, panel in named]
    metas = [meta for members in sets for meta, _ in members]
    tiles = [values for members in sets for _, values in members]
    rows, width = panels[0].shape
    _, slots, tile, _ = tiles[0].shape
    smem = pl.BlockSpec(memory_space=pltpu.SMEM)
    vmem = pl.BlockSpec(memory_space=pltpu.VMEM)
    hbm = pl.BlockSpec(memory_space=pltpu.HBM)
    anywhere = pl.BlockSpec(memory_space=pl.ANY)
    count = len(kinds) * len(sets) * slots
    summed = before is not None
    return pl.pallas_call(
        functools.partial(tile_kernel, kinds, [len(m) for m in sets], summed, len(after)),
        out_shape=jax.ShapeDtypeStruct((rows, width), dtype),
        in_specs=[smem] * len(metas)
        + [hbm] * len(tiles)
        + [anywhere] * len(panels)
        + [vmem] * summed
        + [anywhere] * len(after),
        out_specs=vmem,
        scratch_shapes=[
            pltpu.VMEM((rows + tile, width), jnp.float32),
            pltpu.VMEM((len(kinds), len(sets), slots, tile, tile), tiles[0].dtype),
            pltpu.VMEM((len(kinds), rows, width), panels[0].dtype),
            pltpu.SemaphoreType.DMA((len(kinds), len(sets))),
            pltpu.SemaphoreType.DMA((len(kinds),)),
        ],
        compiler_params=pltpu.CompilerParams(vmem_limit_bytes=8 * 1024 * 1024),
        cost_estimate=pl.CostEstimate(
            flops=2 * count * tile * tile * width,
            bytes_accessed=count * tile * tile * 2 + len(kinds) * rows * width * 2,
            transcendentals=0,
        ),
        name="tile_product",
    )(*metas, *tiles, *panels, *([before] if summed else []), *after)


def middle_kernel(near_ref, far_ref, w_ref, cot_ref, cot_swap_ref, act_ref, adj_ref):
    j, _, p = place()
    half = near_ref.shape[1]
    near = pl.multiple_of(j * half, half)
    far = pl.multiple_of((1 - j) * half, half)
    cols = pl.ds(near, half)
    agg = jnp.dot(
        near_ref[...], w_ref[pl.ds(near, half), cols], preferred_element_type=jnp.float32
    )
    agg += jnp.dot(far_ref[...], w_ref[pl.ds(far, half), cols], preferred_element_type=jnp.float32)
    sig = jax.nn.sigmoid(agg)
    act_ref[...] = (agg * sig).astype(act_ref.dtype)
    slope = sig * (1.0 + agg * (1.0 - sig))
    cot = jnp.where(j == p, cot_ref[...], cot_swap_ref[...])
    adj_ref[...] = (cot.astype(jnp.float32) * slope).astype(adj_ref.dtype)


def middle(near, far, weight, cot, cot_swap):
    vmem = pl.BlockSpec(memory_space=pltpu.VMEM)
    rows, width = near.shape
    out = jax.ShapeDtypeStruct((rows, width), jnp.bfloat16)
    return pl.pallas_call(
        middle_kernel,
        out_shape=(out, out),
        in_specs=[vmem] * 5,
        out_specs=(vmem, vmem),
        compiler_params=pltpu.CompilerParams(vmem_limit_bytes=8 * 1024 * 1024),
        cost_estimate=pl.CostEstimate(
            flops=4 * rows * width * width,
            bytes_accessed=10 * rows * width,
            transcendentals=rows * width,
        ),
        name="middle",
    )(near, far, weight, cot, cot_swap)


def grad_kernel(scale, near_ref, far_ref, adj_ref, after_ref, out_ref):
    j, _, _ = place()
    half = near_ref.shape[1]
    dims = (((0,), (0,)), ((), ()))
    for i, ref in enumerate((near_ref, far_ref)):
        start = pl.multiple_of((j if i == 0 else 1 - j) * half, half)
        out_ref[pl.ds(start, half), :] = scale * lax.dot_general(
            ref[...], adj_ref[...], dims, preferred_element_type=jnp.float32
        )


def grad_block(scale, near, far, adj, after):
    vmem = pl.BlockSpec(memory_space=pltpu.VMEM)
    rows, width = near.shape
    return pl.pallas_call(
        functools.partial(grad_kernel, scale),
        out_shape=jax.ShapeDtypeStruct((2 * width, width), jnp.float32),
        in_specs=[vmem] * 3 + [pl.BlockSpec(memory_space=pl.ANY)],
        out_specs=vmem,
        compiler_params=pltpu.CompilerParams(vmem_limit_bytes=8 * 1024 * 1024),
        cost_estimate=pl.CostEstimate(
            flops=4 * rows * width * width, bytes_accessed=8 * rows * width, transcendentals=0
        ),
        name="grad_block",
    )(near, far, adj, after)


def add_kernel(count, *refs):
    total = refs[0][...].astype(jnp.float32) + refs[1][...].astype(jnp.float32)
    if count == 4:
        total = total + (refs[2][...] + refs[3][...])
    refs[-1][...] = total.astype(refs[-1].dtype)


def add_after(values, *after):
    vmem = pl.BlockSpec(memory_space=pltpu.VMEM)
    return pl.pallas_call(
        functools.partial(add_kernel, len(values)),
        out_shape=jax.ShapeDtypeStruct(values[0].shape, values[0].dtype),
        in_specs=[vmem] * len(values) + [pl.BlockSpec(memory_space=pl.ANY)] * len(after),
        out_specs=vmem,
        compiler_params=pltpu.CompilerParams(vmem_limit_bytes=4 * 1024 * 1024),
        name="add_after",
    )(*values, *after)


def final_kernel(own_ref, one_ref, two_ref, w_ref, grad_ref, rest_ref, out_ref, grad_out_ref):
    j, _, p = place()
    half = own_ref.shape[1]
    near_cols = pl.ds(pl.multiple_of(j * half, half), half)
    far_cols = pl.ds(pl.multiple_of((1 - j) * half, half), half)
    grad_out_ref[:, near_cols] = grad_ref[...]
    grad_out_ref[:, far_cols] = rest_ref[...]
    near = jnp.where(j == p, own_ref[...], one_ref[...])
    far = jnp.where(j == p, one_ref[...], two_ref[...])
    dims = (((1,), (1,)), ((), ()))
    total = lax.dot_general(near, w_ref[:, near_cols], dims, preferred_element_type=jnp.float32)
    total += lax.dot_general(far, w_ref[:, far_cols], dims, preferred_element_type=jnp.float32)
    out_ref[...] = total.astype(out_ref.dtype)


def final(own, one, two, weight, grad, rest):
    vmem = pl.BlockSpec(memory_space=pltpu.VMEM)
    rows = own.shape[0]
    wide = weight.shape[0]
    return pl.pallas_call(
        final_kernel,
        out_shape=(
            jax.ShapeDtypeStruct((rows, wide), jnp.bfloat16),
            jax.ShapeDtypeStruct(weight.shape, jnp.float32),
        ),
        in_specs=[vmem] * 6,
        out_specs=(vmem, vmem),
        compiler_params=pltpu.CompilerParams(vmem_limit_bytes=8 * 1024 * 1024),
        cost_estimate=pl.CostEstimate(
            flops=2 * rows * wide * wide, bytes_accessed=8 * rows * wide, transcendentals=0
        ),
        name="final",
    )(own, one, two, weight, grad, rest)


def per_device(node_feats, weight, cotangent, tile_values, tile_coords, tile_counts):
    groups = lax.axis_size("rows")
    reps = lax.axis_size("rep")
    shape = (groups // 2, reps)
    j, z, p = place()
    home = j == p
    scale = (node_feats.shape[0] * groups) ** (-0.5)

    def send(value, move):
        return lax.ppermute(value, AXES, route(shape, move))

    def sibling(c, j, z):
        return (c, 1 - j, z)

    def across(c, j, z):
        return (c, j, (z + reps // 2) % reps)

    own = tile_values[0]
    blocks = node_feats.shape[0] // own.shape[-1]

    def to_home(c, j, z):
        return (c, 1 - j, z) if j == z % 2 else (c, j, z ^ 1)

    def to_direct(c, j, z):
        return (c ^ 1, j, z)

    def to_second(c, j, z):
        return (c ^ 2, j, z) if shape[0] == 4 else (c + 1 if c % 2 else c - 1, j, z)

    def hand_on(value, direct):
        return send(direct if shape[0] == 4 else value, to_second)

    first = send(own, to_home)
    mine, yours = halves(node_feats)
    feats, feats_other = pick(mine, send(yours, sibling))
    direct = send(feats, to_direct)
    coords, counts, feats_later, direct = lax.optimization_barrier(
        (tile_coords, tile_counts, feats_other, direct)
    )
    second = hand_on(feats, direct)
    far = send(feats_later, lambda c, j, z: (c - 1 if z % 2 else c + 1, j, z))
    meta = slot_blocks(coords[:, 0], counts[0], blocks)
    meta_b = send(meta, to_home)
    meta_far = send(meta, lambda c, j, z: None if j == z % 2 else (c, 1 - j, z ^ 1))
    first, second, far, meta_b, meta_far = lax.optimization_barrier(
        (first, second, far, meta_b, meta_far)
    )
    other_first = send(first, lambda c, j, z: (c, 1 - j, z) if j == z % 2 else None)

    set_first = [(meta_b, first)]
    set_rest = [(meta, own), (meta_far, other_first)]
    panels = [
        ("self", feats),
        ("near", feats_other),
        ("direct", direct),
        ("second", second),
        ("far", far),
    ]
    part = tile_product(panels, [set_first], jnp.float32)
    part = tile_product(panels, [set_rest], jnp.bfloat16, part)

    def join(value):
        other = send(value, across)
        return (value.astype(jnp.float32) + other.astype(jnp.float32)).astype(jnp.bfloat16)

    near = join(part)
    far = send(near, sibling)
    cot, cot_yours = halves(cotangent)
    act, adj = middle(near, far, weight, cot, send(cot_yours, sibling))

    other = send(adj, lambda c, j, z: (c, j, z ^ 1))
    direct = send(adj, to_direct)
    adj_later, direct = lax.optimization_barrier((adj, direct))
    second = hand_on(adj, direct)
    third = send(adj_later, lambda c, j, z: (c + 1 if z % 2 else c - 1, j, z ^ 1))
    grad = grad_block(scale, near, far, adj, other)
    grad_got = send(grad, lambda c, j, z: (c, j, z ^ 1))
    panels = [("self", adj), ("near", other)]
    back_part = tile_product(panels, [set_first, set_rest], jnp.float32)
    panels = [("direct", direct), ("second", second), ("far", third)]
    back_part = tile_product(
        panels, [set_first, set_rest], jnp.bfloat16, back_part, [grad_got]
    )

    def deliver(value):
        one = send(value, lambda c, j, z: (c, j, z ^ 1) if j == z % 2 else (c, 1 - j, z))
        two = send(value, lambda c, j, z: None if j == z % 2 else (c, 1 - j, z ^ 1))
        return one, two

    act, back_part = lax.optimization_barrier((act, back_part))
    act_one, act_two = deliver(act)
    act_near = jnp.where(home, act, act_one)
    act_far = jnp.where(home, act_one, act_two)
    activated = jnp.concatenate(
        [jnp.where(j == 0, act_near, act_far), jnp.where(j == 0, act_far, act_near)], axis=1
    )

    back = join(back_part)
    back_one, back_two = deliver(back)

    grad = add_after([grad, grad_got], back_part)
    step = 1
    while step < shape[0]:
        flips = [step] if step * 2 >= shape[0] else [step, 2 * step, 3 * step]
        got = [send(grad, lambda c, j, z, s=s: (c ^ s, j, z)) for s in flips]
        grad = add_after([grad, *got], back)
        step *= 2 if len(flips) == 1 else 4
    grad_rest = send(grad, sibling)
    input_grad, weight_grad = final(back, back_one, back_two, weight, grad, grad_rest)
    return (activated, input_grad, weight_grad)


def solution(mesh):
    return jax.shard_map(
        per_device,
        mesh=mesh,
        in_specs=(
            P("rows", None),
            P(),
            P("rows", None),
            P("rows", None, "rep", None, None),
            P(None, "rows", None, "rep"),
            P("rows", None),
        ),
        out_specs=(P("rows", None), P("rows", None), P()),
        check_vma=False,
    )
```

```python
import functools

import jax
import jax.numpy as jnp
from jax import lax
from jax.experimental import pallas as pl
from jax.experimental.pallas import tpu as pltpu
from jax.sharding import PartitionSpec as P

AXES = ("rows", "rep")
TOGETHER = 4


def route(shape, move):
    chips, reps = shape
    pairs = []
    for c in range(chips):
        for j in range(2):
            for z in range(reps):
                to = move(c, j, z)
                if to is not None:
                    target = ((to[0] % chips) * 2 + to[1]) * reps + to[2]
                    pairs.append(((c * 2 + j) * reps + z, target))
    return pairs


def place():
    r = lax.axis_index("rows")
    z = lax.axis_index("rep")
    return r % 2, z, z % 2


def when_of(case):
    j, z, p = place()
    home = j == p
    relay = jnp.logical_and(
        lax.axis_size("rows") == 8, (lax.axis_index("rows") // 2 + z) % 2 == 1
    )
    return {
        "home": home,
        "away": jnp.logical_not(home),
        "relay": relay,
        "still": jnp.logical_not(relay),
        "relay home": jnp.logical_and(relay, home),
        "relay away": jnp.logical_and(relay, jnp.logical_not(home)),
        "still home": jnp.logical_and(jnp.logical_not(relay), home),
        "still away": jnp.logical_and(jnp.logical_not(relay), jnp.logical_not(home)),
    }[case]


def start_chosen(choice, make):
    if len(choice) == 1:
        make(choice[0][1]).start()
        return
    for case, ref in choice:

        @pl.when(when_of(case))
        def _(ref=ref):
            make(ref).start()


def halves_kernel(x_ref, near_ref, far_ref, sems):
    j, _, _ = place()
    half = near_ref.shape[1]
    copies = []
    for i, out in enumerate((near_ref, far_ref)):
        start = pl.multiple_of((j if i == 0 else 1 - j) * half, half)
        copy = pltpu.make_async_copy(x_ref.at[:, pl.ds(start, half)], out, sems.at[i])
        copy.start()
        copies.append(copy)
    for copy in copies:
        copy.wait()


def halves(value):
    rows, width = value.shape
    part = jax.ShapeDtypeStruct((rows, width // 2), value.dtype)
    hbm = pl.BlockSpec(memory_space=pltpu.HBM)
    return pl.pallas_call(
        halves_kernel,
        out_shape=(part, part),
        in_specs=[hbm],
        out_specs=(hbm, hbm),
        scratch_shapes=[pltpu.SemaphoreType.DMA((2,))],
        compiler_params=pltpu.CompilerParams(vmem_limit_bytes=1024 * 1024),
        name="halves",
    )(value)


def pick_kernel(cases, *refs):
    refs = list(refs)
    choices = [[(case, refs.pop(0)) for case in each] for each in cases]
    outs, sems = refs[:-1], refs[-1]

    def copy_to(i):
        return lambda ref: pltpu.make_async_copy(ref, outs[i], sems.at[i])

    for i, choice in enumerate(choices):
        start_chosen(choice, copy_to(i))
    for i, choice in enumerate(choices):
        copy_to(i)(choice[0][1]).wait()


def pick(*choices):
    hbm = pl.BlockSpec(memory_space=pltpu.HBM)
    arrays = [array for choice in choices for _, array in choice]
    shape = jax.ShapeDtypeStruct(arrays[0].shape, arrays[0].dtype)
    return pl.pallas_call(
        functools.partial(pick_kernel, [[case for case, _ in choice] for choice in choices]),
        out_shape=(shape,) * len(choices),
        in_specs=[hbm] * len(arrays),
        out_specs=(hbm,) * len(choices),
        scratch_shapes=[pltpu.SemaphoreType.DMA((len(choices),))],
        compiler_params=pltpu.CompilerParams(vmem_limit_bytes=1024 * 1024),
        name="pick",
    )(*arrays)


def slots_kernel(dead, coords_ref, counts_ref, out_ref):
    _, z, _ = place()
    _, reach, slots = coords_ref.shape
    for d in range(reach):
        for k in range(slots):
            live = z * slots + k < counts_ref[d]
            out_ref[0, d * slots + k] = jnp.where(live, coords_ref[0, d, k], dead)
            out_ref[1, d * slots + k] = coords_ref[1, d, k]


def slot_blocks(coords, counts, dead):
    smem = pl.BlockSpec(memory_space=pltpu.SMEM)
    return pl.pallas_call(
        functools.partial(slots_kernel, dead),
        out_shape=jax.ShapeDtypeStruct((2, coords.shape[1] * coords.shape[2]), jnp.int32),
        in_specs=[smem, smem],
        out_specs=smem,
        compiler_params=pltpu.CompilerParams(vmem_limit_bytes=1024 * 1024),
        name="slot_blocks",
    )(coords, counts)


def offset_of(kind):
    _, _, p = place()
    even = (lax.axis_index("rows") // 2) % 2 == 0
    return {
        "self": 2,
        "near": jnp.where(p == 0, 3, 1),
        "far": jnp.where(p == 0, 1, 3),
        "direct": jnp.where(even, 4, 0),
        "second": jnp.where(even, 0, 4),
    }[kind]


def tile_kernel(kinds, cases, sets, summed, waits, *refs):
    refs = list(refs)
    metas = [refs.pop(0) for _ in range(sum(sets))]
    tiles = [refs.pop(0) for _ in range(sum(sets))]
    panels = [[(case, refs.pop(0)) for case in each] for each in cases]
    before = refs.pop(0) if summed else None
    out_ref, acc_ref, tile_buf, panel_buf, tile_sems, panel_sems = refs[waits:]
    slots, tile = tile_buf.shape[2], tile_buf.shape[-1]
    rows = out_ref.shape[0]
    j, _, p = place()
    home = j == p
    offsets = [offset_of(kind) for kind in kinds]

    def tile_copy(ref, i, s):
        return pltpu.make_async_copy(ref.at[offsets[i]], tile_buf.at[i, s], tile_sems.at[i, s])

    def panel_copy(i):
        return lambda ref: pltpu.make_async_copy(ref, panel_buf.at[i], panel_sems.at[i])

    for i in range(len(kinds)):
        start_chosen(panels[i], panel_copy(i))
        at = 0
        for s, members in enumerate(sets):
            cases_of_set = ["home", "away"] if members == 2 else [None]
            start_chosen(
                list(zip(cases_of_set, tiles[at : at + members])),
                lambda ref, i=i, s=s: tile_copy(ref, i, s),
            )
            at += members
    if summed:
        acc_ref[:rows, :] = before[...]
    else:
        acc_ref[...] = jnp.zeros_like(acc_ref)
    for i in range(len(kinds)):
        d = offsets[i]
        panel_copy(i)(panels[i][0][1]).wait()
        at = 0
        for s, members in enumerate(sets):
            tile_copy(tiles[at], i, s).wait()
            for first in range(0, slots, TOGETHER):
                prods = []
                for k in range(first, min(first + TOGETHER, slots)):
                    row = metas[at][0, d * slots + k]
                    col = metas[at][1, d * slots + k]
                    if members == 2:
                        row = jnp.where(home, row, metas[at + 1][0, d * slots + k])
                        col = jnp.where(home, col, metas[at + 1][1, d * slots + k])
                    col = pl.multiple_of(col * tile, tile)
                    prod = jnp.dot(
                        tile_buf[i, s, k],
                        panel_buf[i, pl.ds(col, tile), :],
                        preferred_element_type=jnp.float32,
                    )
                    prods.append((pl.multiple_of(row * tile, tile), prod))
                for row, prod in prods:
                    acc_ref[pl.ds(row, tile), :] += prod
            at += members
    out_ref[...] = acc_ref[:rows, :].astype(out_ref.dtype)


def tile_product(named, sets, dtype, before=None, after=()):
    kinds = [kind for kind, _ in named]
    cases = [[case for case, _ in choice] for _, choice in named]
    panels = [panel for _, choice in named for _, panel in choice]
    metas = [meta for members in sets for meta, _ in members]
    tiles = [values for members in sets for _, values in members]
    rows, width = panels[0].shape
    _, slots, tile, _ = tiles[0].shape
    smem = pl.BlockSpec(memory_space=pltpu.SMEM)
    vmem = pl.BlockSpec(memory_space=pltpu.VMEM)
    hbm = pl.BlockSpec(memory_space=pltpu.HBM)
    anywhere = pl.BlockSpec(memory_space=pl.ANY)
    count = len(kinds) * len(sets) * slots
    summed = before is not None
    return pl.pallas_call(
        functools.partial(
            tile_kernel, kinds, cases, [len(m) for m in sets], summed, len(after)
        ),
        out_shape=jax.ShapeDtypeStruct((rows, width), dtype),
        in_specs=[smem] * len(metas)
        + [hbm] * len(tiles)
        + [anywhere] * len(panels)
        + [vmem] * summed
        + [anywhere] * len(after),
        out_specs=vmem,
        scratch_shapes=[
            pltpu.VMEM((rows + tile, width), jnp.float32),
            pltpu.VMEM((len(kinds), len(sets), slots, tile, tile), tiles[0].dtype),
            pltpu.VMEM((len(kinds), rows, width), panels[0].dtype),
            pltpu.SemaphoreType.DMA((len(kinds), len(sets))),
            pltpu.SemaphoreType.DMA((len(kinds),)),
        ],
        compiler_params=pltpu.CompilerParams(vmem_limit_bytes=8 * 1024 * 1024),
        cost_estimate=pl.CostEstimate(
            flops=2 * count * tile * tile * width,
            bytes_accessed=count * tile * tile * 2 + len(kinds) * rows * width * 2,
            transcendentals=0,
        ),
        name="tile_product",
    )(*metas, *tiles, *panels, *([before] if summed else []), *after)


def middle_kernel(near_ref, far_ref, w_ref, cot_ref, cot_swap_ref, act_ref, adj_ref):
    j, _, p = place()
    half = near_ref.shape[1]
    near = pl.multiple_of(j * half, half)
    far = pl.multiple_of((1 - j) * half, half)
    cols = pl.ds(near, half)
    agg = jnp.dot(
        near_ref[...], w_ref[pl.ds(near, half), cols], preferred_element_type=jnp.float32
    )
    agg += jnp.dot(far_ref[...], w_ref[pl.ds(far, half), cols], preferred_element_type=jnp.float32)
    sig = jax.nn.sigmoid(agg)
    act_ref[...] = (agg * sig).astype(act_ref.dtype)
    slope = sig * (1.0 + agg * (1.0 - sig))
    cot = jnp.where(j == p, cot_ref[...], cot_swap_ref[...])
    adj_ref[...] = (cot.astype(jnp.float32) * slope).astype(adj_ref.dtype)


def middle(near, far, weight, cot, cot_swap):
    vmem = pl.BlockSpec(memory_space=pltpu.VMEM)
    rows, width = near.shape
    out = jax.ShapeDtypeStruct((rows, width), jnp.bfloat16)
    return pl.pallas_call(
        middle_kernel,
        out_shape=(out, out),
        in_specs=[vmem] * 5,
        out_specs=(vmem, vmem),
        compiler_params=pltpu.CompilerParams(vmem_limit_bytes=8 * 1024 * 1024),
        cost_estimate=pl.CostEstimate(
            flops=4 * rows * width * width,
            bytes_accessed=10 * rows * width,
            transcendentals=rows * width,
        ),
        name="middle",
    )(near, far, weight, cot, cot_swap)


def grad_kernel(scale, near_ref, far_ref, adj_ref, after_ref, out_ref):
    j, _, _ = place()
    half = near_ref.shape[1]
    dims = (((0,), (0,)), ((), ()))
    for i, ref in enumerate((near_ref, far_ref)):
        start = pl.multiple_of((j if i == 0 else 1 - j) * half, half)
        block = lax.dot_general(ref[...], adj_ref[...], dims, preferred_element_type=jnp.float32)
        out_ref[pl.ds(start, half), :] = (scale * block).astype(out_ref.dtype)


def grad_block(scale, near, far, adj, after):
    vmem = pl.BlockSpec(memory_space=pltpu.VMEM)
    rows, width = near.shape
    return pl.pallas_call(
        functools.partial(grad_kernel, scale),
        out_shape=jax.ShapeDtypeStruct((2 * width, width), jnp.bfloat16),
        in_specs=[vmem] * 3 + [pl.BlockSpec(memory_space=pl.ANY)],
        out_specs=vmem,
        compiler_params=pltpu.CompilerParams(vmem_limit_bytes=8 * 1024 * 1024),
        cost_estimate=pl.CostEstimate(
            flops=4 * rows * width * width, bytes_accessed=8 * rows * width, transcendentals=0
        ),
        name="grad_block",
    )(near, far, adj, after)


def add_kernel(count, *refs):
    values = [ref[...].astype(jnp.float32) for ref in refs[:count]]
    total = values[0] + values[1]
    if count == 4:
        total = total + (values[2] + values[3])
    refs[-1][...] = total.astype(refs[-1].dtype)


def add_after(values, dtype, *after):
    vmem = pl.BlockSpec(memory_space=pltpu.VMEM)
    return pl.pallas_call(
        functools.partial(add_kernel, len(values)),
        out_shape=jax.ShapeDtypeStruct(values[0].shape, dtype),
        in_specs=[vmem] * len(values) + [pl.BlockSpec(memory_space=pl.ANY)] * len(after),
        out_specs=vmem,
        compiler_params=pltpu.CompilerParams(vmem_limit_bytes=4 * 1024 * 1024),
        name="add_after",
    )(*values, *after)


def final_kernel(own_ref, one_ref, two_ref, w_ref, grad_ref, rest_ref, out_ref, grad_out_ref):
    j, _, p = place()
    half = own_ref.shape[1]
    near_cols = pl.ds(pl.multiple_of(j * half, half), half)
    far_cols = pl.ds(pl.multiple_of((1 - j) * half, half), half)
    grad_out_ref[:, near_cols] = grad_ref[...]
    grad_out_ref[:, far_cols] = rest_ref[...]
    near = jnp.where(j == p, own_ref[...], one_ref[...])
    far = jnp.where(j == p, one_ref[...], two_ref[...])
    dims = (((1,), (1,)), ((), ()))
    total = lax.dot_general(near, w_ref[:, near_cols], dims, preferred_element_type=jnp.float32)
    total += lax.dot_general(far, w_ref[:, far_cols], dims, preferred_element_type=jnp.float32)
    out_ref[...] = total.astype(out_ref.dtype)


def final(own, one, two, weight, grad, rest):
    vmem = pl.BlockSpec(memory_space=pltpu.VMEM)
    rows = own.shape[0]
    wide = weight.shape[0]
    return pl.pallas_call(
        final_kernel,
        out_shape=(
            jax.ShapeDtypeStruct((rows, wide), jnp.bfloat16),
            jax.ShapeDtypeStruct(weight.shape, jnp.float32),
        ),
        in_specs=[vmem] * 6,
        out_specs=(vmem, vmem),
        compiler_params=pltpu.CompilerParams(vmem_limit_bytes=8 * 1024 * 1024),
        cost_estimate=pl.CostEstimate(
            flops=2 * rows * wide * wide, bytes_accessed=8 * rows * wide, transcendentals=0
        ),
        name="final",
    )(own, one, two, weight, grad, rest)


def per_device(node_feats, weight, cotangent, tile_values, tile_coords, tile_counts):
    groups = lax.axis_size("rows")
    reps = lax.axis_size("rep")
    shape = (groups // 2, reps)
    j, z, p = place()
    home = j == p
    scale = (node_feats.shape[0] * groups) ** (-0.5)

    def send(value, move):
        return lax.ppermute(value, AXES, route(shape, move))

    def sibling(c, j, z):
        return (c, 1 - j, z)

    def across(c, j, z):
        return (c, j, (z + reps // 2) % reps)

    own = tile_values[0]
    blocks = node_feats.shape[0] // own.shape[-1]

    def to_home(c, j, z):
        return (c, 1 - j, z) if j == z % 2 else (c, j, z ^ 1)

    four = shape[0] == 4

    def to_direct(c, j, z):
        return (c ^ 1, j, z)

    def to_second(c, j, z):
        return (c ^ 2, j, z) if four else (c + 1 if c % 2 else c - 1, j, z)

    def to_far(c, j, z):
        return (c ^ 1, j, z) if four else (c - 1 if z % 2 else c + 1, j, z)

    def stage_one(c, j, z):
        if j == z % 2:
            return (c ^ 1, j, z)
        return (c ^ 2, j, z) if four and (c + z) % 2 else None

    def stage_one_cross(c, j, z):
        to = stage_one(c, j, z)
        return to and (to[0], 1 - j, z)

    first = send(own, to_home)
    mine, yours = halves(node_feats)
    one = send(mine, stage_one)
    two = send(yours, stage_one_cross)
    swapped = send(yours, sibling)
    self_choice = [("home", mine), ("away", swapped)]
    direct_choice = [("home", one), ("away", two)]
    second, far = pick(
        direct_choice if four else self_choice,
        [
            ("still home", swapped),
            ("still away", mine),
            ("relay home", two),
            ("relay away", one),
        ],
    )
    second = send(second, to_second)
    far = send(far, to_far)
    coords, counts, swapped = lax.optimization_barrier((tile_coords, tile_counts, swapped))
    meta = slot_blocks(coords[:, 0], counts[0], blocks)
    meta_b = send(meta, to_home)
    meta_far = send(meta, lambda c, j, z: None if j == z % 2 else (c, 1 - j, z ^ 1))
    first, second, far, meta_b, meta_far = lax.optimization_barrier(
        (first, second, far, meta_b, meta_far)
    )
    other_first = send(first, lambda c, j, z: (c, 1 - j, z) if j == z % 2 else None)

    set_first = [(meta_b, first)]
    set_rest = [(meta, own), (meta_far, other_first)]
    panels = [
        ("self", [("home", mine), ("away", swapped)]),
        ("near", [("home", swapped), ("away", mine)]),
        ("direct", direct_choice),
        ("second", [(None, second)]),
        ("far", [(None, far)]),
    ]
    part = tile_product(panels, [set_first], jnp.float32)
    part = tile_product(panels, [set_rest], jnp.bfloat16, part)

    def join(value):
        other = send(value, across)
        return (value.astype(jnp.float32) + other.astype(jnp.float32)).astype(jnp.bfloat16)

    near = join(part)
    far_half = send(near, sibling)
    cot, cot_yours = halves(cotangent)
    act, adj = middle(near, far_half, weight, cot, send(cot_yours, sibling))

    direct = send(adj, to_direct)
    near_one = send(
        adj, lambda c, j, z: (c if (c + z) % 2 or not four else c ^ 2, j, z ^ 1)
    )
    adj_later, near_one, direct = lax.optimization_barrier((adj, near_one, direct))
    second = send(direct if four else adj_later, to_second)
    far = send(near_one, to_far)
    near_choice = [("still", near_one)]
    if four:
        near_two = send(
            adj_later, lambda c, j, z: None if (c + z) % 2 else (c, j, z ^ 1)
        )
        near_choice.append(("relay", near_two))
    grad = grad_block(scale, near, far_half, adj, direct)
    grad_got = send(grad, lambda c, j, z: (c, j, z ^ 1))
    panels = [("self", [(None, adj)]), ("direct", [(None, direct)])]
    back_part = tile_product(panels, [set_first, set_rest], jnp.float32)
    panels = [("near", near_choice), ("second", [(None, second)]), ("far", [(None, far)])]
    back_part = tile_product(
        panels, [set_first, set_rest], jnp.bfloat16, back_part, [grad_got]
    )

    def deliver(value):
        one = send(value, lambda c, j, z: (c, j, z ^ 1) if j == z % 2 else (c, 1 - j, z))
        two = send(value, lambda c, j, z: None if j == z % 2 else (c, 1 - j, z ^ 1))
        return one, two

    act, back_part = lax.optimization_barrier((act, back_part))
    act_one, act_two = deliver(act)
    act_near = jnp.where(home, act, act_one)
    act_far = jnp.where(home, act_one, act_two)
    activated = jnp.concatenate(
        [jnp.where(j == 0, act_near, act_far), jnp.where(j == 0, act_far, act_near)], axis=1
    )

    back = join(back_part)
    back_one, back_two = deliver(back)

    grad = add_after([grad, grad_got], jnp.bfloat16, back_part)
    step = 1
    while step < shape[0]:
        flips = [step] if step * 2 >= shape[0] else [step, 2 * step, 3 * step]
        got = [send(grad, lambda c, j, z, s=s: (c ^ s, j, z)) for s in flips]
        step *= 2 if len(flips) == 1 else 4
        grad = add_after([grad, *got], jnp.bfloat16 if step < shape[0] else jnp.float32, back)
    grad_rest = send(grad, sibling)
    input_grad, weight_grad = final(back, back_one, back_two, weight, grad, grad_rest)
    return (activated, input_grad, weight_grad)


def solution(mesh):
    return jax.shard_map(
        per_device,
        mesh=mesh,
        in_specs=(
            P("rows", None),
            P(),
            P("rows", None),
            P("rows", None, "rep", None, None),
            P(None, "rows", None, "rep"),
            P("rows", None),
        ),
        out_specs=(P("rows", None), P("rows", None), P()),
        check_vma=False,
    )
```

```python
import functools

import jax
import jax.numpy as jnp
from jax import lax
from jax.experimental import pallas as pl
from jax.experimental.pallas import tpu as pltpu
from jax.sharding import PartitionSpec as P

AXES = ("rows", "rep")
WEIGH = 200


def route(shape, move):
    chips, reps = shape
    pairs = []
    for c in range(chips):
        for j in range(2):
            for z in range(reps):
                to = move(c, j, z)
                if to is not None:
                    target = ((to[0] % chips) * 2 + to[1]) * reps + to[2]
                    pairs.append(((c * 2 + j) * reps + z, target))
    return pairs


def place():
    r = lax.axis_index("rows")
    z = lax.axis_index("rep")
    return r % 2, z, z % 2


def when_of(case):
    j, z, p = place()
    home = j == p
    relay = jnp.logical_and(
        lax.axis_size("rows") == 8, (lax.axis_index("rows") // 2 + z) % 2 == 1
    )
    return {
        "home": home,
        "away": jnp.logical_not(home),
        "relay": relay,
        "still": jnp.logical_not(relay),
        "relay home": jnp.logical_and(relay, home),
        "relay away": jnp.logical_and(relay, jnp.logical_not(home)),
        "still home": jnp.logical_and(jnp.logical_not(relay), home),
        "still away": jnp.logical_and(jnp.logical_not(relay), jnp.logical_not(home)),
    }[case]


def start_chosen(choice, make):
    if len(choice) == 1:
        make(choice[0][1]).start()
        return
    for case, ref in choice:

        @pl.when(when_of(case))
        def _(ref=ref):
            make(ref).start()


def halves_kernel(x_ref, near_ref, far_ref, sems):
    j, _, _ = place()
    half = near_ref.shape[1]
    copies = []
    for i, out in enumerate((near_ref, far_ref)):
        start = pl.multiple_of((j if i == 0 else 1 - j) * half, half)
        copy = pltpu.make_async_copy(x_ref.at[:, pl.ds(start, half)], out, sems.at[i])
        copy.start()
        copies.append(copy)
    for copy in copies:
        copy.wait()


def halves(value):
    rows, width = value.shape
    part = jax.ShapeDtypeStruct((rows, width // 2), value.dtype)
    hbm = pl.BlockSpec(memory_space=pltpu.HBM)
    return pl.pallas_call(
        halves_kernel,
        out_shape=(part, part),
        in_specs=[hbm],
        out_specs=(hbm, hbm),
        scratch_shapes=[pltpu.SemaphoreType.DMA((2,))],
        compiler_params=pltpu.CompilerParams(vmem_limit_bytes=1024 * 1024),
        name="halves",
    )(value)


def pick_kernel(cases, *refs):
    refs = list(refs)
    choices = [[(case, refs.pop(0)) for case in each] for each in cases]
    outs, sems = refs[:-1], refs[-1]

    def copy_to(i):
        return lambda ref: pltpu.make_async_copy(ref, outs[i], sems.at[i])

    for i, choice in enumerate(choices):
        start_chosen(choice, copy_to(i))
    for i, choice in enumerate(choices):
        copy_to(i)(choice[0][1]).wait()


def pick(*choices):
    hbm = pl.BlockSpec(memory_space=pltpu.HBM)
    arrays = [array for choice in choices for _, array in choice]
    shape = jax.ShapeDtypeStruct(arrays[0].shape, arrays[0].dtype)
    return pl.pallas_call(
        functools.partial(pick_kernel, [[case for case, _ in choice] for choice in choices]),
        out_shape=(shape,) * len(choices),
        in_specs=[hbm] * len(arrays),
        out_specs=(hbm,) * len(choices),
        scratch_shapes=[pltpu.SemaphoreType.DMA((len(choices),))],
        compiler_params=pltpu.CompilerParams(vmem_limit_bytes=1024 * 1024),
        name="pick",
    )(*arrays)


def slots_kernel(dead, coords_ref, counts_ref, out_ref):
    _, z, _ = place()
    _, reach, slots = coords_ref.shape
    for d in range(reach):
        for k in range(slots):
            live = z * slots + k < counts_ref[d]
            out_ref[0, d * slots + k] = jnp.where(live, coords_ref[0, d, k], dead)
            out_ref[1, d * slots + k] = coords_ref[1, d, k]


def slot_blocks(coords, counts, dead):
    smem = pl.BlockSpec(memory_space=pltpu.SMEM)
    return pl.pallas_call(
        functools.partial(slots_kernel, dead),
        out_shape=jax.ShapeDtypeStruct((2, coords.shape[1] * coords.shape[2]), jnp.int32),
        in_specs=[smem, smem],
        out_specs=smem,
        compiler_params=pltpu.CompilerParams(vmem_limit_bytes=1024 * 1024),
        name="slot_blocks",
    )(coords, counts)


def offset_of(kind):
    _, _, p = place()
    even = (lax.axis_index("rows") // 2) % 2 == 0
    return {
        "self": 2,
        "near": jnp.where(p == 0, 3, 1),
        "far": jnp.where(p == 0, 1, 3),
        "direct": jnp.where(even, 4, 0),
        "second": jnp.where(even, 0, 4),
    }[kind]


def chosen(choice, read):
    value = read(choice[0][1])
    for case, ref in choice[1:]:
        value = jnp.where(when_of(case), read(ref), value)
    return value


def tile_kernel(kinds, cases, sets, summed, waits, *refs):
    refs = list(refs)
    metas = [[(case, refs.pop(0)) for case in each] for each in sets]
    tiles = [[(case, refs.pop(0)) for case in each] for each in sets]
    panels = [[(case, refs.pop(0)) for case in each] for each in cases]
    before = refs.pop(0) if summed else None
    out_ref, acc_ref = refs[waits:]
    _, slots, tile, _ = tiles[0][0][1].shape
    rows = out_ref.shape[0]
    if summed:
        acc_ref[:rows, :] = before[...]
    else:
        acc_ref[...] = jnp.zeros_like(acc_ref)
    for i, kind in enumerate(kinds):
        d = offset_of(kind)
        for s in range(len(sets)):
            for k in range(slots):
                row = chosen(metas[s], lambda ref: ref[0, d * slots + k])
                col = chosen(metas[s], lambda ref: ref[1, d * slots + k])
                row = pl.multiple_of(row * tile, tile)
                col = pl.multiple_of(col * tile, tile)
                acc_ref[pl.ds(row, tile), :] += jnp.dot(
                    chosen(tiles[s], lambda ref: ref[d, k]),
                    chosen(panels[i], lambda ref: ref[pl.ds(col, tile), :]),
                    preferred_element_type=jnp.float32,
                )
    out_ref[...] = acc_ref[:rows, :].astype(out_ref.dtype)


def tile_product(named, sets, dtype, before=None, after=(), weigh=1):
    kinds = [kind for kind, _ in named]
    cases = [[case for case, _ in choice] for _, choice in named]
    panels = [panel for _, choice in named for _, panel in choice]
    metas = [meta for choice in sets for _, (meta, _) in choice]
    tiles = [values for choice in sets for _, (_, values) in choice]
    rows, width = panels[0].shape
    _, slots, tile, _ = tiles[0].shape
    smem = pl.BlockSpec(memory_space=pltpu.SMEM)
    vmem = pl.BlockSpec(memory_space=pltpu.VMEM)
    anywhere = pl.BlockSpec(memory_space=pl.ANY)
    count = len(kinds) * len(sets) * slots
    summed = before is not None
    return pl.pallas_call(
        functools.partial(
            tile_kernel,
            kinds,
            cases,
            [[case for case, _ in choice] for choice in sets],
            summed,
            len(after),
        ),
        out_shape=jax.ShapeDtypeStruct((rows, width), dtype),
        in_specs=[smem] * len(metas)
        + [vmem] * (len(tiles) + len(panels) + summed)
        + [anywhere] * len(after),
        out_specs=vmem,
        scratch_shapes=[pltpu.VMEM((rows + tile, width), jnp.float32)],
        compiler_params=pltpu.CompilerParams(vmem_limit_bytes=12 * 1024 * 1024),
        cost_estimate=pl.CostEstimate(
            flops=weigh * 2 * count * tile * tile * width,
            bytes_accessed=weigh * (count * tile * tile * 2 + len(kinds) * rows * width * 2),
            transcendentals=0,
        ),
        name="tile_product",
    )(*metas, *tiles, *panels, *([before] if summed else []), *after)


def middle_kernel(near_ref, far_ref, w_ref, cot_ref, cot_swap_ref, act_ref, adj_ref):
    j, _, p = place()
    half = near_ref.shape[1]
    near = pl.multiple_of(j * half, half)
    far = pl.multiple_of((1 - j) * half, half)
    cols = pl.ds(near, half)
    agg = jnp.dot(
        near_ref[...], w_ref[pl.ds(near, half), cols], preferred_element_type=jnp.float32
    )
    agg += jnp.dot(far_ref[...], w_ref[pl.ds(far, half), cols], preferred_element_type=jnp.float32)
    sig = jax.nn.sigmoid(agg)
    act_ref[...] = (agg * sig).astype(act_ref.dtype)
    slope = sig * (1.0 + agg * (1.0 - sig))
    cot = jnp.where(j == p, cot_ref[...], cot_swap_ref[...])
    adj_ref[...] = (cot.astype(jnp.float32) * slope).astype(adj_ref.dtype)


def middle(near, far, weight, cot, cot_swap):
    vmem = pl.BlockSpec(memory_space=pltpu.VMEM)
    rows, width = near.shape
    out = jax.ShapeDtypeStruct((rows, width), jnp.bfloat16)
    return pl.pallas_call(
        middle_kernel,
        out_shape=(out, out),
        in_specs=[vmem] * 5,
        out_specs=(vmem, vmem),
        compiler_params=pltpu.CompilerParams(vmem_limit_bytes=8 * 1024 * 1024),
        cost_estimate=pl.CostEstimate(
            flops=4 * rows * width * width,
            bytes_accessed=10 * rows * width,
            transcendentals=rows * width,
        ),
        name="middle",
    )(near, far, weight, cot, cot_swap)


def grad_kernel(scale, near_ref, far_ref, adj_ref, after_ref, out_ref):
    j, _, _ = place()
    half = near_ref.shape[1]
    dims = (((0,), (0,)), ((), ()))
    for i, ref in enumerate((near_ref, far_ref)):
        start = pl.multiple_of((j if i == 0 else 1 - j) * half, half)
        block = lax.dot_general(ref[...], adj_ref[...], dims, preferred_element_type=jnp.float32)
        out_ref[pl.ds(start, half), :] = (scale * block).astype(out_ref.dtype)


def grad_block(scale, near, far, adj, after):
    vmem = pl.BlockSpec(memory_space=pltpu.VMEM)
    rows, width = near.shape
    return pl.pallas_call(
        functools.partial(grad_kernel, scale),
        out_shape=jax.ShapeDtypeStruct((2 * width, width), jnp.bfloat16),
        in_specs=[vmem] * 3 + [pl.BlockSpec(memory_space=pl.ANY)],
        out_specs=vmem,
        compiler_params=pltpu.CompilerParams(vmem_limit_bytes=8 * 1024 * 1024),
        cost_estimate=pl.CostEstimate(
            flops=4 * rows * width * width, bytes_accessed=8 * rows * width, transcendentals=0
        ),
        name="grad_block",
    )(near, far, adj, after)


def add_kernel(count, *refs):
    values = [ref[...].astype(jnp.float32) for ref in refs[:count]]
    total = values[0] + values[1]
    if count == 4:
        total = total + (values[2] + values[3])
    refs[-1][...] = total.astype(refs[-1].dtype)


def add_after(values, dtype, *after):
    vmem = pl.BlockSpec(memory_space=pltpu.VMEM)
    return pl.pallas_call(
        functools.partial(add_kernel, len(values)),
        out_shape=jax.ShapeDtypeStruct(values[0].shape, dtype),
        in_specs=[vmem] * len(values) + [pl.BlockSpec(memory_space=pl.ANY)] * len(after),
        out_specs=vmem,
        compiler_params=pltpu.CompilerParams(vmem_limit_bytes=4 * 1024 * 1024),
        name="add_after",
    )(*values, *after)


def final_kernel(*refs):
    back, act, (w_ref, grad_ref, rest_ref), outs = refs[:3], refs[3:6], refs[6:9], refs[9:]
    out_ref, act_ref, grad_out_ref = outs
    j, _, p = place()
    half = back[0].shape[1]
    near_cols = pl.ds(pl.multiple_of(j * half, half), half)
    far_cols = pl.ds(pl.multiple_of((1 - j) * half, half), half)

    def halves_of(parts):
        own, one, two = parts
        near = jnp.where(j == p, own[...], one[...])
        return near, jnp.where(j == p, one[...], two[...])

    near, far = halves_of(back)
    dims = (((1,), (1,)), ((), ()))
    total = lax.dot_general(near, w_ref[:, near_cols], dims, preferred_element_type=jnp.float32)
    total += lax.dot_general(far, w_ref[:, far_cols], dims, preferred_element_type=jnp.float32)
    out_ref[...] = total.astype(out_ref.dtype)
    act_ref[:, near_cols], act_ref[:, far_cols] = halves_of(act)
    grad_out_ref[:, near_cols] = grad_ref[...]
    grad_out_ref[:, far_cols] = rest_ref[...]


def final(back, act, weight, grad, rest):
    vmem = pl.BlockSpec(memory_space=pltpu.VMEM)
    rows = back[0].shape[0]
    wide = weight.shape[0]
    whole = jax.ShapeDtypeStruct((rows, wide), jnp.bfloat16)
    return pl.pallas_call(
        final_kernel,
        out_shape=(whole, whole, jax.ShapeDtypeStruct(weight.shape, jnp.float32)),
        in_specs=[vmem] * 9,
        out_specs=(vmem,) * 3,
        compiler_params=pltpu.CompilerParams(vmem_limit_bytes=8 * 1024 * 1024),
        cost_estimate=pl.CostEstimate(
            flops=2 * rows * wide * wide, bytes_accessed=8 * rows * wide, transcendentals=0
        ),
        name="final",
    )(*back, *act, weight, grad, rest)


def per_device(node_feats, weight, cotangent, tile_values, tile_coords, tile_counts):
    groups = lax.axis_size("rows")
    reps = lax.axis_size("rep")
    shape = (groups // 2, reps)
    j, z, p = place()
    home = j == p
    scale = (node_feats.shape[0] * groups) ** (-0.5)

    def send(value, move):
        return lax.ppermute(value, AXES, route(shape, move))

    def sibling(c, j, z):
        return (c, 1 - j, z)

    def across(c, j, z):
        return (c, j, (z + reps // 2) % reps)

    own = tile_values[0]
    blocks = node_feats.shape[0] // own.shape[-1]

    def to_home(c, j, z):
        return (c, 1 - j, z) if j == z % 2 else (c, j, z ^ 1)

    four = shape[0] == 4

    def to_direct(c, j, z):
        return (c ^ 1, j, z)

    def to_second(c, j, z):
        return (c ^ 2, j, z) if four else (c + 1 if c % 2 else c - 1, j, z)

    def to_far(c, j, z):
        return (c ^ 1, j, z) if four else (c - 1 if z % 2 else c + 1, j, z)

    def stage_one(c, j, z):
        if j == z % 2:
            return (c ^ 1, j, z)
        return (c ^ 2, j, z) if four and (c + z) % 2 else None

    def stage_one_cross(c, j, z):
        to = stage_one(c, j, z)
        return to and (to[0], 1 - j, z)

    first = send(own, to_home)
    mine, yours = halves(node_feats)
    one = send(mine, stage_one)
    two = send(yours, stage_one_cross)
    swapped = send(yours, sibling)
    self_choice = [("home", mine), ("away", swapped)]
    direct_choice = [("home", one), ("away", two)]
    second, far = pick(
        direct_choice if four else self_choice,
        [
            ("still home", swapped),
            ("still away", mine),
            ("relay home", two),
            ("relay away", one),
        ],
    )
    second = send(second, to_second)
    far = send(far, to_far)
    coords, counts, swapped = lax.optimization_barrier((tile_coords, tile_counts, swapped))
    meta = slot_blocks(coords[:, 0], counts[0], blocks)
    meta_b = send(meta, to_home)
    meta_far = send(meta, lambda c, j, z: None if j == z % 2 else (c, 1 - j, z ^ 1))
    first, one, two = lax.optimization_barrier((first, one, two))
    other_first = send(first, lambda c, j, z: (c, 1 - j, z) if j == z % 2 else None)

    set_first = [(None, (meta_b, first))]
    set_rest = [("home", (meta, own)), ("away", (meta_far, other_first))]
    panels = [
        ("self", [("home", mine), ("away", swapped)]),
        ("near", [("home", swapped), ("away", mine)]),
        ("direct", direct_choice),
        ("second", [(None, second)]),
        ("far", [(None, far)]),
    ]
    part = tile_product(panels, [set_first], jnp.float32, weigh=WEIGH)
    part = tile_product(panels, [set_rest], jnp.bfloat16, part)

    def join(value):
        other = send(value, across)
        return (value.astype(jnp.float32) + other.astype(jnp.float32)).astype(jnp.bfloat16)

    near = join(part)
    far_half = send(near, sibling)
    cot, cot_yours = halves(cotangent)
    act, adj = middle(near, far_half, weight, cot, send(cot_yours, sibling))

    direct = send(adj, to_direct)
    near_one = send(
        adj, lambda c, j, z: (c if (c + z) % 2 or not four else c ^ 2, j, z ^ 1)
    )
    adj_later, near_one, direct = lax.optimization_barrier((adj, near_one, direct))
    second = send(direct if four else adj_later, to_second)
    grad = grad_block(scale, near, far_half, adj, direct)
    adj_later, grad = lax.optimization_barrier((adj_later, grad))
    far = send(near_one, to_far)
    near_choice = [("still", near_one)]
    if four:
        near_two = send(
            adj_later, lambda c, j, z: None if (c + z) % 2 else (c, j, z ^ 1)
        )
        near_choice.append(("relay", near_two))
    grad_got = send(grad, lambda c, j, z: (c, j, z ^ 1))
    panels = [("self", [(None, adj)]), ("direct", [(None, direct)])]
    back_part = tile_product(panels, [set_first, set_rest], jnp.float32)
    panels = [("near", near_choice), ("second", [(None, second)]), ("far", [(None, far)])]
    back_part = tile_product(
        panels, [set_first, set_rest], jnp.bfloat16, back_part, [grad_got]
    )

    def deliver(value):
        one = send(value, lambda c, j, z: (c, j, z ^ 1) if j == z % 2 else (c, 1 - j, z))
        two = send(value, lambda c, j, z: None if j == z % 2 else (c, 1 - j, z ^ 1))
        return one, two

    act_later, back_part = lax.optimization_barrier((act, back_part))
    act_parts = [act, *deliver(act_later)]
    grad = add_after([grad, grad_got], jnp.bfloat16, back_part)
    step = 1
    while step < shape[0]:
        got = send(grad, lambda c, j, z, s=step: (c ^ s, j, z))
        step *= 2
        if step < shape[0]:
            grad = add_after([grad, got], jnp.bfloat16)
    back = add_after([back_part, send(back_part, across)], jnp.bfloat16, got)
    back_parts = [back, *deliver(back)]
    grad = add_after([grad, got], jnp.float32, back)
    input_grad, activated, weight_grad = final(
        back_parts, act_parts, weight, grad, send(grad, sibling)
    )
    return (activated, input_grad, weight_grad)


def solution(mesh):
    return jax.shard_map(
        per_device,
        mesh=mesh,
        in_specs=(
            P("rows", None),
            P(),
            P("rows", None),
            P("rows", None, "rep", None, None),
            P(None, "rows", None, "rep"),
            P("rows", None),
        ),
        out_specs=(P("rows", None), P("rows", None), P()),
        check_vma=False,
    )
```

```python
import functools

import jax
import jax.numpy as jnp
from jax import lax
from jax.experimental import pallas as pl
from jax.experimental.pallas import tpu as pltpu
from jax.sharding import PartitionSpec as P

AXES = ("rows", "rep")
WEIGH = 200


def route(shape, move):
    chips, reps = shape
    pairs = []
    for c in range(chips):
        for j in range(2):
            for z in range(reps):
                to = move(c, j, z)
                if to is not None:
                    target = ((to[0] % chips) * 2 + to[1]) * reps + to[2]
                    pairs.append(((c * 2 + j) * reps + z, target))
    return pairs


def place():
    r = lax.axis_index("rows")
    z = lax.axis_index("rep")
    return r % 2, z, z % 2


def when_of(case):
    j, z, p = place()
    home = j == p
    relay = jnp.logical_and(
        lax.axis_size("rows") == 8, (lax.axis_index("rows") // 2 + z) % 2 == 1
    )
    return {
        "home": home,
        "away": jnp.logical_not(home),
        "relay": relay,
        "still": jnp.logical_not(relay),
        "relay home": jnp.logical_and(relay, home),
        "relay away": jnp.logical_and(relay, jnp.logical_not(home)),
        "still home": jnp.logical_and(jnp.logical_not(relay), home),
        "still away": jnp.logical_and(jnp.logical_not(relay), jnp.logical_not(home)),
    }[case]


def start_chosen(choice, make):
    if len(choice) == 1:
        make(choice[0][1]).start()
        return
    for case, ref in choice:

        @pl.when(when_of(case))
        def _(ref=ref):
            make(ref).start()


def halves_kernel(x_ref, near_ref, far_ref, sems):
    j, _, _ = place()
    half = near_ref.shape[1]
    copies = []
    for i, out in enumerate((near_ref, far_ref)):
        start = pl.multiple_of((j if i == 0 else 1 - j) * half, half)
        copy = pltpu.make_async_copy(x_ref.at[:, pl.ds(start, half)], out, sems.at[i])
        copy.start()
        copies.append(copy)
    for copy in copies:
        copy.wait()


def halves(value):
    rows, width = value.shape
    part = jax.ShapeDtypeStruct((rows, width // 2), value.dtype)
    hbm = pl.BlockSpec(memory_space=pltpu.HBM)
    return pl.pallas_call(
        halves_kernel,
        out_shape=(part, part),
        in_specs=[hbm],
        out_specs=(hbm, hbm),
        scratch_shapes=[pltpu.SemaphoreType.DMA((2,))],
        compiler_params=pltpu.CompilerParams(vmem_limit_bytes=1024 * 1024),
        name="halves",
    )(value)


def pick_kernel(cases, *refs):
    refs = list(refs)
    choices = [[(case, refs.pop(0)) for case in each] for each in cases]
    outs, sems = refs[:-1], refs[-1]

    def copy_to(i):
        return lambda ref: pltpu.make_async_copy(ref, outs[i], sems.at[i])

    for i, choice in enumerate(choices):
        start_chosen(choice, copy_to(i))
    for i, choice in enumerate(choices):
        copy_to(i)(choice[0][1]).wait()


def pick(*choices):
    hbm = pl.BlockSpec(memory_space=pltpu.HBM)
    arrays = [array for choice in choices for _, array in choice]
    shape = jax.ShapeDtypeStruct(arrays[0].shape, arrays[0].dtype)
    return pl.pallas_call(
        functools.partial(pick_kernel, [[case for case, _ in choice] for choice in choices]),
        out_shape=(shape,) * len(choices),
        in_specs=[hbm] * len(arrays),
        out_specs=(hbm,) * len(choices),
        scratch_shapes=[pltpu.SemaphoreType.DMA((len(choices),))],
        compiler_params=pltpu.CompilerParams(vmem_limit_bytes=1024 * 1024),
        name="pick",
    )(*arrays)


def slots_kernel(dead, coords_ref, counts_ref, out_ref):
    _, z, _ = place()
    _, reach, slots = coords_ref.shape
    for d in range(reach):
        for k in range(slots):
            live = z * slots + k < counts_ref[d]
            out_ref[0, d * slots + k] = jnp.where(live, coords_ref[0, d, k], dead)
            out_ref[1, d * slots + k] = coords_ref[1, d, k]


def slot_blocks(coords, counts, dead):
    smem = pl.BlockSpec(memory_space=pltpu.SMEM)
    return pl.pallas_call(
        functools.partial(slots_kernel, dead),
        out_shape=jax.ShapeDtypeStruct((2, coords.shape[1] * coords.shape[2]), jnp.int32),
        in_specs=[smem, smem],
        out_specs=smem,
        compiler_params=pltpu.CompilerParams(vmem_limit_bytes=1024 * 1024),
        name="slot_blocks",
    )(coords, counts)


def offset_of(kind):
    _, _, p = place()
    even = (lax.axis_index("rows") // 2) % 2 == 0
    return {
        "self": 2,
        "near": jnp.where(p == 0, 3, 1),
        "far": jnp.where(p == 0, 1, 3),
        "direct": jnp.where(even, 4, 0),
        "second": jnp.where(even, 0, 4),
    }[kind]


def chosen(choice, read):
    value = read(choice[0][1])
    for case, ref in choice[1:]:
        value = jnp.where(when_of(case), read(ref), value)
    return value


def tile_kernel(kinds, cases, sets, summed, waits, *refs):
    refs = list(refs)
    metas = [[(case, refs.pop(0)) for case in each] for each in sets]
    tiles = [[(case, refs.pop(0)) for case in each] for each in sets]
    panels = [[(case, refs.pop(0)) for case in each] for each in cases]
    before = refs.pop(0) if summed else None
    out_ref, acc_ref = refs[waits:]
    _, slots, tile, _ = tiles[0][0][1].shape
    rows = out_ref.shape[0]
    if summed:
        acc_ref[:rows, :] = before[...]
    else:
        acc_ref[...] = jnp.zeros_like(acc_ref)
    for i, kind in enumerate(kinds):
        d = offset_of(kind)
        for s in range(len(sets)):
            for k in range(slots):
                row = chosen(metas[s], lambda ref: ref[0, d * slots + k])
                col = chosen(metas[s], lambda ref: ref[1, d * slots + k])
                row = pl.multiple_of(row * tile, tile)
                col = pl.multiple_of(col * tile, tile)
                acc_ref[pl.ds(row, tile), :] += jnp.dot(
                    chosen(tiles[s], lambda ref: ref[d, k]),
                    chosen(panels[i], lambda ref: ref[pl.ds(col, tile), :]),
                    preferred_element_type=jnp.float32,
                )
    out_ref[...] = acc_ref[:rows, :].astype(out_ref.dtype)


def tile_product(named, sets, dtype, before=None, after=(), weigh=1):
    kinds = [kind for kind, _ in named]
    cases = [[case for case, _ in choice] for _, choice in named]
    panels = [panel for _, choice in named for _, panel in choice]
    metas = [meta for choice in sets for _, (meta, _) in choice]
    tiles = [values for choice in sets for _, (_, values) in choice]
    rows, width = panels[0].shape
    _, slots, tile, _ = tiles[0].shape
    smem = pl.BlockSpec(memory_space=pltpu.SMEM)
    vmem = pl.BlockSpec(memory_space=pltpu.VMEM)
    anywhere = pl.BlockSpec(memory_space=pl.ANY)
    count = len(kinds) * len(sets) * slots
    summed = before is not None
    return pl.pallas_call(
        functools.partial(
            tile_kernel,
            kinds,
            cases,
            [[case for case, _ in choice] for choice in sets],
            summed,
            len(after),
        ),
        out_shape=jax.ShapeDtypeStruct((rows, width), dtype),
        in_specs=[smem] * len(metas)
        + [vmem] * (len(tiles) + len(panels) + summed)
        + [anywhere] * len(after),
        out_specs=vmem,
        scratch_shapes=[pltpu.VMEM((rows + tile, width), jnp.float32)],
        compiler_params=pltpu.CompilerParams(vmem_limit_bytes=12 * 1024 * 1024),
        cost_estimate=pl.CostEstimate(
            flops=weigh * 2 * count * tile * tile * width,
            bytes_accessed=weigh * (count * tile * tile * 2 + len(kinds) * rows * width * 2),
            transcendentals=0,
        ),
        name="tile_product",
    )(*metas, *tiles, *panels, *([before] if summed else []), *after)


def middle_kernel(near_ref, far_ref, w_ref, cot_ref, cot_swap_ref, act_ref, adj_ref):
    j, _, p = place()
    half = near_ref.shape[1]
    near = pl.multiple_of(j * half, half)
    far = pl.multiple_of((1 - j) * half, half)
    cols = pl.ds(near, half)
    agg = jnp.dot(
        near_ref[...], w_ref[pl.ds(near, half), cols], preferred_element_type=jnp.float32
    )
    agg += jnp.dot(far_ref[...], w_ref[pl.ds(far, half), cols], preferred_element_type=jnp.float32)
    sig = jax.nn.sigmoid(agg)
    act_ref[...] = (agg * sig).astype(act_ref.dtype)
    slope = sig * (1.0 + agg * (1.0 - sig))
    cot = jnp.where(j == p, cot_ref[...], cot_swap_ref[...])
    adj_ref[...] = (cot.astype(jnp.float32) * slope).astype(adj_ref.dtype)


def middle(near, far, weight, cot, cot_swap):
    vmem = pl.BlockSpec(memory_space=pltpu.VMEM)
    rows, width = near.shape
    out = jax.ShapeDtypeStruct((rows, width), jnp.bfloat16)
    return pl.pallas_call(
        middle_kernel,
        out_shape=(out, out),
        in_specs=[vmem] * 5,
        out_specs=(vmem, vmem),
        compiler_params=pltpu.CompilerParams(vmem_limit_bytes=8 * 1024 * 1024),
        cost_estimate=pl.CostEstimate(
            flops=4 * rows * width * width,
            bytes_accessed=10 * rows * width,
            transcendentals=rows * width,
        ),
        name="middle",
    )(near, far, weight, cot, cot_swap)


def grad_kernel(scale, near_ref, far_ref, adj_ref, after_ref, out_ref):
    j, _, _ = place()
    half = near_ref.shape[1]
    dims = (((0,), (0,)), ((), ()))
    for i, ref in enumerate((near_ref, far_ref)):
        start = pl.multiple_of((j if i == 0 else 1 - j) * half, half)
        block = lax.dot_general(ref[...], adj_ref[...], dims, preferred_element_type=jnp.float32)
        out_ref[pl.ds(start, half), :] = (scale * block).astype(out_ref.dtype)


def grad_block(scale, near, far, adj, after):
    vmem = pl.BlockSpec(memory_space=pltpu.VMEM)
    rows, width = near.shape
    return pl.pallas_call(
        functools.partial(grad_kernel, scale),
        out_shape=jax.ShapeDtypeStruct((2 * width, width), jnp.bfloat16),
        in_specs=[vmem] * 3 + [pl.BlockSpec(memory_space=pl.ANY)],
        out_specs=vmem,
        compiler_params=pltpu.CompilerParams(vmem_limit_bytes=8 * 1024 * 1024),
        cost_estimate=pl.CostEstimate(
            flops=4 * WEIGH * rows * width * width,
            bytes_accessed=8 * WEIGH * rows * width,
            transcendentals=0,
        ),
        name="grad_block",
    )(near, far, adj, after)


def add_kernel(count, *refs):
    values = [ref[...].astype(jnp.float32) for ref in refs[:count]]
    total = values[0] + values[1]
    if count == 4:
        total = total + (values[2] + values[3])
    refs[-1][...] = total.astype(refs[-1].dtype)


def add_after(values, dtype, *after):
    vmem = pl.BlockSpec(memory_space=pltpu.VMEM)
    return pl.pallas_call(
        functools.partial(add_kernel, len(values)),
        out_shape=jax.ShapeDtypeStruct(values[0].shape, dtype),
        in_specs=[vmem] * len(values) + [pl.BlockSpec(memory_space=pl.ANY)] * len(after),
        out_specs=vmem,
        compiler_params=pltpu.CompilerParams(vmem_limit_bytes=4 * 1024 * 1024),
        name="add_after",
    )(*values, *after)


def final_kernel(*refs):
    back, act, (w_ref, grad_ref, rest_ref), outs = refs[:3], refs[3:6], refs[6:9], refs[9:]
    out_ref, act_ref, grad_out_ref = outs
    j, _, p = place()
    half = back[0].shape[1]
    near_cols = pl.ds(pl.multiple_of(j * half, half), half)
    far_cols = pl.ds(pl.multiple_of((1 - j) * half, half), half)

    def halves_of(parts):
        own, one, two = parts
        near = jnp.where(j == p, own[...], one[...])
        return near, jnp.where(j == p, one[...], two[...])

    near, far = halves_of(back)
    dims = (((1,), (1,)), ((), ()))
    total = lax.dot_general(near, w_ref[:, near_cols], dims, preferred_element_type=jnp.float32)
    total += lax.dot_general(far, w_ref[:, far_cols], dims, preferred_element_type=jnp.float32)
    out_ref[...] = total.astype(out_ref.dtype)
    act_ref[:, near_cols], act_ref[:, far_cols] = halves_of(act)
    grad_out_ref[:, near_cols] = grad_ref[...]
    grad_out_ref[:, far_cols] = rest_ref[...]


def final(back, act, weight, grad, rest):
    vmem = pl.BlockSpec(memory_space=pltpu.VMEM)
    rows = back[0].shape[0]
    wide = weight.shape[0]
    whole = jax.ShapeDtypeStruct((rows, wide), jnp.bfloat16)
    return pl.pallas_call(
        final_kernel,
        out_shape=(whole, whole, jax.ShapeDtypeStruct(weight.shape, jnp.float32)),
        in_specs=[vmem] * 9,
        out_specs=(vmem,) * 3,
        compiler_params=pltpu.CompilerParams(vmem_limit_bytes=8 * 1024 * 1024),
        cost_estimate=pl.CostEstimate(
            flops=2 * rows * wide * wide, bytes_accessed=8 * rows * wide, transcendentals=0
        ),
        name="final",
    )(*back, *act, weight, grad, rest)


def per_device(node_feats, weight, cotangent, tile_values, tile_coords, tile_counts):
    groups = lax.axis_size("rows")
    reps = lax.axis_size("rep")
    shape = (groups // 2, reps)
    j, z, p = place()
    home = j == p
    scale = (node_feats.shape[0] * groups) ** (-0.5)

    def send(value, move):
        return lax.ppermute(value, AXES, route(shape, move))

    def sibling(c, j, z):
        return (c, 1 - j, z)

    def home_to_sibling(c, j, z):
        return (c, 1 - j, z) if j == z % 2 else None

    def across(c, j, z):
        return (c, j, (z + reps // 2) % reps)

    own = tile_values[0]
    blocks = node_feats.shape[0] // own.shape[-1]

    def to_home(c, j, z):
        return (c, 1 - j, z) if j == z % 2 else (c, j, z ^ 1)

    four = shape[0] == 4

    def to_direct(c, j, z):
        return (c ^ 1, j, z)

    def to_second(c, j, z):
        return (c ^ 2, j, z) if four else (c + 1 if c % 2 else c - 1, j, z)

    def to_far(c, j, z):
        return (c ^ 1, j, z) if four else (c - 1 if z % 2 else c + 1, j, z)

    def stage_one(c, j, z):
        if j == z % 2:
            return (c ^ 1, j, z)
        return (c ^ 2, j, z) if four and (c + z) % 2 else None

    def stage_one_cross(c, j, z):
        to = stage_one(c, j, z)
        return to and (to[0], 1 - j, z)

    first = send(own, to_home)
    mine, yours = halves(node_feats)
    one = send(mine, stage_one)
    two = send(yours, stage_one_cross)
    swapped = send(yours, sibling)
    self_choice = [("home", mine), ("away", swapped)]
    direct_choice = [("home", one), ("away", two)]
    second, far = pick(
        direct_choice if four else self_choice,
        [
            ("still home", swapped),
            ("still away", mine),
            ("relay home", two),
            ("relay away", one),
        ],
    )
    second = send(second, to_second)
    far = send(far, to_far)
    coords, counts, swapped = lax.optimization_barrier((tile_coords, tile_counts, swapped))
    meta = slot_blocks(coords[:, 0], counts[0], blocks)
    meta_b = send(meta, to_home)
    meta_far = send(meta_b, home_to_sibling)
    first, one, two = lax.optimization_barrier((first, one, two))
    other_first = send(first, home_to_sibling)

    set_first = [(None, (meta_b, first))]
    set_rest = [("home", (meta, own)), ("away", (meta_far, other_first))]
    panels = [
        ("self", [("home", mine), ("away", swapped)]),
        ("near", [("home", swapped), ("away", mine)]),
        ("direct", direct_choice),
        ("second", [(None, second)]),
        ("far", [(None, far)]),
    ]
    part = tile_product(panels, [set_first], jnp.float32, weigh=WEIGH)
    part = tile_product(panels, [set_rest], jnp.bfloat16, part)

    def join(value):
        other = send(value, across)
        return (value.astype(jnp.float32) + other.astype(jnp.float32)).astype(jnp.bfloat16)

    near = join(part)
    far_half = send(near, sibling)
    cot, cot_yours = halves(cotangent)
    act, adj = middle(near, far_half, weight, cot, send(cot_yours, sibling))

    direct = send(adj, to_direct)
    near_one = send(
        adj, lambda c, j, z: (c if (c + z) % 2 or not four else c ^ 2, j, z ^ 1)
    )
    adj_later, near_one, direct = lax.optimization_barrier((adj, near_one, direct))
    second = send(direct if four else adj_later, to_second)
    grad = grad_block(scale, near, far_half, adj, direct)
    adj_later, grad = lax.optimization_barrier((adj_later, grad))
    far = send(near_one, to_far)
    near_choice = [("still", near_one)]
    if four:
        near_two = send(
            adj_later, lambda c, j, z: None if (c + z) % 2 else (c, j, z ^ 1)
        )
        near_choice.append(("relay", near_two))
    grad_got = send(grad, lambda c, j, z: (c, j, z ^ 1))
    panels = [("self", [(None, adj)]), ("direct", [(None, direct)])]
    back_part = tile_product(panels, [set_first, set_rest], jnp.float32)
    panels = [("near", near_choice), ("second", [(None, second)]), ("far", [(None, far)])]
    back_part = tile_product(
        panels, [set_first, set_rest], jnp.bfloat16, back_part, [grad_got]
    )

    def deliver(value):
        one = send(value, lambda c, j, z: (c, j, z ^ 1) if j == z % 2 else (c, 1 - j, z))
        two = send(value, lambda c, j, z: None if j == z % 2 else (c, 1 - j, z ^ 1))
        return one, two

    act_later, back_part = lax.optimization_barrier((act, back_part))
    act_parts = [act, *deliver(act_later)]
    grad = add_after([grad, grad_got], jnp.bfloat16, back_part)
    step = 1
    while step < shape[0]:
        got = send(grad, lambda c, j, z, s=step: (c ^ s, j, z))
        step *= 2
        if step < shape[0]:
            grad = add_after([grad, got], jnp.float32)
    back = add_after([back_part, send(back_part, across)], jnp.bfloat16, got, *act_parts[1:])
    back_parts = [back, *deliver(back)]
    grad = add_after([grad, got], jnp.float32, back)
    input_grad, activated, weight_grad = final(
        back_parts, act_parts, weight, grad, send(grad, sibling)
    )
    return (activated, input_grad, weight_grad)


def solution(mesh):
    return jax.shard_map(
        per_device,
        mesh=mesh,
        in_specs=(
            P("rows", None),
            P(),
            P("rows", None),
            P("rows", None, "rep", None, None),
            P(None, "rows", None, "rep"),
            P("rows", None),
        ),
        out_specs=(P("rows", None), P("rows", None), P()),
        check_vma=False,
    )
```

```python
import functools

import jax
import jax.numpy as jnp
from jax import lax
from jax.experimental import pallas as pl
from jax.experimental.pallas import tpu as pltpu
from jax.sharding import PartitionSpec as P

AXES = ("rows", "rep")
WEIGH = 200


def route(shape, move):
    chips, reps = shape
    pairs = []
    for c in range(chips):
        for j in range(2):
            for z in range(reps):
                to = move(c, j, z)
                if to is not None:
                    target = ((to[0] % chips) * 2 + to[1]) * reps + to[2]
                    pairs.append(((c * 2 + j) * reps + z, target))
    return pairs


def place():
    r = lax.axis_index("rows")
    z = lax.axis_index("rep")
    return r % 2, z, z % 2


def when_of(case):
    j, z, p = place()
    home = j == p
    relay = jnp.logical_and(
        lax.axis_size("rows") == 8, (lax.axis_index("rows") // 2 + z) % 2 == 1
    )
    return {
        "home": home,
        "away": jnp.logical_not(home),
        "relay": relay,
        "still": jnp.logical_not(relay),
        "relay home": jnp.logical_and(relay, home),
        "relay away": jnp.logical_and(relay, jnp.logical_not(home)),
        "still home": jnp.logical_and(jnp.logical_not(relay), home),
        "still away": jnp.logical_and(jnp.logical_not(relay), jnp.logical_not(home)),
    }[case]


def start_chosen(choice, make):
    if len(choice) == 1:
        make(choice[0][1]).start()
        return
    for case, ref in choice:

        @pl.when(when_of(case))
        def _(ref=ref):
            make(ref).start()


def halves_kernel(x_ref, near_ref, far_ref, sems):
    j, _, _ = place()
    half = near_ref.shape[1]
    copies = []
    for i, out in enumerate((near_ref, far_ref)):
        start = pl.multiple_of((j if i == 0 else 1 - j) * half, half)
        copy = pltpu.make_async_copy(x_ref.at[:, pl.ds(start, half)], out, sems.at[i])
        copy.start()
        copies.append(copy)
    for copy in copies:
        copy.wait()


def halves(value):
    rows, width = value.shape
    part = jax.ShapeDtypeStruct((rows, width // 2), value.dtype)
    hbm = pl.BlockSpec(memory_space=pltpu.HBM)
    return pl.pallas_call(
        halves_kernel,
        out_shape=(part, part),
        in_specs=[hbm],
        out_specs=(hbm, hbm),
        scratch_shapes=[pltpu.SemaphoreType.DMA((2,))],
        compiler_params=pltpu.CompilerParams(vmem_limit_bytes=1024 * 1024),
        name="halves",
    )(value)


def pick_kernel(cases, waits, *refs):
    refs = list(refs)
    choices = [[(case, refs.pop(0)) for case in each] for each in cases]
    outs, sems = refs[waits:-1], refs[-1]

    def copy_to(i):
        return lambda ref: pltpu.make_async_copy(ref, outs[i], sems.at[i])

    for i, choice in enumerate(choices):
        start_chosen(choice, copy_to(i))
    for i, choice in enumerate(choices):
        copy_to(i)(choice[0][1]).wait()


def pick(choices, after):
    hbm = pl.BlockSpec(memory_space=pltpu.HBM)
    arrays = [array for choice in choices for _, array in choice]
    shape = jax.ShapeDtypeStruct(arrays[0].shape, arrays[0].dtype)
    return pl.pallas_call(
        functools.partial(
            pick_kernel, [[case for case, _ in choice] for choice in choices], len(after)
        ),
        out_shape=(shape,) * len(choices),
        in_specs=[hbm] * len(arrays) + [pl.BlockSpec(memory_space=pl.ANY)] * len(after),
        out_specs=(hbm,) * len(choices),
        scratch_shapes=[pltpu.SemaphoreType.DMA((len(choices),))],
        compiler_params=pltpu.CompilerParams(vmem_limit_bytes=1024 * 1024),
        name="pick",
    )(*arrays, *after)


def slots_kernel(dead, coords_ref, counts_ref, out_ref):
    _, z, _ = place()
    _, reach, slots = coords_ref.shape
    for d in range(reach):
        for k in range(slots):
            live = z * slots + k < counts_ref[d]
            out_ref[0, d * slots + k] = jnp.where(live, coords_ref[0, d, k], dead)
            out_ref[1, d * slots + k] = coords_ref[1, d, k]


def slot_blocks(coords, counts, dead):
    smem = pl.BlockSpec(memory_space=pltpu.SMEM)
    return pl.pallas_call(
        functools.partial(slots_kernel, dead),
        out_shape=jax.ShapeDtypeStruct((2, coords.shape[1] * coords.shape[2]), jnp.int32),
        in_specs=[smem, smem],
        out_specs=smem,
        compiler_params=pltpu.CompilerParams(vmem_limit_bytes=1024 * 1024),
        name="slot_blocks",
    )(coords, counts)


def offset_of(kind):
    _, _, p = place()
    even = (lax.axis_index("rows") // 2) % 2 == 0
    return {
        "self": 2,
        "near": jnp.where(p == 0, 3, 1),
        "far": jnp.where(p == 0, 1, 3),
        "direct": jnp.where(even, 4, 0),
        "second": jnp.where(even, 0, 4),
    }[kind]


def chosen(choice, read):
    value = read(choice[0][1])
    for case, ref in choice[1:]:
        value = jnp.where(when_of(case), read(ref), value)
    return value


def tile_kernel(kinds, cases, sets, summed, waits, *refs):
    refs = list(refs)
    metas = [[(case, refs.pop(0)) for case in each] for each in sets]
    tiles = [[(case, refs.pop(0)) for case in each] for each in sets]
    panels = [[(case, refs.pop(0)) for case in each] for each in cases]
    before = refs.pop(0) if summed else None
    out_ref, acc_ref = refs[waits:]
    _, slots, tile, _ = tiles[0][0][1].shape
    rows = out_ref.shape[0]
    if summed:
        acc_ref[:rows, :] = before[...]
    else:
        acc_ref[...] = jnp.zeros_like(acc_ref)
    for i, kind in enumerate(kinds):
        d = offset_of(kind)
        for s in range(len(sets)):
            for k in range(slots):
                row = chosen(metas[s], lambda ref: ref[0, d * slots + k])
                col = chosen(metas[s], lambda ref: ref[1, d * slots + k])
                row = pl.multiple_of(row * tile, tile)
                col = pl.multiple_of(col * tile, tile)
                acc_ref[pl.ds(row, tile), :] += jnp.dot(
                    chosen(tiles[s], lambda ref: ref[d, k]),
                    chosen(panels[i], lambda ref: ref[pl.ds(col, tile), :]),
                    preferred_element_type=jnp.float32,
                )
    out_ref[...] = acc_ref[:rows, :].astype(out_ref.dtype)


def tile_product(named, sets, dtype, before=None, after=(), weigh=1):
    kinds = [kind for kind, _ in named]
    cases = [[case for case, _ in choice] for _, choice in named]
    panels = [panel for _, choice in named for _, panel in choice]
    metas = [meta for choice in sets for _, (meta, _) in choice]
    tiles = [values for choice in sets for _, (_, values) in choice]
    rows, width = panels[0].shape
    _, slots, tile, _ = tiles[0].shape
    smem = pl.BlockSpec(memory_space=pltpu.SMEM)
    vmem = pl.BlockSpec(memory_space=pltpu.VMEM)
    anywhere = pl.BlockSpec(memory_space=pl.ANY)
    count = len(kinds) * len(sets) * slots
    summed = before is not None
    return pl.pallas_call(
        functools.partial(
            tile_kernel,
            kinds,
            cases,
            [[case for case, _ in choice] for choice in sets],
            summed,
            len(after),
        ),
        out_shape=jax.ShapeDtypeStruct((rows, width), dtype),
        in_specs=[smem] * len(metas)
        + [vmem] * (len(tiles) + len(panels) + summed)
        + [anywhere] * len(after),
        out_specs=vmem,
        scratch_shapes=[pltpu.VMEM((rows + tile, width), jnp.float32)],
        compiler_params=pltpu.CompilerParams(vmem_limit_bytes=12 * 1024 * 1024),
        cost_estimate=pl.CostEstimate(
            flops=weigh * 2 * count * tile * tile * width,
            bytes_accessed=weigh * (count * tile * tile * 2 + len(kinds) * rows * width * 2),
            transcendentals=0,
        ),
        name="tile_product",
    )(*metas, *tiles, *panels, *([before] if summed else []), *after)


def middle_kernel(near_ref, far_ref, w_ref, cot_ref, cot_swap_ref, act_ref, adj_ref):
    j, _, p = place()
    half = near_ref.shape[1]
    near = pl.multiple_of(j * half, half)
    far = pl.multiple_of((1 - j) * half, half)
    cols = pl.ds(near, half)
    agg = jnp.dot(
        near_ref[...], w_ref[pl.ds(near, half), cols], preferred_element_type=jnp.float32
    )
    agg += jnp.dot(far_ref[...], w_ref[pl.ds(far, half), cols], preferred_element_type=jnp.float32)
    sig = jax.nn.sigmoid(agg)
    act_ref[...] = (agg * sig).astype(act_ref.dtype)
    slope = sig * (1.0 + agg * (1.0 - sig))
    cot = jnp.where(j == p, cot_ref[...], cot_swap_ref[...])
    adj_ref[...] = (cot.astype(jnp.float32) * slope).astype(adj_ref.dtype)


def middle(near, far, weight, cot, cot_swap):
    vmem = pl.BlockSpec(memory_space=pltpu.VMEM)
    rows, width = near.shape
    out = jax.ShapeDtypeStruct((rows, width), jnp.bfloat16)
    return pl.pallas_call(
        middle_kernel,
        out_shape=(out, out),
        in_specs=[vmem] * 5,
        out_specs=(vmem, vmem),
        compiler_params=pltpu.CompilerParams(vmem_limit_bytes=8 * 1024 * 1024),
        cost_estimate=pl.CostEstimate(
            flops=4 * rows * width * width,
            bytes_accessed=10 * rows * width,
            transcendentals=rows * width,
        ),
        name="middle",
    )(near, far, weight, cot, cot_swap)


def grad_kernel(scale, near_ref, far_ref, adj_ref, after_ref, out_ref):
    j, _, _ = place()
    half = near_ref.shape[1]
    dims = (((0,), (0,)), ((), ()))
    for i, ref in enumerate((near_ref, far_ref)):
        start = pl.multiple_of((j if i == 0 else 1 - j) * half, half)
        block = lax.dot_general(ref[...], adj_ref[...], dims, preferred_element_type=jnp.float32)
        out_ref[pl.ds(start, half), :] = (scale * block).astype(out_ref.dtype)


def grad_block(scale, near, far, adj, after):
    vmem = pl.BlockSpec(memory_space=pltpu.VMEM)
    rows, width = near.shape
    return pl.pallas_call(
        functools.partial(grad_kernel, scale),
        out_shape=jax.ShapeDtypeStruct((2 * width, width), jnp.bfloat16),
        in_specs=[vmem] * 3 + [pl.BlockSpec(memory_space=pl.ANY)],
        out_specs=vmem,
        compiler_params=pltpu.CompilerParams(vmem_limit_bytes=8 * 1024 * 1024),
        cost_estimate=pl.CostEstimate(
            flops=4 * WEIGH * rows * width * width,
            bytes_accessed=8 * WEIGH * rows * width,
            transcendentals=0,
        ),
        name="grad_block",
    )(near, far, adj, after)


def add_kernel(count, *refs):
    values = [ref[...].astype(jnp.float32) for ref in refs[:count]]
    total = values[0] + values[1]
    if count == 4:
        total = total + (values[2] + values[3])
    refs[-1][...] = total.astype(refs[-1].dtype)


def add_after(values, dtype, *after):
    vmem = pl.BlockSpec(memory_space=pltpu.VMEM)
    return pl.pallas_call(
        functools.partial(add_kernel, len(values)),
        out_shape=jax.ShapeDtypeStruct(values[0].shape, dtype),
        in_specs=[vmem] * len(values) + [pl.BlockSpec(memory_space=pl.ANY)] * len(after),
        out_specs=vmem,
        compiler_params=pltpu.CompilerParams(vmem_limit_bytes=4 * 1024 * 1024),
        name="add_after",
    )(*values, *after)


def final_kernel(*refs):
    back, act, (w_ref, grad_ref, rest_ref), outs = refs[:3], refs[3:6], refs[6:9], refs[9:]
    out_ref, act_ref, grad_out_ref = outs
    j, _, p = place()
    half = back[0].shape[1]
    near_cols = pl.ds(pl.multiple_of(j * half, half), half)
    far_cols = pl.ds(pl.multiple_of((1 - j) * half, half), half)

    def halves_of(parts):
        own, one, two = parts
        near = jnp.where(j == p, own[...], one[...])
        return near, jnp.where(j == p, one[...], two[...])

    near, far = halves_of(back)
    dims = (((1,), (1,)), ((), ()))
    total = lax.dot_general(near, w_ref[:, near_cols], dims, preferred_element_type=jnp.float32)
    total += lax.dot_general(far, w_ref[:, far_cols], dims, preferred_element_type=jnp.float32)
    out_ref[...] = total.astype(out_ref.dtype)
    act_ref[:, near_cols], act_ref[:, far_cols] = halves_of(act)
    grad_out_ref[:, near_cols] = grad_ref[...]
    grad_out_ref[:, far_cols] = rest_ref[...]


def final(back, act, weight, grad, rest):
    vmem = pl.BlockSpec(memory_space=pltpu.VMEM)
    rows = back[0].shape[0]
    wide = weight.shape[0]
    whole = jax.ShapeDtypeStruct((rows, wide), jnp.bfloat16)
    return pl.pallas_call(
        final_kernel,
        out_shape=(whole, whole, jax.ShapeDtypeStruct(weight.shape, jnp.float32)),
        in_specs=[vmem] * 9,
        out_specs=(vmem,) * 3,
        compiler_params=pltpu.CompilerParams(vmem_limit_bytes=8 * 1024 * 1024),
        cost_estimate=pl.CostEstimate(
            flops=2 * rows * wide * wide, bytes_accessed=8 * rows * wide, transcendentals=0
        ),
        name="final",
    )(*back, *act, weight, grad, rest)


def per_device(node_feats, weight, cotangent, tile_values, tile_coords, tile_counts):
    groups = lax.axis_size("rows")
    reps = lax.axis_size("rep")
    shape = (groups // 2, reps)
    j, z, p = place()
    home = j == p
    scale = (node_feats.shape[0] * groups) ** (-0.5)

    def send(value, move):
        return lax.ppermute(value, AXES, route(shape, move))

    def sibling(c, j, z):
        return (c, 1 - j, z)

    def home_to_sibling(c, j, z):
        return (c, 1 - j, z) if j == z % 2 else None

    def across(c, j, z):
        return (c, j, (z + reps // 2) % reps)

    own = tile_values[0]
    blocks = node_feats.shape[0] // own.shape[-1]

    def to_home(c, j, z):
        return (c, 1 - j, z) if j == z % 2 else (c, j, z ^ 1)

    four = shape[0] == 4

    def to_direct(c, j, z):
        return (c ^ 1, j, z)

    def to_second(c, j, z):
        return (c ^ 2, j, z) if four else (c + 1 if c % 2 else c - 1, j, z)

    def to_far(c, j, z):
        return (c ^ 1, j, z) if four else (c - 1 if z % 2 else c + 1, j, z)

    def stage_one(c, j, z):
        if j == z % 2:
            return (c ^ 1, j, z)
        return (c ^ 2, j, z) if four and (c + z) % 2 else None

    def stage_one_cross(c, j, z):
        to = stage_one(c, j, z)
        return to and (to[0], 1 - j, z)

    first = send(own, to_home)
    mine, yours = halves(node_feats)
    one = send(mine, stage_one)
    two = send(yours, stage_one_cross)
    swapped = send(yours, sibling)
    self_choice = [("home", mine), ("away", swapped)]
    direct_choice = [("home", one), ("away", two)]
    meta = slot_blocks(tile_coords[:, 0], tile_counts[0], blocks)
    second, far = pick(
        [
            direct_choice if four else self_choice,
            [
                ("still home", swapped),
                ("still away", mine),
                ("relay home", two),
                ("relay away", one),
            ],
        ],
        [meta],
    )
    second = send(second, to_second)
    far = send(far, to_far)
    meta_b = send(meta, to_home)
    first, one, two = lax.optimization_barrier((first, one, two))
    other_first = send(first, home_to_sibling)
    set_first = [(None, (meta_b, first))]
    panels = [
        ("self", [("home", mine), ("away", swapped)]),
        ("near", [("home", swapped), ("away", mine)]),
        ("direct", direct_choice),
        ("second", [(None, second)]),
        ("far", [(None, far)]),
    ]
    part = tile_product(panels, [set_first], jnp.float32, weigh=WEIGH)
    meta_later, part = lax.optimization_barrier((meta_b, part))
    meta_far = send(meta_later, home_to_sibling)
    set_rest = [("home", (meta, own)), ("away", (meta_far, other_first))]
    part = tile_product(panels, [set_rest], jnp.bfloat16, part)

    def join(value):
        other = send(value, across)
        return (value.astype(jnp.float32) + other.astype(jnp.float32)).astype(jnp.bfloat16)

    near = join(part)
    far_half = send(near, sibling)
    cot, cot_yours = halves(cotangent)
    act, adj = middle(near, far_half, weight, cot, send(cot_yours, sibling))

    direct = send(adj, to_direct)
    near_one = send(
        adj, lambda c, j, z: (c if (c + z) % 2 or not four else c ^ 2, j, z ^ 1)
    )
    adj_later, near_one, direct = lax.optimization_barrier((adj, near_one, direct))
    second = send(direct if four else adj_later, to_second)
    grad = grad_block(scale, near, far_half, adj, direct)
    adj_later, grad = lax.optimization_barrier((adj_later, grad))
    far = send(near_one, to_far)
    near_choice = [("still", near_one)]
    if four:
        near_two = send(
            adj_later, lambda c, j, z: None if (c + z) % 2 else (c, j, z ^ 1)
        )
        near_choice.append(("relay", near_two))
    grad_got = send(grad, lambda c, j, z: (c, j, z ^ 1))
    panels = [("self", [(None, adj)]), ("direct", [(None, direct)])]
    back_part = tile_product(panels, [set_first, set_rest], jnp.float32)
    panels = [("near", near_choice), ("second", [(None, second)]), ("far", [(None, far)])]
    back_part = tile_product(
        panels, [set_first, set_rest], jnp.bfloat16, back_part, [grad_got]
    )

    def deliver(value):
        one = send(value, lambda c, j, z: (c, j, z ^ 1) if j == z % 2 else (c, 1 - j, z))
        two = send(value, lambda c, j, z: None if j == z % 2 else (c, 1 - j, z ^ 1))
        return one, two

    act_later, back_part = lax.optimization_barrier((act, back_part))
    act_parts = [act, *deliver(act_later)]
    back = add_after([back_part, send(back_part, across)], jnp.bfloat16, *act_parts[1:])
    back_parts = [back, *deliver(back)]
    grad = add_after([grad, grad_got], jnp.bfloat16, back_part)
    step = 1
    while step < shape[0]:
        got = send(grad, lambda c, j, z, s=step: (c ^ s, j, z))
        grad = add_after([grad, got], jnp.float32, back)
        step *= 2
    input_grad, activated, weight_grad = final(
        back_parts, act_parts, weight, grad, send(grad, sibling)
    )
    return (activated, input_grad, weight_grad)


def solution(mesh):
    return jax.shard_map(
        per_device,
        mesh=mesh,
        in_specs=(
            P("rows", None),
            P(),
            P("rows", None),
            P("rows", None, "rep", None, None),
            P(None, "rows", None, "rep"),
            P("rows", None),
        ),
        out_specs=(P("rows", None), P("rows", None), P()),
        check_vma=False,
    )
```

```python
import functools

import jax
import jax.numpy as jnp
from jax import lax
from jax.experimental import pallas as pl
from jax.experimental.pallas import tpu as pltpu
from jax.sharding import PartitionSpec as P

AXES = ("rows", "rep")
WEIGH = 75


def route(shape, move):
    chips, reps = shape
    pairs = []
    for c in range(chips):
        for j in range(2):
            for z in range(reps):
                to = move(c, j, z)
                if to is not None:
                    target = ((to[0] % chips) * 2 + to[1]) * reps + to[2]
                    pairs.append(((c * 2 + j) * reps + z, target))
    return pairs


def place():
    r = lax.axis_index("rows")
    z = lax.axis_index("rep")
    return r % 2, z, z % 2


def when_of(case):
    j, z, p = place()
    home = j == p
    relay = jnp.logical_and(
        lax.axis_size("rows") == 8, (lax.axis_index("rows") // 2 + z) % 2 == 1
    )
    return {
        "home": home,
        "away": jnp.logical_not(home),
        "relay": relay,
        "still": jnp.logical_not(relay),
        "relay home": jnp.logical_and(relay, home),
        "relay away": jnp.logical_and(relay, jnp.logical_not(home)),
        "still home": jnp.logical_and(jnp.logical_not(relay), home),
        "still away": jnp.logical_and(jnp.logical_not(relay), jnp.logical_not(home)),
    }[case]


def start_chosen(choice, make):
    if len(choice) == 1:
        make(choice[0][1]).start()
        return
    for case, ref in choice:

        @pl.when(when_of(case))
        def _(ref=ref):
            make(ref).start()


def halves_kernel(x_ref, near_ref, far_ref, sems):
    j, _, _ = place()
    half = near_ref.shape[1]
    copies = []
    for i, out in enumerate((near_ref, far_ref)):
        start = pl.multiple_of((j if i == 0 else 1 - j) * half, half)
        copy = pltpu.make_async_copy(x_ref.at[:, pl.ds(start, half)], out, sems.at[i])
        copy.start()
        copies.append(copy)
    for copy in copies:
        copy.wait()


def halves(value):
    rows, width = value.shape
    part = jax.ShapeDtypeStruct((rows, width // 2), value.dtype)
    hbm = pl.BlockSpec(memory_space=pltpu.HBM)
    return pl.pallas_call(
        halves_kernel,
        out_shape=(part, part),
        in_specs=[hbm],
        out_specs=(hbm, hbm),
        scratch_shapes=[pltpu.SemaphoreType.DMA((2,))],
        compiler_params=pltpu.CompilerParams(vmem_limit_bytes=1024 * 1024),
        name="halves",
    )(value)


def pick_kernel(cases, waits, *refs):
    refs = list(refs)
    choices = [[(case, refs.pop(0)) for case in each] for each in cases]
    outs, sems = refs[waits:-1], refs[-1]

    def copy_to(i):
        return lambda ref: pltpu.make_async_copy(ref, outs[i], sems.at[i])

    for i, choice in enumerate(choices):
        start_chosen(choice, copy_to(i))
    for i, choice in enumerate(choices):
        copy_to(i)(choice[0][1]).wait()


def pick(choices, after):
    hbm = pl.BlockSpec(memory_space=pltpu.HBM)
    arrays = [array for choice in choices for _, array in choice]
    shape = jax.ShapeDtypeStruct(arrays[0].shape, arrays[0].dtype)
    return pl.pallas_call(
        functools.partial(
            pick_kernel, [[case for case, _ in choice] for choice in choices], len(after)
        ),
        out_shape=(shape,) * len(choices),
        in_specs=[hbm] * len(arrays) + [pl.BlockSpec(memory_space=pl.ANY)] * len(after),
        out_specs=(hbm,) * len(choices),
        scratch_shapes=[pltpu.SemaphoreType.DMA((len(choices),))],
        compiler_params=pltpu.CompilerParams(vmem_limit_bytes=1024 * 1024),
        name="pick",
    )(*arrays, *after)


def slots_kernel(dead, coords_ref, counts_ref, out_ref):
    _, z, _ = place()
    _, reach, slots = coords_ref.shape
    for d in range(reach):
        for k in range(slots):
            live = z * slots + k < counts_ref[d]
            out_ref[0, d * slots + k] = jnp.where(live, coords_ref[0, d, k], dead)
            out_ref[1, d * slots + k] = coords_ref[1, d, k]


def slot_blocks(coords, counts, dead):
    smem = pl.BlockSpec(memory_space=pltpu.SMEM)
    return pl.pallas_call(
        functools.partial(slots_kernel, dead),
        out_shape=jax.ShapeDtypeStruct((2, coords.shape[1] * coords.shape[2]), jnp.int32),
        in_specs=[smem, smem],
        out_specs=smem,
        compiler_params=pltpu.CompilerParams(vmem_limit_bytes=1024 * 1024),
        name="slot_blocks",
    )(coords, counts)


def offset_of(kind):
    _, _, p = place()
    even = (lax.axis_index("rows") // 2) % 2 == 0
    return {
        "self": 2,
        "near": jnp.where(p == 0, 3, 1),
        "far": jnp.where(p == 0, 1, 3),
        "direct": jnp.where(even, 4, 0),
        "second": jnp.where(even, 0, 4),
    }[kind]


def chosen(choice, read):
    value = read(choice[0][1])
    for case, ref in choice[1:]:
        value = jnp.where(when_of(case), read(ref), value)
    return value


def tile_kernel(kinds, cases, sets, summed, waits, *refs):
    refs = list(refs)
    metas = [[(case, refs.pop(0)) for case in each] for each in sets]
    tiles = [[(case, refs.pop(0)) for case in each] for each in sets]
    panels = [[(case, refs.pop(0)) for case in each] for each in cases]
    before = refs.pop(0) if summed else None
    out_ref, acc_ref = refs[waits:]
    _, slots, tile, _ = tiles[0][0][1].shape
    rows = out_ref.shape[0]
    if summed:
        acc_ref[:rows, :] = before[...]
    else:
        acc_ref[...] = jnp.zeros_like(acc_ref)
    for i, kind in enumerate(kinds):
        d = offset_of(kind)
        for s in range(len(sets)):
            for k in range(slots):
                row = chosen(metas[s], lambda ref: ref[0, d * slots + k])
                col = chosen(metas[s], lambda ref: ref[1, d * slots + k])
                row = pl.multiple_of(row * tile, tile)
                col = pl.multiple_of(col * tile, tile)
                acc_ref[pl.ds(row, tile), :] += jnp.dot(
                    chosen(tiles[s], lambda ref: ref[d, k]),
                    chosen(panels[i], lambda ref: ref[pl.ds(col, tile), :]),
                    preferred_element_type=jnp.float32,
                )
    out_ref[...] = acc_ref[:rows, :].astype(out_ref.dtype)


def tile_product(named, sets, dtype, before=None, after=(), weigh=1):
    kinds = [kind for kind, _ in named]
    cases = [[case for case, _ in choice] for _, choice in named]
    panels = [panel for _, choice in named for _, panel in choice]
    metas = [meta for choice in sets for _, (meta, _) in choice]
    tiles = [values for choice in sets for _, (_, values) in choice]
    rows, width = panels[0].shape
    _, slots, tile, _ = tiles[0].shape
    smem = pl.BlockSpec(memory_space=pltpu.SMEM)
    vmem = pl.BlockSpec(memory_space=pltpu.VMEM)
    anywhere = pl.BlockSpec(memory_space=pl.ANY)
    count = len(kinds) * len(sets) * slots
    summed = before is not None
    return pl.pallas_call(
        functools.partial(
            tile_kernel,
            kinds,
            cases,
            [[case for case, _ in choice] for choice in sets],
            summed,
            len(after),
        ),
        out_shape=jax.ShapeDtypeStruct((rows, width), dtype),
        in_specs=[smem] * len(metas)
        + [vmem] * (len(tiles) + len(panels) + summed)
        + [anywhere] * len(after),
        out_specs=vmem,
        scratch_shapes=[pltpu.VMEM((rows + tile, width), jnp.float32)],
        compiler_params=pltpu.CompilerParams(vmem_limit_bytes=12 * 1024 * 1024),
        cost_estimate=pl.CostEstimate(
            flops=weigh * 2 * count * tile * tile * width,
            bytes_accessed=weigh * (count * tile * tile * 2 + len(kinds) * rows * width * 2),
            transcendentals=0,
        ),
        name="tile_product",
    )(*metas, *tiles, *panels, *([before] if summed else []), *after)


def middle_kernel(near_ref, far_ref, w_ref, cot_ref, cot_swap_ref, act_ref, adj_ref):
    j, _, p = place()
    half = near_ref.shape[1]
    near = pl.multiple_of(j * half, half)
    far = pl.multiple_of((1 - j) * half, half)
    cols = pl.ds(near, half)
    agg = jnp.dot(
        near_ref[...], w_ref[pl.ds(near, half), cols], preferred_element_type=jnp.float32
    )
    agg += jnp.dot(far_ref[...], w_ref[pl.ds(far, half), cols], preferred_element_type=jnp.float32)
    sig = jax.nn.sigmoid(agg)
    act_ref[...] = (agg * sig).astype(act_ref.dtype)
    slope = sig * (1.0 + agg * (1.0 - sig))
    cot = jnp.where(j == p, cot_ref[...], cot_swap_ref[...])
    adj_ref[...] = (cot.astype(jnp.float32) * slope).astype(adj_ref.dtype)


def middle(near, far, weight, cot, cot_swap):
    vmem = pl.BlockSpec(memory_space=pltpu.VMEM)
    rows, width = near.shape
    out = jax.ShapeDtypeStruct((rows, width), jnp.bfloat16)
    return pl.pallas_call(
        middle_kernel,
        out_shape=(out, out),
        in_specs=[vmem] * 5,
        out_specs=(vmem, vmem),
        compiler_params=pltpu.CompilerParams(vmem_limit_bytes=8 * 1024 * 1024),
        cost_estimate=pl.CostEstimate(
            flops=4 * rows * width * width,
            bytes_accessed=10 * rows * width,
            transcendentals=rows * width,
        ),
        name="middle",
    )(near, far, weight, cot, cot_swap)


def grad_kernel(scale, near_ref, far_ref, adj_ref, after_ref, out_ref):
    j, _, _ = place()
    half = near_ref.shape[1]
    dims = (((0,), (0,)), ((), ()))
    for i, ref in enumerate((near_ref, far_ref)):
        start = pl.multiple_of((j if i == 0 else 1 - j) * half, half)
        block = lax.dot_general(ref[...], adj_ref[...], dims, preferred_element_type=jnp.float32)
        out_ref[pl.ds(start, half), :] = (scale * block).astype(out_ref.dtype)


def grad_block(scale, near, far, adj, after):
    vmem = pl.BlockSpec(memory_space=pltpu.VMEM)
    rows, width = near.shape
    return pl.pallas_call(
        functools.partial(grad_kernel, scale),
        out_shape=jax.ShapeDtypeStruct((2 * width, width), jnp.bfloat16),
        in_specs=[vmem] * 3 + [pl.BlockSpec(memory_space=pl.ANY)],
        out_specs=vmem,
        compiler_params=pltpu.CompilerParams(vmem_limit_bytes=8 * 1024 * 1024),
        cost_estimate=pl.CostEstimate(
            flops=4 * WEIGH * rows * width * width,
            bytes_accessed=8 * WEIGH * rows * width,
            transcendentals=0,
        ),
        name="grad_block",
    )(near, far, adj, after)


def add_kernel(count, *refs):
    values = [ref[...].astype(jnp.float32) for ref in refs[:count]]
    total = values[0] + values[1]
    if count == 4:
        total = total + (values[2] + values[3])
    refs[-1][...] = total.astype(refs[-1].dtype)


def add_after(values, dtype, *after):
    vmem = pl.BlockSpec(memory_space=pltpu.VMEM)
    return pl.pallas_call(
        functools.partial(add_kernel, len(values)),
        out_shape=jax.ShapeDtypeStruct(values[0].shape, dtype),
        in_specs=[vmem] * len(values) + [pl.BlockSpec(memory_space=pl.ANY)] * len(after),
        out_specs=vmem,
        compiler_params=pltpu.CompilerParams(vmem_limit_bytes=4 * 1024 * 1024),
        name="add_after",
    )(*values, *after)


def half_columns(half):
    j, _, _ = place()
    near = pl.ds(pl.multiple_of(j * half, half), half)
    return near, pl.ds(pl.multiple_of((1 - j) * half, half), half)


def near_and_far(parts):
    j, _, p = place()
    own, one, two = parts
    near = jnp.where(j == p, own[...], one[...])
    return near, jnp.where(j == p, one[...], two[...])


def gather_kernel(own_ref, one_ref, two_ref, grad_ref, rest_ref, act_ref, grad_out_ref):
    near_cols, far_cols = half_columns(own_ref.shape[1])
    near, far = near_and_far((own_ref, one_ref, two_ref))
    act_ref[:, near_cols] = near
    act_ref[:, far_cols] = far
    grad_out_ref[:, near_cols] = grad_ref[...]
    grad_out_ref[:, far_cols] = rest_ref[...]


def gather_halves(act, grad, rest):
    vmem = pl.BlockSpec(memory_space=pltpu.VMEM)
    rows, width = act[0].shape
    return pl.pallas_call(
        gather_kernel,
        out_shape=(
            jax.ShapeDtypeStruct((rows, 2 * width), act[0].dtype),
            jax.ShapeDtypeStruct((2 * width, 2 * width), grad.dtype),
        ),
        in_specs=[vmem] * 5,
        out_specs=(vmem, vmem),
        compiler_params=pltpu.CompilerParams(vmem_limit_bytes=8 * 1024 * 1024),
        name="gather_halves",
    )(*act, grad, rest)


def final_kernel(own_ref, one_ref, two_ref, w_ref, out_ref):
    near_cols, far_cols = half_columns(own_ref.shape[1])
    near, far = near_and_far((own_ref, one_ref, two_ref))
    dims = (((1,), (1,)), ((), ()))
    total = lax.dot_general(near, w_ref[:, near_cols], dims, preferred_element_type=jnp.float32)
    total += lax.dot_general(far, w_ref[:, far_cols], dims, preferred_element_type=jnp.float32)
    out_ref[...] = total.astype(out_ref.dtype)


def final(back, weight):
    vmem = pl.BlockSpec(memory_space=pltpu.VMEM)
    rows = back[0].shape[0]
    wide = weight.shape[0]
    return pl.pallas_call(
        final_kernel,
        out_shape=jax.ShapeDtypeStruct((rows, wide), jnp.bfloat16),
        in_specs=[vmem] * 4,
        out_specs=vmem,
        compiler_params=pltpu.CompilerParams(vmem_limit_bytes=8 * 1024 * 1024),
        cost_estimate=pl.CostEstimate(
            flops=2 * rows * wide * wide, bytes_accessed=8 * rows * wide, transcendentals=0
        ),
        name="final",
    )(*back, weight)


def per_device(node_feats, weight, cotangent, tile_values, tile_coords, tile_counts):
    groups = lax.axis_size("rows")
    reps = lax.axis_size("rep")
    shape = (groups // 2, reps)
    j, z, p = place()
    home = j == p
    scale = (node_feats.shape[0] * groups) ** (-0.5)

    def send(value, move):
        return lax.ppermute(value, AXES, route(shape, move))

    def sibling(c, j, z):
        return (c, 1 - j, z)

    def home_to_sibling(c, j, z):
        return (c, 1 - j, z) if j == z % 2 else None

    def across(c, j, z):
        return (c, j, (z + reps // 2) % reps)

    own = tile_values[0]
    blocks = node_feats.shape[0] // own.shape[-1]

    def to_home(c, j, z):
        return (c, 1 - j, z) if j == z % 2 else (c, j, z ^ 1)

    four = shape[0] == 4

    def to_direct(c, j, z):
        return (c ^ 1, j, z)

    def to_second(c, j, z):
        return (c ^ 2, j, z) if four else (c + 1 if c % 2 else c - 1, j, z)

    def to_far(c, j, z):
        return (c ^ 1, j, z) if four else (c - 1 if z % 2 else c + 1, j, z)

    def stage_one(c, j, z):
        if j == z % 2:
            return (c ^ 1, j, z)
        return (c ^ 2, j, z) if four and (c + z) % 2 else None

    def stage_one_cross(c, j, z):
        to = stage_one(c, j, z)
        return to and (to[0], 1 - j, z)

    first = send(own, to_home)
    mine, yours = halves(node_feats)
    one = send(mine, stage_one)
    two = send(yours, stage_one_cross)
    swapped = send(yours, sibling)
    self_choice = [("home", mine), ("away", swapped)]
    direct_choice = [("home", one), ("away", two)]
    meta = slot_blocks(tile_coords[:, 0], tile_counts[0], blocks)
    second, far = pick(
        [
            direct_choice if four else self_choice,
            [
                ("still home", swapped),
                ("still away", mine),
                ("relay home", two),
                ("relay away", one),
            ],
        ],
        [meta],
    )
    second = send(second, to_second)
    far = send(far, to_far)
    meta_b = send(meta, to_home)
    first, one, two = lax.optimization_barrier((first, one, two))
    other_first = send(first, home_to_sibling)
    meta_later, second, far = lax.optimization_barrier((meta_b, second, far))
    meta_far = send(meta_later, home_to_sibling)
    set_first = [(None, (meta_b, first))]
    panels = [
        ("self", [("home", mine), ("away", swapped)]),
        ("near", [("home", swapped), ("away", mine)]),
        ("direct", direct_choice),
        ("second", [(None, second)]),
        ("far", [(None, far)]),
    ]
    part = tile_product(panels, [set_first], jnp.float32, weigh=WEIGH)
    set_rest = [("home", (meta, own)), ("away", (meta_far, other_first))]
    part = tile_product(panels, [set_rest], jnp.bfloat16, part)

    def join(value):
        other = send(value, across)
        return (value.astype(jnp.float32) + other.astype(jnp.float32)).astype(jnp.bfloat16)

    near = join(part)
    far_half = send(near, sibling)
    cot, cot_yours = halves(cotangent)
    act, adj = middle(near, far_half, weight, cot, send(cot_yours, sibling))

    direct = send(adj, to_direct)
    near_one = send(
        adj, lambda c, j, z: (c if (c + z) % 2 or not four else c ^ 2, j, z ^ 1)
    )
    adj_later, near_one, direct = lax.optimization_barrier((adj, near_one, direct))
    second = send(direct if four else adj_later, to_second)
    grad = grad_block(scale, near, far_half, adj, adj)
    grad_got = send(grad, lambda c, j, z: (c, j, z ^ 1))
    adj_soon, grad_got = lax.optimization_barrier((adj, grad_got))
    far = send(near_one, to_far)
    near_choice = [("still", near_one)]
    if four:
        near_two = send(
            adj_soon, lambda c, j, z: None if (c + z) % 2 else (c, j, z ^ 1)
        )
        near_choice.append(("relay", near_two))
    panels = [("self", [(None, adj)]), ("direct", [(None, direct)])]
    back_part = tile_product(panels, [set_first, set_rest], jnp.float32)
    panels = [("near", near_choice), ("second", [(None, second)]), ("far", [(None, far)])]
    back_part = tile_product(
        panels, [set_first, set_rest], jnp.bfloat16, back_part, [grad_got]
    )

    def deliver(value):
        one = send(value, lambda c, j, z: (c, j, z ^ 1) if j == z % 2 else (c, 1 - j, z))
        two = send(value, lambda c, j, z: None if j == z % 2 else (c, 1 - j, z ^ 1))
        return one, two

    act_later, back_part = lax.optimization_barrier((act, back_part))
    act_parts = [act, *deliver(act_later)]
    grad = add_after([grad, grad_got], jnp.bfloat16, back_part)
    step = 1
    while step < shape[0]:
        got = send(grad, lambda c, j, z, s=step: (c ^ s, j, z))
        step *= 2
        if step < shape[0]:
            grad = add_after([grad, got], jnp.bfloat16)
    back = add_after([back_part, send(back_part, across)], jnp.bfloat16, got)
    back_parts = [back, *deliver(back)]
    grad = add_after([grad, got], jnp.float32, back)
    activated, weight_grad = gather_halves(act_parts, grad, send(grad, sibling))
    input_grad = final(back_parts, weight)
    return (activated, input_grad, weight_grad)


def solution(mesh):
    return jax.shard_map(
        per_device,
        mesh=mesh,
        in_specs=(
            P("rows", None),
            P(),
            P("rows", None),
            P("rows", None, "rep", None, None),
            P(None, "rows", None, "rep"),
            P("rows", None),
        ),
        out_specs=(P("rows", None), P("rows", None), P()),
        check_vma=False,
    )
```

```python
import functools

import jax
import jax.numpy as jnp
from jax import lax
from jax.experimental import pallas as pl
from jax.experimental.pallas import tpu as pltpu
from jax.sharding import PartitionSpec as P

AXES = ("rows", "rep")
WEIGH = 75


def route(shape, move):
    chips, reps = shape
    pairs = []
    for c in range(chips):
        for j in range(2):
            for z in range(reps):
                to = move(c, j, z)
                if to is not None:
                    target = ((to[0] % chips) * 2 + to[1]) * reps + to[2]
                    pairs.append(((c * 2 + j) * reps + z, target))
    return pairs


def place():
    r = lax.axis_index("rows")
    z = lax.axis_index("rep")
    return r % 2, z, z % 2


def when_of(case):
    j, z, p = place()
    home = j == p
    relay = jnp.logical_and(
        lax.axis_size("rows") == 8, (lax.axis_index("rows") // 2 + z) % 2 == 1
    )
    return {
        "core 0": j == 0,
        "core 1": j == 1,
        "home": home,
        "away": jnp.logical_not(home),
        "relay": relay,
        "still": jnp.logical_not(relay),
        "relay home": jnp.logical_and(relay, home),
        "relay away": jnp.logical_and(relay, jnp.logical_not(home)),
        "still home": jnp.logical_and(jnp.logical_not(relay), home),
        "still away": jnp.logical_and(jnp.logical_not(relay), jnp.logical_not(home)),
    }[case]


def start_chosen(choice, make):
    if len(choice) == 1:
        make(choice[0][1]).start()
        return
    for case, ref in choice:

        @pl.when(when_of(case))
        def _(ref=ref):
            make(ref).start()


def halves_kernel(x_ref, near_ref, far_ref, sems):
    j, _, _ = place()
    half = near_ref.shape[1]
    copies = []
    for i, out in enumerate((near_ref, far_ref)):
        start = pl.multiple_of((j if i == 0 else 1 - j) * half, half)
        copy = pltpu.make_async_copy(x_ref.at[:, pl.ds(start, half)], out, sems.at[i])
        copy.start()
        copies.append(copy)
    for copy in copies:
        copy.wait()


def halves(value):
    rows, width = value.shape
    part = jax.ShapeDtypeStruct((rows, width // 2), value.dtype)
    hbm = pl.BlockSpec(memory_space=pltpu.HBM)
    return pl.pallas_call(
        halves_kernel,
        out_shape=(part, part),
        in_specs=[hbm],
        out_specs=(hbm, hbm),
        scratch_shapes=[pltpu.SemaphoreType.DMA((2,))],
        compiler_params=pltpu.CompilerParams(vmem_limit_bytes=1024 * 1024),
        name="halves",
    )(value)


def transform_kernel(x_ref, w_ref, near_ref, far_ref):
    near_cols, far_cols = half_columns(near_ref.shape[1])
    for cols, out_ref in ((near_cols, near_ref), (far_cols, far_ref)):
        product = jnp.dot(x_ref[...], w_ref[:, cols], preferred_element_type=jnp.float32)
        out_ref[...] = product.astype(out_ref.dtype)


def transform(feats, weight):
    rows, width = feats.shape
    vmem = pl.BlockSpec(memory_space=pltpu.VMEM)
    part = jax.ShapeDtypeStruct((rows, weight.shape[1] // 2), feats.dtype)
    return pl.pallas_call(
        transform_kernel,
        out_shape=(part, part),
        in_specs=[vmem, vmem],
        out_specs=(vmem, vmem),
        compiler_params=pltpu.CompilerParams(vmem_limit_bytes=8 * 1024 * 1024),
        name="transform",
    )(feats, weight)


def pick_kernel(cases, waits, *refs):
    refs = list(refs)
    choices = [[(case, refs.pop(0)) for case in each] for each in cases]
    outs, sems = refs[waits:-1], refs[-1]

    def copy_to(i):
        return lambda ref: pltpu.make_async_copy(ref, outs[i], sems.at[i])

    for i, choice in enumerate(choices):
        start_chosen(choice, copy_to(i))
    for i, choice in enumerate(choices):
        copy_to(i)(choice[0][1]).wait()


def pick(choices, after):
    hbm = pl.BlockSpec(memory_space=pltpu.HBM)
    arrays = [array for choice in choices for _, array in choice]
    shape = jax.ShapeDtypeStruct(arrays[0].shape, arrays[0].dtype)
    return pl.pallas_call(
        functools.partial(
            pick_kernel, [[case for case, _ in choice] for choice in choices], len(after)
        ),
        out_shape=(shape,) * len(choices),
        in_specs=[hbm] * len(arrays) + [pl.BlockSpec(memory_space=pl.ANY)] * len(after),
        out_specs=(hbm,) * len(choices),
        scratch_shapes=[pltpu.SemaphoreType.DMA((len(choices),))],
        compiler_params=pltpu.CompilerParams(vmem_limit_bytes=1024 * 1024),
        name="pick",
    )(*arrays, *after)


def slots_kernel(dead, coords_ref, counts_ref, out_ref):
    _, z, _ = place()
    _, reach, slots = coords_ref.shape
    for d in range(reach):
        for k in range(slots):
            live = z * slots + k < counts_ref[d]
            out_ref[0, d * slots + k] = jnp.where(live, coords_ref[0, d, k], dead)
            out_ref[1, d * slots + k] = coords_ref[1, d, k]


def slot_blocks(coords, counts, dead):
    smem = pl.BlockSpec(memory_space=pltpu.SMEM)
    return pl.pallas_call(
        functools.partial(slots_kernel, dead),
        out_shape=jax.ShapeDtypeStruct((2, coords.shape[1] * coords.shape[2]), jnp.int32),
        in_specs=[smem, smem],
        out_specs=smem,
        compiler_params=pltpu.CompilerParams(vmem_limit_bytes=1024 * 1024),
        name="slot_blocks",
    )(coords, counts)


def offset_of(kind):
    _, _, p = place()
    even = (lax.axis_index("rows") // 2) % 2 == 0
    return {
        "self": 2,
        "near": jnp.where(p == 0, 3, 1),
        "far": jnp.where(p == 0, 1, 3),
        "direct": jnp.where(even, 4, 0),
        "second": jnp.where(even, 0, 4),
    }[kind]


def chosen(choice, read):
    value = read(choice[0][1])
    for case, ref in choice[1:]:
        value = jnp.where(when_of(case), read(ref), value)
    return value


def tile_kernel(kinds, cases, sets, summed, waits, *refs):
    refs = list(refs)
    metas = [[(case, refs.pop(0)) for case in each] for each in sets]
    tiles = [[(case, refs.pop(0)) for case in each] for each in sets]
    panels = [[(case, refs.pop(0)) for case in each] for each in cases]
    before = refs.pop(0) if summed else None
    out_ref, acc_ref = refs[waits:]
    _, slots, tile, _ = tiles[0][0][1].shape
    rows = out_ref.shape[0]
    if summed:
        acc_ref[:rows, :] = before[...]
    else:
        acc_ref[...] = jnp.zeros_like(acc_ref)
    for i, kind in enumerate(kinds):
        d = offset_of(kind)
        for s in range(len(sets)):
            for k in range(slots):
                row = chosen(metas[s], lambda ref: ref[0, d * slots + k])
                col = chosen(metas[s], lambda ref: ref[1, d * slots + k])
                row = pl.multiple_of(row * tile, tile)
                col = pl.multiple_of(col * tile, tile)
                acc_ref[pl.ds(row, tile), :] += jnp.dot(
                    chosen(tiles[s], lambda ref: ref[d, k]),
                    chosen(panels[i], lambda ref: ref[pl.ds(col, tile), :]),
                    preferred_element_type=jnp.float32,
                )
    out_ref[...] = acc_ref[:rows, :].astype(out_ref.dtype)


def tile_product(named, sets, dtype, before=None, after=(), weigh=1):
    kinds = [kind for kind, _ in named]
    cases = [[case for case, _ in choice] for _, choice in named]
    panels = [panel for _, choice in named for _, panel in choice]
    metas = [meta for choice in sets for _, (meta, _) in choice]
    tiles = [values for choice in sets for _, (_, values) in choice]
    rows, width = panels[0].shape
    _, slots, tile, _ = tiles[0].shape
    smem = pl.BlockSpec(memory_space=pltpu.SMEM)
    vmem = pl.BlockSpec(memory_space=pltpu.VMEM)
    anywhere = pl.BlockSpec(memory_space=pl.ANY)
    count = len(kinds) * len(sets) * slots
    summed = before is not None
    return pl.pallas_call(
        functools.partial(
            tile_kernel,
            kinds,
            cases,
            [[case for case, _ in choice] for choice in sets],
            summed,
            len(after),
        ),
        out_shape=jax.ShapeDtypeStruct((rows, width), dtype),
        in_specs=[smem] * len(metas)
        + [vmem] * (len(tiles) + len(panels) + summed)
        + [anywhere] * len(after),
        out_specs=vmem,
        scratch_shapes=[pltpu.VMEM((rows + tile, width), jnp.float32)],
        compiler_params=pltpu.CompilerParams(vmem_limit_bytes=12 * 1024 * 1024),
        cost_estimate=pl.CostEstimate(
            flops=weigh * 2 * count * tile * tile * width,
            bytes_accessed=weigh * (count * tile * tile * 2 + len(kinds) * rows * width * 2),
            transcendentals=0,
        ),
        name="tile_product",
    )(*metas, *tiles, *panels, *([before] if summed else []), *after)


def middle_kernel(part_ref, zero_ref, one_ref, cot_ref, swap_ref, act_ref, adj_ref):
    got = chosen([("core 0", zero_ref), ("core 1", one_ref)], lambda ref: ref[...])
    agg = part_ref[...].astype(jnp.float32) + got.astype(jnp.float32)
    sig = jax.nn.sigmoid(agg)
    act_ref[...] = (agg * sig).astype(act_ref.dtype)
    slope = sig * (1.0 + agg * (1.0 - sig))
    cot = chosen([("home", cot_ref), ("away", swap_ref)], lambda ref: ref[...])
    adj_ref[...] = (cot.astype(jnp.float32) * slope).astype(adj_ref.dtype)


def middle(part, zero, one, cot, cot_swap):
    vmem = pl.BlockSpec(memory_space=pltpu.VMEM)
    out = jax.ShapeDtypeStruct(part.shape, jnp.bfloat16)
    return pl.pallas_call(
        middle_kernel,
        out_shape=(out, out),
        in_specs=[vmem] * 5,
        out_specs=(vmem, vmem),
        compiler_params=pltpu.CompilerParams(vmem_limit_bytes=8 * 1024 * 1024),
        cost_estimate=pl.CostEstimate(
            flops=20 * part.size, bytes_accessed=10 * part.size, transcendentals=part.size
        ),
        name="middle",
    )(part, zero, one, cot, cot_swap)


def grad_kernel(scale, feats_ref, swap_ref, back_ref, out_ref):
    feats = chosen([("home", feats_ref), ("away", swap_ref)], lambda ref: ref[...])
    dims = (((0,), (0,)), ((), ()))
    block = lax.dot_general(feats, back_ref[...], dims, preferred_element_type=jnp.float32)
    out_ref[...] = (scale * block).astype(out_ref.dtype)


def grad_block(scale, feats, feats_swap, back):
    vmem = pl.BlockSpec(memory_space=pltpu.VMEM)
    rows, wide = feats.shape
    width = back.shape[1]
    return pl.pallas_call(
        functools.partial(grad_kernel, scale),
        out_shape=jax.ShapeDtypeStruct((wide, width), jnp.bfloat16),
        in_specs=[vmem] * 3,
        out_specs=vmem,
        compiler_params=pltpu.CompilerParams(vmem_limit_bytes=8 * 1024 * 1024),
        cost_estimate=pl.CostEstimate(
            flops=2 * rows * wide * width, bytes_accessed=8 * rows * width, transcendentals=0
        ),
        name="grad_block",
    )(feats, feats_swap, back)


def add_kernel(count, *refs):
    values = [ref[...].astype(jnp.float32) for ref in refs[:count]]
    total = values[0] + values[1]
    if count == 4:
        total = total + (values[2] + values[3])
    refs[-1][...] = total.astype(refs[-1].dtype)


def add_after(values, dtype, *after):
    vmem = pl.BlockSpec(memory_space=pltpu.VMEM)
    return pl.pallas_call(
        functools.partial(add_kernel, len(values)),
        out_shape=jax.ShapeDtypeStruct(values[0].shape, dtype),
        in_specs=[vmem] * len(values) + [pl.BlockSpec(memory_space=pl.ANY)] * len(after),
        out_specs=vmem,
        compiler_params=pltpu.CompilerParams(vmem_limit_bytes=4 * 1024 * 1024),
        name="add_after",
    )(*values, *after)


def half_columns(half):
    j, _, _ = place()
    near = pl.ds(pl.multiple_of(j * half, half), half)
    return near, pl.ds(pl.multiple_of((1 - j) * half, half), half)


def final_kernel(*refs):
    back, act, (w_ref, grad_ref, rest_ref), outs = refs[:3], refs[3:6], refs[6:9], refs[9:]
    out_ref, act_ref, grad_out_ref = outs
    near_cols, far_cols = half_columns(back[0].shape[1])

    def near_of(parts):
        return chosen([("home", parts[0]), ("away", parts[1])], lambda ref: ref[...])

    dims = (((1,), (1,)), ((), ()))
    total = lax.dot_general(
        near_of(back), w_ref[:, near_cols], dims, preferred_element_type=jnp.float32
    )
    total += lax.dot_general(
        back[2][...], w_ref[:, far_cols], dims, preferred_element_type=jnp.float32
    )
    out_ref[...] = total.astype(out_ref.dtype)
    act_ref[:, near_cols] = near_of(act)
    act_ref[:, far_cols] = act[2][...]
    grad_out_ref[:, near_cols] = grad_ref[...]
    grad_out_ref[:, far_cols] = rest_ref[...]


def final(back, act, weight, grad, rest):
    vmem = pl.BlockSpec(memory_space=pltpu.VMEM)
    rows = back[0].shape[0]
    wide = weight.shape[0]
    whole = jax.ShapeDtypeStruct((rows, wide), jnp.bfloat16)
    return pl.pallas_call(
        final_kernel,
        out_shape=(whole, whole, jax.ShapeDtypeStruct(weight.shape, jnp.float32)),
        in_specs=[vmem] * 9,
        out_specs=(vmem,) * 3,
        compiler_params=pltpu.CompilerParams(vmem_limit_bytes=8 * 1024 * 1024),
        cost_estimate=pl.CostEstimate(
            flops=2 * rows * wide * wide, bytes_accessed=8 * rows * wide, transcendentals=0
        ),
        name="final",
    )(*back, *act, weight, grad, rest)


def per_device(node_feats, weight, cotangent, tile_values, tile_coords, tile_counts):
    groups = lax.axis_size("rows")
    reps = lax.axis_size("rep")
    shape = (groups // 2, reps)
    j, z, p = place()
    home = j == p
    scale = (node_feats.shape[0] * groups) ** (-0.5)

    def send(value, move):
        return lax.ppermute(value, AXES, route(shape, move))

    def sibling(c, j, z):
        return (c, 1 - j, z)

    def home_to_sibling(c, j, z):
        return (c, 1 - j, z) if j == z % 2 else None

    def across(c, j, z):
        return (c, j, (z + reps // 2) % reps)

    own = tile_values[0]
    blocks = node_feats.shape[0] // own.shape[-1]

    def to_home(c, j, z):
        return (c, 1 - j, z) if j == z % 2 else (c, j, z ^ 1)

    four = shape[0] == 4

    def to_direct(c, j, z):
        return (c ^ 1, j, z)

    def to_second(c, j, z):
        return (c ^ 2, j, z) if four else (c + 1 if c % 2 else c - 1, j, z)

    def to_far(c, j, z):
        return (c ^ 1, j, z) if four else (c - 1 if z % 2 else c + 1, j, z)

    def stage_one(c, j, z):
        if j == z % 2:
            return (c ^ 1, j, z)
        return (c ^ 2, j, z) if four and (c + z) % 2 else None

    def stage_one_cross(c, j, z):
        to = stage_one(c, j, z)
        return to and (to[0], 1 - j, z)

    first = send(own, to_home)
    mine, yours = transform(node_feats, weight)
    one = send(mine, stage_one)
    two = send(yours, stage_one_cross)
    swapped = send(yours, sibling)
    self_choice = [("home", mine), ("away", swapped)]
    direct_choice = [("home", one), ("away", two)]
    meta = slot_blocks(tile_coords[:, 0], tile_counts[0], blocks)
    second, far = pick(
        [
            direct_choice if four else self_choice,
            [
                ("still home", swapped),
                ("still away", mine),
                ("relay home", two),
                ("relay away", one),
            ],
        ],
        [meta],
    )
    second = send(second, to_second)
    far = send(far, to_far)
    meta_b = send(meta, to_home)
    first, one, two = lax.optimization_barrier((first, one, two))
    other_first = send(first, home_to_sibling)
    meta_later, second, far = lax.optimization_barrier((meta_b, second, far))
    meta_far = send(meta_later, home_to_sibling)
    set_first = [(None, (meta_b, first))]
    panels = [
        ("self", [("home", mine), ("away", swapped)]),
        ("near", [("home", swapped), ("away", mine)]),
        ("direct", direct_choice),
        ("second", [(None, second)]),
        ("far", [(None, far)]),
    ]
    part = tile_product(panels, [set_first], jnp.float32, weigh=WEIGH)
    set_rest = [("home", (meta, own)), ("away", (meta_far, other_first))]
    cot, cot_yours = halves(cotangent)
    cot_swap = send(cot_yours, sibling)
    feats_swap = send(node_feats, sibling)
    part = tile_product(panels, [set_rest], jnp.bfloat16, part, [cot_swap, feats_swap])

    def core_across(core):
        return lambda c, j, z: across(c, j, z) if j == core else None

    got_zero = send(part, core_across(0))
    token = send(got_zero[:16], lambda c, j, z: (c, 1, z) if j == 0 else None)
    (part_later,) = pick([[(None, part)]], [token])
    got_one = send(part_later, core_across(1))
    act, adj = middle(part, got_zero, got_one, cot, cot_swap)

    direct = send(adj, to_direct)
    near_one = send(
        adj, lambda c, j, z: (c if (c + z) % 2 or not four else c ^ 2, j, z ^ 1)
    )
    adj_later, near_one, direct = lax.optimization_barrier((adj, near_one, direct))
    second = send(direct if four else adj_later, to_second)
    far = send(near_one, to_far)
    near_choice = [("still", near_one)]
    if four:
        near_two = send(
            adj_later, lambda c, j, z: None if (c + z) % 2 else (c, j, z ^ 1)
        )
        near_choice.append(("relay", near_two))
    panels = [("self", [(None, adj)]), ("direct", [(None, direct)])]
    back_part = tile_product(panels, [set_first, set_rest], jnp.float32)
    panels = [("near", near_choice), ("second", [(None, second)]), ("far", [(None, far)])]
    back_part = tile_product(panels, [set_first, set_rest], jnp.bfloat16, back_part)

    def to_other_z(c, j, z):
        return (c, j, z ^ 1)

    def swap(value, got, after):
        (payload,) = pick([[("home", got), ("away", value)]], after)
        return [value, got, send(payload, sibling)]

    grad = grad_block(scale, node_feats, feats_swap, back_part)
    grad = add_after([grad, send(grad, to_other_z)], jnp.bfloat16)
    got = send(grad, to_direct)
    act_later, back_part = lax.optimization_barrier((act, back_part))
    act_got = send(act_later, to_other_z)
    back = add_after([back_part, send(back_part, across)], jnp.bfloat16, got, act_got)
    back_got = send(back, to_other_z)
    back_parts = swap(back, back_got, [])
    act_parts = swap(act, act_got, [back_got])
    grad = add_after([grad, got], jnp.bfloat16, back)
    step = 2
    while step < shape[0]:
        got = send(grad, lambda c, j, z, s=step: (c ^ s, j, z))
        grad = add_after([grad, got], jnp.float32)
        step *= 2
    grad = add_after([grad, send(grad, across)], jnp.float32, back_got)
    input_grad, activated, weight_grad = final(
        back_parts, act_parts, weight, grad, send(grad, sibling)
    )
    return (activated, input_grad, weight_grad)


def solution(mesh):
    return jax.shard_map(
        per_device,
        mesh=mesh,
        in_specs=(
            P("rows", None),
            P(),
            P("rows", None),
            P("rows", None, "rep", None, None),
            P(None, "rows", None, "rep"),
            P("rows", None),
        ),
        out_specs=(P("rows", None), P("rows", None), P()),
        check_vma=False,
    )
```

```python
import functools

import jax
import jax.numpy as jnp
from jax import lax
from jax.experimental import pallas as pl
from jax.experimental.pallas import tpu as pltpu
from jax.sharding import PartitionSpec as P

AXES = ("rows", "rep")
WEIGH = 75


def route(shape, move):
    chips, reps = shape
    pairs = []
    for c in range(chips):
        for j in range(2):
            for z in range(reps):
                to = move(c, j, z)
                if to is not None:
                    target = ((to[0] % chips) * 2 + to[1]) * reps + to[2]
                    pairs.append(((c * 2 + j) * reps + z, target))
    return pairs


def place():
    r = lax.axis_index("rows")
    z = lax.axis_index("rep")
    return r % 2, z, z % 2


def when_of(case):
    j, z, p = place()
    home = j == p
    relay = jnp.logical_and(
        lax.axis_size("rows") == 8, (lax.axis_index("rows") // 2 + z) % 2 == 1
    )
    return {
        "home": home,
        "away": jnp.logical_not(home),
        "relay": relay,
        "still": jnp.logical_not(relay),
        "relay home": jnp.logical_and(relay, home),
        "relay away": jnp.logical_and(relay, jnp.logical_not(home)),
        "still home": jnp.logical_and(jnp.logical_not(relay), home),
        "still away": jnp.logical_and(jnp.logical_not(relay), jnp.logical_not(home)),
    }[case]


def start_chosen(choice, make):
    if len(choice) == 1:
        make(choice[0][1]).start()
        return
    for case, ref in choice:

        @pl.when(when_of(case))
        def _(ref=ref):
            make(ref).start()


def halves_kernel(x_ref, near_ref, far_ref, sems):
    j, _, _ = place()
    half = near_ref.shape[1]
    copies = []
    for i, out in enumerate((near_ref, far_ref)):
        start = pl.multiple_of((j if i == 0 else 1 - j) * half, half)
        copy = pltpu.make_async_copy(x_ref.at[:, pl.ds(start, half)], out, sems.at[i])
        copy.start()
        copies.append(copy)
    for copy in copies:
        copy.wait()


def halves(value):
    rows, width = value.shape
    part = jax.ShapeDtypeStruct((rows, width // 2), value.dtype)
    hbm = pl.BlockSpec(memory_space=pltpu.HBM)
    return pl.pallas_call(
        halves_kernel,
        out_shape=(part, part),
        in_specs=[hbm],
        out_specs=(hbm, hbm),
        scratch_shapes=[pltpu.SemaphoreType.DMA((2,))],
        compiler_params=pltpu.CompilerParams(vmem_limit_bytes=1024 * 1024),
        name="halves",
    )(value)


def pick_kernel(cases, waits, *refs):
    refs = list(refs)
    choices = [[(case, refs.pop(0)) for case in each] for each in cases]
    outs, sems = refs[waits:-1], refs[-1]

    def copy_to(i):
        return lambda ref: pltpu.make_async_copy(ref, outs[i], sems.at[i])

    for i, choice in enumerate(choices):
        start_chosen(choice, copy_to(i))
    for i, choice in enumerate(choices):
        copy_to(i)(choice[0][1]).wait()


def pick(choices, after):
    hbm = pl.BlockSpec(memory_space=pltpu.HBM)
    arrays = [array for choice in choices for _, array in choice]
    shape = jax.ShapeDtypeStruct(arrays[0].shape, arrays[0].dtype)
    return pl.pallas_call(
        functools.partial(
            pick_kernel, [[case for case, _ in choice] for choice in choices], len(after)
        ),
        out_shape=(shape,) * len(choices),
        in_specs=[hbm] * len(arrays) + [pl.BlockSpec(memory_space=pl.ANY)] * len(after),
        out_specs=(hbm,) * len(choices),
        scratch_shapes=[pltpu.SemaphoreType.DMA((len(choices),))],
        compiler_params=pltpu.CompilerParams(vmem_limit_bytes=1024 * 1024),
        name="pick",
    )(*arrays, *after)


def slots_kernel(dead, coords_ref, counts_ref, out_ref):
    _, z, _ = place()
    _, reach, slots = coords_ref.shape
    for d in range(reach):
        for k in range(slots):
            live = z * slots + k < counts_ref[d]
            out_ref[0, d * slots + k] = jnp.where(live, coords_ref[0, d, k], dead)
            out_ref[1, d * slots + k] = coords_ref[1, d, k]


def slot_blocks(coords, counts, dead):
    smem = pl.BlockSpec(memory_space=pltpu.SMEM)
    return pl.pallas_call(
        functools.partial(slots_kernel, dead),
        out_shape=jax.ShapeDtypeStruct((2, coords.shape[1] * coords.shape[2]), jnp.int32),
        in_specs=[smem, smem],
        out_specs=smem,
        compiler_params=pltpu.CompilerParams(vmem_limit_bytes=1024 * 1024),
        name="slot_blocks",
    )(coords, counts)


def offset_of(kind):
    _, _, p = place()
    even = (lax.axis_index("rows") // 2) % 2 == 0
    return {
        "self": 2,
        "near": jnp.where(p == 0, 3, 1),
        "far": jnp.where(p == 0, 1, 3),
        "direct": jnp.where(even, 4, 0),
        "second": jnp.where(even, 0, 4),
    }[kind]


def chosen(choice, read):
    value = read(choice[0][1])
    for case, ref in choice[1:]:
        value = jnp.where(when_of(case), read(ref), value)
    return value


def tile_kernel(kinds, cases, sets, summed, waits, *refs):
    refs = list(refs)
    metas = [[(case, refs.pop(0)) for case in each] for each in sets]
    tiles = [[(case, refs.pop(0)) for case in each] for each in sets]
    panels = [[(case, refs.pop(0)) for case in each] for each in cases]
    before = refs.pop(0) if summed else None
    out_ref, acc_ref = refs[waits:]
    _, slots, tile, _ = tiles[0][0][1].shape
    rows = out_ref.shape[0]
    if summed:
        acc_ref[:rows, :] = before[...]
    else:
        acc_ref[...] = jnp.zeros_like(acc_ref)
    for i, kind in enumerate(kinds):
        d = offset_of(kind)
        for s in range(len(sets)):
            for k in range(slots):
                row = chosen(metas[s], lambda ref: ref[0, d * slots + k])
                col = chosen(metas[s], lambda ref: ref[1, d * slots + k])
                row = pl.multiple_of(row * tile, tile)
                col = pl.multiple_of(col * tile, tile)
                acc_ref[pl.ds(row, tile), :] += jnp.dot(
                    chosen(tiles[s], lambda ref: ref[d, k]),
                    chosen(panels[i], lambda ref: ref[pl.ds(col, tile), :]),
                    preferred_element_type=jnp.float32,
                )
    out_ref[...] = acc_ref[:rows, :].astype(out_ref.dtype)


def tile_product(named, sets, dtype, before=None, after=(), weigh=1):
    kinds = [kind for kind, _ in named]
    cases = [[case for case, _ in choice] for _, choice in named]
    panels = [panel for _, choice in named for _, panel in choice]
    metas = [meta for choice in sets for _, (meta, _) in choice]
    tiles = [values for choice in sets for _, (_, values) in choice]
    rows, width = panels[0].shape
    _, slots, tile, _ = tiles[0].shape
    smem = pl.BlockSpec(memory_space=pltpu.SMEM)
    vmem = pl.BlockSpec(memory_space=pltpu.VMEM)
    anywhere = pl.BlockSpec(memory_space=pl.ANY)
    count = len(kinds) * len(sets) * slots
    summed = before is not None
    return pl.pallas_call(
        functools.partial(
            tile_kernel,
            kinds,
            cases,
            [[case for case, _ in choice] for choice in sets],
            summed,
            len(after),
        ),
        out_shape=jax.ShapeDtypeStruct((rows, width), dtype),
        in_specs=[smem] * len(metas)
        + [vmem] * (len(tiles) + len(panels) + summed)
        + [anywhere] * len(after),
        out_specs=vmem,
        scratch_shapes=[pltpu.VMEM((rows + tile, width), jnp.float32)],
        compiler_params=pltpu.CompilerParams(vmem_limit_bytes=12 * 1024 * 1024),
        cost_estimate=pl.CostEstimate(
            flops=weigh * 2 * count * tile * tile * width,
            bytes_accessed=weigh * (count * tile * tile * 2 + len(kinds) * rows * width * 2),
            transcendentals=0,
        ),
        name="tile_product",
    )(*metas, *tiles, *panels, *([before] if summed else []), *after)


def middle_kernel(near_ref, far_ref, w_ref, cot_ref, cot_swap_ref, act_ref, adj_ref):
    j, _, p = place()
    half = near_ref.shape[1]
    near = pl.multiple_of(j * half, half)
    far = pl.multiple_of((1 - j) * half, half)
    cols = pl.ds(near, half)
    agg = jnp.dot(
        near_ref[...], w_ref[pl.ds(near, half), cols], preferred_element_type=jnp.float32
    )
    agg += jnp.dot(far_ref[...], w_ref[pl.ds(far, half), cols], preferred_element_type=jnp.float32)
    sig = jax.nn.sigmoid(agg)
    act_ref[...] = (agg * sig).astype(act_ref.dtype)
    slope = sig * (1.0 + agg * (1.0 - sig))
    cot = jnp.where(j == p, cot_ref[...], cot_swap_ref[...])
    adj_ref[...] = (cot.astype(jnp.float32) * slope).astype(adj_ref.dtype)


def middle(near, far, weight, cot, cot_swap):
    vmem = pl.BlockSpec(memory_space=pltpu.VMEM)
    rows, width = near.shape
    out = jax.ShapeDtypeStruct((rows, width), jnp.bfloat16)
    return pl.pallas_call(
        middle_kernel,
        out_shape=(out, out),
        in_specs=[vmem] * 5,
        out_specs=(vmem, vmem),
        compiler_params=pltpu.CompilerParams(vmem_limit_bytes=8 * 1024 * 1024),
        cost_estimate=pl.CostEstimate(
            flops=4 * rows * width * width,
            bytes_accessed=10 * rows * width,
            transcendentals=rows * width,
        ),
        name="middle",
    )(near, far, weight, cot, cot_swap)


def grad_kernel(scale, near_ref, far_ref, adj_ref, after_ref, out_ref):
    j, _, _ = place()
    half = near_ref.shape[1]
    dims = (((0,), (0,)), ((), ()))
    for i, ref in enumerate((near_ref, far_ref)):
        start = pl.multiple_of((j if i == 0 else 1 - j) * half, half)
        block = lax.dot_general(ref[...], adj_ref[...], dims, preferred_element_type=jnp.float32)
        out_ref[pl.ds(start, half), :] = (scale * block).astype(out_ref.dtype)


def grad_block(scale, near, far, adj, after):
    vmem = pl.BlockSpec(memory_space=pltpu.VMEM)
    rows, width = near.shape
    return pl.pallas_call(
        functools.partial(grad_kernel, scale),
        out_shape=jax.ShapeDtypeStruct((2 * width, width), jnp.bfloat16),
        in_specs=[vmem] * 3 + [pl.BlockSpec(memory_space=pl.ANY)],
        out_specs=vmem,
        compiler_params=pltpu.CompilerParams(vmem_limit_bytes=8 * 1024 * 1024),
        cost_estimate=pl.CostEstimate(
            flops=4 * WEIGH * rows * width * width,
            bytes_accessed=8 * WEIGH * rows * width,
            transcendentals=0,
        ),
        name="grad_block",
    )(near, far, adj, after)


def add_kernel(count, *refs):
    values = [ref[...].astype(jnp.float32) for ref in refs[:count]]
    total = values[0] + values[1]
    if count == 4:
        total = total + (values[2] + values[3])
    refs[-1][...] = total.astype(refs[-1].dtype)


def add_after(values, dtype, *after):
    vmem = pl.BlockSpec(memory_space=pltpu.VMEM)
    return pl.pallas_call(
        functools.partial(add_kernel, len(values)),
        out_shape=jax.ShapeDtypeStruct(values[0].shape, dtype),
        in_specs=[vmem] * len(values) + [pl.BlockSpec(memory_space=pl.ANY)] * len(after),
        out_specs=vmem,
        compiler_params=pltpu.CompilerParams(vmem_limit_bytes=4 * 1024 * 1024),
        name="add_after",
    )(*values, *after)


def half_columns(half):
    j, _, _ = place()
    near = pl.ds(pl.multiple_of(j * half, half), half)
    return near, pl.ds(pl.multiple_of((1 - j) * half, half), half)


def near_and_far(parts):
    j, _, p = place()
    own, one, two = parts
    near = jnp.where(j == p, own[...], one[...])
    return near, jnp.where(j == p, one[...], two[...])


def gather_kernel(own_ref, one_ref, two_ref, grad_ref, rest_ref, act_ref, grad_out_ref):
    near_cols, far_cols = half_columns(own_ref.shape[1])
    near, far = near_and_far((own_ref, one_ref, two_ref))
    act_ref[:, near_cols] = near
    act_ref[:, far_cols] = far
    grad_out_ref[:, near_cols] = grad_ref[...]
    grad_out_ref[:, far_cols] = rest_ref[...]


def gather_halves(act, grad, rest):
    vmem = pl.BlockSpec(memory_space=pltpu.VMEM)
    rows, width = act[0].shape
    return pl.pallas_call(
        gather_kernel,
        out_shape=(
            jax.ShapeDtypeStruct((rows, 2 * width), act[0].dtype),
            jax.ShapeDtypeStruct((2 * width, 2 * width), grad.dtype),
        ),
        in_specs=[vmem] * 5,
        out_specs=(vmem, vmem),
        compiler_params=pltpu.CompilerParams(vmem_limit_bytes=8 * 1024 * 1024),
        name="gather_halves",
    )(*act, grad, rest)


def final_kernel(own_ref, one_ref, two_ref, w_ref, out_ref):
    near_cols, far_cols = half_columns(own_ref.shape[1])
    near, far = near_and_far((own_ref, one_ref, two_ref))
    dims = (((1,), (1,)), ((), ()))
    total = lax.dot_general(near, w_ref[:, near_cols], dims, preferred_element_type=jnp.float32)
    total += lax.dot_general(far, w_ref[:, far_cols], dims, preferred_element_type=jnp.float32)
    out_ref[...] = total.astype(out_ref.dtype)


def final(back, weight):
    vmem = pl.BlockSpec(memory_space=pltpu.VMEM)
    rows = back[0].shape[0]
    wide = weight.shape[0]
    return pl.pallas_call(
        final_kernel,
        out_shape=jax.ShapeDtypeStruct((rows, wide), jnp.bfloat16),
        in_specs=[vmem] * 4,
        out_specs=vmem,
        compiler_params=pltpu.CompilerParams(vmem_limit_bytes=8 * 1024 * 1024),
        cost_estimate=pl.CostEstimate(
            flops=2 * rows * wide * wide, bytes_accessed=8 * rows * wide, transcendentals=0
        ),
        name="final",
    )(*back, weight)


def per_device(node_feats, weight, cotangent, tile_values, tile_coords, tile_counts):
    groups = lax.axis_size("rows")
    reps = lax.axis_size("rep")
    shape = (groups // 2, reps)
    j, z, p = place()
    home = j == p
    scale = (node_feats.shape[0] * groups) ** (-0.5)

    def send(value, move):
        return lax.ppermute(value, AXES, route(shape, move))

    def sibling(c, j, z):
        return (c, 1 - j, z)

    def home_to_sibling(c, j, z):
        return (c, 1 - j, z) if j == z % 2 else None

    def across(c, j, z):
        return (c, j, (z + reps // 2) % reps)

    own = tile_values[0]
    blocks = node_feats.shape[0] // own.shape[-1]

    def to_home(c, j, z):
        return (c, 1 - j, z) if j == z % 2 else (c, j, z ^ 1)

    four = shape[0] == 4

    def to_direct(c, j, z):
        return (c ^ 1, j, z)

    def to_second(c, j, z):
        return (c ^ 2, j, z) if four else (c + 1 if c % 2 else c - 1, j, z)

    def to_far(c, j, z):
        return (c ^ 1, j, z) if four else (c - 1 if z % 2 else c + 1, j, z)

    def stage_one(c, j, z):
        if j == z % 2:
            return (c ^ 1, j, z)
        return (c ^ 2, j, z) if four and (c + z) % 2 else None

    def stage_one_cross(c, j, z):
        to = stage_one(c, j, z)
        return to and (to[0], 1 - j, z)

    first = send(own, to_home)
    half = node_feats.shape[1] // 2
    mine = lax.dynamic_slice_in_dim(node_feats, j * half, half, 1)
    yours = lax.dynamic_slice_in_dim(node_feats, (1 - j) * half, half, 1)
    one = send(mine, stage_one)
    two = send(yours, stage_one_cross)
    swapped = send(yours, sibling)
    self_choice = [("home", mine), ("away", swapped)]
    direct_choice = [("home", one), ("away", two)]
    meta = slot_blocks(tile_coords[:, 0], tile_counts[0], blocks)
    second, far = pick(
        [
            direct_choice if four else self_choice,
            [
                ("still home", swapped),
                ("still away", mine),
                ("relay home", two),
                ("relay away", one),
            ],
        ],
        [meta],
    )
    second = send(second, to_second)
    far = send(far, to_far)
    meta_b = send(meta, to_home)
    first, meta_b = lax.optimization_barrier((first, meta_b))
    other_first = send(first, home_to_sibling)
    meta_later, second = lax.optimization_barrier((meta_b, second))
    meta_far = send(meta_later, home_to_sibling)
    set_first = [(None, (meta_b, first))]
    panels = [
        ("self", [("home", mine), ("away", swapped)]),
        ("near", [("home", swapped), ("away", mine)]),
        ("direct", direct_choice),
        ("second", [(None, second)]),
        ("far", [(None, far)]),
    ]
    part = tile_product(panels, [set_first], jnp.float32, weigh=WEIGH)
    set_rest = [("home", (meta, own)), ("away", (meta_far, other_first))]
    part = tile_product(panels, [set_rest], jnp.bfloat16, part)

    def join(value):
        other = send(value, across)
        return (value.astype(jnp.float32) + other.astype(jnp.float32)).astype(jnp.bfloat16)

    near = join(part)
    far_half = send(near, sibling)
    cot, cot_yours = halves(cotangent)
    act, adj = middle(near, far_half, weight, cot, send(cot_yours, sibling))

    direct = send(adj, to_direct)
    near_one = send(
        adj, lambda c, j, z: (c if (c + z) % 2 or not four else c ^ 2, j, z ^ 1)
    )
    adj_later, near_one, direct = lax.optimization_barrier((adj, near_one, direct))
    second = send(direct if four else adj_later, to_second)
    grad = grad_block(scale, near, far_half, adj, direct)
    adj_later, grad = lax.optimization_barrier((adj_later, grad))
    far = send(near_one, to_far)
    near_choice = [("still", near_one)]
    if four:
        near_two = send(
            adj_later, lambda c, j, z: None if (c + z) % 2 else (c, j, z ^ 1)
        )
        near_choice.append(("relay", near_two))
    grad_got = send(grad, lambda c, j, z: (c, j, z ^ 1))
    panels = [("self", [(None, adj)]), ("direct", [(None, direct)])]
    back_part = tile_product(panels, [set_first, set_rest], jnp.float32)
    panels = [("near", near_choice), ("second", [(None, second)]), ("far", [(None, far)])]
    back_part = tile_product(
        panels, [set_first, set_rest], jnp.bfloat16, back_part, [grad_got]
    )

    def deliver(value):
        one = send(value, lambda c, j, z: (c, j, z ^ 1) if j == z % 2 else (c, 1 - j, z))
        two = send(value, lambda c, j, z: None if j == z % 2 else (c, 1 - j, z ^ 1))
        return one, two

    act_later, back_part = lax.optimization_barrier((act, back_part))
    act_parts = [act, *deliver(act_later)]
    grad = add_after([grad, grad_got], jnp.bfloat16, back_part)
    step = 1
    while step < shape[0]:
        got = send(grad, lambda c, j, z, s=step: (c ^ s, j, z))
        step *= 2
        if step < shape[0]:
            grad = add_after([grad, got], jnp.bfloat16)
    back = add_after([back_part, send(back_part, across)], jnp.bfloat16, got)
    back_parts = [back, *deliver(back)]
    grad = add_after([grad, got], jnp.float32, back)
    activated, weight_grad = gather_halves(act_parts, grad, send(grad, sibling))
    input_grad = final(back_parts, weight)
    return (activated, input_grad, weight_grad)


def solution(mesh):
    return jax.shard_map(
        per_device,
        mesh=mesh,
        in_specs=(
            P("rows", None),
            P(),
            P("rows", None),
            P("rows", None, "rep", None, None),
            P(None, "rows", None, "rep"),
            P("rows", None),
        ),
        out_specs=(P("rows", None), P("rows", None), P()),
        check_vma=False,
    )
```

```python
import functools

import jax
import jax.numpy as jnp
from jax import lax
from jax.experimental import pallas as pl
from jax.experimental.pallas import tpu as pltpu
from jax.sharding import PartitionSpec as P

AXES = ("rows", "rep")
WEIGH = 75


def route(shape, move):
    chips, reps = shape
    pairs = []
    for c in range(chips):
        for j in range(2):
            for z in range(reps):
                to = move(c, j, z)
                if to is not None:
                    target = ((to[0] % chips) * 2 + to[1]) * reps + to[2]
                    pairs.append(((c * 2 + j) * reps + z, target))
    return pairs


def place():
    r = lax.axis_index("rows")
    z = lax.axis_index("rep")
    return r % 2, z, z % 2


def when_of(case):
    j, z, p = place()
    home = j == p
    relay = jnp.logical_and(
        lax.axis_size("rows") == 8, (lax.axis_index("rows") // 2 + z) % 2 == 1
    )
    return {
        "home": home,
        "away": jnp.logical_not(home),
        "relay": relay,
        "still": jnp.logical_not(relay),
        "relay home": jnp.logical_and(relay, home),
        "relay away": jnp.logical_and(relay, jnp.logical_not(home)),
        "still home": jnp.logical_and(jnp.logical_not(relay), home),
        "still away": jnp.logical_and(jnp.logical_not(relay), jnp.logical_not(home)),
    }[case]


def start_chosen(choice, make):
    if len(choice) == 1:
        make(choice[0][1]).start()
        return
    for case, ref in choice:

        @pl.when(when_of(case))
        def _(ref=ref):
            make(ref).start()


def halves_kernel(x_ref, near_ref, far_ref, sems):
    j, _, _ = place()
    half = near_ref.shape[1]
    copies = []
    for i, out in enumerate((near_ref, far_ref)):
        start = pl.multiple_of((j if i == 0 else 1 - j) * half, half)
        copy = pltpu.make_async_copy(x_ref.at[:, pl.ds(start, half)], out, sems.at[i])
        copy.start()
        copies.append(copy)
    for copy in copies:
        copy.wait()


def halves(value):
    rows, width = value.shape
    part = jax.ShapeDtypeStruct((rows, width // 2), value.dtype)
    hbm = pl.BlockSpec(memory_space=pltpu.HBM)
    return pl.pallas_call(
        halves_kernel,
        out_shape=(part, part),
        in_specs=[hbm],
        out_specs=(hbm, hbm),
        scratch_shapes=[pltpu.SemaphoreType.DMA((2,))],
        compiler_params=pltpu.CompilerParams(vmem_limit_bytes=1024 * 1024),
        name="halves",
    )(value)


def pick_kernel(cases, waits, *refs):
    refs = list(refs)
    choices = [[(case, refs.pop(0)) for case in each] for each in cases]
    outs, sems = refs[waits:-1], refs[-1]

    def copy_to(i):
        return lambda ref: pltpu.make_async_copy(ref, outs[i], sems.at[i])

    for i, choice in enumerate(choices):
        start_chosen(choice, copy_to(i))
    for i, choice in enumerate(choices):
        copy_to(i)(choice[0][1]).wait()


def pick(choices, after):
    hbm = pl.BlockSpec(memory_space=pltpu.HBM)
    arrays = [array for choice in choices for _, array in choice]
    shape = jax.ShapeDtypeStruct(arrays[0].shape, arrays[0].dtype)
    return pl.pallas_call(
        functools.partial(
            pick_kernel, [[case for case, _ in choice] for choice in choices], len(after)
        ),
        out_shape=(shape,) * len(choices),
        in_specs=[hbm] * len(arrays) + [pl.BlockSpec(memory_space=pl.ANY)] * len(after),
        out_specs=(hbm,) * len(choices),
        scratch_shapes=[pltpu.SemaphoreType.DMA((len(choices),))],
        compiler_params=pltpu.CompilerParams(vmem_limit_bytes=1024 * 1024),
        name="pick",
    )(*arrays, *after)


def slots_kernel(dead, coords_ref, counts_ref, out_ref):
    _, z, _ = place()
    _, reach, slots = coords_ref.shape
    for d in range(reach):
        for k in range(slots):
            live = z * slots + k < counts_ref[d]
            out_ref[0, d * slots + k] = jnp.where(live, coords_ref[0, d, k], dead)
            out_ref[1, d * slots + k] = coords_ref[1, d, k]


def slot_blocks(coords, counts, dead):
    smem = pl.BlockSpec(memory_space=pltpu.SMEM)
    return pl.pallas_call(
        functools.partial(slots_kernel, dead),
        out_shape=jax.ShapeDtypeStruct((2, coords.shape[1] * coords.shape[2]), jnp.int32),
        in_specs=[smem, smem],
        out_specs=smem,
        compiler_params=pltpu.CompilerParams(vmem_limit_bytes=1024 * 1024),
        name="slot_blocks",
    )(coords, counts)


def offset_of(kind):
    _, _, p = place()
    even = (lax.axis_index("rows") // 2) % 2 == 0
    return {
        "self": 2,
        "near": jnp.where(p == 0, 3, 1),
        "far": jnp.where(p == 0, 1, 3),
        "direct": jnp.where(even, 4, 0),
        "second": jnp.where(even, 0, 4),
    }[kind]


def chosen(choice, read):
    value = read(choice[0][1])
    for case, ref in choice[1:]:
        value = jnp.where(when_of(case), read(ref), value)
    return value


def tile_kernel(kinds, cases, sets, summed, waits, *refs):
    refs = list(refs)
    metas = [[(case, refs.pop(0)) for case in each] for each in sets]
    tiles = [[(case, refs.pop(0)) for case in each] for each in sets]
    panels = [[(case, refs.pop(0)) for case in each] for each in cases]
    before = refs.pop(0) if summed else None
    out_ref, acc_ref = refs[waits:]
    _, slots, tile, _ = tiles[0][0][1].shape
    rows = out_ref.shape[0]
    if summed:
        acc_ref[:rows, :] = before[...]
    else:
        acc_ref[...] = jnp.zeros_like(acc_ref)
    for i, kind in enumerate(kinds):
        d = offset_of(kind)
        for s in range(len(sets)):
            for k in range(slots):
                row = chosen(metas[s], lambda ref: ref[0, d * slots + k])
                col = chosen(metas[s], lambda ref: ref[1, d * slots + k])
                row = pl.multiple_of(row * tile, tile)
                col = pl.multiple_of(col * tile, tile)
                acc_ref[pl.ds(row, tile), :] += jnp.dot(
                    chosen(tiles[s], lambda ref: ref[d, k]),
                    chosen(panels[i], lambda ref: ref[pl.ds(col, tile), :]),
                    preferred_element_type=jnp.float32,
                )
    out_ref[...] = acc_ref[:rows, :].astype(out_ref.dtype)


def tile_product(named, sets, dtype, before=None, after=(), weigh=1):
    kinds = [kind for kind, _ in named]
    cases = [[case for case, _ in choice] for _, choice in named]
    panels = [panel for _, choice in named for _, panel in choice]
    metas = [meta for choice in sets for _, (meta, _) in choice]
    tiles = [values for choice in sets for _, (_, values) in choice]
    rows, width = panels[0].shape if before is None else before.shape
    _, slots, tile, _ = tiles[0].shape
    smem = pl.BlockSpec(memory_space=pltpu.SMEM)
    vmem = pl.BlockSpec(memory_space=pltpu.VMEM)
    anywhere = pl.BlockSpec(memory_space=pl.ANY)
    count = len(kinds) * len(sets) * slots
    summed = before is not None
    return pl.pallas_call(
        functools.partial(
            tile_kernel,
            kinds,
            cases,
            [[case for case, _ in choice] for choice in sets],
            summed,
            len(after),
        ),
        out_shape=jax.ShapeDtypeStruct((rows, width), dtype),
        in_specs=[smem] * len(metas)
        + [vmem] * (len(tiles) + len(panels) + summed)
        + [anywhere] * len(after),
        out_specs=vmem,
        scratch_shapes=[pltpu.VMEM((rows + tile, width), jnp.float32)],
        compiler_params=pltpu.CompilerParams(vmem_limit_bytes=12 * 1024 * 1024),
        cost_estimate=pl.CostEstimate(
            flops=weigh * 2 * count * tile * tile * width,
            bytes_accessed=weigh * (count * tile * tile * 2 + len(kinds) * rows * width * 2),
            transcendentals=0,
        ),
        name="tile_product",
    )(*metas, *tiles, *panels, *([before] if summed else []), *after)


def middle_kernel(near_ref, far_ref, w_ref, cot_ref, cot_swap_ref, act_ref, *adj_refs):
    j, _, p = place()
    half = near_ref.shape[1]
    near = pl.multiple_of(j * half, half)
    far = pl.multiple_of((1 - j) * half, half)
    cols = pl.ds(near, half)
    agg = jnp.dot(
        near_ref[...], w_ref[pl.ds(near, half), cols], preferred_element_type=jnp.float32
    )
    agg += jnp.dot(far_ref[...], w_ref[pl.ds(far, half), cols], preferred_element_type=jnp.float32)
    sig = jax.nn.sigmoid(agg)
    act_ref[...] = (agg * sig).astype(act_ref.dtype)
    slope = sig * (1.0 + agg * (1.0 - sig))
    cot = jnp.where(j == p, cot_ref[...], cot_swap_ref[...])
    adj = (cot.astype(jnp.float32) * slope).astype(act_ref.dtype)
    rows = adj.shape[0]
    for ref in adj_refs:
        ref[:rows, :] = adj
        if ref.shape[0] > rows:
            ref[rows:, :] = jnp.zeros((ref.shape[0] - rows, ref.shape[1]), ref.dtype)


def middle(near, far, weight, cot, cot_swap):
    vmem = pl.BlockSpec(memory_space=pltpu.VMEM)
    rows, width = near.shape
    out = jax.ShapeDtypeStruct((rows, width), jnp.bfloat16)
    longer = tuple(jax.ShapeDtypeStruct((rows + n, width), jnp.bfloat16) for n in (32, 16))
    return pl.pallas_call(
        middle_kernel,
        out_shape=(out, out) + longer,
        in_specs=[vmem] * 5,
        out_specs=(vmem,) * 4,
        compiler_params=pltpu.CompilerParams(vmem_limit_bytes=8 * 1024 * 1024),
        cost_estimate=pl.CostEstimate(
            flops=4 * rows * width * width,
            bytes_accessed=10 * rows * width,
            transcendentals=rows * width,
        ),
        name="middle",
    )(near, far, weight, cot, cot_swap)


def grad_kernel(scale, near_ref, far_ref, adj_ref, after_ref, out_ref):
    j, _, _ = place()
    half = near_ref.shape[1]
    dims = (((0,), (0,)), ((), ()))
    for i, ref in enumerate((near_ref, far_ref)):
        start = pl.multiple_of((j if i == 0 else 1 - j) * half, half)
        block = lax.dot_general(ref[...], adj_ref[...], dims, preferred_element_type=jnp.float32)
        out_ref[pl.ds(start, half), :] = (scale * block).astype(out_ref.dtype)


def grad_block(scale, near, far, adj, after):
    vmem = pl.BlockSpec(memory_space=pltpu.VMEM)
    rows, width = near.shape
    return pl.pallas_call(
        functools.partial(grad_kernel, scale),
        out_shape=jax.ShapeDtypeStruct((2 * width, width), jnp.bfloat16),
        in_specs=[vmem] * 3 + [pl.BlockSpec(memory_space=pl.ANY)],
        out_specs=vmem,
        compiler_params=pltpu.CompilerParams(vmem_limit_bytes=8 * 1024 * 1024),
        cost_estimate=pl.CostEstimate(
            flops=4 * WEIGH * rows * width * width,
            bytes_accessed=8 * WEIGH * rows * width,
            transcendentals=0,
        ),
        name="grad_block",
    )(near, far, adj, after)


def add_kernel(count, *refs):
    values = [ref[...].astype(jnp.float32) for ref in refs[:count]]
    total = values[0] + values[1]
    if count == 4:
        total = total + (values[2] + values[3])
    refs[-1][...] = total.astype(refs[-1].dtype)


def add_after(values, dtype, *after):
    vmem = pl.BlockSpec(memory_space=pltpu.VMEM)
    return pl.pallas_call(
        functools.partial(add_kernel, len(values)),
        out_shape=jax.ShapeDtypeStruct(values[0].shape, dtype),
        in_specs=[vmem] * len(values) + [pl.BlockSpec(memory_space=pl.ANY)] * len(after),
        out_specs=vmem,
        compiler_params=pltpu.CompilerParams(vmem_limit_bytes=4 * 1024 * 1024),
        name="add_after",
    )(*values, *after)


def half_columns(half):
    j, _, _ = place()
    near = pl.ds(pl.multiple_of(j * half, half), half)
    return near, pl.ds(pl.multiple_of((1 - j) * half, half), half)


def near_and_far(parts):
    j, _, p = place()
    own, one, two = parts
    near = jnp.where(j == p, own[...], one[...])
    return near, jnp.where(j == p, one[...], two[...])


def gather_kernel(own_ref, one_ref, two_ref, grad_ref, rest_ref, act_ref, grad_out_ref):
    near_cols, far_cols = half_columns(own_ref.shape[1])
    near, far = near_and_far((own_ref, one_ref, two_ref))
    act_ref[:, near_cols] = near
    act_ref[:, far_cols] = far
    grad_out_ref[:, near_cols] = grad_ref[...]
    grad_out_ref[:, far_cols] = rest_ref[...]


def gather_halves(act, grad, rest):
    vmem = pl.BlockSpec(memory_space=pltpu.VMEM)
    rows, width = act[0].shape
    return pl.pallas_call(
        gather_kernel,
        out_shape=(
            jax.ShapeDtypeStruct((rows, 2 * width), act[0].dtype),
            jax.ShapeDtypeStruct((2 * width, 2 * width), grad.dtype),
        ),
        in_specs=[vmem] * 5,
        out_specs=(vmem, vmem),
        compiler_params=pltpu.CompilerParams(vmem_limit_bytes=8 * 1024 * 1024),
        name="gather_halves",
    )(*act, grad, rest)


def final_kernel(own_ref, one_ref, two_ref, w_ref, out_ref):
    near_cols, far_cols = half_columns(own_ref.shape[1])
    near, far = near_and_far((own_ref, one_ref, two_ref))
    dims = (((1,), (1,)), ((), ()))
    total = lax.dot_general(near, w_ref[:, near_cols], dims, preferred_element_type=jnp.float32)
    total += lax.dot_general(far, w_ref[:, far_cols], dims, preferred_element_type=jnp.float32)
    out_ref[...] = total.astype(out_ref.dtype)


def final(back, weight):
    vmem = pl.BlockSpec(memory_space=pltpu.VMEM)
    rows = back[0].shape[0]
    wide = weight.shape[0]
    return pl.pallas_call(
        final_kernel,
        out_shape=jax.ShapeDtypeStruct((rows, wide), jnp.bfloat16),
        in_specs=[vmem] * 4,
        out_specs=vmem,
        compiler_params=pltpu.CompilerParams(vmem_limit_bytes=8 * 1024 * 1024),
        cost_estimate=pl.CostEstimate(
            flops=2 * rows * wide * wide, bytes_accessed=8 * rows * wide, transcendentals=0
        ),
        name="final",
    )(*back, weight)


def per_device(node_feats, weight, cotangent, tile_values, tile_coords, tile_counts):
    groups = lax.axis_size("rows")
    reps = lax.axis_size("rep")
    shape = (groups // 2, reps)
    j, z, p = place()
    home = j == p
    scale = (node_feats.shape[0] * groups) ** (-0.5)

    def send(value, move):
        return lax.ppermute(value, AXES, route(shape, move))

    def sibling(c, j, z):
        return (c, 1 - j, z)

    def home_to_sibling(c, j, z):
        return (c, 1 - j, z) if j == z % 2 else None

    def across(c, j, z):
        return (c, j, (z + reps // 2) % reps)

    own = tile_values[0]
    blocks = node_feats.shape[0] // own.shape[-1]

    def to_home(c, j, z):
        return (c, 1 - j, z) if j == z % 2 else (c, j, z ^ 1)

    four = shape[0] == 4

    def to_direct(c, j, z):
        return (c ^ 1, j, z)

    def to_second(c, j, z):
        return (c ^ 2, j, z) if four else (c + 1 if c % 2 else c - 1, j, z)

    def to_far(c, j, z):
        return (c ^ 1, j, z) if four else (c - 1 if z % 2 else c + 1, j, z)

    def stage_one(c, j, z):
        if j == z % 2:
            return (c ^ 1, j, z)
        return (c ^ 2, j, z) if four and (c + z) % 2 else None

    def stage_one_cross(c, j, z):
        to = stage_one(c, j, z)
        return to and (to[0], 1 - j, z)

    first = send(own, to_home)
    half = node_feats.shape[1] // 2
    mine = lax.dynamic_slice_in_dim(node_feats, j * half, half, 1)
    yours = lax.dynamic_slice_in_dim(node_feats, (1 - j) * half, half, 1)
    one = send(mine, stage_one)
    two = send(yours, stage_one_cross)
    swapped = send(yours, sibling)
    self_choice = [("home", mine), ("away", swapped)]
    direct_choice = [("home", one), ("away", two)]
    meta = slot_blocks(tile_coords[:, 0], tile_counts[0], blocks)
    second, far = pick(
        [
            direct_choice if four else self_choice,
            [
                ("still home", swapped),
                ("still away", mine),
                ("relay home", two),
                ("relay away", one),
            ],
        ],
        [meta],
    )
    second = send(second, to_second)
    far = send(far, to_far)
    meta_b = send(meta, to_home)
    first, meta_b = lax.optimization_barrier((first, meta_b))
    other_first = send(first, home_to_sibling)
    meta_later, second = lax.optimization_barrier((meta_b, second))
    meta_far = send(meta_later, home_to_sibling)
    set_first = [(None, (meta_b, first))]
    panels = [
        ("self", [("home", mine), ("away", swapped)]),
        ("near", [("home", swapped), ("away", mine)]),
        ("direct", direct_choice),
        ("second", [(None, second)]),
        ("far", [(None, far)]),
    ]
    part = tile_product(panels, [set_first], jnp.float32, weigh=WEIGH)
    set_rest = [("home", (meta, own)), ("away", (meta_far, other_first))]
    part = tile_product(panels, [set_rest], jnp.bfloat16, part)

    def join(value):
        other = send(value, across)
        return (value.astype(jnp.float32) + other.astype(jnp.float32)).astype(jnp.bfloat16)

    near = join(part)
    far_half = send(near, sibling)
    cot, cot_yours = halves(cotangent)
    act, adj, adj_longer, adj_long = middle(
        near, far_half, weight, cot, send(cot_yours, sibling)
    )

    direct = send(adj_longer, to_direct)
    near_one = send(
        adj_long, lambda c, j, z: (c if (c + z) % 2 or not four else c ^ 2, j, z ^ 1)
    )
    adj_later, near_one, direct = lax.optimization_barrier((adj, near_one, direct))
    second = send(direct if four else adj_longer, to_second)
    grad = grad_block(scale, near, far_half, adj, direct)
    adj_later, grad = lax.optimization_barrier((adj_later, grad))
    far = send(near_one, to_far)
    near_choice = [("still", near_one)]
    if four:
        near_two = send(
            adj_later, lambda c, j, z: None if (c + z) % 2 else (c, j, z ^ 1)
        )
        near_choice.append(("relay", near_two))
    grad_got = send(grad, lambda c, j, z: (c, j, z ^ 1))
    panels = [("self", [(None, adj)]), ("direct", [(None, direct)])]
    back_part = tile_product(panels, [set_first, set_rest], jnp.float32)
    panels = [("second", [(None, second)]), ("far", [(None, far)]), ("near", near_choice)]
    back_part = tile_product(
        panels, [set_first, set_rest], jnp.bfloat16, back_part, [grad_got]
    )

    def deliver(value):
        one = send(value, lambda c, j, z: (c, j, z ^ 1) if j == z % 2 else (c, 1 - j, z))
        two = send(value, lambda c, j, z: None if j == z % 2 else (c, 1 - j, z ^ 1))
        return one, two

    act_later, back_part = lax.optimization_barrier((act, back_part))
    act_parts = [act, *deliver(act_later)]
    grad = add_after([grad, grad_got], jnp.bfloat16, back_part)
    step = 1
    while step < shape[0]:
        got = send(grad, lambda c, j, z, s=step: (c ^ s, j, z))
        step *= 2
        if step < shape[0]:
            grad = add_after([grad, got], jnp.bfloat16)
    back = add_after([back_part, send(back_part, across)], jnp.bfloat16, got)
    back_parts = [back, *deliver(back)]
    grad = add_after([grad, got], jnp.float32, back, *act_parts[1:])
    activated, weight_grad = gather_halves(act_parts, grad, send(grad, sibling))
    input_grad = final(back_parts, weight)
    return (activated, input_grad, weight_grad)


def solution(mesh):
    return jax.shard_map(
        per_device,
        mesh=mesh,
        in_specs=(
            P("rows", None),
            P(),
            P("rows", None),
            P("rows", None, "rep", None, None),
            P(None, "rows", None, "rep"),
            P("rows", None),
        ),
        out_specs=(P("rows", None), P("rows", None), P()),
        check_vma=False,
    )
```

```python
import functools

import jax
import jax.numpy as jnp
from jax import lax
from jax.experimental import pallas as pl
from jax.experimental.pallas import tpu as pltpu
from jax.sharding import PartitionSpec as P

AXES = ("rows", "rep")
WEIGH = 75


def route(shape, move):
    chips, reps = shape
    pairs = []
    for c in range(chips):
        for j in range(2):
            for z in range(reps):
                to = move(c, j, z)
                if to is not None:
                    target = ((to[0] % chips) * 2 + to[1]) * reps + to[2]
                    pairs.append(((c * 2 + j) * reps + z, target))
    return pairs


def place():
    r = lax.axis_index("rows")
    z = lax.axis_index("rep")
    return r % 2, z, z % 2


def when_of(case):
    j, z, p = place()
    home = j == p
    relay = jnp.logical_and(
        lax.axis_size("rows") == 8, (lax.axis_index("rows") // 2 + z) % 2 == 1
    )
    return {
        "home": home,
        "away": jnp.logical_not(home),
        "relay": relay,
        "still": jnp.logical_not(relay),
        "relay home": jnp.logical_and(relay, home),
        "relay away": jnp.logical_and(relay, jnp.logical_not(home)),
        "still home": jnp.logical_and(jnp.logical_not(relay), home),
        "still away": jnp.logical_and(jnp.logical_not(relay), jnp.logical_not(home)),
    }[case]


def start_chosen(choice, make):
    if len(choice) == 1:
        make(choice[0][1]).start()
        return
    for case, ref in choice:

        @pl.when(when_of(case))
        def _(ref=ref):
            make(ref).start()


def halves_kernel(x_ref, near_ref, far_ref, sems):
    j, _, _ = place()
    half = near_ref.shape[1]
    copies = []
    for i, out in enumerate((near_ref, far_ref)):
        start = pl.multiple_of((j if i == 0 else 1 - j) * half, half)
        copy = pltpu.make_async_copy(x_ref.at[:, pl.ds(start, half)], out, sems.at[i])
        copy.start()
        copies.append(copy)
    for copy in copies:
        copy.wait()


def halves(value):
    rows, width = value.shape
    part = jax.ShapeDtypeStruct((rows, width // 2), value.dtype)
    hbm = pl.BlockSpec(memory_space=pltpu.HBM)
    return pl.pallas_call(
        halves_kernel,
        out_shape=(part, part),
        in_specs=[hbm],
        out_specs=(hbm, hbm),
        scratch_shapes=[pltpu.SemaphoreType.DMA((2,))],
        compiler_params=pltpu.CompilerParams(vmem_limit_bytes=1024 * 1024),
        name="halves",
    )(value)


def pick_kernel(cases, waits, *refs):
    refs = list(refs)
    choices = [[(case, refs.pop(0)) for case in each] for each in cases]
    outs, sems = refs[waits:-1], refs[-1]

    def copy_to(i):
        return lambda ref: pltpu.make_async_copy(ref, outs[i], sems.at[i])

    for i, choice in enumerate(choices):
        start_chosen(choice, copy_to(i))
    for i, choice in enumerate(choices):
        copy_to(i)(choice[0][1]).wait()


def pick(choices, after):
    hbm = pl.BlockSpec(memory_space=pltpu.HBM)
    arrays = [array for choice in choices for _, array in choice]
    shape = jax.ShapeDtypeStruct(arrays[0].shape, arrays[0].dtype)
    return pl.pallas_call(
        functools.partial(
            pick_kernel, [[case for case, _ in choice] for choice in choices], len(after)
        ),
        out_shape=(shape,) * len(choices),
        in_specs=[hbm] * len(arrays) + [pl.BlockSpec(memory_space=pl.ANY)] * len(after),
        out_specs=(hbm,) * len(choices),
        scratch_shapes=[pltpu.SemaphoreType.DMA((len(choices),))],
        compiler_params=pltpu.CompilerParams(vmem_limit_bytes=1024 * 1024),
        name="pick",
    )(*arrays, *after)


def slots_kernel(dead, coords_ref, counts_ref, out_ref):
    _, z, _ = place()
    _, reach, slots = coords_ref.shape
    for d in range(reach):
        for k in range(slots):
            live = z * slots + k < counts_ref[d]
            out_ref[0, d * slots + k] = jnp.where(live, coords_ref[0, d, k], dead)
            out_ref[1, d * slots + k] = coords_ref[1, d, k]


def slot_blocks(coords, counts, dead):
    smem = pl.BlockSpec(memory_space=pltpu.SMEM)
    return pl.pallas_call(
        functools.partial(slots_kernel, dead),
        out_shape=jax.ShapeDtypeStruct((2, coords.shape[1] * coords.shape[2]), jnp.int32),
        in_specs=[smem, smem],
        out_specs=smem,
        compiler_params=pltpu.CompilerParams(vmem_limit_bytes=1024 * 1024),
        name="slot_blocks",
    )(coords, counts)


def offset_of(kind):
    _, _, p = place()
    even = (lax.axis_index("rows") // 2) % 2 == 0
    return {
        "self": 2,
        "near": jnp.where(p == 0, 3, 1),
        "far": jnp.where(p == 0, 1, 3),
        "direct": jnp.where(even, 4, 0),
        "second": jnp.where(even, 0, 4),
    }[kind]


def chosen(choice, read):
    value = read(choice[0][1])
    for case, ref in choice[1:]:
        value = jnp.where(when_of(case), read(ref), value)
    return value


def tile_kernel(kinds, cases, sets, summed, waits, *refs):
    refs = list(refs)
    metas = [[(case, refs.pop(0)) for case in each] for each in sets]
    tiles = [[(case, refs.pop(0)) for case in each] for each in sets]
    panels = [[(case, refs.pop(0)) for case in each] for each in cases]
    before = refs.pop(0) if summed else None
    out_ref, acc_ref = refs[waits:]
    _, slots, tile, _ = tiles[0][0][1].shape
    rows = out_ref.shape[0]
    if summed:
        acc_ref[:rows, :] = before[...]
    else:
        acc_ref[...] = jnp.zeros_like(acc_ref)
    for i, kind in enumerate(kinds):
        d = offset_of(kind)
        for s in range(len(sets)):
            for k in range(slots):
                row = chosen(metas[s], lambda ref: ref[0, d * slots + k])
                col = chosen(metas[s], lambda ref: ref[1, d * slots + k])
                row = pl.multiple_of(row * tile, tile)
                col = pl.multiple_of(col * tile, tile)
                acc_ref[pl.ds(row, tile), :] += jnp.dot(
                    chosen(tiles[s], lambda ref: ref[d, k]),
                    chosen(panels[i], lambda ref: ref[pl.ds(col, tile), :]),
                    preferred_element_type=jnp.float32,
                )
    out_ref[...] = acc_ref[:rows, :].astype(out_ref.dtype)


def tile_product(named, sets, dtype, before=None, after=(), weigh=1):
    kinds = [kind for kind, _ in named]
    cases = [[case for case, _ in choice] for _, choice in named]
    panels = [panel for _, choice in named for _, panel in choice]
    metas = [meta for choice in sets for _, (meta, _) in choice]
    tiles = [values for choice in sets for _, (_, values) in choice]
    rows, width = panels[0].shape if before is None else before.shape
    _, slots, tile, _ = tiles[0].shape
    smem = pl.BlockSpec(memory_space=pltpu.SMEM)
    vmem = pl.BlockSpec(memory_space=pltpu.VMEM)
    anywhere = pl.BlockSpec(memory_space=pl.ANY)
    count = len(kinds) * len(sets) * slots
    summed = before is not None
    return pl.pallas_call(
        functools.partial(
            tile_kernel,
            kinds,
            cases,
            [[case for case, _ in choice] for choice in sets],
            summed,
            len(after),
        ),
        out_shape=jax.ShapeDtypeStruct((rows, width), dtype),
        in_specs=[smem] * len(metas)
        + [vmem] * (len(tiles) + len(panels) + summed)
        + [anywhere] * len(after),
        out_specs=vmem,
        scratch_shapes=[pltpu.VMEM((rows + tile, width), jnp.float32)],
        compiler_params=pltpu.CompilerParams(vmem_limit_bytes=12 * 1024 * 1024),
        cost_estimate=pl.CostEstimate(
            flops=weigh * 2 * count * tile * tile * width,
            bytes_accessed=weigh * (count * tile * tile * 2 + len(kinds) * rows * width * 2),
            transcendentals=0,
        ),
        name="tile_product",
    )(*metas, *tiles, *panels, *([before] if summed else []), *after)


def middle_kernel(near_ref, far_ref, w_ref, cot_ref, cot_swap_ref, act_ref, *adj_refs):
    j, _, p = place()
    half = near_ref.shape[1]
    near = pl.multiple_of(j * half, half)
    far = pl.multiple_of((1 - j) * half, half)
    cols = pl.ds(near, half)
    agg = jnp.dot(
        near_ref[...], w_ref[pl.ds(near, half), cols], preferred_element_type=jnp.float32
    )
    agg += jnp.dot(far_ref[...], w_ref[pl.ds(far, half), cols], preferred_element_type=jnp.float32)
    sig = jax.nn.sigmoid(agg)
    act_ref[...] = (agg * sig).astype(act_ref.dtype)
    slope = sig * (1.0 + agg * (1.0 - sig))
    cot = jnp.where(j == p, cot_ref[...], cot_swap_ref[...])
    adj = (cot.astype(jnp.float32) * slope).astype(act_ref.dtype)
    rows = adj.shape[0]
    for ref in adj_refs:
        ref[:rows, :] = adj
        if ref.shape[0] > rows:
            ref[rows:, :] = jnp.zeros((ref.shape[0] - rows, ref.shape[1]), ref.dtype)


def middle(near, far, weight, cot, cot_swap):
    vmem = pl.BlockSpec(memory_space=pltpu.VMEM)
    rows, width = near.shape
    out = jax.ShapeDtypeStruct((rows, width), jnp.bfloat16)
    longer = tuple(jax.ShapeDtypeStruct((rows + n, width), jnp.bfloat16) for n in (32, 16))
    return pl.pallas_call(
        middle_kernel,
        out_shape=(out, out) + longer,
        in_specs=[vmem] * 5,
        out_specs=(vmem,) * 4,
        compiler_params=pltpu.CompilerParams(vmem_limit_bytes=8 * 1024 * 1024),
        cost_estimate=pl.CostEstimate(
            flops=4 * rows * width * width,
            bytes_accessed=10 * rows * width,
            transcendentals=rows * width,
        ),
        name="middle",
    )(near, far, weight, cot, cot_swap)


def grad_kernel(scale, near_ref, far_ref, adj_ref, out_ref):
    j, _, _ = place()
    half = near_ref.shape[1]
    dims = (((0,), (0,)), ((), ()))
    for i, ref in enumerate((near_ref, far_ref)):
        start = pl.multiple_of((j if i == 0 else 1 - j) * half, half)
        block = lax.dot_general(ref[...], adj_ref[...], dims, preferred_element_type=jnp.float32)
        out_ref[pl.ds(start, half), :] = (scale * block).astype(out_ref.dtype)


def grad_block(scale, near, far, adj):
    vmem = pl.BlockSpec(memory_space=pltpu.VMEM)
    rows, width = near.shape
    return pl.pallas_call(
        functools.partial(grad_kernel, scale),
        out_shape=jax.ShapeDtypeStruct((2 * width, width), jnp.bfloat16),
        in_specs=[vmem] * 3,
        out_specs=vmem,
        compiler_params=pltpu.CompilerParams(vmem_limit_bytes=8 * 1024 * 1024),
        cost_estimate=pl.CostEstimate(
            flops=4 * WEIGH * rows * width * width,
            bytes_accessed=8 * WEIGH * rows * width,
            transcendentals=0,
        ),
        name="grad_block",
    )(near, far, adj)


def add_kernel(count, *refs):
    values = [ref[...].astype(jnp.float32) for ref in refs[:count]]
    total = values[0] + values[1]
    if count == 4:
        total = total + (values[2] + values[3])
    refs[-1][...] = total.astype(refs[-1].dtype)


def add_after(values, dtype, *after):
    vmem = pl.BlockSpec(memory_space=pltpu.VMEM)
    return pl.pallas_call(
        functools.partial(add_kernel, len(values)),
        out_shape=jax.ShapeDtypeStruct(values[0].shape, dtype),
        in_specs=[vmem] * len(values) + [pl.BlockSpec(memory_space=pl.ANY)] * len(after),
        out_specs=vmem,
        compiler_params=pltpu.CompilerParams(vmem_limit_bytes=4 * 1024 * 1024),
        name="add_after",
    )(*values, *after)


def half_columns(half):
    j, _, _ = place()
    near = pl.ds(pl.multiple_of(j * half, half), half)
    return near, pl.ds(pl.multiple_of((1 - j) * half, half), half)


def near_and_far(parts):
    j, _, p = place()
    own, one, two = parts
    near = jnp.where(j == p, own[...], one[...])
    return near, jnp.where(j == p, one[...], two[...])


def gather_kernel(own_ref, one_ref, two_ref, grad_ref, rest_ref, act_ref, grad_out_ref):
    near_cols, far_cols = half_columns(own_ref.shape[1])
    near, far = near_and_far((own_ref, one_ref, two_ref))
    act_ref[:, near_cols] = near
    act_ref[:, far_cols] = far
    grad_out_ref[:, near_cols] = grad_ref[...]
    grad_out_ref[:, far_cols] = rest_ref[...]


def gather_halves(act, grad, rest):
    vmem = pl.BlockSpec(memory_space=pltpu.VMEM)
    rows, width = act[0].shape
    return pl.pallas_call(
        gather_kernel,
        out_shape=(
            jax.ShapeDtypeStruct((rows, 2 * width), act[0].dtype),
            jax.ShapeDtypeStruct((2 * width, 2 * width), grad.dtype),
        ),
        in_specs=[vmem] * 5,
        out_specs=(vmem, vmem),
        compiler_params=pltpu.CompilerParams(vmem_limit_bytes=8 * 1024 * 1024),
        name="gather_halves",
    )(*act, grad, rest)


def final_kernel(own_ref, one_ref, two_ref, w_ref, out_ref):
    near_cols, far_cols = half_columns(own_ref.shape[1])
    near, far = near_and_far((own_ref, one_ref, two_ref))
    dims = (((1,), (1,)), ((), ()))
    total = lax.dot_general(near, w_ref[:, near_cols], dims, preferred_element_type=jnp.float32)
    total += lax.dot_general(far, w_ref[:, far_cols], dims, preferred_element_type=jnp.float32)
    out_ref[...] = total.astype(out_ref.dtype)


def final(back, weight):
    vmem = pl.BlockSpec(memory_space=pltpu.VMEM)
    rows = back[0].shape[0]
    wide = weight.shape[0]
    return pl.pallas_call(
        final_kernel,
        out_shape=jax.ShapeDtypeStruct((rows, wide), jnp.bfloat16),
        in_specs=[vmem] * 4,
        out_specs=vmem,
        compiler_params=pltpu.CompilerParams(vmem_limit_bytes=8 * 1024 * 1024),
        cost_estimate=pl.CostEstimate(
            flops=2 * rows * wide * wide, bytes_accessed=8 * rows * wide, transcendentals=0
        ),
        name="final",
    )(*back, weight)


def per_device(node_feats, weight, cotangent, tile_values, tile_coords, tile_counts):
    groups = lax.axis_size("rows")
    reps = lax.axis_size("rep")
    shape = (groups // 2, reps)
    j, z, p = place()
    home = j == p
    scale = (node_feats.shape[0] * groups) ** (-0.5)

    def send(value, move):
        return lax.ppermute(value, AXES, route(shape, move))

    def sibling(c, j, z):
        return (c, 1 - j, z)

    def home_to_sibling(c, j, z):
        return (c, 1 - j, z) if j == z % 2 else None

    def across(c, j, z):
        return (c, j, (z + reps // 2) % reps)

    own = tile_values[0]
    blocks = node_feats.shape[0] // own.shape[-1]

    def to_home(c, j, z):
        return (c, 1 - j, z) if j == z % 2 else (c, j, z ^ 1)

    four = shape[0] == 4

    def to_direct(c, j, z):
        return (c ^ 1, j, z)

    def to_second(c, j, z):
        return (c ^ 2, j, z) if four else (c + 1 if c % 2 else c - 1, j, z)

    def to_far(c, j, z):
        return (c ^ 1, j, z) if four else (c - 1 if z % 2 else c + 1, j, z)

    def stage_one(c, j, z):
        if j == z % 2:
            return (c ^ 1, j, z)
        return (c ^ 2, j, z) if four and (c + z) % 2 else None

    def stage_one_cross(c, j, z):
        to = stage_one(c, j, z)
        return to and (to[0], 1 - j, z)

    first = send(own, to_home)
    half = node_feats.shape[1] // 2
    mine = lax.dynamic_slice_in_dim(node_feats, j * half, half, 1)
    yours = lax.dynamic_slice_in_dim(node_feats, (1 - j) * half, half, 1)
    one = send(mine, stage_one)
    two = send(yours, stage_one_cross)
    swapped = send(yours, sibling)
    self_choice = [("home", mine), ("away", swapped)]
    direct_choice = [("home", one), ("away", two)]
    meta = slot_blocks(tile_coords[:, 0], tile_counts[0], blocks)
    second, far = pick(
        [
            direct_choice if four else self_choice,
            [
                ("still home", swapped),
                ("still away", mine),
                ("relay home", two),
                ("relay away", one),
            ],
        ],
        [meta],
    )
    second = send(second, to_second)
    far = send(far, to_far)
    meta_b = send(meta, to_home)
    first, meta_b = lax.optimization_barrier((first, meta_b))
    other_first = send(first, home_to_sibling)
    meta_later, second = lax.optimization_barrier((meta_b, second))
    meta_far = send(meta_later, home_to_sibling)
    set_first = [(None, (meta_b, first))]
    panels = [
        ("self", [("home", mine), ("away", swapped)]),
        ("near", [("home", swapped), ("away", mine)]),
        ("direct", direct_choice),
        ("second", [(None, second)]),
        ("far", [(None, far)]),
    ]
    part = tile_product(panels, [set_first], jnp.float32, weigh=WEIGH)
    set_rest = [("home", (meta, own)), ("away", (meta_far, other_first))]
    part = tile_product(panels, [set_rest], jnp.bfloat16, part)

    def join(value):
        other = send(value, across)
        return (value.astype(jnp.float32) + other.astype(jnp.float32)).astype(jnp.bfloat16)

    near = join(part)
    far_half = send(near, sibling)
    cot, cot_yours = halves(cotangent)
    act, adj, adj_longer, adj_long = middle(
        near, far_half, weight, cot, send(cot_yours, sibling)
    )

    direct = send(adj_longer, to_direct)
    near_one = send(
        adj_long, lambda c, j, z: (c if (c + z) % 2 or not four else c ^ 2, j, z ^ 1)
    )
    second = send(direct if four else adj_longer, to_second)
    grad = grad_block(scale, near, far_half, adj)
    grad_got = send(grad, lambda c, j, z: (c, j, z ^ 1))
    adj_later, grad_got = lax.optimization_barrier((adj, grad_got))
    far = send(near_one, to_far)
    near_choice = [("still", near_one)]
    if four:
        near_two = send(
            adj_later, lambda c, j, z: None if (c + z) % 2 else (c, j, z ^ 1)
        )
        near_choice.append(("relay", near_two))
    panels = [("self", [(None, adj)]), ("direct", [(None, direct)])]
    back_part = tile_product(panels, [set_first, set_rest], jnp.float32)
    panels = [("second", [(None, second)]), ("far", [(None, far)]), ("near", near_choice)]
    back_part = tile_product(panels, [set_first, set_rest], jnp.bfloat16, back_part)

    def deliver(value):
        one = send(value, lambda c, j, z: (c, j, z ^ 1) if j == z % 2 else (c, 1 - j, z))
        two = send(value, lambda c, j, z: None if j == z % 2 else (c, 1 - j, z ^ 1))
        return one, two

    act_later, back_part = lax.optimization_barrier((act, back_part))
    act_parts = [act, *deliver(act_later)]
    grad = add_after([grad, grad_got], jnp.bfloat16, back_part)
    step = 1
    while step < shape[0]:
        got = send(grad, lambda c, j, z, s=step: (c ^ s, j, z))
        step *= 2
        if step < shape[0]:
            grad = add_after([grad, got], jnp.bfloat16)
    back = add_after([back_part, send(back_part, across)], jnp.bfloat16, got)
    back_parts = [back, *deliver(back)]
    grad = add_after([grad, got], jnp.float32, back, *act_parts[1:])
    activated, weight_grad = gather_halves(act_parts, grad, send(grad, sibling))
    input_grad = final(back_parts, weight)
    return (activated, input_grad, weight_grad)


def solution(mesh):
    return jax.shard_map(
        per_device,
        mesh=mesh,
        in_specs=(
            P("rows", None),
            P(),
            P("rows", None),
            P("rows", None, "rep", None, None),
            P(None, "rows", None, "rep"),
            P("rows", None),
        ),
        out_specs=(P("rows", None), P("rows", None), P()),
        check_vma=False,
    )
```

```python
import functools

import jax
import jax.numpy as jnp
from jax import lax
from jax.experimental import pallas as pl
from jax.experimental.pallas import tpu as pltpu
from jax.sharding import PartitionSpec as P

AXES = ("rows", "rep")
WEIGH = 75


def route(shape, move):
    chips, reps = shape
    pairs = []
    for c in range(chips):
        for j in range(2):
            for z in range(reps):
                to = move(c, j, z)
                if to is not None:
                    target = ((to[0] % chips) * 2 + to[1]) * reps + to[2]
                    pairs.append(((c * 2 + j) * reps + z, target))
    return pairs


def place():
    r = lax.axis_index("rows")
    z = lax.axis_index("rep")
    return r % 2, z, z % 2


def when_of(case):
    j, z, p = place()
    home = j == p
    relay = jnp.logical_and(
        lax.axis_size("rows") == 8, (lax.axis_index("rows") // 2 + z) % 2 == 1
    )
    return {
        "home": home,
        "away": jnp.logical_not(home),
        "relay": relay,
        "still": jnp.logical_not(relay),
        "relay home": jnp.logical_and(relay, home),
        "relay away": jnp.logical_and(relay, jnp.logical_not(home)),
        "still home": jnp.logical_and(jnp.logical_not(relay), home),
        "still away": jnp.logical_and(jnp.logical_not(relay), jnp.logical_not(home)),
    }[case]


def start_chosen(choice, make):
    if len(choice) == 1:
        make(choice[0][1]).start()
        return
    for case, ref in choice:

        @pl.when(when_of(case))
        def _(ref=ref):
            make(ref).start()


def halves_kernel(x_ref, near_ref, far_ref, sems):
    j, _, _ = place()
    half = near_ref.shape[1]
    copies = []
    for i, out in enumerate((near_ref, far_ref)):
        start = pl.multiple_of((j if i == 0 else 1 - j) * half, half)
        copy = pltpu.make_async_copy(x_ref.at[:, pl.ds(start, half)], out, sems.at[i])
        copy.start()
        copies.append(copy)
    for copy in copies:
        copy.wait()


def halves(value):
    rows, width = value.shape
    part = jax.ShapeDtypeStruct((rows, width // 2), value.dtype)
    hbm = pl.BlockSpec(memory_space=pltpu.HBM)
    return pl.pallas_call(
        halves_kernel,
        out_shape=(part, part),
        in_specs=[hbm],
        out_specs=(hbm, hbm),
        scratch_shapes=[pltpu.SemaphoreType.DMA((2,))],
        compiler_params=pltpu.CompilerParams(vmem_limit_bytes=1024 * 1024),
        name="halves",
    )(value)


def pick_kernel(cases, waits, *refs):
    refs = list(refs)
    choices = [[(case, refs.pop(0)) for case in each] for each in cases]
    outs, sems = refs[waits:-1], refs[-1]

    def copy_to(i):
        return lambda ref: pltpu.make_async_copy(ref, outs[i], sems.at[i])

    for i, choice in enumerate(choices):
        start_chosen(choice, copy_to(i))
    for i, choice in enumerate(choices):
        copy_to(i)(choice[0][1]).wait()


def pick(choices, after):
    hbm = pl.BlockSpec(memory_space=pltpu.HBM)
    arrays = [array for choice in choices for _, array in choice]
    shape = jax.ShapeDtypeStruct(arrays[0].shape, arrays[0].dtype)
    return pl.pallas_call(
        functools.partial(
            pick_kernel, [[case for case, _ in choice] for choice in choices], len(after)
        ),
        out_shape=(shape,) * len(choices),
        in_specs=[hbm] * len(arrays) + [pl.BlockSpec(memory_space=pl.ANY)] * len(after),
        out_specs=(hbm,) * len(choices),
        scratch_shapes=[pltpu.SemaphoreType.DMA((len(choices),))],
        compiler_params=pltpu.CompilerParams(vmem_limit_bytes=1024 * 1024),
        name="pick",
    )(*arrays, *after)


def slots_kernel(dead, coords_ref, counts_ref, out_ref):
    _, z, _ = place()
    _, reach, slots = coords_ref.shape
    for d in range(reach):
        for k in range(slots):
            live = z * slots + k < counts_ref[d]
            out_ref[0, d * slots + k] = jnp.where(live, coords_ref[0, d, k], dead)
            out_ref[1, d * slots + k] = coords_ref[1, d, k]


def slot_blocks(coords, counts, dead):
    smem = pl.BlockSpec(memory_space=pltpu.SMEM)
    return pl.pallas_call(
        functools.partial(slots_kernel, dead),
        out_shape=jax.ShapeDtypeStruct((2, coords.shape[1] * coords.shape[2]), jnp.int32),
        in_specs=[smem, smem],
        out_specs=smem,
        compiler_params=pltpu.CompilerParams(vmem_limit_bytes=1024 * 1024),
        name="slot_blocks",
    )(coords, counts)


def offset_of(kind):
    _, _, p = place()
    even = (lax.axis_index("rows") // 2) % 2 == 0
    return {
        "self": 2,
        "near": jnp.where(p == 0, 3, 1),
        "far": jnp.where(p == 0, 1, 3),
        "direct": jnp.where(even, 4, 0),
        "second": jnp.where(even, 0, 4),
    }[kind]


def chosen(choice, read):
    value = read(choice[0][1])
    for case, ref in choice[1:]:
        value = jnp.where(when_of(case), read(ref), value)
    return value


def tile_kernel(kinds, cases, sets, summed, waits, *refs):
    refs = list(refs)
    metas = [[(case, refs.pop(0)) for case in each] for each in sets]
    tiles = [[(case, refs.pop(0)) for case in each] for each in sets]
    panels = [[(case, refs.pop(0)) for case in each] for each in cases]
    before = refs.pop(0) if summed else None
    out_ref, acc_ref = refs[waits:]
    _, slots, tile, _ = tiles[0][0][1].shape
    rows = out_ref.shape[0]
    if summed:
        acc_ref[:rows, :] = before[...]
    else:
        acc_ref[...] = jnp.zeros_like(acc_ref)
    for i, kind in enumerate(kinds):
        d = offset_of(kind)
        for s in range(len(sets)):
            for k in range(slots):
                row = chosen(metas[s], lambda ref: ref[0, d * slots + k])
                col = chosen(metas[s], lambda ref: ref[1, d * slots + k])
                row = pl.multiple_of(row * tile, tile)
                col = pl.multiple_of(col * tile, tile)
                acc_ref[pl.ds(row, tile), :] += jnp.dot(
                    chosen(tiles[s], lambda ref: ref[d, k]),
                    chosen(panels[i], lambda ref: ref[pl.ds(col, tile), :]),
                    preferred_element_type=jnp.float32,
                )
    out_ref[...] = acc_ref[:rows, :].astype(out_ref.dtype)


def tile_product(named, sets, dtype, before=None, after=(), weigh=1):
    kinds = [kind for kind, _ in named]
    cases = [[case for case, _ in choice] for _, choice in named]
    panels = [panel for _, choice in named for _, panel in choice]
    metas = [meta for choice in sets for _, (meta, _) in choice]
    tiles = [values for choice in sets for _, (_, values) in choice]
    rows, width = panels[0].shape if before is None else before.shape
    _, slots, tile, _ = tiles[0].shape
    smem = pl.BlockSpec(memory_space=pltpu.SMEM)
    vmem = pl.BlockSpec(memory_space=pltpu.VMEM)
    anywhere = pl.BlockSpec(memory_space=pl.ANY)
    count = len(kinds) * len(sets) * slots
    summed = before is not None
    return pl.pallas_call(
        functools.partial(
            tile_kernel,
            kinds,
            cases,
            [[case for case, _ in choice] for choice in sets],
            summed,
            len(after),
        ),
        out_shape=jax.ShapeDtypeStruct((rows, width), dtype),
        in_specs=[smem] * len(metas)
        + [vmem] * (len(tiles) + len(panels) + summed)
        + [anywhere] * len(after),
        out_specs=vmem,
        scratch_shapes=[pltpu.VMEM((rows + tile, width), jnp.float32)],
        compiler_params=pltpu.CompilerParams(vmem_limit_bytes=12 * 1024 * 1024),
        cost_estimate=pl.CostEstimate(
            flops=weigh * 2 * count * tile * tile * width,
            bytes_accessed=weigh * (count * tile * tile * 2 + len(kinds) * rows * width * 2),
            transcendentals=0,
        ),
        name="tile_product",
    )(*metas, *tiles, *panels, *([before] if summed else []), *after)


def middle_kernel(near_ref, far_ref, w_ref, cot_ref, cot_swap_ref, act_ref, *adj_refs):
    j, _, p = place()
    half = near_ref.shape[1]
    near = pl.multiple_of(j * half, half)
    far = pl.multiple_of((1 - j) * half, half)
    cols = pl.ds(near, half)
    agg = jnp.dot(
        near_ref[...], w_ref[pl.ds(near, half), cols], preferred_element_type=jnp.float32
    )
    agg += jnp.dot(far_ref[...], w_ref[pl.ds(far, half), cols], preferred_element_type=jnp.float32)
    sig = jax.nn.sigmoid(agg)
    act_ref[...] = (agg * sig).astype(act_ref.dtype)
    slope = sig * (1.0 + agg * (1.0 - sig))
    cot = jnp.where(j == p, cot_ref[...], cot_swap_ref[...])
    adj = (cot.astype(jnp.float32) * slope).astype(act_ref.dtype)
    rows = adj.shape[0]
    for ref in adj_refs:
        ref[:rows, :] = adj
        if ref.shape[0] > rows:
            ref[rows:, :] = jnp.zeros((ref.shape[0] - rows, ref.shape[1]), ref.dtype)


def middle(near, far, weight, cot, cot_swap):
    vmem = pl.BlockSpec(memory_space=pltpu.VMEM)
    rows, width = near.shape
    out = jax.ShapeDtypeStruct((rows, width), jnp.bfloat16)
    longer = tuple(jax.ShapeDtypeStruct((rows + n, width), jnp.bfloat16) for n in (32, 16))
    return pl.pallas_call(
        middle_kernel,
        out_shape=(out, out) + longer,
        in_specs=[vmem] * 5,
        out_specs=(vmem,) * 4,
        compiler_params=pltpu.CompilerParams(vmem_limit_bytes=8 * 1024 * 1024),
        cost_estimate=pl.CostEstimate(
            flops=4 * rows * width * width,
            bytes_accessed=10 * rows * width,
            transcendentals=rows * width,
        ),
        name="middle",
    )(near, far, weight, cot, cot_swap)


def grad_kernel(scale, near_ref, far_ref, adj_ref, out_ref):
    j, _, _ = place()
    half = near_ref.shape[1]
    dims = (((0,), (0,)), ((), ()))
    for i, ref in enumerate((near_ref, far_ref)):
        start = pl.multiple_of((j if i == 0 else 1 - j) * half, half)
        block = lax.dot_general(ref[...], adj_ref[...], dims, preferred_element_type=jnp.float32)
        out_ref[pl.ds(start, half), :] = (scale * block).astype(out_ref.dtype)


def grad_block(scale, near, far, adj):
    vmem = pl.BlockSpec(memory_space=pltpu.VMEM)
    rows, width = near.shape
    return pl.pallas_call(
        functools.partial(grad_kernel, scale),
        out_shape=jax.ShapeDtypeStruct((2 * width, width), jnp.bfloat16),
        in_specs=[vmem] * 3,
        out_specs=vmem,
        compiler_params=pltpu.CompilerParams(vmem_limit_bytes=8 * 1024 * 1024),
        cost_estimate=pl.CostEstimate(
            flops=4 * WEIGH * rows * width * width,
            bytes_accessed=8 * WEIGH * rows * width,
            transcendentals=0,
        ),
        name="grad_block",
    )(near, far, adj)


def add_kernel(count, *refs):
    values = [ref[...].astype(jnp.float32) for ref in refs[:count]]
    total = values[0] + values[1]
    if count == 4:
        total = total + (values[2] + values[3])
    refs[-1][...] = total.astype(refs[-1].dtype)


def add_after(values, dtype, *after):
    vmem = pl.BlockSpec(memory_space=pltpu.VMEM)
    return pl.pallas_call(
        functools.partial(add_kernel, len(values)),
        out_shape=jax.ShapeDtypeStruct(values[0].shape, dtype),
        in_specs=[vmem] * len(values) + [pl.BlockSpec(memory_space=pl.ANY)] * len(after),
        out_specs=vmem,
        compiler_params=pltpu.CompilerParams(vmem_limit_bytes=4 * 1024 * 1024),
        name="add_after",
    )(*values, *after)


def half_columns(half):
    j, _, _ = place()
    near = pl.ds(pl.multiple_of(j * half, half), half)
    return near, pl.ds(pl.multiple_of((1 - j) * half, half), half)


def near_and_far(parts):
    j, _, p = place()
    own, one, two = parts
    near = jnp.where(j == p, own[...], one[...])
    return near, jnp.where(j == p, one[...], two[...])


def gather_kernel(own_ref, one_ref, two_ref, grad_ref, rest_ref, act_ref, grad_out_ref):
    near_cols, far_cols = half_columns(own_ref.shape[1])
    near, far = near_and_far((own_ref, one_ref, two_ref))
    act_ref[:, near_cols] = near
    act_ref[:, far_cols] = far
    grad_out_ref[:, near_cols] = grad_ref[...]
    grad_out_ref[:, far_cols] = rest_ref[...]


def gather_halves(act, grad, rest):
    vmem = pl.BlockSpec(memory_space=pltpu.VMEM)
    rows, width = act[0].shape
    return pl.pallas_call(
        gather_kernel,
        out_shape=(
            jax.ShapeDtypeStruct((rows, 2 * width), act[0].dtype),
            jax.ShapeDtypeStruct((2 * width, 2 * width), grad.dtype),
        ),
        in_specs=[vmem] * 5,
        out_specs=(vmem, vmem),
        compiler_params=pltpu.CompilerParams(vmem_limit_bytes=8 * 1024 * 1024),
        name="gather_halves",
    )(*act, grad, rest)


def final_kernel(own_ref, one_ref, two_ref, w_ref, out_ref):
    near_cols, far_cols = half_columns(own_ref.shape[1])
    near, far = near_and_far((own_ref, one_ref, two_ref))
    dims = (((1,), (1,)), ((), ()))
    total = lax.dot_general(near, w_ref[:, near_cols], dims, preferred_element_type=jnp.float32)
    total += lax.dot_general(far, w_ref[:, far_cols], dims, preferred_element_type=jnp.float32)
    out_ref[...] = total.astype(out_ref.dtype)


def final(back, weight):
    vmem = pl.BlockSpec(memory_space=pltpu.VMEM)
    rows = back[0].shape[0]
    wide = weight.shape[0]
    return pl.pallas_call(
        final_kernel,
        out_shape=jax.ShapeDtypeStruct((rows, wide), jnp.bfloat16),
        in_specs=[vmem] * 4,
        out_specs=vmem,
        compiler_params=pltpu.CompilerParams(vmem_limit_bytes=8 * 1024 * 1024),
        cost_estimate=pl.CostEstimate(
            flops=2 * rows * wide * wide, bytes_accessed=8 * rows * wide, transcendentals=0
        ),
        name="final",
    )(*back, weight)


def per_device(node_feats, weight, cotangent, tile_values, tile_coords, tile_counts):
    groups = lax.axis_size("rows")
    reps = lax.axis_size("rep")
    shape = (groups // 2, reps)
    j, z, p = place()
    home = j == p
    scale = (node_feats.shape[0] * groups) ** (-0.5)

    def send(value, move):
        return lax.ppermute(value, AXES, route(shape, move))

    def sibling(c, j, z):
        return (c, 1 - j, z)

    def home_to_sibling(c, j, z):
        return (c, 1 - j, z) if j == z % 2 else None

    def across(c, j, z):
        return (c, j, (z + reps // 2) % reps)

    own = tile_values[0]
    blocks = node_feats.shape[0] // own.shape[-1]

    def to_home(c, j, z):
        return (c, 1 - j, z) if j == z % 2 else (c, j, z ^ 1)

    four = shape[0] == 4

    def to_direct(c, j, z):
        return (c ^ 1, j, z)

    def to_second(c, j, z):
        return (c ^ 2, j, z) if four else (c + 1 if c % 2 else c - 1, j, z)

    def to_far(c, j, z):
        return (c ^ 1, j, z) if four else (c - 1 if z % 2 else c + 1, j, z)

    def stage_one(c, j, z):
        if j == z % 2:
            return (c ^ 1, j, z)
        return (c ^ 2, j, z) if four and (c + z) % 2 else None

    def stage_one_cross(c, j, z):
        to = stage_one(c, j, z)
        return to and (to[0], 1 - j, z)

    first = send(own, to_home)
    half = node_feats.shape[1] // 2
    mine = lax.dynamic_slice_in_dim(node_feats, j * half, half, 1)
    yours = lax.dynamic_slice_in_dim(node_feats, (1 - j) * half, half, 1)
    one = send(mine, stage_one)
    two = send(yours, stage_one_cross)
    swapped = send(yours, sibling)
    self_choice = [("home", mine), ("away", swapped)]
    direct_choice = [("home", one), ("away", two)]
    meta = slot_blocks(tile_coords[:, 0], tile_counts[0], blocks)
    second, far = pick(
        [
            direct_choice if four else self_choice,
            [
                ("relay home", two),
                ("relay away", one),
                ("still home", swapped),
                ("still away", mine),
            ],
        ],
        [meta],
    )
    second = send(second, to_second)
    far = send(far, to_far)
    meta_b = send(meta, to_home)
    meta_far = send(meta_b, home_to_sibling)
    first, meta_far = lax.optimization_barrier((first, meta_far))
    other_first = send(first, home_to_sibling)
    set_first = [(None, (meta_b, first))]
    panels = [
        ("direct", direct_choice),
        ("second", [(None, second)]),
        ("far", [(None, far)]),
        ("self", [("home", mine), ("away", swapped)]),
        ("near", [("home", swapped), ("away", mine)]),
    ]
    part = tile_product(panels, [set_first], jnp.float32, weigh=WEIGH)
    set_rest = [("home", (meta, own)), ("away", (meta_far, other_first))]
    part = tile_product(panels, [set_rest], jnp.bfloat16, part)

    def join(value):
        other = send(value, across)
        return (value.astype(jnp.float32) + other.astype(jnp.float32)).astype(jnp.bfloat16)

    near = join(part)
    far_half = send(near, sibling)
    cot, cot_yours = halves(cotangent)
    act, adj, adj_longer, adj_long = middle(
        near, far_half, weight, cot, send(cot_yours, sibling)
    )

    direct = send(adj_longer, to_direct)
    near_one = send(
        adj_long, lambda c, j, z: (c if (c + z) % 2 or not four else c ^ 2, j, z ^ 1)
    )
    second = send(direct if four else adj_longer, to_second)
    grad = grad_block(scale, near, far_half, adj)
    grad_got = send(grad, lambda c, j, z: (c, j, z ^ 1))
    adj_later, grad_got = lax.optimization_barrier((adj, grad_got))
    far = send(near_one, to_far)
    near_choice = [("still", near_one)]
    if four:
        near_two = send(
            adj_later, lambda c, j, z: None if (c + z) % 2 else (c, j, z ^ 1)
        )
        near_choice.append(("relay", near_two))
    panels = [("self", [(None, adj)]), ("direct", [(None, direct)])]
    back_part = tile_product(panels, [set_first, set_rest], jnp.float32)
    panels = [("second", [(None, second)]), ("far", [(None, far)]), ("near", near_choice)]
    back_part = tile_product(panels, [set_first, set_rest], jnp.bfloat16, back_part)

    def deliver(value):
        one = send(value, lambda c, j, z: (c, j, z ^ 1) if j == z % 2 else (c, 1 - j, z))
        two = send(value, lambda c, j, z: None if j == z % 2 else (c, 1 - j, z ^ 1))
        return one, two

    act_later, back_part = lax.optimization_barrier((act, back_part))
    act_parts = [act, *deliver(act_later)]
    grad = add_after([grad, grad_got], jnp.bfloat16, back_part)
    step = 1
    while step < shape[0]:
        got = send(grad, lambda c, j, z, s=step: (c ^ s, j, z))
        step *= 2
        if step < shape[0]:
            grad = add_after([grad, got], jnp.bfloat16)
    back = add_after([back_part, send(back_part, across)], jnp.bfloat16, got)
    back_parts = [back, *deliver(back)]
    grad = add_after([grad, got], jnp.float32, back, *act_parts[1:])
    activated, weight_grad = gather_halves(act_parts, grad, send(grad, sibling))
    input_grad = final(back_parts, weight)
    return (activated, input_grad, weight_grad)


def solution(mesh):
    return jax.shard_map(
        per_device,
        mesh=mesh,
        in_specs=(
            P("rows", None),
            P(),
            P("rows", None),
            P("rows", None, "rep", None, None),
            P(None, "rows", None, "rep"),
            P("rows", None),
        ),
        out_specs=(P("rows", None), P("rows", None), P()),
        check_vma=False,
    )
```

```python
import functools

import jax
import jax.numpy as jnp
from jax import lax
from jax.experimental import pallas as pl
from jax.experimental.pallas import tpu as pltpu
from jax.sharding import PartitionSpec as P

AXES = ("rows", "rep")
TOGETHER = 2
ROWS = 256
WEIGH = 75


def route(shape, move):
    chips, reps = shape
    pairs = []
    for c in range(chips):
        for j in range(2):
            for z in range(reps):
                to = move(c, j, z)
                if to is not None:
                    target = ((to[0] % chips) * 2 + to[1]) * reps + to[2]
                    pairs.append(((c * 2 + j) * reps + z, target))
    return pairs


def place():
    r = lax.axis_index("rows")
    z = lax.axis_index("rep")
    return r % 2, z, z % 2


def when_of(case):
    j, z, p = place()
    home = j == p
    relay = jnp.logical_and(
        lax.axis_size("rows") == 8, (lax.axis_index("rows") // 2 + z) % 2 == 1
    )
    return {
        "home": home,
        "away": jnp.logical_not(home),
        "relay": relay,
        "still": jnp.logical_not(relay),
        "relay home": jnp.logical_and(relay, home),
        "relay away": jnp.logical_and(relay, jnp.logical_not(home)),
        "still home": jnp.logical_and(jnp.logical_not(relay), home),
        "still away": jnp.logical_and(jnp.logical_not(relay), jnp.logical_not(home)),
    }[case]


def start_chosen(choice, make):
    if len(choice) == 1:
        make(choice[0][1]).start()
        return
    for case, ref in choice:

        @pl.when(when_of(case))
        def _(ref=ref):
            make(ref).start()


def halves_kernel(x_ref, near_ref, far_ref, sems):
    j, _, _ = place()
    half = near_ref.shape[1]
    copies = []
    for i, out in enumerate((near_ref, far_ref)):
        start = pl.multiple_of((j if i == 0 else 1 - j) * half, half)
        copy = pltpu.make_async_copy(x_ref.at[:, pl.ds(start, half)], out, sems.at[i])
        copy.start()
        copies.append(copy)
    for copy in copies:
        copy.wait()


def halves(value):
    rows, width = value.shape
    part = jax.ShapeDtypeStruct((rows, width // 2), value.dtype)
    hbm = pl.BlockSpec(memory_space=pltpu.HBM)
    return pl.pallas_call(
        halves_kernel,
        out_shape=(part, part),
        in_specs=[hbm],
        out_specs=(hbm, hbm),
        scratch_shapes=[pltpu.SemaphoreType.DMA((2,))],
        compiler_params=pltpu.CompilerParams(vmem_limit_bytes=1024 * 1024),
        name="halves",
    )(value)


def pick_kernel(cases, waits, *refs):
    refs = list(refs)
    choices = [[(case, refs.pop(0)) for case in each] for each in cases]
    outs, sems = refs[waits:-1], refs[-1]

    def copy_to(i):
        return lambda ref: pltpu.make_async_copy(ref, outs[i], sems.at[i])

    for i, choice in enumerate(choices):
        start_chosen(choice, copy_to(i))
    for i, choice in enumerate(choices):
        copy_to(i)(choice[0][1]).wait()


def pick(choices, after):
    hbm = pl.BlockSpec(memory_space=pltpu.HBM)
    arrays = [array for choice in choices for _, array in choice]
    shape = jax.ShapeDtypeStruct(arrays[0].shape, arrays[0].dtype)
    return pl.pallas_call(
        functools.partial(
            pick_kernel, [[case for case, _ in choice] for choice in choices], len(after)
        ),
        out_shape=(shape,) * len(choices),
        in_specs=[hbm] * len(arrays) + [pl.BlockSpec(memory_space=pl.ANY)] * len(after),
        out_specs=(hbm,) * len(choices),
        scratch_shapes=[pltpu.SemaphoreType.DMA((len(choices),))],
        compiler_params=pltpu.CompilerParams(vmem_limit_bytes=1024 * 1024),
        name="pick",
    )(*arrays, *after)


def slots_kernel(dead, coords_ref, counts_ref, out_ref):
    _, z, _ = place()
    _, reach, slots = coords_ref.shape
    for d in range(reach):
        for k in range(slots):
            live = z * slots + k < counts_ref[d]
            out_ref[0, d * slots + k] = jnp.where(live, coords_ref[0, d, k], dead)
            out_ref[1, d * slots + k] = coords_ref[1, d, k]


def slot_blocks(coords, counts, dead):
    smem = pl.BlockSpec(memory_space=pltpu.SMEM)
    return pl.pallas_call(
        functools.partial(slots_kernel, dead),
        out_shape=jax.ShapeDtypeStruct((2, coords.shape[1] * coords.shape[2]), jnp.int32),
        in_specs=[smem, smem],
        out_specs=smem,
        compiler_params=pltpu.CompilerParams(vmem_limit_bytes=1024 * 1024),
        name="slot_blocks",
    )(coords, counts)


def offset_of(kind):
    _, _, p = place()
    even = (lax.axis_index("rows") // 2) % 2 == 0
    return {
        "self": 2,
        "near": jnp.where(p == 0, 3, 1),
        "far": jnp.where(p == 0, 1, 3),
        "direct": jnp.where(even, 4, 0),
        "second": jnp.where(even, 0, 4),
    }[kind]


def chosen(choice, read):
    value = read(choice[0][1])
    for case, ref in choice[1:]:
        value = jnp.where(when_of(case), read(ref), value)
    return value


def tile_kernel(kinds, cases, sets, summed, waits, *refs):
    refs = list(refs)
    metas = [[(case, refs.pop(0)) for case in each] for each in sets]
    tiles = [[(case, refs.pop(0)) for case in each] for each in sets]
    panels = [[(case, refs.pop(0)) for case in each] for each in cases]
    before = refs.pop(0) if summed else None
    out_ref, acc_ref = refs[waits:]
    _, slots, tile, _ = tiles[0][0][1].shape
    rows = out_ref.shape[0]
    if summed:
        acc_ref[:rows, :] = before[...]
    else:
        acc_ref[...] = jnp.zeros_like(acc_ref)
    for i, kind in enumerate(kinds):
        d = offset_of(kind)
        for s in range(len(sets)):
            for first in range(0, slots, TOGETHER):
                prods = []
                for k in range(first, min(first + TOGETHER, slots)):
                    row = chosen(metas[s], lambda ref: ref[0, d * slots + k])
                    col = chosen(metas[s], lambda ref: ref[1, d * slots + k])
                    col = pl.multiple_of(col * tile, tile)
                    prod = jnp.dot(
                        chosen(tiles[s], lambda ref: ref[d, k]),
                        chosen(panels[i], lambda ref: ref[pl.ds(col, tile), :]),
                        preferred_element_type=jnp.float32,
                    )
                    prods.append((pl.multiple_of(row * tile, tile), prod))
                for row, prod in prods:
                    acc_ref[pl.ds(row, tile), :] += prod
    out_ref[...] = acc_ref[:rows, :].astype(out_ref.dtype)


def tile_product(named, sets, dtype, before=None, after=(), weigh=1):
    kinds = [kind for kind, _ in named]
    cases = [[case for case, _ in choice] for _, choice in named]
    panels = [panel for _, choice in named for _, panel in choice]
    metas = [meta for choice in sets for _, (meta, _) in choice]
    tiles = [values for choice in sets for _, (_, values) in choice]
    rows, width = panels[0].shape if before is None else before.shape
    _, slots, tile, _ = tiles[0].shape
    smem = pl.BlockSpec(memory_space=pltpu.SMEM)
    vmem = pl.BlockSpec(memory_space=pltpu.VMEM)
    anywhere = pl.BlockSpec(memory_space=pl.ANY)
    count = len(kinds) * len(sets) * slots
    summed = before is not None
    return pl.pallas_call(
        functools.partial(
            tile_kernel,
            kinds,
            cases,
            [[case for case, _ in choice] for choice in sets],
            summed,
            len(after),
        ),
        out_shape=jax.ShapeDtypeStruct((rows, width), dtype),
        in_specs=[smem] * len(metas)
        + [vmem] * (len(tiles) + len(panels) + summed)
        + [anywhere] * len(after),
        out_specs=vmem,
        scratch_shapes=[pltpu.VMEM((rows + tile, width), jnp.float32)],
        compiler_params=pltpu.CompilerParams(vmem_limit_bytes=12 * 1024 * 1024),
        cost_estimate=pl.CostEstimate(
            flops=weigh * 2 * count * tile * tile * width,
            bytes_accessed=weigh * (count * tile * tile * 2 + len(kinds) * rows * width * 2),
            transcendentals=0,
        ),
        name="tile_product",
    )(*metas, *tiles, *panels, *([before] if summed else []), *after)


def middle_kernel(near_ref, far_ref, w_ref, cot_ref, cot_swap_ref, act_ref, *adj_refs):
    j, _, p = place()
    near_cols, far_cols = half_columns(near_ref.shape[1])
    weight = jnp.concatenate([w_ref[near_cols, near_cols], w_ref[far_cols, near_cols]], axis=0)
    count = near_ref.shape[0]
    for start in range(0, count, ROWS):
        rows = pl.ds(start, ROWS)
        both = jnp.concatenate([near_ref[rows, :], far_ref[rows, :]], axis=1)
        agg = jnp.dot(both, weight, preferred_element_type=jnp.float32)
        sig = jax.nn.sigmoid(agg)
        act_ref[rows, :] = (agg * sig).astype(act_ref.dtype)
        slope = sig * (1.0 + agg * (1.0 - sig))
        cot = jnp.where(j == p, cot_ref[rows, :], cot_swap_ref[rows, :])
        adj = (cot.astype(jnp.float32) * slope).astype(act_ref.dtype)
        for ref in adj_refs:
            ref[rows, :] = adj
    for ref in adj_refs:
        if ref.shape[0] > count:
            ref[count:, :] = jnp.zeros((ref.shape[0] - count, ref.shape[1]), ref.dtype)


def middle(near, far, weight, cot, cot_swap):
    vmem = pl.BlockSpec(memory_space=pltpu.VMEM)
    rows, width = near.shape
    out = jax.ShapeDtypeStruct((rows, width), jnp.bfloat16)
    longer = tuple(jax.ShapeDtypeStruct((rows + n, width), jnp.bfloat16) for n in (32, 16))
    return pl.pallas_call(
        middle_kernel,
        out_shape=(out, out) + longer,
        in_specs=[vmem] * 5,
        out_specs=(vmem,) * 4,
        compiler_params=pltpu.CompilerParams(vmem_limit_bytes=8 * 1024 * 1024),
        cost_estimate=pl.CostEstimate(
            flops=4 * rows * width * width,
            bytes_accessed=10 * rows * width,
            transcendentals=rows * width,
        ),
        name="middle",
    )(near, far, weight, cot, cot_swap)


def grad_kernel(scale, near_ref, far_ref, adj_ref, out_ref):
    j, _, _ = place()
    half = near_ref.shape[1]
    dims = (((0,), (0,)), ((), ()))
    for i, ref in enumerate((near_ref, far_ref)):
        start = pl.multiple_of((j if i == 0 else 1 - j) * half, half)
        block = lax.dot_general(ref[...], adj_ref[...], dims, preferred_element_type=jnp.float32)
        out_ref[pl.ds(start, half), :] = (scale * block).astype(out_ref.dtype)


def grad_block(scale, near, far, adj):
    vmem = pl.BlockSpec(memory_space=pltpu.VMEM)
    rows, width = near.shape
    return pl.pallas_call(
        functools.partial(grad_kernel, scale),
        out_shape=jax.ShapeDtypeStruct((2 * width, width), jnp.bfloat16),
        in_specs=[vmem] * 3,
        out_specs=vmem,
        compiler_params=pltpu.CompilerParams(vmem_limit_bytes=8 * 1024 * 1024),
        cost_estimate=pl.CostEstimate(
            flops=4 * WEIGH * rows * width * width,
            bytes_accessed=8 * WEIGH * rows * width,
            transcendentals=0,
        ),
        name="grad_block",
    )(near, far, adj)


def add_kernel(count, *refs):
    values = [ref[...].astype(jnp.float32) for ref in refs[:count]]
    total = values[0] + values[1]
    if count == 4:
        total = total + (values[2] + values[3])
    refs[-1][...] = total.astype(refs[-1].dtype)


def add_after(values, dtype, *after):
    vmem = pl.BlockSpec(memory_space=pltpu.VMEM)
    return pl.pallas_call(
        functools.partial(add_kernel, len(values)),
        out_shape=jax.ShapeDtypeStruct(values[0].shape, dtype),
        in_specs=[vmem] * len(values) + [pl.BlockSpec(memory_space=pl.ANY)] * len(after),
        out_specs=vmem,
        compiler_params=pltpu.CompilerParams(vmem_limit_bytes=4 * 1024 * 1024),
        name="add_after",
    )(*values, *after)


def half_columns(half):
    j, _, _ = place()
    near = pl.ds(pl.multiple_of(j * half, half), half)
    return near, pl.ds(pl.multiple_of((1 - j) * half, half), half)


def near_and_far(parts):
    j, _, p = place()
    own, one, two = parts
    near = jnp.where(j == p, own[...], one[...])
    return near, jnp.where(j == p, one[...], two[...])


def gather_kernel(own_ref, one_ref, two_ref, grad_ref, rest_ref, act_ref, grad_out_ref):
    near_cols, far_cols = half_columns(own_ref.shape[1])
    near, far = near_and_far((own_ref, one_ref, two_ref))
    act_ref[:, near_cols] = near
    act_ref[:, far_cols] = far
    grad_out_ref[:, near_cols] = grad_ref[...]
    grad_out_ref[:, far_cols] = rest_ref[...]


def gather_halves(act, grad, rest):
    vmem = pl.BlockSpec(memory_space=pltpu.VMEM)
    rows, width = act[0].shape
    return pl.pallas_call(
        gather_kernel,
        out_shape=(
            jax.ShapeDtypeStruct((rows, 2 * width), act[0].dtype),
            jax.ShapeDtypeStruct((2 * width, 2 * width), grad.dtype),
        ),
        in_specs=[vmem] * 5,
        out_specs=(vmem, vmem),
        compiler_params=pltpu.CompilerParams(vmem_limit_bytes=8 * 1024 * 1024),
        name="gather_halves",
    )(*act, grad, rest)


def final_kernel(own_ref, one_ref, two_ref, w_ref, out_ref):
    j, _, p = place()
    near_cols, far_cols = half_columns(own_ref.shape[1])
    weight = jnp.concatenate([w_ref[:, near_cols], w_ref[:, far_cols]], axis=1)
    for start in range(0, own_ref.shape[0], ROWS):
        rows = pl.ds(start, ROWS)
        own, one, two = own_ref[rows, :], one_ref[rows, :], two_ref[rows, :]
        near, far = jnp.where(j == p, own, one), jnp.where(j == p, one, two)
        product = lax.dot_general(
            jnp.concatenate([near, far], axis=1),
            weight,
            (((1,), (1,)), ((), ())),
            preferred_element_type=jnp.float32,
        )
        out_ref[rows, :] = product.astype(out_ref.dtype)


def final(back, weight):
    vmem = pl.BlockSpec(memory_space=pltpu.VMEM)
    rows = back[0].shape[0]
    wide = weight.shape[0]
    return pl.pallas_call(
        final_kernel,
        out_shape=jax.ShapeDtypeStruct((rows, wide), jnp.bfloat16),
        in_specs=[vmem] * 4,
        out_specs=vmem,
        compiler_params=pltpu.CompilerParams(vmem_limit_bytes=8 * 1024 * 1024),
        cost_estimate=pl.CostEstimate(
            flops=2 * rows * wide * wide, bytes_accessed=8 * rows * wide, transcendentals=0
        ),
        name="final",
    )(*back, weight)


def per_device(node_feats, weight, cotangent, tile_values, tile_coords, tile_counts):
    groups = lax.axis_size("rows")
    reps = lax.axis_size("rep")
    shape = (groups // 2, reps)
    j, z, p = place()
    home = j == p
    scale = (node_feats.shape[0] * groups) ** (-0.5)

    def send(value, move):
        return lax.ppermute(value, AXES, route(shape, move))

    def sibling(c, j, z):
        return (c, 1 - j, z)

    def home_to_sibling(c, j, z):
        return (c, 1 - j, z) if j == z % 2 else None

    def across(c, j, z):
        return (c, j, (z + reps // 2) % reps)

    own = tile_values[0]
    blocks = node_feats.shape[0] // own.shape[-1]

    def to_home(c, j, z):
        return (c, 1 - j, z) if j == z % 2 else (c, j, z ^ 1)

    four = shape[0] == 4

    def to_direct(c, j, z):
        return (c ^ 1, j, z)

    def to_second(c, j, z):
        return (c ^ 2, j, z) if four else (c + 1 if c % 2 else c - 1, j, z)

    def to_far(c, j, z):
        return (c ^ 1, j, z) if four else (c - 1 if z % 2 else c + 1, j, z)

    def stage_one(c, j, z):
        if j == z % 2:
            return (c ^ 1, j, z)
        return (c ^ 2, j, z) if four and (c + z) % 2 else None

    def stage_one_cross(c, j, z):
        to = stage_one(c, j, z)
        return to and (to[0], 1 - j, z)

    first = send(own, to_home)
    half = node_feats.shape[1] // 2
    mine = lax.dynamic_slice_in_dim(node_feats, j * half, half, 1)
    yours = lax.dynamic_slice_in_dim(node_feats, (1 - j) * half, half, 1)
    one = send(mine, stage_one)
    two = send(yours, stage_one_cross)
    swapped = send(yours, sibling)
    self_choice = [("home", mine), ("away", swapped)]
    direct_choice = [("home", one), ("away", two)]
    meta = slot_blocks(tile_coords[:, 0], tile_counts[0], blocks)
    second, far = pick(
        [
            direct_choice if four else self_choice,
            [
                ("still home", swapped),
                ("still away", mine),
                ("relay home", two),
                ("relay away", one),
            ],
        ],
        [meta],
    )
    second = send(second, to_second)
    far = send(far, to_far)
    meta_b = send(meta, to_home)
    first, meta_b = lax.optimization_barrier((first, meta_b))
    other_first = send(first, home_to_sibling)
    meta_later, second = lax.optimization_barrier((meta_b, second))
    meta_far = send(meta_later, home_to_sibling)
    set_first = [(None, (meta_b, first))]
    panels = [
        ("self", [("home", mine), ("away", swapped)]),
        ("near", [("home", swapped), ("away", mine)]),
        ("direct", direct_choice),
        ("second", [(None, second)]),
        ("far", [(None, far)]),
    ]
    part = tile_product(panels, [set_first], jnp.float32, weigh=WEIGH)
    set_rest = [("home", (meta, own)), ("away", (meta_far, other_first))]
    part = tile_product(panels, [set_rest], jnp.bfloat16, part)

    def join(value):
        other = send(value, across)
        return (value.astype(jnp.float32) + other.astype(jnp.float32)).astype(jnp.bfloat16)

    near = join(part)
    far_half = send(near, sibling)
    cot, cot_yours = halves(cotangent)
    act, adj, adj_longer, adj_long = middle(
        near, far_half, weight, cot, send(cot_yours, sibling)
    )

    direct = send(adj_longer, to_direct)
    near_one = send(
        adj_long, lambda c, j, z: (c if (c + z) % 2 or not four else c ^ 2, j, z ^ 1)
    )
    second = send(direct if four else adj_longer, to_second)
    grad = grad_block(scale, near, far_half, adj)
    grad_got = send(grad, lambda c, j, z: (c, j, z ^ 1))
    adj_later, grad_got = lax.optimization_barrier((adj, grad_got))
    far = send(near_one, to_far)
    near_choice = [("still", near_one)]
    if four:
        near_two = send(
            adj_later, lambda c, j, z: None if (c + z) % 2 else (c, j, z ^ 1)
        )
        near_choice.append(("relay", near_two))
    panels = [("self", [(None, adj)]), ("direct", [(None, direct)])]
    back_part = tile_product(panels, [set_first, set_rest], jnp.float32)
    panels = [("second", [(None, second)]), ("far", [(None, far)]), ("near", near_choice)]
    back_part = tile_product(panels, [set_first, set_rest], jnp.bfloat16, back_part)

    def deliver(value):
        one = send(value, lambda c, j, z: (c, j, z ^ 1) if j == z % 2 else (c, 1 - j, z))
        two = send(value, lambda c, j, z: None if j == z % 2 else (c, 1 - j, z ^ 1))
        return one, two

    act_later, back_part = lax.optimization_barrier((act, back_part))
    act_parts = [act, *deliver(act_later)]
    grad = add_after([grad, grad_got], jnp.bfloat16, back_part)
    step = 1
    while step < shape[0]:
        got = send(grad, lambda c, j, z, s=step: (c ^ s, j, z))
        step *= 2
        if step < shape[0]:
            grad = add_after([grad, got], jnp.bfloat16)
    back = add_after([back_part, send(back_part, across)], jnp.bfloat16, got)
    back_parts = [back, *deliver(back)]
    grad = add_after([grad, got], jnp.float32, back, *act_parts[1:])
    activated, weight_grad = gather_halves(act_parts, grad, send(grad, sibling))
    input_grad = final(back_parts, weight)
    return (activated, input_grad, weight_grad)


def solution(mesh):
    return jax.shard_map(
        per_device,
        mesh=mesh,
        in_specs=(
            P("rows", None),
            P(),
            P("rows", None),
            P("rows", None, "rep", None, None),
            P(None, "rows", None, "rep"),
            P("rows", None),
        ),
        out_specs=(P("rows", None), P("rows", None), P()),
        check_vma=False,
    )
```

```python
import functools

import jax
import jax.numpy as jnp
from jax import lax
from jax.experimental import pallas as pl
from jax.experimental.pallas import tpu as pltpu
from jax.sharding import PartitionSpec as P

AXES = ("rows", "rep")
TOGETHER = 2
ROWS = 256
WEIGH = 75


def route(shape, move):
    chips, reps = shape
    pairs = []
    for c in range(chips):
        for j in range(2):
            for z in range(reps):
                to = move(c, j, z)
                if to is not None:
                    target = ((to[0] % chips) * 2 + to[1]) * reps + to[2]
                    pairs.append(((c * 2 + j) * reps + z, target))
    return pairs


def place():
    r = lax.axis_index("rows")
    z = lax.axis_index("rep")
    return r % 2, z, z % 2


def when_of(case):
    j, z, p = place()
    home = j == p
    relay = jnp.logical_and(
        lax.axis_size("rows") == 8, (lax.axis_index("rows") // 2 + z) % 2 == 1
    )
    return {
        "home": home,
        "away": jnp.logical_not(home),
        "relay": relay,
        "still": jnp.logical_not(relay),
        "relay home": jnp.logical_and(relay, home),
        "relay away": jnp.logical_and(relay, jnp.logical_not(home)),
        "still home": jnp.logical_and(jnp.logical_not(relay), home),
        "still away": jnp.logical_and(jnp.logical_not(relay), jnp.logical_not(home)),
    }[case]


def start_chosen(choice, make):
    if len(choice) == 1:
        make(choice[0][1]).start()
        return
    for case, ref in choice:

        @pl.when(when_of(case))
        def _(ref=ref):
            make(ref).start()


def halves_kernel(x_ref, near_ref, far_ref, sems):
    j, _, _ = place()
    half = near_ref.shape[1]
    copies = []
    for i, out in enumerate((near_ref, far_ref)):
        start = pl.multiple_of((j if i == 0 else 1 - j) * half, half)
        copy = pltpu.make_async_copy(x_ref.at[:, pl.ds(start, half)], out, sems.at[i])
        copy.start()
        copies.append(copy)
    for copy in copies:
        copy.wait()


def halves(value):
    rows, width = value.shape
    part = jax.ShapeDtypeStruct((rows, width // 2), value.dtype)
    hbm = pl.BlockSpec(memory_space=pltpu.HBM)
    return pl.pallas_call(
        halves_kernel,
        out_shape=(part, part),
        in_specs=[hbm],
        out_specs=(hbm, hbm),
        scratch_shapes=[pltpu.SemaphoreType.DMA((2,))],
        compiler_params=pltpu.CompilerParams(vmem_limit_bytes=1024 * 1024),
        name="halves",
    )(value)


def pick_kernel(cases, waits, *refs):
    refs = list(refs)
    choices = [[(case, refs.pop(0)) for case in each] for each in cases]
    outs, sems = refs[waits:-1], refs[-1]

    def copy_to(i):
        return lambda ref: pltpu.make_async_copy(ref, outs[i], sems.at[i])

    for i, choice in enumerate(choices):
        start_chosen(choice, copy_to(i))
    for i, choice in enumerate(choices):
        copy_to(i)(choice[0][1]).wait()


def pick(choices, after):
    hbm = pl.BlockSpec(memory_space=pltpu.HBM)
    arrays = [array for choice in choices for _, array in choice]
    shape = jax.ShapeDtypeStruct(arrays[0].shape, arrays[0].dtype)
    return pl.pallas_call(
        functools.partial(
            pick_kernel, [[case for case, _ in choice] for choice in choices], len(after)
        ),
        out_shape=(shape,) * len(choices),
        in_specs=[hbm] * len(arrays) + [pl.BlockSpec(memory_space=pl.ANY)] * len(after),
        out_specs=(hbm,) * len(choices),
        scratch_shapes=[pltpu.SemaphoreType.DMA((len(choices),))],
        compiler_params=pltpu.CompilerParams(vmem_limit_bytes=1024 * 1024),
        name="pick",
    )(*arrays, *after)


def slots_kernel(dead, coords_ref, counts_ref, out_ref):
    _, z, _ = place()
    _, reach, slots = coords_ref.shape
    for d in range(reach):
        for k in range(slots):
            live = z * slots + k < counts_ref[d]
            out_ref[0, d * slots + k] = jnp.where(live, coords_ref[0, d, k], dead)
            out_ref[1, d * slots + k] = coords_ref[1, d, k]


def slot_blocks(coords, counts, dead):
    smem = pl.BlockSpec(memory_space=pltpu.SMEM)
    return pl.pallas_call(
        functools.partial(slots_kernel, dead),
        out_shape=jax.ShapeDtypeStruct((2, coords.shape[1] * coords.shape[2]), jnp.int32),
        in_specs=[smem, smem],
        out_specs=smem,
        compiler_params=pltpu.CompilerParams(vmem_limit_bytes=1024 * 1024),
        name="slot_blocks",
    )(coords, counts)


def offset_of(kind):
    _, _, p = place()
    even = (lax.axis_index("rows") // 2) % 2 == 0
    return {
        "self": 2,
        "near": jnp.where(p == 0, 3, 1),
        "far": jnp.where(p == 0, 1, 3),
        "direct": jnp.where(even, 4, 0),
        "second": jnp.where(even, 0, 4),
    }[kind]


def chosen(choice, read):
    value = read(choice[0][1])
    for case, ref in choice[1:]:
        value = jnp.where(when_of(case), read(ref), value)
    return value


def tile_kernel(kinds, cases, sets, summed, waits, *refs):
    refs = list(refs)
    metas = [[(case, refs.pop(0)) for case in each] for each in sets]
    tiles = [[(case, refs.pop(0)) for case in each] for each in sets]
    panels = [[(case, refs.pop(0)) for case in each] for each in cases]
    before = refs.pop(0) if summed else None
    out_ref, acc_ref = refs[waits:]
    _, slots, tile, _ = tiles[0][0][1].shape
    rows = out_ref.shape[0]
    if summed:
        acc_ref[:rows, :] = before[...]
    else:
        acc_ref[...] = jnp.zeros_like(acc_ref)
    for i, kind in enumerate(kinds):
        d = offset_of(kind)
        for s in range(len(sets)):
            for first in range(0, slots, TOGETHER):
                prods = []
                for k in range(first, min(first + TOGETHER, slots)):
                    row = chosen(metas[s], lambda ref: ref[0, d * slots + k])
                    col = chosen(metas[s], lambda ref: ref[1, d * slots + k])
                    col = pl.multiple_of(col * tile, tile)
                    prod = jnp.dot(
                        chosen(tiles[s], lambda ref: ref[d, k]),
                        chosen(panels[i], lambda ref: ref[pl.ds(col, tile), :]),
                        preferred_element_type=jnp.float32,
                    )
                    prods.append((pl.multiple_of(row * tile, tile), prod))
                for row, prod in prods:
                    acc_ref[pl.ds(row, tile), :] += prod
    out_ref[...] = acc_ref[:rows, :].astype(out_ref.dtype)


def tile_product(named, sets, dtype, before=None, after=(), weigh=1):
    kinds = [kind for kind, _ in named]
    cases = [[case for case, _ in choice] for _, choice in named]
    panels = [panel for _, choice in named for _, panel in choice]
    metas = [meta for choice in sets for _, (meta, _) in choice]
    tiles = [values for choice in sets for _, (_, values) in choice]
    rows, width = panels[0].shape if before is None else before.shape
    _, slots, tile, _ = tiles[0].shape
    smem = pl.BlockSpec(memory_space=pltpu.SMEM)
    vmem = pl.BlockSpec(memory_space=pltpu.VMEM)
    anywhere = pl.BlockSpec(memory_space=pl.ANY)
    count = len(kinds) * len(sets) * slots
    summed = before is not None
    return pl.pallas_call(
        functools.partial(
            tile_kernel,
            kinds,
            cases,
            [[case for case, _ in choice] for choice in sets],
            summed,
            len(after),
        ),
        out_shape=jax.ShapeDtypeStruct((rows, width), dtype),
        in_specs=[smem] * len(metas)
        + [vmem] * (len(tiles) + len(panels) + summed)
        + [anywhere] * len(after),
        out_specs=vmem,
        scratch_shapes=[pltpu.VMEM((rows + tile, width), jnp.float32)],
        compiler_params=pltpu.CompilerParams(vmem_limit_bytes=12 * 1024 * 1024),
        cost_estimate=pl.CostEstimate(
            flops=weigh * 2 * count * tile * tile * width,
            bytes_accessed=weigh * (count * tile * tile * 2 + len(kinds) * rows * width * 2),
            transcendentals=0,
        ),
        name="tile_product",
    )(*metas, *tiles, *panels, *([before] if summed else []), *after)


def middle_kernel(near_ref, far_ref, w_ref, cot_ref, cot_swap_ref, act_ref, *adj_refs):
    j, _, p = place()
    near_cols, far_cols = half_columns(near_ref.shape[1])
    weight = jnp.concatenate([w_ref[near_cols, near_cols], w_ref[far_cols, near_cols]], axis=0)
    count = near_ref.shape[0]
    for start in range(0, count, ROWS):
        rows = pl.ds(start, ROWS)
        both = jnp.concatenate([near_ref[rows, :], far_ref[rows, :]], axis=1)
        agg = jnp.dot(both, weight, preferred_element_type=jnp.float32)
        sig = jax.nn.sigmoid(agg)
        act_ref[rows, :] = (agg * sig).astype(act_ref.dtype)
        slope = sig * (1.0 + agg * (1.0 - sig))
        cot = jnp.where(j == p, cot_ref[rows, :], cot_swap_ref[rows, :])
        adj = (cot.astype(jnp.float32) * slope).astype(act_ref.dtype)
        for ref in adj_refs:
            ref[rows, :] = adj
    for ref in adj_refs:
        if ref.shape[0] > count:
            ref[count:, :] = jnp.zeros((ref.shape[0] - count, ref.shape[1]), ref.dtype)


def middle(near, far, weight, cot, cot_swap):
    vmem = pl.BlockSpec(memory_space=pltpu.VMEM)
    rows, width = near.shape
    out = jax.ShapeDtypeStruct((rows, width), jnp.bfloat16)
    longer = tuple(jax.ShapeDtypeStruct((rows + n, width), jnp.bfloat16) for n in (32, 16))
    return pl.pallas_call(
        middle_kernel,
        out_shape=(out, out) + longer,
        in_specs=[vmem] * 5,
        out_specs=(vmem,) * 4,
        compiler_params=pltpu.CompilerParams(vmem_limit_bytes=8 * 1024 * 1024),
        cost_estimate=pl.CostEstimate(
            flops=4 * rows * width * width,
            bytes_accessed=10 * rows * width,
            transcendentals=rows * width,
        ),
        name="middle",
    )(near, far, weight, cot, cot_swap)


def grad_kernel(scale, near_ref, far_ref, adj_ref, out_ref):
    j, _, _ = place()
    half = near_ref.shape[1]
    dims = (((0,), (0,)), ((), ()))
    for i, ref in enumerate((near_ref, far_ref)):
        start = pl.multiple_of((j if i == 0 else 1 - j) * half, half)
        block = lax.dot_general(ref[...], adj_ref[...], dims, preferred_element_type=jnp.float32)
        out_ref[pl.ds(start, half), :] = (scale * block).astype(out_ref.dtype)


def grad_block(scale, near, far, adj):
    vmem = pl.BlockSpec(memory_space=pltpu.VMEM)
    rows, width = near.shape
    return pl.pallas_call(
        functools.partial(grad_kernel, scale),
        out_shape=jax.ShapeDtypeStruct((2 * width, width), jnp.bfloat16),
        in_specs=[vmem] * 3,
        out_specs=vmem,
        compiler_params=pltpu.CompilerParams(vmem_limit_bytes=8 * 1024 * 1024),
        cost_estimate=pl.CostEstimate(
            flops=4 * WEIGH * rows * width * width,
            bytes_accessed=8 * WEIGH * rows * width,
            transcendentals=0,
        ),
        name="grad_block",
    )(near, far, adj)


def add_kernel(count, *refs):
    values = [ref[...].astype(jnp.float32) for ref in refs[:count]]
    total = values[0] + values[1]
    if count == 4:
        total = total + (values[2] + values[3])
    refs[-1][...] = total.astype(refs[-1].dtype)


def add_after(values, dtype, *after):
    vmem = pl.BlockSpec(memory_space=pltpu.VMEM)
    return pl.pallas_call(
        functools.partial(add_kernel, len(values)),
        out_shape=jax.ShapeDtypeStruct(values[0].shape, dtype),
        in_specs=[vmem] * len(values) + [pl.BlockSpec(memory_space=pl.ANY)] * len(after),
        out_specs=vmem,
        compiler_params=pltpu.CompilerParams(vmem_limit_bytes=4 * 1024 * 1024),
        name="add_after",
    )(*values, *after)


def half_columns(half):
    j, _, _ = place()
    near = pl.ds(pl.multiple_of(j * half, half), half)
    return near, pl.ds(pl.multiple_of((1 - j) * half, half), half)


def near_and_far(parts):
    j, _, p = place()
    own, one, two = parts
    near = jnp.where(j == p, own[...], one[...])
    return near, jnp.where(j == p, one[...], two[...])


def gather_kernel(own_ref, one_ref, two_ref, grad_ref, rest_ref, act_ref, grad_out_ref):
    near_cols, far_cols = half_columns(own_ref.shape[1])
    near, far = near_and_far((own_ref, one_ref, two_ref))
    act_ref[:, near_cols] = near
    act_ref[:, far_cols] = far
    grad_out_ref[:, near_cols] = grad_ref[...]
    grad_out_ref[:, far_cols] = rest_ref[...]


def gather_halves(act, grad, rest):
    vmem = pl.BlockSpec(memory_space=pltpu.VMEM)
    rows, width = act[0].shape
    return pl.pallas_call(
        gather_kernel,
        out_shape=(
            jax.ShapeDtypeStruct((rows, 2 * width), act[0].dtype),
            jax.ShapeDtypeStruct((2 * width, 2 * width), grad.dtype),
        ),
        in_specs=[vmem] * 5,
        out_specs=(vmem, vmem),
        compiler_params=pltpu.CompilerParams(vmem_limit_bytes=8 * 1024 * 1024),
        name="gather_halves",
    )(*act, grad, rest)


def final_kernel(own_ref, one_ref, two_ref, w_ref, out_ref):
    j, _, p = place()
    near_cols, far_cols = half_columns(own_ref.shape[1])
    weight = jnp.concatenate([w_ref[:, near_cols], w_ref[:, far_cols]], axis=1)
    for start in range(0, own_ref.shape[0], ROWS):
        rows = pl.ds(start, ROWS)
        own, one, two = own_ref[rows, :], one_ref[rows, :], two_ref[rows, :]
        near, far = jnp.where(j == p, own, one), jnp.where(j == p, one, two)
        product = lax.dot_general(
            jnp.concatenate([near, far], axis=1),
            weight,
            (((1,), (1,)), ((), ())),
            preferred_element_type=jnp.float32,
        )
        out_ref[rows, :] = product.astype(out_ref.dtype)


def final(back, weight):
    vmem = pl.BlockSpec(memory_space=pltpu.VMEM)
    rows = back[0].shape[0]
    wide = weight.shape[0]
    return pl.pallas_call(
        final_kernel,
        out_shape=jax.ShapeDtypeStruct((rows, wide), jnp.bfloat16),
        in_specs=[vmem] * 4,
        out_specs=vmem,
        compiler_params=pltpu.CompilerParams(vmem_limit_bytes=8 * 1024 * 1024),
        cost_estimate=pl.CostEstimate(
            flops=2 * rows * wide * wide, bytes_accessed=8 * rows * wide, transcendentals=0
        ),
        name="final",
    )(*back, weight)


def per_device(node_feats, weight, cotangent, tile_values, tile_coords, tile_counts):
    groups = lax.axis_size("rows")
    reps = lax.axis_size("rep")
    shape = (groups // 2, reps)
    j, z, p = place()
    home = j == p
    scale = (node_feats.shape[0] * groups) ** (-0.5)

    def send(value, move):
        return lax.ppermute(value, AXES, route(shape, move))

    def sibling(c, j, z):
        return (c, 1 - j, z)

    def home_to_sibling(c, j, z):
        return (c, 1 - j, z) if j == z % 2 else None

    def across(c, j, z):
        return (c, j, (z + reps // 2) % reps)

    own = tile_values[0]
    blocks = node_feats.shape[0] // own.shape[-1]

    def to_home(c, j, z):
        return (c, 1 - j, z) if j == z % 2 else (c, j, z ^ 1)

    four = shape[0] == 4

    def to_direct(c, j, z):
        return (c ^ 1, j, z)

    def to_second(c, j, z):
        return (c ^ 2, j, z) if four else (c + 1 if c % 2 else c - 1, j, z)

    def to_far(c, j, z):
        return (c ^ 1, j, z) if four else (c - 1 if z % 2 else c + 1, j, z)

    def stage_one(c, j, z):
        if j == z % 2:
            return (c ^ 1, j, z)
        return (c ^ 2, j, z) if four and (c + z) % 2 else None

    def stage_one_cross(c, j, z):
        to = stage_one(c, j, z)
        return to and (to[0], 1 - j, z)

    first = send(own, to_home)
    half = node_feats.shape[1] // 2
    mine = lax.dynamic_slice_in_dim(node_feats, j * half, half, 1)
    yours = lax.dynamic_slice_in_dim(node_feats, (1 - j) * half, half, 1)
    one = send(mine, stage_one)
    two = send(yours, stage_one_cross)
    swapped = send(yours, sibling)
    self_choice = [("home", mine), ("away", swapped)]
    direct_choice = [("home", one), ("away", two)]
    meta = slot_blocks(tile_coords[:, 0], tile_counts[0], blocks)
    second, far = pick(
        [
            direct_choice if four else self_choice,
            [
                ("still home", swapped),
                ("still away", mine),
                ("relay home", two),
                ("relay away", one),
            ],
        ],
        [meta],
    )
    second = send(second, to_second)
    far = send(far, to_far)
    meta_b = send(meta, to_home)
    first, meta_b = lax.optimization_barrier((first, meta_b))
    other_first = send(first, home_to_sibling)
    meta_later, second = lax.optimization_barrier((meta_b, second))
    meta_far = send(meta_later, home_to_sibling)
    set_first = [(None, (meta_b, first))]
    panels = [
        ("self", [("home", mine), ("away", swapped)]),
        ("near", [("home", swapped), ("away", mine)]),
        ("direct", direct_choice),
        ("second", [(None, second)]),
        ("far", [(None, far)]),
    ]
    part = tile_product(panels, [set_first], jnp.float32, weigh=WEIGH)
    set_rest = [("home", (meta, own)), ("away", (meta_far, other_first))]
    part = tile_product(panels, [set_rest], jnp.bfloat16, part)

    def join(value):
        other = send(value, across)
        return (value.astype(jnp.float32) + other.astype(jnp.float32)).astype(jnp.bfloat16)

    near = join(part)
    far_half = send(near, sibling)
    cot, cot_yours = halves(cotangent)
    act, adj, adj_longer, adj_long = middle(
        near, far_half, weight, cot, send(cot_yours, sibling)
    )

    direct = send(adj_longer, to_direct)
    near_one = send(
        adj_long, lambda c, j, z: (c if (c + z) % 2 or not four else c ^ 2, j, z ^ 1)
    )
    second = send(direct if four else adj_longer, to_second)
    grad = grad_block(scale, near, far_half, adj)
    far = send(near_one, to_far)
    near_choice = [("still", near_one)]
    if four:
        near_two = send(
            adj, lambda c, j, z: None if (c + z) % 2 else (c, j, z ^ 1)
        )
        near_choice.append(("relay", near_two))
    panels = [("self", [(None, adj)]), ("direct", [(None, direct)])]
    back_part = tile_product(panels, [set_first, set_rest], jnp.float32)
    panels = [("second", [(None, second)]), ("far", [(None, far)]), ("near", near_choice)]
    back_part = tile_product(panels, [set_first, set_rest], jnp.bfloat16, back_part)

    def deliver(value):
        one = send(value, lambda c, j, z: (c, j, z ^ 1) if j == z % 2 else (c, 1 - j, z))
        two = send(value, lambda c, j, z: None if j == z % 2 else (c, 1 - j, z ^ 1))
        return one, two

    act_later, back_part = lax.optimization_barrier((act, back_part))
    act_parts = [act, *deliver(act_later)]
    grad, back_part = lax.optimization_barrier((grad, back_part))
    grad_got = send(grad, lambda c, j, z: (c, j, z ^ 1))
    grad = add_after([grad, grad_got], jnp.bfloat16)
    step = 1
    while step < shape[0]:
        got = send(grad, lambda c, j, z, s=step: (c ^ s, j, z))
        step *= 2
        if step < shape[0]:
            grad = add_after([grad, got], jnp.bfloat16)
    back = add_after([back_part, send(back_part, across)], jnp.bfloat16, got)
    back_parts = [back, *deliver(back)]
    grad = add_after([grad, got], jnp.float32, back, *act_parts[1:])
    activated, weight_grad = gather_halves(act_parts, grad, send(grad, sibling))
    input_grad = final(back_parts, weight)
    return (activated, input_grad, weight_grad)


def solution(mesh):
    return jax.shard_map(
        per_device,
        mesh=mesh,
        in_specs=(
            P("rows", None),
            P(),
            P("rows", None),
            P("rows", None, "rep", None, None),
            P(None, "rows", None, "rep"),
            P("rows", None),
        ),
        out_specs=(P("rows", None), P("rows", None), P()),
        check_vma=False,
    )
```

```python
import functools

import jax
import jax.numpy as jnp
from jax import lax
from jax.experimental import pallas as pl
from jax.experimental.pallas import tpu as pltpu
from jax.sharding import PartitionSpec as P

AXES = ("rows", "rep")
TOGETHER = 2
ROWS = 256
WEIGH = 75


def route(shape, move):
    chips, reps = shape
    pairs = []
    for c in range(chips):
        for j in range(2):
            for z in range(reps):
                to = move(c, j, z)
                if to is not None:
                    target = ((to[0] % chips) * 2 + to[1]) * reps + to[2]
                    pairs.append(((c * 2 + j) * reps + z, target))
    return pairs


def place():
    r = lax.axis_index("rows")
    z = lax.axis_index("rep")
    return r % 2, z, z % 2


def when_of(case):
    j, z, p = place()
    home = j == p
    relay = jnp.logical_and(
        lax.axis_size("rows") == 8, (lax.axis_index("rows") // 2 + z) % 2 == 1
    )
    return {
        "home": home,
        "away": jnp.logical_not(home),
        "relay": relay,
        "still": jnp.logical_not(relay),
        "relay home": jnp.logical_and(relay, home),
        "relay away": jnp.logical_and(relay, jnp.logical_not(home)),
        "still home": jnp.logical_and(jnp.logical_not(relay), home),
        "still away": jnp.logical_and(jnp.logical_not(relay), jnp.logical_not(home)),
    }[case]


def start_chosen(choice, make):
    if len(choice) == 1:
        make(choice[0][1]).start()
        return
    for case, ref in choice:

        @pl.when(when_of(case))
        def _(ref=ref):
            make(ref).start()


def halves_kernel(x_ref, near_ref, far_ref, sems):
    j, _, _ = place()
    half = near_ref.shape[1]
    copies = []
    for i, out in enumerate((near_ref, far_ref)):
        start = pl.multiple_of((j if i == 0 else 1 - j) * half, half)
        copy = pltpu.make_async_copy(x_ref.at[:, pl.ds(start, half)], out, sems.at[i])
        copy.start()
        copies.append(copy)
    for copy in copies:
        copy.wait()


def halves(value):
    rows, width = value.shape
    part = jax.ShapeDtypeStruct((rows, width // 2), value.dtype)
    hbm = pl.BlockSpec(memory_space=pltpu.HBM)
    return pl.pallas_call(
        halves_kernel,
        out_shape=(part, part),
        in_specs=[hbm],
        out_specs=(hbm, hbm),
        scratch_shapes=[pltpu.SemaphoreType.DMA((2,))],
        compiler_params=pltpu.CompilerParams(vmem_limit_bytes=1024 * 1024),
        name="halves",
    )(value)


def pick_kernel(cases, waits, *refs):
    refs = list(refs)
    choices = [[(case, refs.pop(0)) for case in each] for each in cases]
    outs, sems = refs[waits:-1], refs[-1]

    def copy_to(i):
        return lambda ref: pltpu.make_async_copy(ref, outs[i], sems.at[i])

    for i, choice in enumerate(choices):
        start_chosen(choice, copy_to(i))
    for i, choice in enumerate(choices):
        copy_to(i)(choice[0][1]).wait()


def pick(choices, after):
    hbm = pl.BlockSpec(memory_space=pltpu.HBM)
    arrays = [array for choice in choices for _, array in choice]
    shape = jax.ShapeDtypeStruct(arrays[0].shape, arrays[0].dtype)
    return pl.pallas_call(
        functools.partial(
            pick_kernel, [[case for case, _ in choice] for choice in choices], len(after)
        ),
        out_shape=(shape,) * len(choices),
        in_specs=[hbm] * len(arrays) + [pl.BlockSpec(memory_space=pl.ANY)] * len(after),
        out_specs=(hbm,) * len(choices),
        scratch_shapes=[pltpu.SemaphoreType.DMA((len(choices),))],
        compiler_params=pltpu.CompilerParams(vmem_limit_bytes=1024 * 1024),
        name="pick",
    )(*arrays, *after)


def slots_kernel(dead, coords_ref, counts_ref, out_ref):
    _, z, _ = place()
    _, reach, slots = coords_ref.shape
    for d in range(reach):
        for k in range(slots):
            live = z * slots + k < counts_ref[d]
            out_ref[0, d * slots + k] = jnp.where(live, coords_ref[0, d, k], dead)
            out_ref[1, d * slots + k] = coords_ref[1, d, k]


def slot_blocks(coords, counts, dead):
    smem = pl.BlockSpec(memory_space=pltpu.SMEM)
    return pl.pallas_call(
        functools.partial(slots_kernel, dead),
        out_shape=jax.ShapeDtypeStruct((2, coords.shape[1] * coords.shape[2]), jnp.int32),
        in_specs=[smem, smem],
        out_specs=smem,
        compiler_params=pltpu.CompilerParams(vmem_limit_bytes=1024 * 1024),
        name="slot_blocks",
    )(coords, counts)


def offset_of(kind):
    _, _, p = place()
    even = (lax.axis_index("rows") // 2) % 2 == 0
    return {
        "self": 2,
        "near": jnp.where(p == 0, 3, 1),
        "far": jnp.where(p == 0, 1, 3),
        "direct": jnp.where(even, 4, 0),
        "second": jnp.where(even, 0, 4),
    }[kind]


def chosen(choice, read):
    value = read(choice[0][1])
    for case, ref in choice[1:]:
        value = jnp.where(when_of(case), read(ref), value)
    return value


def tile_kernel(kinds, cases, sets, summed, waits, *refs):
    refs = list(refs)
    metas = [[(case, refs.pop(0)) for case in each] for each in sets]
    tiles = [[(case, refs.pop(0)) for case in each] for each in sets]
    panels = [[(case, refs.pop(0)) for case in each] for each in cases]
    before = refs.pop(0) if summed else None
    out_ref, acc_ref = refs[waits:]
    _, slots, tile, _ = tiles[0][0][1].shape
    rows = out_ref.shape[0]
    if summed:
        acc_ref[:rows, :] = before[...]
    else:
        acc_ref[...] = jnp.zeros_like(acc_ref)
    for i, kind in enumerate(kinds):
        d = offset_of(kind)
        for s in range(len(sets)):
            for first in range(0, slots, TOGETHER):
                prods = []
                for k in range(first, min(first + TOGETHER, slots)):
                    row = chosen(metas[s], lambda ref: ref[0, d * slots + k])
                    col = chosen(metas[s], lambda ref: ref[1, d * slots + k])
                    col = pl.multiple_of(col * tile, tile)
                    prod = jnp.dot(
                        chosen(tiles[s], lambda ref: ref[d, k]),
                        chosen(panels[i], lambda ref: ref[pl.ds(col, tile), :]),
                        preferred_element_type=jnp.float32,
                    )
                    prods.append((pl.multiple_of(row * tile, tile), prod))
                for row, prod in prods:
                    acc_ref[pl.ds(row, tile), :] += prod
    out_ref[...] = acc_ref[:rows, :].astype(out_ref.dtype)


def tile_product(named, sets, dtype, before=None, after=(), weigh=1):
    kinds = [kind for kind, _ in named]
    cases = [[case for case, _ in choice] for _, choice in named]
    panels = [panel for _, choice in named for _, panel in choice]
    metas = [meta for choice in sets for _, (meta, _) in choice]
    tiles = [values for choice in sets for _, (_, values) in choice]
    rows, width = panels[0].shape if before is None else before.shape
    _, slots, tile, _ = tiles[0].shape
    smem = pl.BlockSpec(memory_space=pltpu.SMEM)
    vmem = pl.BlockSpec(memory_space=pltpu.VMEM)
    anywhere = pl.BlockSpec(memory_space=pl.ANY)
    count = len(kinds) * len(sets) * slots
    summed = before is not None
    return pl.pallas_call(
        functools.partial(
            tile_kernel,
            kinds,
            cases,
            [[case for case, _ in choice] for choice in sets],
            summed,
            len(after),
        ),
        out_shape=jax.ShapeDtypeStruct((rows, width), dtype),
        in_specs=[smem] * len(metas)
        + [vmem] * (len(tiles) + len(panels) + summed)
        + [anywhere] * len(after),
        out_specs=vmem,
        scratch_shapes=[pltpu.VMEM((rows + tile, width), jnp.float32)],
        compiler_params=pltpu.CompilerParams(vmem_limit_bytes=12 * 1024 * 1024),
        cost_estimate=pl.CostEstimate(
            flops=weigh * 2 * count * tile * tile * width,
            bytes_accessed=weigh * (count * tile * tile * 2 + len(kinds) * rows * width * 2),
            transcendentals=0,
        ),
        name="tile_product",
    )(*metas, *tiles, *panels, *([before] if summed else []), *after)


def middle_kernel(near_ref, far_ref, w_ref, cot_ref, cot_swap_ref, act_ref, *adj_refs):
    j, _, p = place()
    near_cols, far_cols = half_columns(near_ref.shape[1])
    weight = jnp.concatenate([w_ref[near_cols, near_cols], w_ref[far_cols, near_cols]], axis=0)
    count = near_ref.shape[0]
    for start in range(0, count, ROWS):
        rows = pl.ds(start, ROWS)
        both = jnp.concatenate([near_ref[rows, :], far_ref[rows, :]], axis=1)
        agg = jnp.dot(both, weight, preferred_element_type=jnp.float32)
        sig = jax.nn.sigmoid(agg)
        act_ref[rows, :] = (agg * sig).astype(act_ref.dtype)
        slope = sig * (1.0 + agg * (1.0 - sig))
        cot = jnp.where(j == p, cot_ref[rows, :], cot_swap_ref[rows, :])
        adj = (cot.astype(jnp.float32) * slope).astype(act_ref.dtype)
        for ref in adj_refs:
            ref[rows, :] = adj
    for ref in adj_refs:
        if ref.shape[0] > count:
            ref[count:, :] = jnp.zeros((ref.shape[0] - count, ref.shape[1]), ref.dtype)


def middle(near, far, weight, cot, cot_swap):
    vmem = pl.BlockSpec(memory_space=pltpu.VMEM)
    rows, width = near.shape
    out = jax.ShapeDtypeStruct((rows, width), jnp.bfloat16)
    longer = tuple(jax.ShapeDtypeStruct((rows + n, width), jnp.bfloat16) for n in (32, 16))
    return pl.pallas_call(
        middle_kernel,
        out_shape=(out, out) + longer,
        in_specs=[vmem] * 5,
        out_specs=(vmem,) * 4,
        compiler_params=pltpu.CompilerParams(vmem_limit_bytes=8 * 1024 * 1024),
        cost_estimate=pl.CostEstimate(
            flops=4 * rows * width * width,
            bytes_accessed=10 * rows * width,
            transcendentals=rows * width,
        ),
        name="middle",
    )(near, far, weight, cot, cot_swap)


def grad_kernel(scale, near_ref, far_ref, adj_ref, out_ref):
    j, _, _ = place()
    half = near_ref.shape[1]
    dims = (((0,), (0,)), ((), ()))
    for i, ref in enumerate((near_ref, far_ref)):
        start = pl.multiple_of((j if i == 0 else 1 - j) * half, half)
        block = lax.dot_general(ref[...], adj_ref[...], dims, preferred_element_type=jnp.float32)
        out_ref[pl.ds(start, half), :] = (scale * block).astype(out_ref.dtype)


def grad_block(scale, near, far, adj):
    vmem = pl.BlockSpec(memory_space=pltpu.VMEM)
    rows, width = near.shape
    return pl.pallas_call(
        functools.partial(grad_kernel, scale),
        out_shape=jax.ShapeDtypeStruct((2 * width, width), jnp.bfloat16),
        in_specs=[vmem] * 3,
        out_specs=vmem,
        compiler_params=pltpu.CompilerParams(vmem_limit_bytes=8 * 1024 * 1024),
        cost_estimate=pl.CostEstimate(
            flops=4 * WEIGH * rows * width * width,
            bytes_accessed=8 * WEIGH * rows * width,
            transcendentals=0,
        ),
        name="grad_block",
    )(near, far, adj)


def add_kernel(count, *refs):
    values = [ref[...].astype(jnp.float32) for ref in refs[:count]]
    total = values[0] + values[1]
    if count == 4:
        total = total + (values[2] + values[3])
    refs[-1][...] = total.astype(refs[-1].dtype)


def add_after(values, dtype, *after):
    vmem = pl.BlockSpec(memory_space=pltpu.VMEM)
    return pl.pallas_call(
        functools.partial(add_kernel, len(values)),
        out_shape=jax.ShapeDtypeStruct(values[0].shape, dtype),
        in_specs=[vmem] * len(values) + [pl.BlockSpec(memory_space=pl.ANY)] * len(after),
        out_specs=vmem,
        compiler_params=pltpu.CompilerParams(vmem_limit_bytes=4 * 1024 * 1024),
        name="add_after",
    )(*values, *after)


def half_columns(half):
    j, _, _ = place()
    near = pl.ds(pl.multiple_of(j * half, half), half)
    return near, pl.ds(pl.multiple_of((1 - j) * half, half), half)


def near_and_far(parts):
    j, _, p = place()
    own, one, two = parts
    near = jnp.where(j == p, own[...], one[...])
    return near, jnp.where(j == p, one[...], two[...])


def gather_kernel(own_ref, one_ref, two_ref, grad_ref, rest_ref, act_ref, grad_out_ref):
    near_cols, far_cols = half_columns(own_ref.shape[1])
    near, far = near_and_far((own_ref, one_ref, two_ref))
    act_ref[:, near_cols] = near
    act_ref[:, far_cols] = far
    grad_out_ref[:, near_cols] = grad_ref[...]
    grad_out_ref[:, far_cols] = rest_ref[...]


def gather_halves(act, grad, rest):
    vmem = pl.BlockSpec(memory_space=pltpu.VMEM)
    rows, width = act[0].shape
    return pl.pallas_call(
        gather_kernel,
        out_shape=(
            jax.ShapeDtypeStruct((rows, 2 * width), act[0].dtype),
            jax.ShapeDtypeStruct((2 * width, 2 * width), grad.dtype),
        ),
        in_specs=[vmem] * 5,
        out_specs=(vmem, vmem),
        compiler_params=pltpu.CompilerParams(vmem_limit_bytes=8 * 1024 * 1024),
        name="gather_halves",
    )(*act, grad, rest)


def final_kernel(own_ref, one_ref, two_ref, w_ref, out_ref):
    j, _, p = place()
    near_cols, far_cols = half_columns(own_ref.shape[1])
    weight = jnp.concatenate([w_ref[:, near_cols], w_ref[:, far_cols]], axis=1)
    for start in range(0, own_ref.shape[0], ROWS):
        rows = pl.ds(start, ROWS)
        own, one, two = own_ref[rows, :], one_ref[rows, :], two_ref[rows, :]
        near, far = jnp.where(j == p, own, one), jnp.where(j == p, one, two)
        product = lax.dot_general(
            jnp.concatenate([near, far], axis=1),
            weight,
            (((1,), (1,)), ((), ())),
            preferred_element_type=jnp.float32,
        )
        out_ref[rows, :] = product.astype(out_ref.dtype)


def final(back, weight):
    vmem = pl.BlockSpec(memory_space=pltpu.VMEM)
    rows = back[0].shape[0]
    wide = weight.shape[0]
    return pl.pallas_call(
        final_kernel,
        out_shape=jax.ShapeDtypeStruct((rows, wide), jnp.bfloat16),
        in_specs=[vmem] * 4,
        out_specs=vmem,
        compiler_params=pltpu.CompilerParams(vmem_limit_bytes=8 * 1024 * 1024),
        cost_estimate=pl.CostEstimate(
            flops=2 * rows * wide * wide, bytes_accessed=8 * rows * wide, transcendentals=0
        ),
        name="final",
    )(*back, weight)


def per_device(node_feats, weight, cotangent, tile_values, tile_coords, tile_counts):
    groups = lax.axis_size("rows")
    reps = lax.axis_size("rep")
    shape = (groups // 2, reps)
    j, z, p = place()
    home = j == p
    scale = (node_feats.shape[0] * groups) ** (-0.5)

    def send(value, move):
        return lax.ppermute(value, AXES, route(shape, move))

    def sibling(c, j, z):
        return (c, 1 - j, z)

    def home_to_sibling(c, j, z):
        return (c, 1 - j, z) if j == z % 2 else None

    def across(c, j, z):
        return (c, j, (z + reps // 2) % reps)

    own = tile_values[0]
    blocks = node_feats.shape[0] // own.shape[-1]

    def to_home(c, j, z):
        return (c, 1 - j, z) if j == z % 2 else (c, j, z ^ 1)

    four = shape[0] == 4

    def to_direct(c, j, z):
        return (c ^ 1, j, z)

    def to_second(c, j, z):
        return (c ^ 2, j, z) if four else (c + 1 if c % 2 else c - 1, j, z)

    def to_far(c, j, z):
        return (c ^ 1, j, z) if four else (c - 1 if z % 2 else c + 1, j, z)

    def stage_one(c, j, z):
        if j == z % 2:
            return (c ^ 1, j, z)
        return (c ^ 2, j, z) if four and (c + z) % 2 else None

    def stage_one_cross(c, j, z):
        to = stage_one(c, j, z)
        return to and (to[0], 1 - j, z)

    first = send(own, to_home)
    half = node_feats.shape[1] // 2
    mine = lax.dynamic_slice_in_dim(node_feats, j * half, half, 1)
    yours = lax.dynamic_slice_in_dim(node_feats, (1 - j) * half, half, 1)
    one = send(mine, stage_one)
    two = send(yours, stage_one_cross)
    swapped = send(yours, sibling)
    self_choice = [("home", mine), ("away", swapped)]
    direct_choice = [("home", one), ("away", two)]
    meta = slot_blocks(tile_coords[:, 0], tile_counts[0], blocks)
    second, far = pick(
        [
            direct_choice if four else self_choice,
            [
                ("still home", swapped),
                ("still away", mine),
                ("relay home", two),
                ("relay away", one),
            ],
        ],
        [meta],
    )
    second = send(second, to_second)
    far = send(far, to_far)
    meta_b = send(meta, to_home)
    first, meta_b = lax.optimization_barrier((first, meta_b))
    other_first = send(first, home_to_sibling)
    meta_later, second = lax.optimization_barrier((meta_b, second))
    meta_far = send(meta_later, home_to_sibling)
    set_first = [(None, (meta_b, first))]
    panels = [
        ("self", [("home", mine), ("away", swapped)]),
        ("near", [("home", swapped), ("away", mine)]),
        ("direct", direct_choice),
        ("second", [(None, second)]),
        ("far", [(None, far)]),
    ]
    part = tile_product(panels, [set_first], jnp.float32, weigh=WEIGH)
    set_rest = [("home", (meta, own)), ("away", (meta_far, other_first))]
    part = tile_product(panels, [set_rest], jnp.bfloat16, part)

    def join(value):
        other = send(value, across)
        return (value.astype(jnp.float32) + other.astype(jnp.float32)).astype(jnp.bfloat16)

    near = join(part)
    far_half = send(near, sibling)
    cot, cot_yours = halves(cotangent)
    act, adj, adj_longer, adj_long = middle(
        near, far_half, weight, cot, send(cot_yours, sibling)
    )

    direct = send(adj_longer, to_direct)
    near_one = send(
        adj_long, lambda c, j, z: (c if (c + z) % 2 or not four else c ^ 2, j, z ^ 1)
    )
    second = send(direct if four else adj_longer, to_second)
    grad = grad_block(scale, near, far_half, adj)
    far = send(near_one, to_far)
    near_choice = [("still", near_one)]
    if four:
        near_two = send(
            adj, lambda c, j, z: None if (c + z) % 2 else (c, j, z ^ 1)
        )
        near_choice.append(("relay", near_two))
    panels = [("self", [(None, adj)]), ("direct", [(None, direct)])]
    back_part = tile_product(panels, [set_first, set_rest], jnp.float32)
    panels = [("second", [(None, second)]), ("far", [(None, far)]), ("near", near_choice)]
    grad_got = send(grad, lambda c, j, z: (c, j, z ^ 1))
    back_part = tile_product(
        panels, [set_first, set_rest], jnp.bfloat16, back_part, [grad_got]
    )

    def deliver(value):
        one = send(value, lambda c, j, z: (c, j, z ^ 1) if j == z % 2 else (c, 1 - j, z))
        two = send(value, lambda c, j, z: None if j == z % 2 else (c, 1 - j, z ^ 1))
        return one, two

    act_later, back_part = lax.optimization_barrier((act, back_part))
    act_parts = [act, *deliver(act_later)]
    grad = add_after([grad, grad_got], jnp.bfloat16, back_part)
    step = 1
    while step < shape[0]:
        got = send(grad, lambda c, j, z, s=step: (c ^ s, j, z))
        step *= 2
        if step < shape[0]:
            grad = add_after([grad, got], jnp.bfloat16)
    back = add_after([back_part, send(back_part, across)], jnp.bfloat16, got)
    back_parts = [back, *deliver(back)]
    grad = add_after([grad, got], jnp.float32, back, *act_parts[1:])
    activated, weight_grad = gather_halves(act_parts, grad, send(grad, sibling))
    input_grad = final(back_parts, weight)
    return (activated, input_grad, weight_grad)


def solution(mesh):
    return jax.shard_map(
        per_device,
        mesh=mesh,
        in_specs=(
            P("rows", None),
            P(),
            P("rows", None),
            P("rows", None, "rep", None, None),
            P(None, "rows", None, "rep"),
            P("rows", None),
        ),
        out_specs=(P("rows", None), P("rows", None), P()),
        check_vma=False,
    )
```

```python
import functools

import jax
import jax.numpy as jnp
from jax import lax
from jax.experimental import pallas as pl
from jax.experimental.pallas import tpu as pltpu
from jax.sharding import PartitionSpec as P

AXES = ("rows", "rep")
TOGETHER = 2
ROWS = 256
WEIGH = 180


def route(shape, move):
    chips, reps = shape
    pairs = []
    for c in range(chips):
        for j in range(2):
            for z in range(reps):
                to = move(c, j, z)
                if to is not None:
                    target = ((to[0] % chips) * 2 + to[1]) * reps + to[2]
                    pairs.append(((c * 2 + j) * reps + z, target))
    return pairs


def place():
    r = lax.axis_index("rows")
    z = lax.axis_index("rep")
    return r % 2, z, z % 2


def when_of(case):
    j, z, p = place()
    home = j == p
    relay = jnp.logical_and(
        lax.axis_size("rows") == 8, (lax.axis_index("rows") // 2 + z) % 2 == 1
    )
    return {
        "home": home,
        "away": jnp.logical_not(home),
        "relay": relay,
        "still": jnp.logical_not(relay),
        "relay home": jnp.logical_and(relay, home),
        "relay away": jnp.logical_and(relay, jnp.logical_not(home)),
        "still home": jnp.logical_and(jnp.logical_not(relay), home),
        "still away": jnp.logical_and(jnp.logical_not(relay), jnp.logical_not(home)),
    }[case]


def start_chosen(choice, make):
    if len(choice) == 1:
        make(choice[0][1]).start()
        return
    for case, ref in choice:

        @pl.when(when_of(case))
        def _(ref=ref):
            make(ref).start()


def halves_kernel(x_ref, near_ref, far_ref, sems):
    j, _, _ = place()
    half = near_ref.shape[1]
    copies = []
    for i, out in enumerate((near_ref, far_ref)):
        start = pl.multiple_of((j if i == 0 else 1 - j) * half, half)
        copy = pltpu.make_async_copy(x_ref.at[:, pl.ds(start, half)], out, sems.at[i])
        copy.start()
        copies.append(copy)
    for copy in copies:
        copy.wait()


def halves(value):
    rows, width = value.shape
    part = jax.ShapeDtypeStruct((rows, width // 2), value.dtype)
    hbm = pl.BlockSpec(memory_space=pltpu.HBM)
    return pl.pallas_call(
        halves_kernel,
        out_shape=(part, part),
        in_specs=[hbm],
        out_specs=(hbm, hbm),
        scratch_shapes=[pltpu.SemaphoreType.DMA((2,))],
        compiler_params=pltpu.CompilerParams(vmem_limit_bytes=1024 * 1024),
        name="halves",
    )(value)


def pick_kernel(cases, waits, *refs):
    refs = list(refs)
    choices = [[(case, refs.pop(0)) for case in each] for each in cases]
    outs, sems = refs[waits:-1], refs[-1]

    def copy_to(i):
        return lambda ref: pltpu.make_async_copy(ref, outs[i], sems.at[i])

    for i, choice in enumerate(choices):
        start_chosen(choice, copy_to(i))
    for i, choice in enumerate(choices):
        copy_to(i)(choice[0][1]).wait()


def pick(choices, after):
    hbm = pl.BlockSpec(memory_space=pltpu.HBM)
    arrays = [array for choice in choices for _, array in choice]
    shape = jax.ShapeDtypeStruct(arrays[0].shape, arrays[0].dtype)
    return pl.pallas_call(
        functools.partial(
            pick_kernel, [[case for case, _ in choice] for choice in choices], len(after)
        ),
        out_shape=(shape,) * len(choices),
        in_specs=[hbm] * len(arrays) + [pl.BlockSpec(memory_space=pl.ANY)] * len(after),
        out_specs=(hbm,) * len(choices),
        scratch_shapes=[pltpu.SemaphoreType.DMA((len(choices),))],
        compiler_params=pltpu.CompilerParams(vmem_limit_bytes=1024 * 1024),
        name="pick",
    )(*arrays, *after)


def slots_kernel(dead, coords_ref, counts_ref, out_ref):
    _, z, _ = place()
    _, reach, slots = coords_ref.shape
    for d in range(reach):
        for k in range(slots):
            live = z * slots + k < counts_ref[d]
            out_ref[0, d * slots + k] = jnp.where(live, coords_ref[0, d, k], dead)
            out_ref[1, d * slots + k] = coords_ref[1, d, k]


def slot_blocks(coords, counts, dead):
    smem = pl.BlockSpec(memory_space=pltpu.SMEM)
    return pl.pallas_call(
        functools.partial(slots_kernel, dead),
        out_shape=jax.ShapeDtypeStruct((2, coords.shape[1] * coords.shape[2]), jnp.int32),
        in_specs=[smem, smem],
        out_specs=smem,
        compiler_params=pltpu.CompilerParams(vmem_limit_bytes=1024 * 1024),
        name="slot_blocks",
    )(coords, counts)


def offset_of(kind):
    _, _, p = place()
    even = (lax.axis_index("rows") // 2) % 2 == 0
    return {
        "self": 2,
        "near": jnp.where(p == 0, 3, 1),
        "far": jnp.where(p == 0, 1, 3),
        "direct": jnp.where(even, 4, 0),
        "second": jnp.where(even, 0, 4),
    }[kind]


def chosen(choice, read):
    value = read(choice[0][1])
    for case, ref in choice[1:]:
        value = jnp.where(when_of(case), read(ref), value)
    return value


def tile_kernel(kinds, cases, sets, summed, waits, *refs):
    refs = list(refs)
    metas = [[(case, refs.pop(0)) for case in each] for each in sets]
    tiles = [[(case, refs.pop(0)) for case in each] for each in sets]
    panels = [[(case, refs.pop(0)) for case in each] for each in cases]
    before = refs.pop(0) if summed else None
    out_ref, acc_ref = refs[waits:]
    _, slots, tile, _ = tiles[0][0][1].shape
    rows = out_ref.shape[0]
    if summed:
        acc_ref[:rows, :] = before[...]
    else:
        acc_ref[...] = jnp.zeros_like(acc_ref)
    for i, kind in enumerate(kinds):
        d = offset_of(kind)
        for s in range(len(sets)):
            for first in range(0, slots, TOGETHER):
                prods = []
                for k in range(first, min(first + TOGETHER, slots)):
                    row = chosen(metas[s], lambda ref: ref[0, d * slots + k])
                    col = chosen(metas[s], lambda ref: ref[1, d * slots + k])
                    col = pl.multiple_of(col * tile, tile)
                    prod = jnp.dot(
                        chosen(tiles[s], lambda ref: ref[d, k]),
                        chosen(panels[i], lambda ref: ref[pl.ds(col, tile), :]),
                        preferred_element_type=jnp.float32,
                    )
                    prods.append((pl.multiple_of(row * tile, tile), prod))
                for row, prod in prods:
                    acc_ref[pl.ds(row, tile), :] += prod
    out_ref[...] = acc_ref[:rows, :].astype(out_ref.dtype)


def tile_product(named, sets, dtype, before=None, after=(), weigh=1):
    kinds = [kind for kind, _ in named]
    cases = [[case for case, _ in choice] for _, choice in named]
    panels = [panel for _, choice in named for _, panel in choice]
    metas = [meta for choice in sets for _, (meta, _) in choice]
    tiles = [values for choice in sets for _, (_, values) in choice]
    rows, width = panels[0].shape if before is None else before.shape
    _, slots, tile, _ = tiles[0].shape
    smem = pl.BlockSpec(memory_space=pltpu.SMEM)
    vmem = pl.BlockSpec(memory_space=pltpu.VMEM)
    anywhere = pl.BlockSpec(memory_space=pl.ANY)
    count = len(kinds) * len(sets) * slots
    summed = before is not None
    return pl.pallas_call(
        functools.partial(
            tile_kernel,
            kinds,
            cases,
            [[case for case, _ in choice] for choice in sets],
            summed,
            len(after),
        ),
        out_shape=jax.ShapeDtypeStruct((rows, width), dtype),
        in_specs=[smem] * len(metas)
        + [vmem] * (len(tiles) + len(panels) + summed)
        + [anywhere] * len(after),
        out_specs=vmem,
        scratch_shapes=[pltpu.VMEM((rows + tile, width), jnp.float32)],
        compiler_params=pltpu.CompilerParams(vmem_limit_bytes=12 * 1024 * 1024),
        cost_estimate=pl.CostEstimate(
            flops=weigh * 2 * count * tile * tile * width,
            bytes_accessed=weigh * (count * tile * tile * 2 + len(kinds) * rows * width * 2),
            transcendentals=0,
        ),
        name="tile_product",
    )(*metas, *tiles, *panels, *([before] if summed else []), *after)


def middle_kernel(near_ref, far_ref, w_ref, cot_ref, cot_swap_ref, act_ref, *adj_refs):
    j, _, p = place()
    near_cols, far_cols = half_columns(near_ref.shape[1])
    weight = jnp.concatenate([w_ref[near_cols, near_cols], w_ref[far_cols, near_cols]], axis=0)
    count = near_ref.shape[0]
    for start in range(0, count, ROWS):
        rows = pl.ds(start, ROWS)
        both = jnp.concatenate([near_ref[rows, :], far_ref[rows, :]], axis=1)
        agg = jnp.dot(both, weight, preferred_element_type=jnp.float32)
        sig = jax.nn.sigmoid(agg)
        act_ref[rows, :] = (agg * sig).astype(act_ref.dtype)
        slope = sig * (1.0 + agg * (1.0 - sig))
        cot = jnp.where(j == p, cot_ref[rows, :], cot_swap_ref[rows, :])
        adj = (cot.astype(jnp.float32) * slope).astype(act_ref.dtype)
        for ref in adj_refs:
            ref[rows, :] = adj
    for ref in adj_refs:
        if ref.shape[0] > count:
            ref[count:, :] = jnp.zeros((ref.shape[0] - count, ref.shape[1]), ref.dtype)


def middle(near, far, weight, cot, cot_swap):
    vmem = pl.BlockSpec(memory_space=pltpu.VMEM)
    rows, width = near.shape
    out = jax.ShapeDtypeStruct((rows, width), jnp.bfloat16)
    longer = tuple(jax.ShapeDtypeStruct((rows + n, width), jnp.bfloat16) for n in (32, 16))
    return pl.pallas_call(
        middle_kernel,
        out_shape=(out, out) + longer,
        in_specs=[vmem] * 5,
        out_specs=(vmem,) * 4,
        compiler_params=pltpu.CompilerParams(vmem_limit_bytes=8 * 1024 * 1024),
        cost_estimate=pl.CostEstimate(
            flops=4 * rows * width * width,
            bytes_accessed=10 * rows * width,
            transcendentals=rows * width,
        ),
        name="middle",
    )(near, far, weight, cot, cot_swap)


def grad_kernel(scale, near_ref, far_ref, adj_ref, out_ref):
    j, _, _ = place()
    half = near_ref.shape[1]
    dims = (((0,), (0,)), ((), ()))
    for i, ref in enumerate((near_ref, far_ref)):
        start = pl.multiple_of((j if i == 0 else 1 - j) * half, half)
        block = lax.dot_general(ref[...], adj_ref[...], dims, preferred_element_type=jnp.float32)
        out_ref[pl.ds(start, half), :] = (scale * block).astype(out_ref.dtype)


def grad_block(scale, near, far, adj):
    vmem = pl.BlockSpec(memory_space=pltpu.VMEM)
    rows, width = near.shape
    return pl.pallas_call(
        functools.partial(grad_kernel, scale),
        out_shape=jax.ShapeDtypeStruct((2 * width, width), jnp.bfloat16),
        in_specs=[vmem] * 3,
        out_specs=vmem,
        compiler_params=pltpu.CompilerParams(vmem_limit_bytes=8 * 1024 * 1024),
        cost_estimate=pl.CostEstimate(
            flops=4 * WEIGH * rows * width * width,
            bytes_accessed=8 * WEIGH * rows * width,
            transcendentals=0,
        ),
        name="grad_block",
    )(near, far, adj)


def add_kernel(count, *refs):
    values = [ref[...].astype(jnp.float32) for ref in refs[:count]]
    total = values[0] + values[1]
    if count == 4:
        total = total + (values[2] + values[3])
    refs[-1][...] = total.astype(refs[-1].dtype)


def add_after(values, dtype, *after):
    vmem = pl.BlockSpec(memory_space=pltpu.VMEM)
    return pl.pallas_call(
        functools.partial(add_kernel, len(values)),
        out_shape=jax.ShapeDtypeStruct(values[0].shape, dtype),
        in_specs=[vmem] * len(values) + [pl.BlockSpec(memory_space=pl.ANY)] * len(after),
        out_specs=vmem,
        compiler_params=pltpu.CompilerParams(vmem_limit_bytes=4 * 1024 * 1024),
        name="add_after",
    )(*values, *after)


def half_columns(half):
    j, _, _ = place()
    near = pl.ds(pl.multiple_of(j * half, half), half)
    return near, pl.ds(pl.multiple_of((1 - j) * half, half), half)


def near_and_far(parts):
    j, _, p = place()
    own, one, two = parts
    near = jnp.where(j == p, own[...], one[...])
    return near, jnp.where(j == p, one[...], two[...])


def gather_kernel(own_ref, one_ref, two_ref, grad_ref, rest_ref, act_ref, grad_out_ref):
    near_cols, far_cols = half_columns(own_ref.shape[1])
    near, far = near_and_far((own_ref, one_ref, two_ref))
    act_ref[:, near_cols] = near
    act_ref[:, far_cols] = far
    grad_out_ref[:, near_cols] = grad_ref[...]
    grad_out_ref[:, far_cols] = rest_ref[...]


def gather_halves(act, grad, rest):
    vmem = pl.BlockSpec(memory_space=pltpu.VMEM)
    rows, width = act[0].shape
    return pl.pallas_call(
        gather_kernel,
        out_shape=(
            jax.ShapeDtypeStruct((rows, 2 * width), act[0].dtype),
            jax.ShapeDtypeStruct((2 * width, 2 * width), grad.dtype),
        ),
        in_specs=[vmem] * 5,
        out_specs=(vmem, vmem),
        compiler_params=pltpu.CompilerParams(vmem_limit_bytes=8 * 1024 * 1024),
        name="gather_halves",
    )(*act, grad, rest)


def final_kernel(own_ref, one_ref, two_ref, w_ref, out_ref):
    j, _, p = place()
    near_cols, far_cols = half_columns(own_ref.shape[1])
    weight = jnp.concatenate([w_ref[:, near_cols], w_ref[:, far_cols]], axis=1)
    for start in range(0, own_ref.shape[0], ROWS):
        rows = pl.ds(start, ROWS)
        own, one, two = own_ref[rows, :], one_ref[rows, :], two_ref[rows, :]
        near, far = jnp.where(j == p, own, one), jnp.where(j == p, one, two)
        product = lax.dot_general(
            jnp.concatenate([near, far], axis=1),
            weight,
            (((1,), (1,)), ((), ())),
            preferred_element_type=jnp.float32,
        )
        out_ref[rows, :] = product.astype(out_ref.dtype)


def final(back, weight):
    vmem = pl.BlockSpec(memory_space=pltpu.VMEM)
    rows = back[0].shape[0]
    wide = weight.shape[0]
    return pl.pallas_call(
        final_kernel,
        out_shape=jax.ShapeDtypeStruct((rows, wide), jnp.bfloat16),
        in_specs=[vmem] * 4,
        out_specs=vmem,
        compiler_params=pltpu.CompilerParams(vmem_limit_bytes=8 * 1024 * 1024),
        cost_estimate=pl.CostEstimate(
            flops=2 * rows * wide * wide, bytes_accessed=8 * rows * wide, transcendentals=0
        ),
        name="final",
    )(*back, weight)


def per_device(node_feats, weight, cotangent, tile_values, tile_coords, tile_counts):
    groups = lax.axis_size("rows")
    reps = lax.axis_size("rep")
    shape = (groups // 2, reps)
    j, z, p = place()
    home = j == p
    scale = (node_feats.shape[0] * groups) ** (-0.5)

    def send(value, move):
        return lax.ppermute(value, AXES, route(shape, move))

    def sibling(c, j, z):
        return (c, 1 - j, z)

    def home_to_sibling(c, j, z):
        return (c, 1 - j, z) if j == z % 2 else None

    def across(c, j, z):
        return (c, j, (z + reps // 2) % reps)

    own = tile_values[0]
    blocks = node_feats.shape[0] // own.shape[-1]

    def to_home(c, j, z):
        return (c, 1 - j, z) if j == z % 2 else (c, j, z ^ 1)

    four = shape[0] == 4

    def to_direct(c, j, z):
        return (c ^ 1, j, z)

    def to_second(c, j, z):
        return (c ^ 2, j, z) if four else (c + 1 if c % 2 else c - 1, j, z)

    def to_far(c, j, z):
        return (c ^ 1, j, z) if four else (c - 1 if z % 2 else c + 1, j, z)

    def stage_one(c, j, z):
        if j == z % 2:
            return (c ^ 1, j, z)
        return (c ^ 2, j, z) if four and (c + z) % 2 else None

    def stage_one_cross(c, j, z):
        to = stage_one(c, j, z)
        return to and (to[0], 1 - j, z)

    first = send(own, to_home)
    half = node_feats.shape[1] // 2
    mine = lax.dynamic_slice_in_dim(node_feats, j * half, half, 1)
    yours = lax.dynamic_slice_in_dim(node_feats, (1 - j) * half, half, 1)
    one = send(mine, stage_one)
    two = send(yours, stage_one_cross)
    swapped = send(yours, sibling)
    self_choice = [("home", mine), ("away", swapped)]
    direct_choice = [("home", one), ("away", two)]
    meta = slot_blocks(tile_coords[:, 0], tile_counts[0], blocks)
    second, far = pick(
        [
            direct_choice if four else self_choice,
            [
                ("still home", swapped),
                ("still away", mine),
                ("relay home", two),
                ("relay away", one),
            ],
        ],
        [meta],
    )
    second = send(second, to_second)
    far = send(far, to_far)
    meta_b = send(meta, to_home)
    first, meta_b = lax.optimization_barrier((first, meta_b))
    other_first = send(first, home_to_sibling)
    meta_later, second = lax.optimization_barrier((meta_b, second))
    meta_far = send(meta_later, home_to_sibling)
    set_first = [(None, (meta_b, first))]
    set_rest = [("home", (meta, own)), ("away", (meta_far, other_first))]
    early = [
        ("self", [("home", mine), ("away", swapped)]),
        ("near", [("home", swapped), ("away", mine)]),
        ("direct", direct_choice),
    ]
    late = [("second", [(None, second)]), ("far", [(None, far)])]
    part = tile_product(early, [set_first], jnp.float32)
    part = tile_product(late, [set_first], jnp.float32, part, weigh=WEIGH)
    part = tile_product(early + late, [set_rest], jnp.bfloat16, part)

    def join(value):
        other = send(value, across)
        return (value.astype(jnp.float32) + other.astype(jnp.float32)).astype(jnp.bfloat16)

    near = join(part)
    far_half = send(near, sibling)
    cot, cot_yours = halves(cotangent)
    act, adj, adj_longer, adj_long = middle(
        near, far_half, weight, cot, send(cot_yours, sibling)
    )

    direct = send(adj_longer, to_direct)
    near_one = send(
        adj_long, lambda c, j, z: (c if (c + z) % 2 or not four else c ^ 2, j, z ^ 1)
    )
    second = send(direct if four else adj_longer, to_second)
    grad = grad_block(scale, near, far_half, adj)
    far = send(near_one, to_far)
    near_choice = [("still", near_one)]
    if four:
        near_two = send(
            adj, lambda c, j, z: None if (c + z) % 2 else (c, j, z ^ 1)
        )
        near_choice.append(("relay", near_two))
    panels = [("self", [(None, adj)]), ("direct", [(None, direct)])]
    back_part = tile_product(panels, [set_first, set_rest], jnp.float32)
    panels = [("second", [(None, second)]), ("far", [(None, far)]), ("near", near_choice)]
    grad_got = send(grad, lambda c, j, z: (c, j, z ^ 1))
    back_part = tile_product(
        panels, [set_first, set_rest], jnp.bfloat16, back_part, [grad_got]
    )

    def deliver(value):
        one = send(value, lambda c, j, z: (c, j, z ^ 1) if j == z % 2 else (c, 1 - j, z))
        two = send(value, lambda c, j, z: None if j == z % 2 else (c, 1 - j, z ^ 1))
        return one, two

    act_later, back_part = lax.optimization_barrier((act, back_part))
    act_parts = [act, *deliver(act_later)]
    grad = add_after([grad, grad_got], jnp.bfloat16, back_part)
    step = 1
    while step < shape[0]:
        got = send(grad, lambda c, j, z, s=step: (c ^ s, j, z))
        step *= 2
        if step < shape[0]:
            grad = add_after([grad, got], jnp.bfloat16)
    back = add_after([back_part, send(back_part, across)], jnp.bfloat16, got)
    back_parts = [back, *deliver(back)]
    grad = add_after([grad, got], jnp.float32, back, *act_parts[1:])
    activated, weight_grad = gather_halves(act_parts, grad, send(grad, sibling))
    input_grad = final(back_parts, weight)
    return (activated, input_grad, weight_grad)


def solution(mesh):
    return jax.shard_map(
        per_device,
        mesh=mesh,
        in_specs=(
            P("rows", None),
            P(),
            P("rows", None),
            P("rows", None, "rep", None, None),
            P(None, "rows", None, "rep"),
            P("rows", None),
        ),
        out_specs=(P("rows", None), P("rows", None), P()),
        check_vma=False,
    )
```

```python
import functools

import jax
import jax.numpy as jnp
from jax import lax
from jax.experimental import pallas as pl
from jax.experimental.pallas import tpu as pltpu
from jax.sharding import PartitionSpec as P

AXES = ("rows", "rep")
TOGETHER = 2
ROWS = 256
WEIGH = 75


def route(shape, move):
    chips, reps = shape
    pairs = []
    for c in range(chips):
        for j in range(2):
            for z in range(reps):
                to = move(c, j, z)
                if to is not None:
                    target = ((to[0] % chips) * 2 + to[1]) * reps + to[2]
                    pairs.append(((c * 2 + j) * reps + z, target))
    return pairs


def place():
    r = lax.axis_index("rows")
    z = lax.axis_index("rep")
    return r % 2, z, z % 2


def when_of(case):
    j, z, p = place()
    home = j == p
    relay = jnp.logical_and(
        lax.axis_size("rows") == 8, (lax.axis_index("rows") // 2 + z) % 2 == 1
    )
    return {
        "home": home,
        "away": jnp.logical_not(home),
        "relay": relay,
        "still": jnp.logical_not(relay),
        "relay home": jnp.logical_and(relay, home),
        "relay away": jnp.logical_and(relay, jnp.logical_not(home)),
        "still home": jnp.logical_and(jnp.logical_not(relay), home),
        "still away": jnp.logical_and(jnp.logical_not(relay), jnp.logical_not(home)),
    }[case]


def start_chosen(choice, make):
    if len(choice) == 1:
        make(choice[0][1]).start()
        return
    for case, ref in choice:

        @pl.when(when_of(case))
        def _(ref=ref):
            make(ref).start()


def halves_kernel(x_ref, near_ref, far_ref, sems):
    j, _, _ = place()
    half = near_ref.shape[1]
    copies = []
    for i, out in enumerate((near_ref, far_ref)):
        start = pl.multiple_of((j if i == 0 else 1 - j) * half, half)
        copy = pltpu.make_async_copy(x_ref.at[:, pl.ds(start, half)], out, sems.at[i])
        copy.start()
        copies.append(copy)
    for copy in copies:
        copy.wait()


def halves(value):
    rows, width = value.shape
    part = jax.ShapeDtypeStruct((rows, width // 2), value.dtype)
    hbm = pl.BlockSpec(memory_space=pltpu.HBM)
    return pl.pallas_call(
        halves_kernel,
        out_shape=(part, part),
        in_specs=[hbm],
        out_specs=(hbm, hbm),
        scratch_shapes=[pltpu.SemaphoreType.DMA((2,))],
        compiler_params=pltpu.CompilerParams(vmem_limit_bytes=1024 * 1024),
        name="halves",
    )(value)


def pick_kernel(cases, waits, *refs):
    refs = list(refs)
    choices = [[(case, refs.pop(0)) for case in each] for each in cases]
    outs, sems = refs[waits:-1], refs[-1]

    def copy_to(i):
        return lambda ref: pltpu.make_async_copy(ref, outs[i], sems.at[i])

    for i, choice in enumerate(choices):
        start_chosen(choice, copy_to(i))
    for i, choice in enumerate(choices):
        copy_to(i)(choice[0][1]).wait()


def pick(choices, after):
    hbm = pl.BlockSpec(memory_space=pltpu.HBM)
    arrays = [array for choice in choices for _, array in choice]
    shape = jax.ShapeDtypeStruct(arrays[0].shape, arrays[0].dtype)
    return pl.pallas_call(
        functools.partial(
            pick_kernel, [[case for case, _ in choice] for choice in choices], len(after)
        ),
        out_shape=(shape,) * len(choices),
        in_specs=[hbm] * len(arrays) + [pl.BlockSpec(memory_space=pl.ANY)] * len(after),
        out_specs=(hbm,) * len(choices),
        scratch_shapes=[pltpu.SemaphoreType.DMA((len(choices),))],
        compiler_params=pltpu.CompilerParams(vmem_limit_bytes=1024 * 1024),
        name="pick",
    )(*arrays, *after)


def slots_kernel(dead, coords_ref, counts_ref, out_ref):
    _, z, _ = place()
    _, reach, slots = coords_ref.shape
    for d in range(reach):
        for k in range(slots):
            live = z * slots + k < counts_ref[d]
            out_ref[0, d * slots + k] = jnp.where(live, coords_ref[0, d, k], dead)
            out_ref[1, d * slots + k] = coords_ref[1, d, k]


def slot_blocks(coords, counts, dead):
    smem = pl.BlockSpec(memory_space=pltpu.SMEM)
    return pl.pallas_call(
        functools.partial(slots_kernel, dead),
        out_shape=jax.ShapeDtypeStruct((2, coords.shape[1] * coords.shape[2]), jnp.int32),
        in_specs=[smem, smem],
        out_specs=smem,
        compiler_params=pltpu.CompilerParams(vmem_limit_bytes=1024 * 1024),
        name="slot_blocks",
    )(coords, counts)


def offset_of(kind):
    _, _, p = place()
    even = (lax.axis_index("rows") // 2) % 2 == 0
    return {
        "self": 2,
        "near": jnp.where(p == 0, 3, 1),
        "far": jnp.where(p == 0, 1, 3),
        "direct": jnp.where(even, 4, 0),
        "second": jnp.where(even, 0, 4),
    }[kind]


def chosen(choice, read):
    value = read(choice[0][1])
    for case, ref in choice[1:]:
        value = jnp.where(when_of(case), read(ref), value)
    return value


def tile_kernel(kinds, cases, sets, summed, waits, *refs):
    refs = list(refs)
    metas = [[(case, refs.pop(0)) for case in each] for each in sets]
    tiles = [[(case, refs.pop(0)) for case in each] for each in sets]
    panels = [[(case, refs.pop(0)) for case in each] for each in cases]
    before = refs.pop(0) if summed else None
    out_ref, acc_ref = refs[waits:]
    _, slots, tile, _ = tiles[0][0][1].shape
    rows = out_ref.shape[0]
    if summed:
        acc_ref[:rows, :] = before[...]
    else:
        acc_ref[...] = jnp.zeros_like(acc_ref)
    for i, kind in enumerate(kinds):
        d = offset_of(kind)
        for s in range(len(sets)):
            for first in range(0, slots, TOGETHER):
                prods = []
                for k in range(first, min(first + TOGETHER, slots)):
                    row = chosen(metas[s], lambda ref: ref[0, d * slots + k])
                    col = chosen(metas[s], lambda ref: ref[1, d * slots + k])
                    col = pl.multiple_of(col * tile, tile)
                    prod = jnp.dot(
                        chosen(tiles[s], lambda ref: ref[d, k]),
                        chosen(panels[i], lambda ref: ref[pl.ds(col, tile), :]),
                        preferred_element_type=jnp.float32,
                    )
                    prods.append((pl.multiple_of(row * tile, tile), prod))
                for row, prod in prods:
                    acc_ref[pl.ds(row, tile), :] += prod
    out_ref[...] = acc_ref[:rows, :].astype(out_ref.dtype)


def tile_product(named, sets, dtype, before=None, after=(), weigh=1):
    kinds = [kind for kind, _ in named]
    cases = [[case for case, _ in choice] for _, choice in named]
    panels = [panel for _, choice in named for _, panel in choice]
    metas = [meta for choice in sets for _, (meta, _) in choice]
    tiles = [values for choice in sets for _, (_, values) in choice]
    rows, width = panels[0].shape if before is None else before.shape
    _, slots, tile, _ = tiles[0].shape
    smem = pl.BlockSpec(memory_space=pltpu.SMEM)
    vmem = pl.BlockSpec(memory_space=pltpu.VMEM)
    anywhere = pl.BlockSpec(memory_space=pl.ANY)
    count = len(kinds) * len(sets) * slots
    summed = before is not None
    return pl.pallas_call(
        functools.partial(
            tile_kernel,
            kinds,
            cases,
            [[case for case, _ in choice] for choice in sets],
            summed,
            len(after),
        ),
        out_shape=jax.ShapeDtypeStruct((rows, width), dtype),
        in_specs=[smem] * len(metas)
        + [vmem] * (len(tiles) + len(panels) + summed)
        + [anywhere] * len(after),
        out_specs=vmem,
        scratch_shapes=[pltpu.VMEM((rows + tile, width), jnp.float32)],
        compiler_params=pltpu.CompilerParams(vmem_limit_bytes=12 * 1024 * 1024),
        cost_estimate=pl.CostEstimate(
            flops=weigh * 2 * count * tile * tile * width,
            bytes_accessed=weigh * (count * tile * tile * 2 + len(kinds) * rows * width * 2),
            transcendentals=0,
        ),
        name="tile_product",
    )(*metas, *tiles, *panels, *([before] if summed else []), *after)


def middle_kernel(near_ref, far_ref, w_ref, cot_ref, cot_swap_ref, act_ref, *adj_refs):
    j, _, p = place()
    near_cols, far_cols = half_columns(near_ref.shape[1])
    weight = jnp.concatenate([w_ref[near_cols, near_cols], w_ref[far_cols, near_cols]], axis=0)
    count = near_ref.shape[0]
    for start in range(0, count, ROWS):
        rows = pl.ds(start, ROWS)
        both = jnp.concatenate([near_ref[rows, :], far_ref[rows, :]], axis=1)
        agg = jnp.dot(both, weight, preferred_element_type=jnp.float32)
        sig = jax.nn.sigmoid(agg)
        act_ref[rows, :] = (agg * sig).astype(act_ref.dtype)
        slope = sig * (1.0 + agg * (1.0 - sig))
        cot = jnp.where(j == p, cot_ref[rows, :], cot_swap_ref[rows, :])
        adj = (cot.astype(jnp.float32) * slope).astype(act_ref.dtype)
        for ref in adj_refs:
            ref[rows, :] = adj
    for ref in adj_refs:
        if ref.shape[0] > count:
            ref[count:, :] = jnp.zeros((ref.shape[0] - count, ref.shape[1]), ref.dtype)


def middle(near, far, weight, cot, cot_swap):
    vmem = pl.BlockSpec(memory_space=pltpu.VMEM)
    rows, width = near.shape
    out = jax.ShapeDtypeStruct((rows, width), jnp.bfloat16)
    longer = tuple(jax.ShapeDtypeStruct((rows + n, width), jnp.bfloat16) for n in (32, 16))
    return pl.pallas_call(
        middle_kernel,
        out_shape=(out, out) + longer,
        in_specs=[vmem] * 5,
        out_specs=(vmem,) * 4,
        compiler_params=pltpu.CompilerParams(vmem_limit_bytes=8 * 1024 * 1024),
        cost_estimate=pl.CostEstimate(
            flops=4 * rows * width * width,
            bytes_accessed=10 * rows * width,
            transcendentals=rows * width,
        ),
        name="middle",
    )(near, far, weight, cot, cot_swap)


def grad_kernel(scale, near_ref, far_ref, adj_ref, out_ref):
    j, _, _ = place()
    half = near_ref.shape[1]
    dims = (((0,), (0,)), ((), ()))
    for i, ref in enumerate((near_ref, far_ref)):
        start = pl.multiple_of((j if i == 0 else 1 - j) * half, half)
        block = lax.dot_general(ref[...], adj_ref[...], dims, preferred_element_type=jnp.float32)
        out_ref[pl.ds(start, half), :] = (scale * block).astype(out_ref.dtype)


def grad_block(scale, near, far, adj):
    vmem = pl.BlockSpec(memory_space=pltpu.VMEM)
    rows, width = near.shape
    return pl.pallas_call(
        functools.partial(grad_kernel, scale),
        out_shape=jax.ShapeDtypeStruct((2 * width, width), jnp.bfloat16),
        in_specs=[vmem] * 3,
        out_specs=vmem,
        compiler_params=pltpu.CompilerParams(vmem_limit_bytes=8 * 1024 * 1024),
        cost_estimate=pl.CostEstimate(
            flops=4 * WEIGH * rows * width * width,
            bytes_accessed=8 * WEIGH * rows * width,
            transcendentals=0,
        ),
        name="grad_block",
    )(near, far, adj)


def add_kernel(count, *refs):
    values = [ref[...].astype(jnp.float32) for ref in refs[:count]]
    total = values[0] + values[1]
    if count == 4:
        total = total + (values[2] + values[3])
    refs[-1][...] = total.astype(refs[-1].dtype)


def add_after(values, dtype, *after):
    vmem = pl.BlockSpec(memory_space=pltpu.VMEM)
    return pl.pallas_call(
        functools.partial(add_kernel, len(values)),
        out_shape=jax.ShapeDtypeStruct(values[0].shape, dtype),
        in_specs=[vmem] * len(values) + [pl.BlockSpec(memory_space=pl.ANY)] * len(after),
        out_specs=vmem,
        compiler_params=pltpu.CompilerParams(vmem_limit_bytes=4 * 1024 * 1024),
        name="add_after",
    )(*values, *after)


def half_columns(half):
    j, _, _ = place()
    near = pl.ds(pl.multiple_of(j * half, half), half)
    return near, pl.ds(pl.multiple_of((1 - j) * half, half), half)


def near_and_far(parts):
    j, _, p = place()
    own, one, two = parts
    near = jnp.where(j == p, own[...], one[...])
    return near, jnp.where(j == p, one[...], two[...])


def gather_kernel(own_ref, one_ref, two_ref, grad_ref, rest_ref, act_ref, grad_out_ref):
    near_cols, far_cols = half_columns(own_ref.shape[1])
    near, far = near_and_far((own_ref, one_ref, two_ref))
    act_ref[:, near_cols] = near
    act_ref[:, far_cols] = far
    grad_out_ref[:, near_cols] = grad_ref[...]
    grad_out_ref[:, far_cols] = rest_ref[...]


def gather_halves(act, grad, rest):
    vmem = pl.BlockSpec(memory_space=pltpu.VMEM)
    rows, width = act[0].shape
    return pl.pallas_call(
        gather_kernel,
        out_shape=(
            jax.ShapeDtypeStruct((rows, 2 * width), act[0].dtype),
            jax.ShapeDtypeStruct((2 * width, 2 * width), grad.dtype),
        ),
        in_specs=[vmem] * 5,
        out_specs=(vmem, vmem),
        compiler_params=pltpu.CompilerParams(vmem_limit_bytes=8 * 1024 * 1024),
        name="gather_halves",
    )(*act, grad, rest)


def final_kernel(own_ref, one_ref, two_ref, w_ref, out_ref):
    j, _, p = place()
    near_cols, far_cols = half_columns(own_ref.shape[1])
    weight = jnp.concatenate([w_ref[:, near_cols], w_ref[:, far_cols]], axis=1)
    for start in range(0, own_ref.shape[0], ROWS):
        rows = pl.ds(start, ROWS)
        own, one, two = own_ref[rows, :], one_ref[rows, :], two_ref[rows, :]
        near, far = jnp.where(j == p, own, one), jnp.where(j == p, one, two)
        product = lax.dot_general(
            jnp.concatenate([near, far], axis=1),
            weight,
            (((1,), (1,)), ((), ())),
            preferred_element_type=jnp.float32,
        )
        out_ref[rows, :] = product.astype(out_ref.dtype)


def final(back, weight):
    vmem = pl.BlockSpec(memory_space=pltpu.VMEM)
    rows = back[0].shape[0]
    wide = weight.shape[0]
    return pl.pallas_call(
        final_kernel,
        out_shape=jax.ShapeDtypeStruct((rows, wide), jnp.bfloat16),
        in_specs=[vmem] * 4,
        out_specs=vmem,
        compiler_params=pltpu.CompilerParams(vmem_limit_bytes=8 * 1024 * 1024),
        cost_estimate=pl.CostEstimate(
            flops=2 * rows * wide * wide, bytes_accessed=8 * rows * wide, transcendentals=0
        ),
        name="final",
    )(*back, weight)


def per_device(node_feats, weight, cotangent, tile_values, tile_coords, tile_counts):
    groups = lax.axis_size("rows")
    reps = lax.axis_size("rep")
    shape = (groups // 2, reps)
    j, z, p = place()
    home = j == p
    scale = (node_feats.shape[0] * groups) ** (-0.5)

    def send(value, move):
        return lax.ppermute(value, AXES, route(shape, move))

    def sibling(c, j, z):
        return (c, 1 - j, z)

    def home_to_sibling(c, j, z):
        return (c, 1 - j, z) if j == z % 2 else None

    def across(c, j, z):
        return (c, j, (z + reps // 2) % reps)

    own = tile_values[0]
    blocks = node_feats.shape[0] // own.shape[-1]

    def to_home(c, j, z):
        return (c, 1 - j, z) if j == z % 2 else (c, j, z ^ 1)

    four = shape[0] == 4

    def to_direct(c, j, z):
        return (c ^ 1, j, z)

    def to_second(c, j, z):
        return (c ^ 2, j, z) if four else (c + 1 if c % 2 else c - 1, j, z)

    def to_far(c, j, z):
        return (c ^ 1, j, z) if four else (c - 1 if z % 2 else c + 1, j, z)

    def stage_one(c, j, z):
        if j == z % 2:
            return (c ^ 1, j, z)
        return (c ^ 2, j, z) if four and (c + z) % 2 else None

    def stage_one_cross(c, j, z):
        to = stage_one(c, j, z)
        return to and (to[0], 1 - j, z)

    first = send(own, to_home)
    half = node_feats.shape[1] // 2
    mine = lax.dynamic_slice_in_dim(node_feats, j * half, half, 1)
    yours = lax.dynamic_slice_in_dim(node_feats, (1 - j) * half, half, 1)
    one = send(mine, stage_one)
    two = send(yours, stage_one_cross)
    swapped = send(yours, sibling)
    self_choice = [("home", mine), ("away", swapped)]
    direct_choice = [("home", one), ("away", two)]
    meta = slot_blocks(tile_coords[:, 0], tile_counts[0], blocks)
    second, far = pick(
        [
            direct_choice if four else self_choice,
            [
                ("still home", swapped),
                ("still away", mine),
                ("relay home", two),
                ("relay away", one),
            ],
        ],
        [meta],
    )
    second = send(second, to_second)
    far = send(far, to_far)
    meta_b = send(meta, to_home)
    first, meta_b = lax.optimization_barrier((first, meta_b))
    other_first = send(first, home_to_sibling)
    meta_later, second = lax.optimization_barrier((meta_b, second))
    meta_far = send(meta_later, home_to_sibling)
    set_first = [(None, (meta_b, first))]
    panels = [
        ("self", [("home", mine), ("away", swapped)]),
        ("near", [("home", swapped), ("away", mine)]),
        ("direct", direct_choice),
        ("second", [(None, second)]),
        ("far", [(None, far)]),
    ]
    part = tile_product(panels, [set_first], jnp.float32, weigh=WEIGH)
    set_rest = [("home", (meta, own)), ("away", (meta_far, other_first))]
    part = tile_product(panels, [set_rest], jnp.bfloat16, part)

    def join(value):
        other = send(value, across)
        return (value.astype(jnp.float32) + other.astype(jnp.float32)).astype(jnp.bfloat16)

    near = join(part)
    far_half = send(near, sibling)
    cot, cot_yours = halves(cotangent)
    act, adj, adj_longer, adj_long = middle(
        near, far_half, weight, cot, send(cot_yours, sibling)
    )

    direct = send(adj_longer, to_direct)
    near_one = send(
        adj_long, lambda c, j, z: (c if (c + z) % 2 or not four else c ^ 2, j, z ^ 1)
    )
    second = send(direct if four else adj_longer, to_second)
    grad = grad_block(scale, near, far_half, adj)
    far = send(near_one, to_far)
    near_choice = [("still", near_one)]
    if four:
        near_two = send(
            adj, lambda c, j, z: None if (c + z) % 2 else (c, j, z ^ 1)
        )
        near_choice.append(("relay", near_two))
    panels = [("self", [(None, adj)]), ("direct", [(None, direct)])]
    back_part = tile_product(panels, [set_first, set_rest], jnp.float32)
    panels = [("second", [(None, second)]), ("far", [(None, far)]), ("near", near_choice)]
    grad_got = send(grad, lambda c, j, z: (c, j, z ^ 1))
    back_part = tile_product(
        panels, [set_first, set_rest], jnp.bfloat16, back_part, [grad_got]
    )

    def deliver(value):
        one = send(value, lambda c, j, z: (c, j, z ^ 1) if j == z % 2 else (c, 1 - j, z))
        two = send(value, lambda c, j, z: None if j == z % 2 else (c, 1 - j, z ^ 1))
        return one, two

    act_later, direct = lax.optimization_barrier((act, direct))
    act_parts = [act, *deliver(act_later)]
    grad = add_after([grad, grad_got], jnp.bfloat16, back_part, *act_parts[1:])
    step = 1
    while step < shape[0]:
        got = send(grad, lambda c, j, z, s=step: (c ^ s, j, z))
        step *= 2
        if step < shape[0]:
            grad = add_after([grad, got], jnp.bfloat16)
    back = add_after([back_part, send(back_part, across)], jnp.bfloat16, got)
    back_parts = [back, *deliver(back)]
    grad = add_after([grad, got], jnp.float32, back, *act_parts[1:])
    activated, weight_grad = gather_halves(act_parts, grad, send(grad, sibling))
    input_grad = final(back_parts, weight)
    return (activated, input_grad, weight_grad)


def solution(mesh):
    return jax.shard_map(
        per_device,
        mesh=mesh,
        in_specs=(
            P("rows", None),
            P(),
            P("rows", None),
            P("rows", None, "rep", None, None),
            P(None, "rows", None, "rep"),
            P("rows", None),
        ),
        out_specs=(P("rows", None), P("rows", None), P()),
        check_vma=False,
    )
```

```python
import functools

import jax
import jax.numpy as jnp
from jax import lax
from jax.experimental import pallas as pl
from jax.experimental.pallas import tpu as pltpu
from jax.sharding import PartitionSpec as P

AXES = ("rows", "rep")
TOGETHER = 2
ROWS = 256
WEIGH = 75


def route(shape, move):
    chips, reps = shape
    pairs = []
    for c in range(chips):
        for j in range(2):
            for z in range(reps):
                to = move(c, j, z)
                if to is not None:
                    target = ((to[0] % chips) * 2 + to[1]) * reps + to[2]
                    pairs.append(((c * 2 + j) * reps + z, target))
    return pairs


def place():
    r = lax.axis_index("rows")
    z = lax.axis_index("rep")
    return r % 2, z, z % 2


def when_of(case):
    j, z, p = place()
    home = j == p
    relay = jnp.logical_and(
        lax.axis_size("rows") == 8, (lax.axis_index("rows") // 2 + z) % 2 == 1
    )
    return {
        "home": home,
        "away": jnp.logical_not(home),
        "relay": relay,
        "still": jnp.logical_not(relay),
        "relay home": jnp.logical_and(relay, home),
        "relay away": jnp.logical_and(relay, jnp.logical_not(home)),
        "still home": jnp.logical_and(jnp.logical_not(relay), home),
        "still away": jnp.logical_and(jnp.logical_not(relay), jnp.logical_not(home)),
    }[case]


def start_chosen(choice, make):
    if len(choice) == 1:
        make(choice[0][1]).start()
        return
    for case, ref in choice:

        @pl.when(when_of(case))
        def _(ref=ref):
            make(ref).start()


def halves_kernel(x_ref, near_ref, far_ref, sems):
    j, _, _ = place()
    half = near_ref.shape[1]
    copies = []
    for i, out in enumerate((near_ref, far_ref)):
        start = pl.multiple_of((j if i == 0 else 1 - j) * half, half)
        copy = pltpu.make_async_copy(x_ref.at[:, pl.ds(start, half)], out, sems.at[i])
        copy.start()
        copies.append(copy)
    for copy in copies:
        copy.wait()


def halves(value):
    rows, width = value.shape
    part = jax.ShapeDtypeStruct((rows, width // 2), value.dtype)
    hbm = pl.BlockSpec(memory_space=pltpu.HBM)
    return pl.pallas_call(
        halves_kernel,
        out_shape=(part, part),
        in_specs=[hbm],
        out_specs=(hbm, hbm),
        scratch_shapes=[pltpu.SemaphoreType.DMA((2,))],
        compiler_params=pltpu.CompilerParams(vmem_limit_bytes=1024 * 1024),
        name="halves",
    )(value)


def pick_kernel(cases, waits, *refs):
    refs = list(refs)
    choices = [[(case, refs.pop(0)) for case in each] for each in cases]
    outs, sems = refs[waits:-1], refs[-1]

    def copy_to(i):
        return lambda ref: pltpu.make_async_copy(ref, outs[i], sems.at[i])

    for i, choice in enumerate(choices):
        start_chosen(choice, copy_to(i))
    for i, choice in enumerate(choices):
        copy_to(i)(choice[0][1]).wait()


def pick(choices, after):
    hbm = pl.BlockSpec(memory_space=pltpu.HBM)
    arrays = [array for choice in choices for _, array in choice]
    shape = jax.ShapeDtypeStruct(arrays[0].shape, arrays[0].dtype)
    return pl.pallas_call(
        functools.partial(
            pick_kernel, [[case for case, _ in choice] for choice in choices], len(after)
        ),
        out_shape=(shape,) * len(choices),
        in_specs=[hbm] * len(arrays) + [pl.BlockSpec(memory_space=pl.ANY)] * len(after),
        out_specs=(hbm,) * len(choices),
        scratch_shapes=[pltpu.SemaphoreType.DMA((len(choices),))],
        compiler_params=pltpu.CompilerParams(vmem_limit_bytes=1024 * 1024),
        name="pick",
    )(*arrays, *after)


def slots_kernel(dead, coords_ref, counts_ref, out_ref):
    _, z, _ = place()
    _, reach, slots = coords_ref.shape
    for d in range(reach):
        for k in range(slots):
            live = z * slots + k < counts_ref[d]
            out_ref[0, d * slots + k] = jnp.where(live, coords_ref[0, d, k], dead)
            out_ref[1, d * slots + k] = coords_ref[1, d, k]


def slot_blocks(coords, counts, dead):
    smem = pl.BlockSpec(memory_space=pltpu.SMEM)
    return pl.pallas_call(
        functools.partial(slots_kernel, dead),
        out_shape=jax.ShapeDtypeStruct((2, coords.shape[1] * coords.shape[2]), jnp.int32),
        in_specs=[smem, smem],
        out_specs=smem,
        compiler_params=pltpu.CompilerParams(vmem_limit_bytes=1024 * 1024),
        name="slot_blocks",
    )(coords, counts)


def offset_of(kind):
    _, _, p = place()
    even = (lax.axis_index("rows") // 2) % 2 == 0
    return {
        "self": 2,
        "near": jnp.where(p == 0, 3, 1),
        "far": jnp.where(p == 0, 1, 3),
        "direct": jnp.where(even, 4, 0),
        "second": jnp.where(even, 0, 4),
    }[kind]


def chosen(choice, read):
    value = read(choice[0][1])
    for case, ref in choice[1:]:
        value = jnp.where(when_of(case), read(ref), value)
    return value


def tile_kernel(kinds, cases, sets, summed, waits, *refs):
    refs = list(refs)
    metas = [[(case, refs.pop(0)) for case in each] for each in sets]
    tiles = [[(case, refs.pop(0)) for case in each] for each in sets]
    panels = [[(case, refs.pop(0)) for case in each] for each in cases]
    before = refs.pop(0) if summed else None
    out_ref, acc_ref = refs[waits:]
    _, slots, tile, _ = tiles[0][0][1].shape
    rows = out_ref.shape[0]
    if summed:
        acc_ref[:rows, :] = before[...]
    else:
        acc_ref[...] = jnp.zeros_like(acc_ref)
    for i, kind in enumerate(kinds):
        d = offset_of(kind)
        for s in range(len(sets)):
            for first in range(0, slots, TOGETHER):
                prods = []
                for k in range(first, min(first + TOGETHER, slots)):
                    row = chosen(metas[s], lambda ref: ref[0, d * slots + k])
                    col = chosen(metas[s], lambda ref: ref[1, d * slots + k])
                    col = pl.multiple_of(col * tile, tile)
                    prod = jnp.dot(
                        chosen(tiles[s], lambda ref: ref[d, k]),
                        chosen(panels[i], lambda ref: ref[pl.ds(col, tile), :]),
                        preferred_element_type=jnp.float32,
                    )
                    prods.append((pl.multiple_of(row * tile, tile), prod))
                for row, prod in prods:
                    acc_ref[pl.ds(row, tile), :] += prod
    out_ref[...] = acc_ref[:rows, :].astype(out_ref.dtype)


def tile_product(named, sets, dtype, before=None, after=(), weigh=1):
    kinds = [kind for kind, _ in named]
    cases = [[case for case, _ in choice] for _, choice in named]
    panels = [panel for _, choice in named for _, panel in choice]
    metas = [meta for choice in sets for _, (meta, _) in choice]
    tiles = [values for choice in sets for _, (_, values) in choice]
    rows, width = panels[0].shape if before is None else before.shape
    _, slots, tile, _ = tiles[0].shape
    smem = pl.BlockSpec(memory_space=pltpu.SMEM)
    vmem = pl.BlockSpec(memory_space=pltpu.VMEM)
    anywhere = pl.BlockSpec(memory_space=pl.ANY)
    count = len(kinds) * len(sets) * slots
    summed = before is not None
    return pl.pallas_call(
        functools.partial(
            tile_kernel,
            kinds,
            cases,
            [[case for case, _ in choice] for choice in sets],
            summed,
            len(after),
        ),
        out_shape=jax.ShapeDtypeStruct((rows, width), dtype),
        in_specs=[smem] * len(metas)
        + [vmem] * (len(tiles) + len(panels) + summed)
        + [anywhere] * len(after),
        out_specs=vmem,
        scratch_shapes=[pltpu.VMEM((rows + tile, width), jnp.float32)],
        compiler_params=pltpu.CompilerParams(vmem_limit_bytes=12 * 1024 * 1024),
        cost_estimate=pl.CostEstimate(
            flops=weigh * 2 * count * tile * tile * width,
            bytes_accessed=weigh * (count * tile * tile * 2 + len(kinds) * rows * width * 2),
            transcendentals=0,
        ),
        name="tile_product",
    )(*metas, *tiles, *panels, *([before] if summed else []), *after)


def middle_kernel(near_ref, far_ref, w_ref, cot_ref, cot_swap_ref, act_ref, *adj_refs):
    j, _, p = place()
    near_cols, far_cols = half_columns(near_ref.shape[1])
    weight = jnp.concatenate([w_ref[near_cols, near_cols], w_ref[far_cols, near_cols]], axis=0)
    count = near_ref.shape[0]
    for start in range(0, count, ROWS):
        rows = pl.ds(start, ROWS)
        both = jnp.concatenate([near_ref[rows, :], far_ref[rows, :]], axis=1)
        agg = jnp.dot(both, weight, preferred_element_type=jnp.float32)
        sig = jax.nn.sigmoid(agg)
        act_ref[rows, :] = (agg * sig).astype(act_ref.dtype)
        slope = sig * (1.0 + agg * (1.0 - sig))
        cot = jnp.where(j == p, cot_ref[rows, :], cot_swap_ref[rows, :])
        adj = (cot.astype(jnp.float32) * slope).astype(act_ref.dtype)
        for ref in adj_refs:
            ref[rows, :] = adj
    for ref in adj_refs:
        if ref.shape[0] > count:
            ref[count:, :] = jnp.zeros((ref.shape[0] - count, ref.shape[1]), ref.dtype)


def middle(near, far, weight, cot, cot_swap):
    vmem = pl.BlockSpec(memory_space=pltpu.VMEM)
    rows, width = near.shape
    out = jax.ShapeDtypeStruct((rows, width), jnp.bfloat16)
    longer = tuple(jax.ShapeDtypeStruct((rows + n, width), jnp.bfloat16) for n in (32, 16))
    return pl.pallas_call(
        middle_kernel,
        out_shape=(out, out) + longer,
        in_specs=[vmem] * 5,
        out_specs=(vmem,) * 4,
        compiler_params=pltpu.CompilerParams(vmem_limit_bytes=8 * 1024 * 1024),
        cost_estimate=pl.CostEstimate(
            flops=4 * rows * width * width,
            bytes_accessed=10 * rows * width,
            transcendentals=rows * width,
        ),
        name="middle",
    )(near, far, weight, cot, cot_swap)


def grad_kernel(scale, near_ref, far_ref, adj_ref, out_ref):
    j, _, _ = place()
    half = near_ref.shape[1]
    dims = (((0,), (0,)), ((), ()))
    for i, ref in enumerate((near_ref, far_ref)):
        start = pl.multiple_of((j if i == 0 else 1 - j) * half, half)
        block = lax.dot_general(ref[...], adj_ref[...], dims, preferred_element_type=jnp.float32)
        out_ref[pl.ds(start, half), :] = (scale * block).astype(out_ref.dtype)


def grad_block(scale, near, far, adj):
    vmem = pl.BlockSpec(memory_space=pltpu.VMEM)
    rows, width = near.shape
    return pl.pallas_call(
        functools.partial(grad_kernel, scale),
        out_shape=jax.ShapeDtypeStruct((2 * width, width), jnp.bfloat16),
        in_specs=[vmem] * 3,
        out_specs=vmem,
        compiler_params=pltpu.CompilerParams(vmem_limit_bytes=8 * 1024 * 1024),
        cost_estimate=pl.CostEstimate(
            flops=4 * WEIGH * rows * width * width,
            bytes_accessed=8 * WEIGH * rows * width,
            transcendentals=0,
        ),
        name="grad_block",
    )(near, far, adj)


def add_kernel(count, *refs):
    values = [ref[...].astype(jnp.float32) for ref in refs[:count]]
    total = values[0] + values[1]
    if count == 4:
        total = total + (values[2] + values[3])
    refs[-1][...] = total.astype(refs[-1].dtype)


def add_after(values, dtype, *after):
    vmem = pl.BlockSpec(memory_space=pltpu.VMEM)
    return pl.pallas_call(
        functools.partial(add_kernel, len(values)),
        out_shape=jax.ShapeDtypeStruct(values[0].shape, dtype),
        in_specs=[vmem] * len(values) + [pl.BlockSpec(memory_space=pl.ANY)] * len(after),
        out_specs=vmem,
        compiler_params=pltpu.CompilerParams(vmem_limit_bytes=4 * 1024 * 1024),
        name="add_after",
    )(*values, *after)


def half_columns(half):
    j, _, _ = place()
    near = pl.ds(pl.multiple_of(j * half, half), half)
    return near, pl.ds(pl.multiple_of((1 - j) * half, half), half)


def near_and_far(parts):
    j, _, p = place()
    own, one, two = parts
    near = jnp.where(j == p, own[...], one[...])
    return near, jnp.where(j == p, one[...], two[...])


def gather_kernel(own_ref, one_ref, two_ref, grad_ref, rest_ref, act_ref, grad_out_ref):
    near_cols, far_cols = half_columns(own_ref.shape[1])
    near, far = near_and_far((own_ref, one_ref, two_ref))
    act_ref[:, near_cols] = near
    act_ref[:, far_cols] = far
    grad_out_ref[:, near_cols] = grad_ref[...]
    grad_out_ref[:, far_cols] = rest_ref[...]


def gather_halves(act, grad, rest):
    vmem = pl.BlockSpec(memory_space=pltpu.VMEM)
    rows, width = act[0].shape
    return pl.pallas_call(
        gather_kernel,
        out_shape=(
            jax.ShapeDtypeStruct((rows, 2 * width), act[0].dtype),
            jax.ShapeDtypeStruct((2 * width, 2 * width), grad.dtype),
        ),
        in_specs=[vmem] * 5,
        out_specs=(vmem, vmem),
        compiler_params=pltpu.CompilerParams(vmem_limit_bytes=8 * 1024 * 1024),
        name="gather_halves",
    )(*act, grad, rest)


def final_kernel(own_ref, one_ref, two_ref, w_ref, out_ref):
    j, _, p = place()
    near_cols, far_cols = half_columns(own_ref.shape[1])
    weight = jnp.concatenate([w_ref[:, near_cols], w_ref[:, far_cols]], axis=1)
    for start in range(0, own_ref.shape[0], ROWS):
        rows = pl.ds(start, ROWS)
        own, one, two = own_ref[rows, :], one_ref[rows, :], two_ref[rows, :]
        near, far = jnp.where(j == p, own, one), jnp.where(j == p, one, two)
        product = lax.dot_general(
            jnp.concatenate([near, far], axis=1),
            weight,
            (((1,), (1,)), ((), ())),
            preferred_element_type=jnp.float32,
        )
        out_ref[rows, :] = product.astype(out_ref.dtype)


def final(back, weight):
    vmem = pl.BlockSpec(memory_space=pltpu.VMEM)
    rows = back[0].shape[0]
    wide = weight.shape[0]
    return pl.pallas_call(
        final_kernel,
        out_shape=jax.ShapeDtypeStruct((rows, wide), jnp.bfloat16),
        in_specs=[vmem] * 4,
        out_specs=vmem,
        compiler_params=pltpu.CompilerParams(vmem_limit_bytes=8 * 1024 * 1024),
        cost_estimate=pl.CostEstimate(
            flops=2 * rows * wide * wide, bytes_accessed=8 * rows * wide, transcendentals=0
        ),
        name="final",
    )(*back, weight)


def per_device(node_feats, weight, cotangent, tile_values, tile_coords, tile_counts):
    groups = lax.axis_size("rows")
    reps = lax.axis_size("rep")
    shape = (groups // 2, reps)
    j, z, p = place()
    home = j == p
    scale = (node_feats.shape[0] * groups) ** (-0.5)

    def send(value, move):
        return lax.ppermute(value, AXES, route(shape, move))

    def sibling(c, j, z):
        return (c, 1 - j, z)

    def home_to_sibling(c, j, z):
        return (c, 1 - j, z) if j == z % 2 else None

    def across(c, j, z):
        return (c, j, (z + reps // 2) % reps)

    own = tile_values[0]
    blocks = node_feats.shape[0] // own.shape[-1]

    def to_home(c, j, z):
        return (c, 1 - j, z) if j == z % 2 else (c, j, z ^ 1)

    four = shape[0] == 4

    def to_direct(c, j, z):
        return (c ^ 1, j, z)

    def to_second(c, j, z):
        return (c ^ 2, j, z) if four else (c + 1 if c % 2 else c - 1, j, z)

    def to_far(c, j, z):
        return (c ^ 1, j, z) if four else (c - 1 if z % 2 else c + 1, j, z)

    def stage_one(c, j, z):
        if j == z % 2:
            return (c ^ 1, j, z)
        return (c ^ 2, j, z) if four and (c + z) % 2 else None

    def stage_one_cross(c, j, z):
        to = stage_one(c, j, z)
        return to and (to[0], 1 - j, z)

    first = send(own, to_home)
    half = node_feats.shape[1] // 2
    mine = lax.dynamic_slice_in_dim(node_feats, j * half, half, 1)
    yours = lax.dynamic_slice_in_dim(node_feats, (1 - j) * half, half, 1)
    one = send(mine, stage_one)
    two = send(yours, stage_one_cross)
    swapped = send(yours, sibling)
    self_choice = [("home", mine), ("away", swapped)]
    direct_choice = [("home", one), ("away", two)]
    meta = slot_blocks(tile_coords[:, 0], tile_counts[0], blocks)
    second, far = pick(
        [
            direct_choice if four else self_choice,
            [
                ("still home", swapped),
                ("still away", mine),
                ("relay home", two),
                ("relay away", one),
            ],
        ],
        [meta],
    )
    second = send(second, to_second)
    far = send(far, to_far)
    meta_b = send(meta, to_home)
    first, meta_b = lax.optimization_barrier((first, meta_b))
    other_first = send(first, home_to_sibling)
    meta_later, second = lax.optimization_barrier((meta_b, second))
    meta_far = send(meta_later, home_to_sibling)
    set_first = [(None, (meta_b, first))]
    panels = [
        ("self", [("home", mine), ("away", swapped)]),
        ("near", [("home", swapped), ("away", mine)]),
        ("direct", direct_choice),
        ("second", [(None, second)]),
        ("far", [(None, far)]),
    ]
    part = tile_product(panels, [set_first], jnp.float32, weigh=WEIGH)
    set_rest = [("home", (meta, own)), ("away", (meta_far, other_first))]
    part = tile_product(panels, [set_rest], jnp.bfloat16, part)

    def join(value):
        other = send(value, across)
        return (value.astype(jnp.float32) + other.astype(jnp.float32)).astype(jnp.bfloat16)

    near = join(part)
    far_half = send(near, sibling)
    cot, cot_yours = halves(cotangent)
    act, adj, adj_longer, adj_long = middle(
        near, far_half, weight, cot, send(cot_yours, sibling)
    )

    direct = send(adj_long, to_direct)
    near_one = send(
        adj_longer, lambda c, j, z: (c if (c + z) % 2 or not four else c ^ 2, j, z ^ 1)
    )
    second = send(direct if four else adj_long, to_second)
    grad = grad_block(scale, near, far_half, adj)
    far = send(near_one, to_far)
    near_choice = [("still", near_one)]
    if four:
        near_two = send(
            adj, lambda c, j, z: None if (c + z) % 2 else (c, j, z ^ 1)
        )
        near_choice.append(("relay", near_two))
    panels = [("self", [(None, adj)]), ("direct", [(None, direct)])]
    back_part = tile_product(panels, [set_first, set_rest], jnp.float32)
    panels = [("second", [(None, second)]), ("far", [(None, far)]), ("near", near_choice)]
    grad_got = send(grad, lambda c, j, z: (c, j, z ^ 1))
    back_part = tile_product(
        panels, [set_first, set_rest], jnp.bfloat16, back_part, [grad_got]
    )

    def deliver(value):
        one = send(value, lambda c, j, z: (c, j, z ^ 1) if j == z % 2 else (c, 1 - j, z))
        two = send(value, lambda c, j, z: None if j == z % 2 else (c, 1 - j, z ^ 1))
        return one, two

    act_later, back_part = lax.optimization_barrier((act, back_part))
    act_parts = [act, *deliver(act_later)]
    grad = add_after([grad, grad_got], jnp.bfloat16, back_part)
    step = 1
    while step < shape[0]:
        got = send(grad, lambda c, j, z, s=step: (c ^ s, j, z))
        step *= 2
        if step < shape[0]:
            grad = add_after([grad, got], jnp.bfloat16)
    back = add_after([back_part, send(back_part, across)], jnp.bfloat16, got)
    back_parts = [back, *deliver(back)]
    grad = add_after([grad, got], jnp.float32, back, *act_parts[1:])
    activated, weight_grad = gather_halves(act_parts, grad, send(grad, sibling))
    input_grad = final(back_parts, weight)
    return (activated, input_grad, weight_grad)


def solution(mesh):
    return jax.shard_map(
        per_device,
        mesh=mesh,
        in_specs=(
            P("rows", None),
            P(),
            P("rows", None),
            P("rows", None, "rep", None, None),
            P(None, "rows", None, "rep"),
            P("rows", None),
        ),
        out_specs=(P("rows", None), P("rows", None), P()),
        check_vma=False,
    )
```

```python
import functools

import jax
import jax.numpy as jnp
from jax import lax
from jax.experimental import pallas as pl
from jax.experimental.pallas import tpu as pltpu
from jax.sharding import PartitionSpec as P

AXES = ("rows", "rep")
TOGETHER = 2
ROWS = 256
WEIGH = 75


def route(shape, move):
    chips, reps = shape
    pairs = []
    for c in range(chips):
        for j in range(2):
            for z in range(reps):
                to = move(c, j, z)
                if to is not None:
                    target = ((to[0] % chips) * 2 + to[1]) * reps + to[2]
                    pairs.append(((c * 2 + j) * reps + z, target))
    return pairs


def place():
    r = lax.axis_index("rows")
    z = lax.axis_index("rep")
    return r % 2, z, z % 2


def when_of(case):
    j, z, p = place()
    home = j == p
    relay = jnp.logical_and(
        lax.axis_size("rows") == 8, (lax.axis_index("rows") // 2 + z) % 2 == 1
    )
    return {
        "home": home,
        "away": jnp.logical_not(home),
        "relay": relay,
        "still": jnp.logical_not(relay),
        "relay home": jnp.logical_and(relay, home),
        "relay away": jnp.logical_and(relay, jnp.logical_not(home)),
        "still home": jnp.logical_and(jnp.logical_not(relay), home),
        "still away": jnp.logical_and(jnp.logical_not(relay), jnp.logical_not(home)),
    }[case]


def start_chosen(choice, make):
    if len(choice) == 1:
        make(choice[0][1]).start()
        return
    for case, ref in choice:

        @pl.when(when_of(case))
        def _(ref=ref):
            make(ref).start()


def halves_kernel(x_ref, near_ref, far_ref, sems):
    j, _, _ = place()
    half = near_ref.shape[1]
    copies = []
    for i, out in enumerate((near_ref, far_ref)):
        start = pl.multiple_of((j if i == 0 else 1 - j) * half, half)
        copy = pltpu.make_async_copy(x_ref.at[:, pl.ds(start, half)], out, sems.at[i])
        copy.start()
        copies.append(copy)
    for copy in copies:
        copy.wait()


def halves(value):
    rows, width = value.shape
    part = jax.ShapeDtypeStruct((rows, width // 2), value.dtype)
    hbm = pl.BlockSpec(memory_space=pltpu.HBM)
    return pl.pallas_call(
        halves_kernel,
        out_shape=(part, part),
        in_specs=[hbm],
        out_specs=(hbm, hbm),
        scratch_shapes=[pltpu.SemaphoreType.DMA((2,))],
        compiler_params=pltpu.CompilerParams(vmem_limit_bytes=1024 * 1024),
        name="halves",
    )(value)


def pick_kernel(cases, waits, *refs):
    refs = list(refs)
    choices = [[(case, refs.pop(0)) for case in each] for each in cases]
    outs, sems = refs[waits:-1], refs[-1]

    def copy_to(i):
        return lambda ref: pltpu.make_async_copy(ref, outs[i], sems.at[i])

    for i, choice in enumerate(choices):
        start_chosen(choice, copy_to(i))
    for i, choice in enumerate(choices):
        copy_to(i)(choice[0][1]).wait()


def pick(choices, after):
    hbm = pl.BlockSpec(memory_space=pltpu.HBM)
    arrays = [array for choice in choices for _, array in choice]
    shape = jax.ShapeDtypeStruct(arrays[0].shape, arrays[0].dtype)
    return pl.pallas_call(
        functools.partial(
            pick_kernel, [[case for case, _ in choice] for choice in choices], len(after)
        ),
        out_shape=(shape,) * len(choices),
        in_specs=[hbm] * len(arrays) + [pl.BlockSpec(memory_space=pl.ANY)] * len(after),
        out_specs=(hbm,) * len(choices),
        scratch_shapes=[pltpu.SemaphoreType.DMA((len(choices),))],
        compiler_params=pltpu.CompilerParams(vmem_limit_bytes=1024 * 1024),
        name="pick",
    )(*arrays, *after)


def slots_kernel(dead, coords_ref, counts_ref, out_ref):
    _, z, _ = place()
    _, reach, slots = coords_ref.shape
    for d in range(reach):
        for k in range(slots):
            live = z * slots + k < counts_ref[d]
            out_ref[0, d * slots + k] = jnp.where(live, coords_ref[0, d, k], dead)
            out_ref[1, d * slots + k] = coords_ref[1, d, k]


def slot_blocks(coords, counts, dead):
    smem = pl.BlockSpec(memory_space=pltpu.SMEM)
    return pl.pallas_call(
        functools.partial(slots_kernel, dead),
        out_shape=jax.ShapeDtypeStruct((2, coords.shape[1] * coords.shape[2]), jnp.int32),
        in_specs=[smem, smem],
        out_specs=smem,
        compiler_params=pltpu.CompilerParams(vmem_limit_bytes=1024 * 1024),
        name="slot_blocks",
    )(coords, counts)


def offset_of(kind):
    _, _, p = place()
    even = (lax.axis_index("rows") // 2) % 2 == 0
    return {
        "self": 2,
        "near": jnp.where(p == 0, 3, 1),
        "far": jnp.where(p == 0, 1, 3),
        "direct": jnp.where(even, 4, 0),
        "second": jnp.where(even, 0, 4),
    }[kind]


def chosen(choice, read):
    value = read(choice[0][1])
    for case, ref in choice[1:]:
        value = jnp.where(when_of(case), read(ref), value)
    return value


def tile_kernel(kinds, cases, sets, summed, waits, *refs):
    refs = list(refs)
    metas = [[(case, refs.pop(0)) for case in each] for each in sets]
    tiles = [[(case, refs.pop(0)) for case in each] for each in sets]
    panels = [[(case, refs.pop(0)) for case in each] for each in cases]
    before = refs.pop(0) if summed else None
    out_ref, acc_ref = refs[waits:]
    _, slots, tile, _ = tiles[0][0][1].shape
    rows = out_ref.shape[0]
    if summed:
        acc_ref[:rows, :] = before[...]
    else:
        acc_ref[...] = jnp.zeros_like(acc_ref)
    for i, kind in enumerate(kinds):
        d = offset_of(kind)
        for s in range(len(sets)):
            for first in range(0, slots, TOGETHER):
                prods = []
                for k in range(first, min(first + TOGETHER, slots)):
                    row = chosen(metas[s], lambda ref: ref[0, d * slots + k])
                    col = chosen(metas[s], lambda ref: ref[1, d * slots + k])
                    col = pl.multiple_of(col * tile, tile)
                    prod = jnp.dot(
                        chosen(tiles[s], lambda ref: ref[d, k]),
                        chosen(panels[i], lambda ref: ref[pl.ds(col, tile), :]),
                        preferred_element_type=jnp.float32,
                    )
                    prods.append((pl.multiple_of(row * tile, tile), prod))
                for row, prod in prods:
                    acc_ref[pl.ds(row, tile), :] += prod
    out_ref[...] = acc_ref[:rows, :].astype(out_ref.dtype)


def tile_product(named, sets, dtype, before=None, after=(), weigh=1):
    kinds = [kind for kind, _ in named]
    cases = [[case for case, _ in choice] for _, choice in named]
    panels = [panel for _, choice in named for _, panel in choice]
    metas = [meta for choice in sets for _, (meta, _) in choice]
    tiles = [values for choice in sets for _, (_, values) in choice]
    rows, width = panels[0].shape if before is None else before.shape
    _, slots, tile, _ = tiles[0].shape
    smem = pl.BlockSpec(memory_space=pltpu.SMEM)
    vmem = pl.BlockSpec(memory_space=pltpu.VMEM)
    anywhere = pl.BlockSpec(memory_space=pl.ANY)
    count = len(kinds) * len(sets) * slots
    summed = before is not None
    return pl.pallas_call(
        functools.partial(
            tile_kernel,
            kinds,
            cases,
            [[case for case, _ in choice] for choice in sets],
            summed,
            len(after),
        ),
        out_shape=jax.ShapeDtypeStruct((rows, width), dtype),
        in_specs=[smem] * len(metas)
        + [vmem] * (len(tiles) + len(panels) + summed)
        + [anywhere] * len(after),
        out_specs=vmem,
        scratch_shapes=[pltpu.VMEM((rows + tile, width), jnp.float32)],
        compiler_params=pltpu.CompilerParams(vmem_limit_bytes=12 * 1024 * 1024),
        cost_estimate=pl.CostEstimate(
            flops=weigh * 2 * count * tile * tile * width,
            bytes_accessed=weigh * (count * tile * tile * 2 + len(kinds) * rows * width * 2),
            transcendentals=0,
        ),
        name="tile_product",
    )(*metas, *tiles, *panels, *([before] if summed else []), *after)


def middle_kernel(near_ref, far_ref, w_ref, cot_ref, cot_swap_ref, act_ref, *adj_refs):
    j, _, p = place()
    near_cols, far_cols = half_columns(near_ref.shape[1])
    weight = jnp.concatenate([w_ref[near_cols, near_cols], w_ref[far_cols, near_cols]], axis=0)
    count = near_ref.shape[0]
    for start in range(0, count, ROWS):
        rows = pl.ds(start, ROWS)
        both = jnp.concatenate([near_ref[rows, :], far_ref[rows, :]], axis=1)
        agg = jnp.dot(both, weight, preferred_element_type=jnp.float32)
        sig = jax.nn.sigmoid(agg)
        act_ref[rows, :] = (agg * sig).astype(act_ref.dtype)
        slope = sig * (1.0 + agg * (1.0 - sig))
        cot = jnp.where(j == p, cot_ref[rows, :], cot_swap_ref[rows, :])
        adj = (cot.astype(jnp.float32) * slope).astype(act_ref.dtype)
        for ref in adj_refs:
            ref[rows, :] = adj
    for ref in adj_refs:
        if ref.shape[0] > count:
            ref[count:, :] = jnp.zeros((ref.shape[0] - count, ref.shape[1]), ref.dtype)


def middle(near, far, weight, cot, cot_swap):
    vmem = pl.BlockSpec(memory_space=pltpu.VMEM)
    rows, width = near.shape
    out = jax.ShapeDtypeStruct((rows, width), jnp.bfloat16)
    longer = tuple(jax.ShapeDtypeStruct((rows + n, width), jnp.bfloat16) for n in (32, 16))
    return pl.pallas_call(
        middle_kernel,
        out_shape=(out, out) + longer,
        in_specs=[vmem] * 5,
        out_specs=(vmem,) * 4,
        compiler_params=pltpu.CompilerParams(vmem_limit_bytes=8 * 1024 * 1024),
        cost_estimate=pl.CostEstimate(
            flops=4 * rows * width * width,
            bytes_accessed=10 * rows * width,
            transcendentals=rows * width,
        ),
        name="middle",
    )(near, far, weight, cot, cot_swap)


def grad_kernel(scale, near_ref, far_ref, adj_ref, out_ref):
    j, _, _ = place()
    half = near_ref.shape[1]
    dims = (((0,), (0,)), ((), ()))
    for i, ref in enumerate((near_ref, far_ref)):
        start = pl.multiple_of((j if i == 0 else 1 - j) * half, half)
        block = lax.dot_general(ref[...], adj_ref[...], dims, preferred_element_type=jnp.float32)
        out_ref[pl.ds(start, half), :] = (scale * block).astype(out_ref.dtype)


def grad_block(scale, near, far, adj):
    vmem = pl.BlockSpec(memory_space=pltpu.VMEM)
    rows, width = near.shape
    return pl.pallas_call(
        functools.partial(grad_kernel, scale),
        out_shape=jax.ShapeDtypeStruct((2 * width, width), jnp.bfloat16),
        in_specs=[vmem] * 3,
        out_specs=vmem,
        compiler_params=pltpu.CompilerParams(vmem_limit_bytes=8 * 1024 * 1024),
        cost_estimate=pl.CostEstimate(
            flops=4 * WEIGH * rows * width * width,
            bytes_accessed=8 * WEIGH * rows * width,
            transcendentals=0,
        ),
        name="grad_block",
    )(near, far, adj)


def add_kernel(count, *refs):
    values = [ref[...].astype(jnp.float32) for ref in refs[:count]]
    total = values[0] + values[1]
    if count == 4:
        total = total + (values[2] + values[3])
    refs[-1][...] = total.astype(refs[-1].dtype)


def add_after(values, dtype, *after):
    vmem = pl.BlockSpec(memory_space=pltpu.VMEM)
    return pl.pallas_call(
        functools.partial(add_kernel, len(values)),
        out_shape=jax.ShapeDtypeStruct(values[0].shape, dtype),
        in_specs=[vmem] * len(values) + [pl.BlockSpec(memory_space=pl.ANY)] * len(after),
        out_specs=vmem,
        compiler_params=pltpu.CompilerParams(vmem_limit_bytes=4 * 1024 * 1024),
        name="add_after",
    )(*values, *after)


def half_columns(half):
    j, _, _ = place()
    near = pl.ds(pl.multiple_of(j * half, half), half)
    return near, pl.ds(pl.multiple_of((1 - j) * half, half), half)


def near_and_far(parts):
    j, _, p = place()
    own, one, two = parts
    near = jnp.where(j == p, own[...], one[...])
    return near, jnp.where(j == p, one[...], two[...])


def gather_kernel(own_ref, one_ref, two_ref, grad_ref, rest_ref, act_ref, grad_out_ref):
    near_cols, far_cols = half_columns(own_ref.shape[1])
    near, far = near_and_far((own_ref, one_ref, two_ref))
    act_ref[:, near_cols] = near
    act_ref[:, far_cols] = far
    grad_out_ref[:, near_cols] = grad_ref[...]
    grad_out_ref[:, far_cols] = rest_ref[...]


def gather_halves(act, grad, rest):
    vmem = pl.BlockSpec(memory_space=pltpu.VMEM)
    rows, width = act[0].shape
    return pl.pallas_call(
        gather_kernel,
        out_shape=(
            jax.ShapeDtypeStruct((rows, 2 * width), act[0].dtype),
            jax.ShapeDtypeStruct((2 * width, 2 * width), grad.dtype),
        ),
        in_specs=[vmem] * 5,
        out_specs=(vmem, vmem),
        compiler_params=pltpu.CompilerParams(vmem_limit_bytes=8 * 1024 * 1024),
        name="gather_halves",
    )(*act, grad, rest)


def final_kernel(own_ref, one_ref, two_ref, w_ref, out_ref):
    j, _, p = place()
    near_cols, far_cols = half_columns(own_ref.shape[1])
    weight = jnp.concatenate([w_ref[:, near_cols], w_ref[:, far_cols]], axis=1)
    for start in range(0, own_ref.shape[0], ROWS):
        rows = pl.ds(start, ROWS)
        own, one, two = own_ref[rows, :], one_ref[rows, :], two_ref[rows, :]
        near, far = jnp.where(j == p, own, one), jnp.where(j == p, one, two)
        product = lax.dot_general(
            jnp.concatenate([near, far], axis=1),
            weight,
            (((1,), (1,)), ((), ())),
            preferred_element_type=jnp.float32,
        )
        out_ref[rows, :] = product.astype(out_ref.dtype)


def final(back, weight):
    vmem = pl.BlockSpec(memory_space=pltpu.VMEM)
    rows = back[0].shape[0]
    wide = weight.shape[0]
    return pl.pallas_call(
        final_kernel,
        out_shape=jax.ShapeDtypeStruct((rows, wide), jnp.bfloat16),
        in_specs=[vmem] * 4,
        out_specs=vmem,
        compiler_params=pltpu.CompilerParams(vmem_limit_bytes=8 * 1024 * 1024),
        cost_estimate=pl.CostEstimate(
            flops=2 * rows * wide * wide, bytes_accessed=8 * rows * wide, transcendentals=0
        ),
        name="final",
    )(*back, weight)


def per_device(node_feats, weight, cotangent, tile_values, tile_coords, tile_counts):
    groups = lax.axis_size("rows")
    reps = lax.axis_size("rep")
    shape = (groups // 2, reps)
    j, z, p = place()
    home = j == p
    scale = (node_feats.shape[0] * groups) ** (-0.5)

    def send(value, move):
        return lax.ppermute(value, AXES, route(shape, move))

    def sibling(c, j, z):
        return (c, 1 - j, z)

    def home_to_sibling(c, j, z):
        return (c, 1 - j, z) if j == z % 2 else None

    def across(c, j, z):
        return (c, j, (z + reps // 2) % reps)

    own = tile_values[0]
    blocks = node_feats.shape[0] // own.shape[-1]

    def to_home(c, j, z):
        return (c, 1 - j, z) if j == z % 2 else (c, j, z ^ 1)

    four = shape[0] == 4

    def to_direct(c, j, z):
        return (c ^ 1, j, z)

    def to_second(c, j, z):
        return (c ^ 2, j, z) if four else (c + 1 if c % 2 else c - 1, j, z)

    def to_far(c, j, z):
        return (c ^ 1, j, z) if four else (c - 1 if z % 2 else c + 1, j, z)

    def stage_one(c, j, z):
        if j == z % 2:
            return (c ^ 1, j, z)
        return (c ^ 2, j, z) if four and (c + z) % 2 else None

    def stage_one_cross(c, j, z):
        to = stage_one(c, j, z)
        return to and (to[0], 1 - j, z)

    first = send(own, to_home)
    half = node_feats.shape[1] // 2
    mine = lax.dynamic_slice_in_dim(node_feats, j * half, half, 1)
    yours = lax.dynamic_slice_in_dim(node_feats, (1 - j) * half, half, 1)
    one = send(mine, stage_one)
    two = send(yours, stage_one_cross)
    swapped = send(yours, sibling)
    self_choice = [("home", mine), ("away", swapped)]
    direct_choice = [("home", one), ("away", two)]
    meta = slot_blocks(tile_coords[:, 0], tile_counts[0], blocks)
    second, far = pick(
        [
            direct_choice if four else self_choice,
            [
                ("still home", swapped),
                ("still away", mine),
                ("relay home", two),
                ("relay away", one),
            ],
        ],
        [meta],
    )
    second = send(second, to_second)
    far = send(far, to_far)
    meta_b = send(meta, to_home)
    first, meta_b = lax.optimization_barrier((first, meta_b))
    other_first = send(first, home_to_sibling)
    meta_later, second = lax.optimization_barrier((meta_b, second))
    meta_far = send(meta_later, home_to_sibling)
    set_first = [(None, (meta_b, first))]
    panels = [
        ("self", [("home", mine), ("away", swapped)]),
        ("near", [("home", swapped), ("away", mine)]),
        ("direct", direct_choice),
        ("second", [(None, second)]),
        ("far", [(None, far)]),
    ]
    part = tile_product(panels, [set_first], jnp.float32, weigh=WEIGH)
    set_rest = [("home", (meta, own)), ("away", (meta_far, other_first))]
    part = tile_product(panels, [set_rest], jnp.bfloat16, part)

    def join(value):
        other = send(value, across)
        return (value.astype(jnp.float32) + other.astype(jnp.float32)).astype(jnp.bfloat16)

    near = join(part)
    far_half = send(near, sibling)
    cot, cot_yours = halves(cotangent)
    act, adj, adj_longer, adj_long = middle(
        near, far_half, weight, cot, send(cot_yours, sibling)
    )

    direct = send(adj_longer, to_direct)
    near_one = send(
        adj_long, lambda c, j, z: (c if (c + z) % 2 or not four else c ^ 2, j, z ^ 1)
    )
    second = send(direct if four else adj_longer, to_second)
    grad = grad_block(scale, near, far_half, adj)
    far = send(near_one, to_far)
    near_choice = [("still", near_one)]
    if four:
        near_two = send(
            adj, lambda c, j, z: None if (c + z) % 2 else (c, j, z ^ 1)
        )
        near_choice.append(("relay", near_two))
    panels = [("self", [(None, adj)]), ("direct", [(None, direct)])]
    back_part = tile_product(panels, [set_first, set_rest], jnp.float32)
    panels = [("second", [(None, second)]), ("far", [(None, far)]), ("near", near_choice)]
    grad_got = send(grad, lambda c, j, z: (c, j, z ^ 1))
    back_part = tile_product(
        panels, [set_first, set_rest], jnp.bfloat16, back_part, [grad_got]
    )

    def deliver(value):
        one = send(value, lambda c, j, z: (c, j, z ^ 1) if j == z % 2 else (c, 1 - j, z))
        two = send(value, lambda c, j, z: None if j == z % 2 else (c, 1 - j, z ^ 1))
        return one, two

    grad = add_after([grad, grad_got], jnp.bfloat16, back_part)
    step = 1
    while step < shape[0]:
        got = send(grad, lambda c, j, z, s=step: (c ^ s, j, z))
        step *= 2
        if step < shape[0]:
            grad = add_after([grad, got], jnp.bfloat16)
        if step == 2:
            act_later, grad = lax.optimization_barrier((act, grad))
    act_parts = [act, *deliver(act_later)]
    back = add_after([back_part, send(back_part, across)], jnp.bfloat16, got)
    back_parts = [back, *deliver(back)]
    grad = add_after([grad, got], jnp.float32, back, *act_parts[1:])
    activated, weight_grad = gather_halves(act_parts, grad, send(grad, sibling))
    input_grad = final(back_parts, weight)
    return (activated, input_grad, weight_grad)


def solution(mesh):
    return jax.shard_map(
        per_device,
        mesh=mesh,
        in_specs=(
            P("rows", None),
            P(),
            P("rows", None),
            P("rows", None, "rep", None, None),
            P(None, "rows", None, "rep"),
            P("rows", None),
        ),
        out_specs=(P("rows", None), P("rows", None), P()),
        check_vma=False,
    )
```
